32 devices in a mesh: gx: 8 (over z, y), gy: 4 (over x, core).
Axes of the slice: x: 2, y: 2, z: 4, core: 2. Of those that a mesh axis runs over, the one named last changes fastest.
Arguments:
- atmospheric_constituents: float32 [5, 72, 32, 1024], P(None, None, 'gy', 'gx'), may hold values from 0.001 to 2
- thermal_ratio: float32 [72, 32, 1024], P(None, 'gy', 'gx'), may hold values from 0.5 to 1.5
- flow_velocity: float32 [2, 72, 32, 1024], P(None, None, 'gy', 'gx'), may hold values from -4 to 4
- solar_elevation_factor: float32 [32, 1024], P('gy', 'gx'), may hold values from 0.1 to 1
- ground_reflectivity: float32 [32, 1024], P('gy', 'gx'), may hold values from 0.05 to 0.6
- sunlit_indicator: int32 [32, 1024], P('gy', 'gx'), may hold values from 0 to 1, as said below
- molecular_optics_lookup: float32 [3, 112, 72], replicated, may hold values from 0.0001 to 0.05
- condensate_optics_lookup: float32 [7, 112], replicated, may hold values from 0.1 to 0.9
Outputs:
- radiative_warming_rate: float32 [72, 32, 1024], P(None, 'gy', 'gx')
- advected_thermal_ratio: float32 [72, 32, 1024], P(None, 'gy', 'gx')
The draws below stay inside these ranges and needn't reach their ends.
Inputs may be any that keep to these rules, and one draw needn't show every extreme that they name: `sunlit_indicator`: A column's flag and that of the column 512 further along the last dimension in the same row (round the end) sum to one.
All inputs are finite; a program needn't handle non-finite values.
Results may differ from the reference program's by a relative error of at most 0.0003.
Values sent between devices are 32-bit elements; how exact they have to be, the bound alone decides.
No kernel may reach another device: no remote copies, remote signals or barrier semaphores. Data moves between devices by JAX's collectives and lax.ppermute only.
A program may use at most 128 MiB of HBM per device.

```python
import math
import jax
import jax.numpy as jnp
import numpy as np
from jax import lax

LEVEL_NUMBER = 72
GPOINTS = 112
NODES = 4
POINTS_EASTWARD = 1024
POINTS_NORTHWARD = 32


def draw_sunlit_indicator(key, part):
    shift_key = jax.random.fold_in(key, 11)
    pick_key = jax.random.fold_in(key, 12)
    shift_phase = jax.random.randint(shift_key, (), 0, 2000)
    chance = jax.random.randint(pick_key, (POINTS_NORTHWARD, POINTS_EASTWARD // 2), 0, 1000)
    positions = jnp.arange(POINTS_EASTWARD // 2, dtype=jnp.int32)
    phase = (positions * 2000 // POINTS_EASTWARD + shift_phase) % 2000
    triangle = jnp.abs(phase - 1000)
    threshold = jnp.clip(2 * triangle - 500, 0, 1000)
    first_half = (chance < threshold[None, :]).astype(jnp.int32)
    return jnp.concatenate([first_half, 1 - first_half], axis=1)


def log_between(key, shape, lowest, highest):
    unit = jax.random.uniform(key, shape, jnp.float32)
    return jnp.exp(jnp.log(lowest) + unit * (jnp.log(highest) - jnp.log(lowest)))


def draw_atmospheric_constituents(key, part):
    gas_key = jax.random.fold_in(key, 21)
    column_key = jax.random.fold_in(key, 22)
    layer_key = jax.random.fold_in(key, 23)
    cloud_key = jax.random.fold_in(key, 24)
    trace_key = jax.random.fold_in(key, 25)
    gas_shape = (3, LEVEL_NUMBER, POINTS_NORTHWARD, POINTS_EASTWARD)
    water_shape = (2, LEVEL_NUMBER, POINTS_NORTHWARD, POINTS_EASTWARD)
    column_pick = jax.random.uniform(column_key, (POINTS_NORTHWARD, POINTS_EASTWARD), jnp.float32)
    layer_pick = jax.random.uniform(layer_key, water_shape, jnp.float32)
    gas_part = log_between(gas_key, gas_shape, 0.1, 2.0)
    cloud_part = log_between(cloud_key, water_shape, 0.1, 2.0)
    trace_part = log_between(trace_key, water_shape, 0.001, 0.02)
    cloudy = (column_pick < 0.35)[None, None, :, :] & (layer_pick < 0.3)
    water_part = jnp.where(cloudy, cloud_part, trace_part)
    return jnp.concatenate([gas_part, water_part], axis=0).astype(jnp.float32)


def levels(rng, shape, cuts, smallest, top_value):
    level, own = 1.0, jax.random.fold_in(rng, 6)
    for dim, parts in cuts:
        draws = jnp.exp(jax.random.uniform(jax.random.fold_in(own, dim), (parts,), jnp.float32, smallest / len(cuts), top_value / len(cuts)))
        level = level * jnp.repeat(draws, shape[dim] // parts).reshape([-1 if axis == dim else 1 for axis in range(len(shape))])
    return level


def normal_values(stream_key, extent, width, most, shards=(), kind=jnp.bfloat16):
    result = jax.random.normal(stream_key, extent, jnp.float32) * width
    if len(shards) > 0:
        result = levels(stream_key, extent, shards, -0.22, 0.18) * result
    return jnp.clip(result, min=-most, max=most).astype(kind)


def setup_inputs(seed: int = 0) -> dict:
    keys = jax.random.split(jax.random.key(seed), 9)
    return {
        "atmospheric_constituents": draw_atmospheric_constituents(jax.random.fold_in(keys[8], 71), 0),
        "thermal_ratio": jnp.clip(0.5 + 1.0 * jax.random.uniform(keys[1], (LEVEL_NUMBER, POINTS_NORTHWARD, POINTS_EASTWARD), jnp.float32) ** levels(keys[1], (LEVEL_NUMBER, POINTS_NORTHWARD, POINTS_EASTWARD), ((1, 4), (2, 8)), -0.2, 0.2), 0.5, 1.5),
        "flow_velocity": normal_values(keys[2], (2, LEVEL_NUMBER, POINTS_NORTHWARD, POINTS_EASTWARD), 1.0, 4.0, ((2, 4), (3, 8)), jnp.float32),
        "solar_elevation_factor": jnp.clip(0.1 + 0.9 * jax.random.uniform(keys[3], (POINTS_NORTHWARD, POINTS_EASTWARD), jnp.float32) ** levels(keys[3], (POINTS_NORTHWARD, POINTS_EASTWARD), ((0, 4), (1, 8)), -0.2, 0.2), 0.1, 1.0),
        "ground_reflectivity": jnp.clip(0.05 + 0.55 * jax.random.uniform(keys[4], (POINTS_NORTHWARD, POINTS_EASTWARD), jnp.float32) ** levels(keys[4], (POINTS_NORTHWARD, POINTS_EASTWARD), ((0, 4), (1, 8)), -0.2, 0.2), 0.05, 0.6),
        "sunlit_indicator": draw_sunlit_indicator(jax.random.fold_in(keys[8], 71), 0),
        "molecular_optics_lookup": jnp.clip(jnp.exp(jax.random.uniform(keys[6], (3, GPOINTS, LEVEL_NUMBER), jnp.float32, math.log(0.0001), math.log(0.05))), 0.0001, 0.05),
        "condensate_optics_lookup": jnp.clip(jax.random.uniform(keys[7], (7, GPOINTS), jnp.float32, 0.1, 0.9), 0.1, 0.9),
    }


TIME_INCREMENT = 0.05

def gll_derivative():
    points = np.array([-1.0, -1.0 / np.sqrt(5.0), 1.0 / np.sqrt(5.0), 1.0])
    legendre = 0.5 * (5.0 * points ** 3 - 3.0 * points)
    derivative = np.zeros((4, 4))
    for source in range(4):
        for target in range(4):
            if source != target:
                derivative[source, target] = legendre[source] / (legendre[target] * (points[source] - points[target]))
    derivative[0, 0] = -3.0
    derivative[3, 3] = 3.0
    return derivative

def depth_terms(coeffs, optics_table, columns):
    vapour, ozone_amount, thickness, liquid, frozen, temper = columns
    weighted = thickness * temper * temper
    gas_depth = coeffs[0][:, None] * (weighted * vapour)[None, :] + coeffs[1][:, None] * (weighted * ozone_amount)[None, :]
    rayleigh = coeffs[2][:, None] * thickness[None, :]
    liquid_depth = optics_table[0][:, None] * liquid[None, :]
    ice_depth = optics_table[3][:, None] * frozen[None, :]
    liquid_scatter = optics_table[1][:, None] * liquid_depth
    ice_scatter = optics_table[4][:, None] * ice_depth
    scattering = rayleigh + liquid_scatter + ice_scatter
    absorption = gas_depth + (liquid_depth - liquid_scatter) + (ice_depth - ice_scatter)
    forward = optics_table[2][:, None] * liquid_scatter + optics_table[5][:, None] * ice_scatter
    return (scattering, absorption, forward)

def layer_optics(coeffs, optics_table, columns, cosine):
    scattering, absorption, forward = depth_terms(coeffs, optics_table, columns)
    optical_depth = scattering + absorption
    single_albedo = scattering / optical_depth
    asymmetry = forward / scattering
    eigen_rate = 2.0 * jnp.sqrt(absorption / optical_depth * (1.0 - single_albedo * asymmetry))
    gamma_one = 2.0 - single_albedo * (1.0 + asymmetry)
    gamma_two = single_albedo * (1.0 - asymmetry)
    shrink = jnp.expm1(-eigen_rate * optical_depth)
    decay_factor = 1.0 + shrink
    spread = -shrink * (2.0 + shrink)
    denominator = gamma_one * spread + eigen_rate * (1.0 + decay_factor * decay_factor)
    reflect = gamma_two * spread / denominator
    transmit = 2.0 * eigen_rate * decay_factor / denominator
    beam_loss = jnp.expm1(-optical_depth / cosine[None, :])
    direct = 1.0 + beam_loss
    reflect_beam = -0.5 * single_albedo * beam_loss * (1.0 - asymmetry)
    transmit_beam = -0.5 * single_albedo * beam_loss * (1.0 + asymmetry)
    return (reflect, transmit, reflect_beam, transmit_beam, direct)

def pair_average(values, axis_index):
    count = values.shape[axis_index]
    before = jnp.roll(values, 1, axis_index)
    beyond = jnp.roll(values, -1, axis_index)
    node_index = jnp.arange(count) % NODES
    if axis_index == 2:
        node_index = node_index[None, None, :]
    else:
        node_index = node_index[None, :, None]
    return jnp.where(node_index == NODES - 1, 0.5 * (values + beyond), jnp.where(node_index == 0, 0.5 * (before + values), values))

def reference(atmospheric_constituents, thermal_ratio, flow_velocity, solar_elevation_factor, ground_reflectivity, sunlit_indicator, molecular_optics_lookup, condensate_optics_lookup):
    level_coeffs = jnp.moveaxis(molecular_optics_lookup, 2, 0)

    def warming_rate_each_line(inputs):
        state_row, temp_row, cosine, ground, day_flags = inputs

        def level_optics(per_level):
            return layer_optics(per_level[0], condensate_optics_lookup, per_level[1:], cosine)
        reflect, transmit, reflect_beam, transmit_beam, direct = lax.map(level_optics, (level_coeffs, state_row[0], state_row[1], state_row[2], state_row[3], state_row[4], temp_row))
        plane = reflect.shape[1:]

        def beam_step(beam_flux, direct_now):
            return (beam_flux * direct_now, beam_flux)
        surface_beam, beams = lax.scan(beam_step, jnp.broadcast_to(cosine[None, :], plane), direct)
        ground_full = jnp.broadcast_to(ground[None, :], plane)

        def below_step(below, per_level):
            albedo_below, source_below = below
            reflect_now, transmit_now, rbeam_now, tbeam_now, beam_now = per_level
            inverse = 1.0 / (1.0 - reflect_now * albedo_below)
            albedo_here = reflect_now + transmit_now * transmit_now * albedo_below * inverse
            source_here = beam_now * rbeam_now + transmit_now * inverse * (source_below + albedo_below * beam_now * tbeam_now)
            return ((albedo_here, source_here), (albedo_here, source_here, albedo_below, source_below))
        _, (albedos, sources, albedo_next, source_next) = lax.scan(below_step, (ground_full, ground_full * surface_beam), (reflect, transmit, reflect_beam, transmit_beam, beams), reverse=True)

        def down_step(diffuse_now, per_level):
            reflect_now, transmit_now, tbeam_now, beam_now, albedo_after, source_after = per_level
            diffuse_new = (transmit_now * diffuse_now + beam_now * tbeam_now + reflect_now * source_after) / (1.0 - reflect_now * albedo_after)
            return (diffuse_new, diffuse_new)
        _, diffuse = lax.scan(down_step, jnp.zeros_like(ground_full), (reflect, transmit, transmit_beam, beams, albedo_next, source_next))
        beam_all = jnp.concatenate([beams, surface_beam[None]], axis=0)
        albedo_all = jnp.concatenate([albedos, ground_full[None]], axis=0)
        source_all = jnp.concatenate([sources, (ground_full * surface_beam)[None]], axis=0)
        diffuse_all = jnp.concatenate([jnp.zeros_like(ground_full)[None], diffuse], axis=0)
        net_flux = beam_all + diffuse_all - (albedo_all * diffuse_all + source_all)
        interface = lax.optimization_barrier(jnp.sum(condensate_optics_lookup[6][None, :, None] * net_flux, axis=1))
        heating_row = LEVEL_NUMBER / GPOINTS * (interface[:-1] - interface[1:])
        return jnp.where(day_flags[None, :] == 1, heating_row, 0.0)
    warming_rate_lines = lax.map(warming_rate_each_line, (jnp.moveaxis(atmospheric_constituents, 2, 0), jnp.moveaxis(thermal_ratio, 1, 0), solar_elevation_factor, ground_reflectivity, sunlit_indicator))
    radiative_warming_rate = jnp.moveaxis(warming_rate_lines, 0, 1)
    derivative = jnp.asarray(gll_derivative(), jnp.float32)

    def warming_change_rate(field_now):
        level_sum_entries, rows_all, width_all = field_now.shape
        blocks_x = field_now.reshape(level_sum_entries, rows_all, width_all // NODES, NODES)
        slope_x = jnp.einsum('ij,lyej->lyei', derivative, blocks_x, precision=lax.Precision.HIGHEST).reshape(field_now.shape)
        blocks_y = field_now.reshape(level_sum_entries, rows_all // NODES, NODES, width_all)
        slope_y = jnp.einsum('ij,lejx->leix', derivative, blocks_y, precision=lax.Precision.HIGHEST).reshape(field_now.shape)
        raw = radiative_warming_rate - (flow_velocity[0] * slope_x + flow_velocity[1] * slope_y)
        return pair_average(pair_average(raw, 2), 1)
    opening_advection_part = thermal_ratio + TIME_INCREMENT * warming_change_rate(thermal_ratio)
    middle_advection_part = 0.75 * thermal_ratio + 0.25 * (opening_advection_part + TIME_INCREMENT * warming_change_rate(opening_advection_part))
    advected_thermal_ratio = 1.0 / 3.0 * thermal_ratio + 2.0 / 3.0 * (middle_advection_part + TIME_INCREMENT * warming_change_rate(middle_advection_part))
    return (radiative_warming_rate, advected_thermal_ratio)
```

```python
import functools

import jax
import jax.numpy as jnp
import numpy as np
from jax import lax
from jax.experimental import pallas as pl
from jax.experimental.pallas import tpu as pltpu
from jax.sharding import PartitionSpec as P

NODES = 4
TIME_INCREMENT = 0.05
LOG2E = 1.4426950408889634

GROUP = 8
TERMS = 16
QUANTITIES = 6


def padded_2(block, sides, width):
    for axis, dim in sides:
        count = lax.axis_size(axis)
        forward = [(i, i + 1) for i in range(count - 1)]
        forward.append((count - 1, 0))
        backward = [(target, source) for source, target in forward]
        low = lax.ppermute(
            lax.slice_in_dim(block, block.shape[dim] - width, None, axis=dim), axis, forward
        )
        high = lax.ppermute(lax.slice_in_dim(block, 0, width, axis=dim), axis, backward)
        block = jnp.concatenate([low, block, high], axis=dim)
    return block


def gll_derivative():
    points = np.array([-1.0, -1.0 / np.sqrt(5.0), 1.0 / np.sqrt(5.0), 1.0])
    legendre = 0.5 * (5.0 * points**3 - 3.0 * points)
    derivative = np.zeros((4, 4))
    for source in range(4):
        for target in range(4):
            if source != target:
                derivative[source, target] = legendre[source] / (
                    legendre[target] * (points[source] - points[target])
                )
    derivative[0, 0] = -3.0
    derivative[3, 3] = 3.0
    return derivative


def high_low(values):
    high = lax.reduce_precision(values, exponent_bits=8, mantissa_bits=7)
    return high.astype(jnp.bfloat16), (values - high).astype(jnp.bfloat16)


def optics_matrices(molecular, condensate):
    gpoints, level_count = molecular.shape[1:]
    groups = level_count // GROUP
    k0, k1, k2 = molecular
    w = condensate[:, :, None]
    zero = jnp.zeros((gpoints, level_count), jnp.float32)
    full = functools.partial(jnp.broadcast_to, shape=(gpoints, level_count))
    ls, li = w[0] * w[1], w[3] * w[4]
    la, ia = w[0] * (1.0 - w[1]), w[3] * (1.0 - w[4])
    absorption = (k0, k1, zero, full(la), full(ia))
    away = (zero, zero, k2, full(ls * (1.0 - w[2])), full(li * (1.0 - w[5])))
    along = (zero, zero, k2, full(ls * (1.0 + w[2])), full(li * (1.0 + w[5])))
    depth = (k0, k1, k2, full(w[0]), full(w[3]))
    rows = [
        absorption,
        [a + b for a, b in zip(absorption, away)],
        [2.0 * a + b for a, b in zip(absorption, away)],
        [0.5 * b for b in away],
        [0.5 * b for b in along],
        depth,
        [-LOG2E * b for b in depth],
    ]
    table = jnp.stack([jnp.stack(list(row)) for row in rows])
    high, low = high_low(table)
    empty = jnp.zeros_like(high[:, :1])
    terms = jnp.concatenate([high, low, high, empty], axis=1)
    terms = terms.reshape(len(rows), TERMS, gpoints, groups, GROUP)
    terms = terms.transpose(3, 0, 2, 4, 1).reshape(groups, len(rows) * gpoints, GROUP * TERMS)
    return terms[:, : QUANTITIES * gpoints], terms[:, QUANTITIES * gpoints :]


def radiation_kernel(
    state_ref, temp_ref, cosine_ref, ground_ref, day_ref, optics_ref, slant_ref, weight_ref,
    heat_ref,
    terms_ref, slant_terms_ref, right_ref, slant_right_ref, beam_ref, gain_ref, offset_ref,
    clear_ref, open_ref, partial_ref,
):
    level_count = temp_ref.shape[0]
    gpoints = weight_ref.shape[0]
    groups = level_count // GROUP
    lanes = temp_ref.shape[2]
    row = pl.program_id(0)
    rows = pl.num_programs(0)

    @pl.when(row == 0)
    def prepare():
        right_ref[...] = jnp.zeros_like(right_ref)
        slant_right_ref[...] = jnp.zeros_like(slant_right_ref)
        slant = 1.0 / cosine_ref[...]

        def level(l, carry):
            thickness = state_ref[2, l]
            weighted = thickness * temp_ref[l] * temp_ref[l]
            values = (
                weighted * state_ref[0, l], weighted * state_ref[1, l], thickness,
                state_ref[3, l], state_ref[4, l],
            )
            for ref, scale in ((terms_ref, None), (slant_terms_ref, slant)):
                for k, value in enumerate(values):
                    value = value if scale is None else value * scale
                    high = value.astype(jnp.bfloat16).astype(jnp.float32)
                    for place, part in ((k, high), (k + 5, high), (k + 10, value - high)):
                        start = pl.multiple_of((l * TERMS + place) * 8, 8)
                        ref[pl.ds(start, 8), :] = part
                ref[pl.ds(pl.multiple_of((l * TERMS + 15) * 8, 8), 8), :] = jnp.zeros_like(slant)
            return carry

        lax.fori_loop(0, level_count, level, 0)

    def place_terms(group, carry):
        for j in range(GROUP):
            start = (group * GROUP + j) * TERMS * 8 + row
            for source, target in ((terms_ref, right_ref), (slant_terms_ref, slant_right_ref)):
                tile = source[pl.ds(start, TERMS, stride=8), :]
                target[group, TERMS * j : TERMS * (j + 1), lanes * j : lanes * (j + 1)] = (
                    tile.astype(jnp.bfloat16)
                )
        return carry

    lax.fori_loop(0, groups, place_terms, 0)

    top = weight_ref[...] * cosine_ref[pl.ds(row, 1), :]
    beam_ref[0] = top

    def beam_group(group, beam):
        exponents = jnp.dot(
            slant_ref[group], slant_right_ref[group], preferred_element_type=jnp.float32
        )
        for j in range(GROUP):
            beam = beam * jnp.exp2(exponents[:, lanes * j : lanes * (j + 1)])
            beam_ref[group * GROUP + j + 1] = beam
        return beam

    surface = lax.fori_loop(0, groups, beam_group, top)
    albedo = jnp.broadcast_to(ground_ref[pl.ds(row, 1), :], surface.shape)

    def below_group(step, carry):
        group = groups - 1 - step
        albedo, source, beam_below = carry
        for pair in reversed(range(GROUP // 2)):
            both = jnp.dot(
                optics_ref[group],
                right_ref[group, :, 2 * pair * lanes : 2 * (pair + 1) * lanes],
                preferred_element_type=jnp.float32,
            )
            for half in (1, 0):
                level = group * GROUP + 2 * pair + half
                part = both[:, half * lanes : (half + 1) * lanes]
                a, b, ab, away, along, depth = [
                    part[n * gpoints : (n + 1) * gpoints] for n in range(QUANTITIES)
                ]
                square = a * b
                inverse_root = lax.rsqrt(square)
                h = jnp.tanh(square * inverse_root)
                g = h * inverse_root
                spread = ab * g
                differ = (away + away) * g
                h2 = h * h
                one = 1.0 + h2
                inverse = 1.0 / ((one + spread) - differ * albedo)
                through = 1.0 - h2
                beam = beam_ref[level]
                factor = (beam - beam_below) * (1.0 / depth)
                up, down = factor * away, factor * along
                push = inverse * (source + albedo * down)
                gain_ref[level] = through * inverse
                offset_ref[level] = down + differ * push
                open_ref[level] = 1.0 - albedo
                clear_ref[level] = beam_below - source
                albedo = (differ + (one - spread) * albedo) * inverse
                source = up + through * push
                beam_below = beam
        return (albedo, source, beam_below)

    albedo, source, beam = lax.fori_loop(
        0, groups, below_group, (albedo, albedo * surface, surface)
    )

    def folded(net):
        return sum(net[8 * k : 8 * (k + 1)] for k in range(gpoints // 8))

    partial_ref[pl.ds(pl.multiple_of(row * 8, 8), 8), :] = folded(beam - source)

    def down_group(group, diffuse):
        for j in range(GROUP):
            level = group * GROUP + j
            diffuse = gain_ref[level] * diffuse + offset_ref[level]
            net = folded(clear_ref[level] + open_ref[level] * diffuse)
            start = pl.multiple_of(((level + 1) * rows + row) * 8, 8)
            partial_ref[pl.ds(start, 8), :] = net
        return diffuse

    lax.fori_loop(0, groups, down_group, jnp.zeros_like(surface))

    @pl.when(row == rows - 1)
    def finish():
        scale = jnp.where(day_ref[...] == 1, level_count / gpoints, 0.0)

        def flux(level):
            start = level * rows * 8
            return sum(
                partial_ref[pl.ds(start + k, rows, stride=8), :] for k in range(8)
            )

        def level_heat(level, upper):
            lower = flux(level + 1)
            heat_ref[level] = jnp.where(scale > 0.0, scale * (upper - lower), 0.0)
            return lower

        lax.fori_loop(0, level_count, level_heat, flux(0))


def radiation(state, temper, cosine, ground, day, molecular, condensate):
    level_count, rows, lanes = temper.shape
    gpoints = molecular.shape[1]
    optics, slant = optics_matrices(molecular, condensate)
    weight = jnp.broadcast_to(condensate[6][:, None], (gpoints, lanes))
    groups = level_count // GROUP
    full = (level_count, gpoints, lanes)
    whole = pl.BlockSpec(memory_space=pltpu.VMEM)
    return pl.pallas_call(
        radiation_kernel,
        out_shape=jax.ShapeDtypeStruct(temper.shape, jnp.float32),
        grid=(rows,),
        in_specs=[whole] * 8,
        out_specs=whole,
        scratch_shapes=[
            pltpu.VMEM((level_count * TERMS * 8, lanes), jnp.float32),
            pltpu.VMEM((level_count * TERMS * 8, lanes), jnp.float32),
            pltpu.VMEM((groups, GROUP * TERMS, GROUP * lanes), jnp.bfloat16),
            pltpu.VMEM((groups, GROUP * TERMS, GROUP * lanes), jnp.bfloat16),
            pltpu.VMEM((level_count + 1, gpoints, lanes), jnp.float32),
            pltpu.VMEM(full, jnp.float32),
            pltpu.VMEM(full, jnp.float32),
            pltpu.VMEM(full, jnp.float32),
            pltpu.VMEM(full, jnp.float32),
            pltpu.VMEM(((level_count + 1) * rows * 8, lanes), jnp.float32),
        ],
        compiler_params=pltpu.CompilerParams(vmem_limit_bytes=60 * 1024 * 1024),
        name="radiation",
    )(state, temper, cosine, ground, day, optics, slant, weight)


def pair_average(values, before, beyond, node_index):
    return jnp.where(
        node_index == NODES - 1,
        0.5 * (values + beyond),
        jnp.where(node_index == 0, 0.5 * (before + values), values),
    )


def local(
    atmospheric_constituents,
    thermal_ratio,
    flow_velocity,
    solar_elevation_factor,
    ground_reflectivity,
    sunlit_indicator,
    molecular_optics_lookup,
    condensate_optics_lookup,
):
    level_count, line_count, span = thermal_ratio.shape
    radiative_warming_rate = radiation(
        atmospheric_constituents, thermal_ratio, solar_elevation_factor, ground_reflectivity,
        sunlit_indicator, molecular_optics_lookup, condensate_optics_lookup,
    )
    derivative = gll_derivative()
    x_derivative = jnp.asarray(np.kron(np.eye(span // NODES), derivative).T, jnp.float32)
    y_derivative = jnp.asarray(np.kron(np.eye(line_count // NODES), derivative), jnp.float32)
    x_nodes = (jnp.arange(span) % NODES)[None, None, :]
    y_nodes = (jnp.arange(line_count) % NODES)[None, :, None]

    def averaged(values):
        padded = padded_2(values, (("gx", 2),), 1)
        along_x = pair_average(values, padded[:, :, :-2], padded[:, :, 2:], x_nodes)
        padded_y = padded_2(along_x, (("gy", 1),), 1)
        return pair_average(along_x, padded_y[:, :-2], padded_y[:, 2:], y_nodes)

    def warming_change_rate(field_now):
        slope_x = jnp.dot(
            field_now.reshape(-1, span), x_derivative, precision=lax.Precision.HIGHEST
        ).reshape(field_now.shape)
        slope_y = jnp.einsum(
            "ij,ljx->lix", y_derivative, field_now, precision=lax.Precision.HIGHEST
        )
        return averaged(
            radiative_warming_rate - (flow_velocity[0] * slope_x + flow_velocity[1] * slope_y)
        )

    opening = thermal_ratio + TIME_INCREMENT * warming_change_rate(thermal_ratio)
    middle = 0.75 * thermal_ratio + 0.25 * (
        opening + TIME_INCREMENT * warming_change_rate(opening)
    )
    advected_thermal_ratio = 1.0 / 3.0 * thermal_ratio + 2.0 / 3.0 * (
        middle + TIME_INCREMENT * warming_change_rate(middle)
    )
    return (radiative_warming_rate, advected_thermal_ratio)


def solution(mesh):
    in_specs = (
        P(None, None, "gy", "gx"),
        P(None, "gy", "gx"),
        P(None, None, "gy", "gx"),
        P("gy", "gx"),
        P("gy", "gx"),
        P("gy", "gx"),
        P(),
        P(),
    )
    out_specs = (P(None, "gy", "gx"), P(None, "gy", "gx"))
    return jax.shard_map(local, mesh=mesh, in_specs=in_specs, out_specs=out_specs, check_vma=False)
```

```python
import functools

import jax
import jax.numpy as jnp
import numpy as np
from jax import lax
from jax.experimental import pallas as pl
from jax.experimental.pallas import tpu as pltpu
from jax.sharding import PartitionSpec as P

NODES = 4
TIME_INCREMENT = 0.05
EDGE = 16
LOG2E = 1.4426950408889634

GROUP = 8
TERMS = 16
BLOCK = 4
QUANTITIES = 3


def gll_derivative():
    points = np.array([-1.0, -1.0 / np.sqrt(5.0), 1.0 / np.sqrt(5.0), 1.0])
    legendre = 0.5 * (5.0 * points**3 - 3.0 * points)
    derivative = np.zeros((4, 4))
    for source in range(4):
        for target in range(4):
            if source != target:
                derivative[source, target] = legendre[source] / (
                    legendre[target] * (points[source] - points[target])
                )
    derivative[0, 0] = -3.0
    derivative[3, 3] = 3.0
    return derivative


def high_low(values):
    high = values.astype(jnp.bfloat16)
    return high, (values - high.astype(jnp.float32)).astype(jnp.bfloat16)


def optics_matrices(molecular_ref, table_ref, optics_ref):
    gpoints, level_count = molecular_ref.shape[1:]
    groups = level_count // GROUP
    width = GROUP * TERMS
    level = lax.broadcasted_iota(jnp.int32, (level_count, groups * width), 0)
    lane = lax.broadcasted_iota(jnp.int32, (level_count, groups * width), 1)
    here = level == lane // TERMS
    term = lane % TERMS
    gases = []
    for k in range(3):
        high, low = high_low(molecular_ref[k])
        spread = [
            jnp.where(here & chosen, 1.0, 0.0).astype(jnp.bfloat16)
            for chosen in ((term == k) | (term == k + 10), term == k + 5)
        ]
        gases.append(
            jnp.dot(high, spread[0], preferred_element_type=jnp.float32)
            + jnp.dot(low, spread[1], preferred_element_type=jnp.float32)
        )
    w = [table_ref[:, n : n + 1] for n in range(6)]
    ls, li = w[0] * w[1], w[3] * w[4]
    la, ia = w[0] * (1.0 - w[1]), w[3] * (1.0 - w[4])
    term = lax.broadcasted_iota(jnp.int32, (gpoints, width), 1) % TERMS

    def water(*values):
        total = jnp.zeros((gpoints, width), jnp.float32)
        for k, value in zip((3, 4), values):
            high = value.astype(jnp.bfloat16).astype(jnp.float32)
            total = jnp.where((term == k) | (term == k + 10), high, total)
            total = jnp.where(term == k + 5, value - high, total)
        return total

    absorbed = gases[0] + gases[1]
    gas = absorbed + gases[2]
    pairs = (
        (absorbed, water(la, ia)),
        (gas, water(la + ls * (1.0 - w[2]), ia + li * (1.0 - w[5]))),
        (gas + gas, water(2.0 * w[0], 2.0 * w[3])),
    )
    for n, (values, constant) in enumerate(pairs):
        for group in range(groups):
            optics_ref[group, n * gpoints : (n + 1) * gpoints, :] = (
                values[:, group * width : (group + 1) * width] + constant
            ).astype(jnp.bfloat16)


def pack_edges(source_ref, base, part, first_ref, last_ref):
    lanes = source_ref.shape[-1]
    lane = lax.broadcasted_iota(jnp.int32, (8, lanes), 1)
    first = last = jnp.zeros((8, lanes), jnp.float32)
    for j in range(8):
        tile = source_ref[base * 8 + j]
        chosen = lane // EDGE == j
        first = jnp.where(chosen, tile if j == 0 else pltpu.roll(tile, EDGE * j, 1), first)
        turn = (EDGE * (j + 1)) % lanes
        last = jnp.where(chosen, tile if turn == 0 else pltpu.roll(tile, turn, 1), last)
    first_ref[part] = first
    last_ref[part] = last


def radiation_kernel(
    state_ref, temp_ref, cosine_ref, ground_ref, day_ref, molecular_ref, table_ref,
    heat_ref, first_ref, last_ref,
    optics_ref, weight_ref, terms_ref, right_ref, depths_ref, gain_ref, offset_ref, direct_ref, partial_ref, ratio_ref,
    source_ref, slant_ref,
):
    level_count = temp_ref.shape[0]
    gpoints = molecular_ref.shape[1]
    lanes = temp_ref.shape[2]
    row = pl.program_id(0)
    rows = pl.num_programs(0)
    blocks = level_count // BLOCK

    @pl.when(row == 0)
    def prepare():
        optics_matrices(molecular_ref, table_ref, optics_ref)
        weight_ref[...] = jnp.broadcast_to(table_ref[:, 6:7], (gpoints, lanes))
        right_ref[...] = jnp.zeros_like(right_ref)

        def level(l, carry):
            thickness = state_ref[2, l]
            weighted = thickness * temp_ref[l] * temp_ref[l]
            values = (
                weighted * state_ref[0, l], weighted * state_ref[1, l], thickness,
                state_ref[3, l], state_ref[4, l],
            )
            for k, value in enumerate(values):
                high = value.astype(jnp.bfloat16).astype(jnp.float32)
                for place, part in ((k, high), (k + 5, high), (k + 10, value - high)):
                    start = pl.multiple_of((l * TERMS + place) * 8, 8)
                    terms_ref[pl.ds(start, 8), :] = part
            last = pl.multiple_of((l * TERMS + 15) * 8, 8)
            terms_ref[pl.ds(last, 8), :] = jnp.zeros((8, lanes), jnp.float32)
            return carry

        lax.fori_loop(0, level_count, level, 0)

    def place_group(group, carry):
        for j in range(GROUP):
            start = (group * GROUP + j) * TERMS * 8 + row
            tile = terms_ref[pl.ds(start, TERMS, stride=8), :].astype(jnp.bfloat16)
            half = lanes * (j % 2)
            pair = group * (GROUP // 2) + j // 2
            right_ref[pair, TERMS * j : TERMS * (j + 1), half : half + lanes] = tile
        return carry

    lax.fori_loop(0, level_count // GROUP, place_group, 0)

    cosine = cosine_ref[pl.ds(row, 1), :]
    ground = ground_ref[pl.ds(row, 1), :]
    slant_ref[...] = jnp.broadcast_to((-0.5 * LOG2E) / cosine, (8, lanes))

    def over_rows(values):
        return jnp.broadcast_to(values[None], (gpoints // 8, 8, lanes)).reshape(gpoints, lanes)

    clear = 1.0 / (1.0 - ground)
    ratio_ref[...] = over_rows(jnp.broadcast_to((1.0 + ground) * clear, (8, lanes)))
    source_ref[...] = over_rows(jnp.broadcast_to(2.0 * ground * clear, (8, lanes)))

    def fill(block):
        for p in range(BLOCK // 2):
            pair = block * (BLOCK // 2) + p
            depths_ref[p] = jnp.dot(
                optics_ref[pair // (GROUP // 2)], right_ref[pair],
                preferred_element_type=jnp.float32,
            )

    def below_block(step, carry):
        block = blocks - 1 - step
        ratio, source = ratio_ref[...], source_ref[...]
        slant = over_rows(slant_ref[...])
        for j in reversed(range(BLOCK)):
            level = block * BLOCK + j
            part = depths_ref.at[j // 2, :, (j % 2) * lanes : (j % 2 + 1) * lanes]
            a, b, depth = [part[n * gpoints : (n + 1) * gpoints] for n in range(QUANTITIES)]
            away = b - a
            along = (depth - a) - b
            square = a * b
            inverse_root = lax.rsqrt(square)
            h = jnp.tanh(square * inverse_root)
            g = h * inverse_root
            g = g + g
            s, p = a * g, b * g
            h2 = h * h
            one = 1.0 + h2
            through = 1.0 - h2
            inverse = 1.0 / (one + s * ratio)
            direct = jnp.exp2(depth * slant)
            factor = (1.0 - direct) * (1.0 / depth)
            up, down = factor * away, factor * along
            push = inverse * (direct * source + (ratio - 1.0) * down)
            ratio = (one * ratio + p) * inverse
            gain = through * inverse
            source = through * push + (ratio + 1.0) * up
            gain_ref[level] = gain
            offset_ref[level] = (gain * up + down) - s * push
            direct_ref[level] = direct
        ratio_ref[...] = ratio
        source_ref[...] = source
        fill(jnp.maximum(block - 1, 0))
        return carry

    fill(blocks - 1)
    lax.fori_loop(0, blocks, below_block, 0)

    def folded(net):
        return sum(net[8 * k : 8 * (k + 1)] for k in range(gpoints // 8))

    beam = weight_ref[...] * cosine
    net = -(source_ref[...] * beam) / (1.0 + ratio_ref[...])
    partial_ref[pl.ds(pl.multiple_of(row * 8, 8), 8), :] = folded(beam) + folded(net)

    def down_group(group, carry):
        net, beam = carry
        for j in range(GROUP):
            level = group * GROUP + j
            net = gain_ref[level] * net + offset_ref[level] * beam
            beam = beam * direct_ref[level]
            start = pl.multiple_of(((level + 1) * rows + row) * 8, 8)
            partial_ref[pl.ds(start, 8), :] = folded(net) + folded(beam)
        return (net, beam)

    lax.fori_loop(0, level_count // GROUP, down_group, (net, beam))

    @pl.when(row == rows - 1)
    def finish():
        scale = jnp.where(day_ref[...] == 1, level_count / gpoints, 0.0)

        def flux(level):
            start = level * rows * 8
            return sum(
                partial_ref[pl.ds(start + k, rows, stride=8), :] for k in range(8)
            )

        def level_heat(level, upper):
            lower = flux(level + 1)
            heat_ref[level] = jnp.where(scale > 0.0, scale * (upper - lower), 0.0)
            return lower

        lax.fori_loop(0, level_count, level_heat, flux(0))

        def pack(part, carry):
            pack_edges(heat_ref, part, part, first_ref, last_ref)
            return carry

        lax.fori_loop(0, level_count // 8, pack, 0)


def radiation(state, temper, cosine, ground, day, molecular, condensate):
    level_count, rows, lanes = temper.shape
    gpoints = molecular.shape[1]
    full = pltpu.VMEM((level_count, gpoints, lanes), jnp.float32)
    plane = pltpu.VMEM((gpoints, lanes), jnp.float32)
    whole = pl.BlockSpec(memory_space=pltpu.VMEM)
    edge = jax.ShapeDtypeStruct((level_count // 8, rows, lanes), jnp.float32)
    return pl.pallas_call(
        radiation_kernel,
        out_shape=(jax.ShapeDtypeStruct(temper.shape, jnp.float32), edge, edge),
        grid=(rows,),
        in_specs=[whole] * 7,
        out_specs=(whole,) * 3,
        scratch_shapes=[
            pltpu.VMEM((level_count // GROUP, QUANTITIES * gpoints, GROUP * TERMS), jnp.bfloat16),
            plane,
            pltpu.VMEM((level_count * TERMS * 8, lanes), jnp.float32),
            pltpu.VMEM((level_count // 2, GROUP * TERMS, 2 * lanes), jnp.bfloat16),
            pltpu.VMEM((BLOCK // 2, QUANTITIES * gpoints, 2 * lanes), jnp.float32),
            full, full, full,
            pltpu.VMEM(((level_count + 1) * rows * 8, lanes), jnp.float32),
            plane, plane,
            pltpu.VMEM((8, lanes), jnp.float32),
        ],
        compiler_params=pltpu.CompilerParams(vmem_limit_bytes=60 * 1024 * 1024),
        cost_estimate=pl.CostEstimate(
            flops=45 * level_count * gpoints * rows * lanes, bytes_accessed=4 * 8 * temper.size,
            transcendentals=5 * level_count * gpoints * rows * lanes,
        ),
        name="radiation",
    )(state, temper, cosine, ground, day, molecular, condensate.T)


def pack_kernel(temp_ref, flow_ref, first_ref, last_ref):
    parts = temp_ref.shape[0] // 8
    for n, ref in enumerate((temp_ref, flow_ref.at[0], flow_ref.at[1])):
        def pack(part, carry, ref=ref, n=n):
            pack_edges(ref, part, n * parts + part, first_ref, last_ref)
            return carry

        lax.fori_loop(0, parts, pack, 0)


def packed_edges(temper, flow):
    level_count, rows, lanes = temper.shape
    whole = pl.BlockSpec(memory_space=pltpu.VMEM)
    edge = jax.ShapeDtypeStruct((3 * level_count // 8, rows, lanes), jnp.float32)
    return pl.pallas_call(
        pack_kernel, out_shape=(edge, edge), in_specs=[whole] * 2, out_specs=(whole, whole),
        name="pack",
    )(temper, flow)


def node_coefficients(shape, axis):
    derivative = gll_derivative()
    node = lax.broadcasted_iota(jnp.int32, shape, axis) % NODES
    result = {}
    for shift in range(1 - NODES, NODES):
        value = jnp.zeros(shape, jnp.float32)
        for i in range(NODES):
            if 0 <= i + shift < NODES and derivative[i, i + shift] != 0.0:
                value = jnp.where(node == i, np.float32(derivative[i, i + shift]), value)
        result[shift] = value
    return result


def slope(tile, weights, axis):
    size = tile.shape[axis]
    total = weights[0] * tile
    for shift, weight in weights.items():
        if shift:
            total = total + weight * pltpu.roll(tile, -shift % size, axis)
    return total


def along_x(main, side):
    lane = lax.broadcasted_iota(jnp.int32, main.shape, 1)
    lanes = main.shape[1]
    node = lane % NODES
    before = [pltpu.roll(tile, 1, 1) for tile in (main, side)]
    beyond = [pltpu.roll(tile, lanes - 1, 1) for tile in (main, side)]
    results = []
    for n, tile in enumerate((main, side)):
        back = jnp.where(lane == 0, before[1 - n], before[n])
        ahead = jnp.where(lane == lanes - 1, beyond[1 - n], beyond[n])
        other = jnp.where(node == NODES - 1, ahead, jnp.where(node == 0, back, tile))
        results.append(0.5 * (tile + other))
    return results


def along_y(tile, below, above):
    row = lax.broadcasted_iota(jnp.int32, tile.shape, 0)
    rows = tile.shape[0]
    node = row % NODES
    back = jnp.where(row == 0, below, pltpu.roll(tile, 1, 0))
    ahead = jnp.where(row == rows - 1, above, pltpu.roll(tile, rows - 1, 0))
    other = jnp.where(node == NODES - 1, ahead, jnp.where(node == 0, back, tile))
    return 0.5 * (tile + other)


def side_tile(after_ref, before_ref, part, j):
    lanes = after_ref.shape[-1]
    lane = lax.broadcasted_iota(jnp.int32, after_ref.shape[1:], 1)
    after, before = after_ref[part], before_ref[part]
    turn = (lanes - EDGE * j) % lanes
    after = after if turn == 0 else pltpu.roll(after, turn, 1)
    turn = (2 * lanes - EDGE * (j + 1)) % lanes
    before = before if turn == 0 else pltpu.roll(before, turn, 1)
    return jnp.where(lane < EDGE, after, jnp.where(lane >= lanes - EDGE, before, 0.0))


def write_lines(field_ref, low_ref, high_ref, level_count, rows):
    for n in range(2):
        start = n * level_count * rows
        low_ref[n] = field_ref[pl.ds(start, level_count, stride=rows), :]
        high_ref[n] = field_ref[pl.ds(start + rows - 1, level_count, stride=rows), :]


def first_stage_kernel(
    heat_ref, temp_ref, flow_ref, after_ref, before_ref, heat_after_ref, heat_before_ref,
    out_ref, low_ref, high_ref, flow_side_ref,
):
    level_count, rows, lanes = temp_ref.shape
    parts = level_count // 8
    x_weights = node_coefficients((rows, lanes), 1)
    y_weights = node_coefficients((rows, lanes), 0)

    def eight(part, carry):
        for j in range(8):
            level = part * 8 + j
            sides = [side_tile(after_ref, before_ref, n * parts + part, j) for n in range(3)]
            heat_side = side_tile(heat_after_ref, heat_before_ref, part, j)
            flow_side_ref[0, level], flow_side_ref[1, level] = sides[1], sides[2]
            raw = []
            for t, u, v, heat in (
                (temp_ref[level], flow_ref[0, level], flow_ref[1, level], heat_ref[level]),
                (*sides, heat_side),
            ):
                change = heat - (u * slope(t, x_weights, 1) + v * slope(t, y_weights, 0))
                raw.append(TIME_INCREMENT * change)
            for n, tile in enumerate(along_x(*raw)):
                start = pl.multiple_of((n * level_count + level) * rows, 8)
                out_ref[pl.ds(start, rows), :] = tile
        return carry

    lax.fori_loop(0, parts, eight, 0)
    write_lines(out_ref, low_ref, high_ref, level_count, rows)


def next_stage_kernel(
    share, field_ref, below_ref, above_ref, flow_ref, flow_side_ref, sum_ref,
    out_ref, low_ref, high_ref, total_ref,
):
    level_count, rows, lanes = flow_ref.shape[1:]
    x_weights = node_coefficients((rows, lanes), 1)
    y_weights = node_coefficients((rows, lanes), 0)

    def eight(part, carry):
        for j in range(8):
            level = part * 8 + j
            raw = []
            for n, flows in enumerate((flow_ref, flow_side_ref)):
                start = pl.multiple_of((n * level_count + level) * rows, 8)
                tile = along_y(
                    field_ref[pl.ds(start, rows), :],
                    below_ref[n, pl.ds(level, 1), :], above_ref[n, pl.ds(level, 1), :],
                )
                if n == 0:
                    total_ref[level] = sum_ref[level] + share * tile
                change = flows[0, level] * slope(tile, x_weights, 1)
                change = change + flows[1, level] * slope(tile, y_weights, 0)
                raw.append(-TIME_INCREMENT * change)
            for n, tile in enumerate(along_x(*raw)):
                start = pl.multiple_of((n * level_count + level) * rows, 8)
                out_ref[pl.ds(start, rows), :] = tile
        return carry

    lax.fori_loop(0, level_count // 8, eight, 0)
    write_lines(out_ref, low_ref, high_ref, level_count, rows)


def last_kernel(share, field_ref, below_ref, above_ref, sum_ref, total_ref):
    level_count, rows, lanes = sum_ref.shape

    def eight(part, carry):
        for j in range(8):
            level = part * 8 + j
            start = pl.multiple_of(level * rows, 8)
            tile = along_y(
                field_ref[pl.ds(start, rows), :],
                below_ref[0, pl.ds(level, 1), :], above_ref[0, pl.ds(level, 1), :],
            )
            total_ref[level] = sum_ref[level] + share * tile
        return carry

    lax.fori_loop(0, level_count // 8, eight, 0)


def shifted(value, axis, steps):
    count = lax.axis_size(axis)
    return lax.ppermute(value, axis, [(i, (i + steps) % count) for i in range(count)])


def local(
    atmospheric_constituents,
    thermal_ratio,
    flow_velocity,
    solar_elevation_factor,
    ground_reflectivity,
    sunlit_indicator,
    molecular_optics_lookup,
    condensate_optics_lookup,
):
    level_count, rows, lanes = thermal_ratio.shape
    field = jax.ShapeDtypeStruct(thermal_ratio.shape, jnp.float32)
    wide = jax.ShapeDtypeStruct((2 * level_count * rows, lanes), jnp.float32)
    line = jax.ShapeDtypeStruct((2, level_count, lanes), jnp.float32)
    whole = pl.BlockSpec(memory_space=pltpu.VMEM)

    def call(kernel, name, outs, *values):
        return pl.pallas_call(
            kernel, out_shape=outs, in_specs=[whole] * len(values),
            out_specs=jax.tree.map(lambda _: whole, outs), name=name,
        )(*values)

    first, last = packed_edges(thermal_ratio, flow_velocity)
    after, before = shifted(first, "gx", -1), shifted(last, "gx", 1)
    heat, heat_first, heat_last = radiation(
        atmospheric_constituents, thermal_ratio, solar_elevation_factor, ground_reflectivity,
        sunlit_indicator, molecular_optics_lookup, condensate_optics_lookup,
    )
    heat_after, heat_before = shifted(heat_first, "gx", -1), shifted(heat_last, "gx", 1)
    flow_side = jax.ShapeDtypeStruct(flow_velocity.shape, jnp.float32)
    wave, low, high, flow_side = call(
        first_stage_kernel, "first_stage", (wide, line, line, flow_side),
        heat, thermal_ratio, flow_velocity, after, before, heat_after, heat_before,
    )
    total = thermal_ratio
    for name, share in (("second_stage", 1.0), ("third_stage", 0.5)):
        below, above = shifted(high, "gy", 1), shifted(low, "gy", -1)
        wave, low, high, total = call(
            functools.partial(next_stage_kernel, share), name, (wide, line, line, field),
            wave, below, above, flow_velocity, flow_side, total,
        )
    below, above = shifted(high, "gy", 1), shifted(low, "gy", -1)
    total = call(
        functools.partial(last_kernel, 1.0 / 6.0), "last_stage", field, wave, below, above, total
    )
    return (heat, total)


def solution(mesh):
    in_specs = (
        P(None, None, "gy", "gx"),
        P(None, "gy", "gx"),
        P(None, None, "gy", "gx"),
        P("gy", "gx"),
        P("gy", "gx"),
        P("gy", "gx"),
        P(),
        P(),
    )
    out_specs = (P(None, "gy", "gx"), P(None, "gy", "gx"))
    return jax.shard_map(local, mesh=mesh, in_specs=in_specs, out_specs=out_specs, check_vma=False)
```

```python
import functools

import jax
import jax.numpy as jnp
import numpy as np
from jax import lax
from jax.experimental import pallas as pl
from jax.experimental.pallas import tpu as pltpu
from jax.sharding import PartitionSpec as P

NODES = 4
TIME_INCREMENT = 0.05
EDGE = 16
ROWS = 8
LOG2E = 1.4426950408889634

GROUP = 8
TERMS = 16
BLOCK = 4
QUANTITIES = 3


def gll_derivative():
    points = np.array([-1.0, -1.0 / np.sqrt(5.0), 1.0 / np.sqrt(5.0), 1.0])
    legendre = 0.5 * (5.0 * points**3 - 3.0 * points)
    derivative = np.zeros((4, 4))
    for source in range(4):
        for target in range(4):
            if source != target:
                derivative[source, target] = legendre[source] / (
                    legendre[target] * (points[source] - points[target])
                )
    derivative[0, 0] = -3.0
    derivative[3, 3] = 3.0
    return derivative


def high_low(values):
    high = values.astype(jnp.bfloat16)
    return high, (values - high.astype(jnp.float32)).astype(jnp.bfloat16)


def across(left, right, precision=None):
    return lax.dot_general(
        left, right, (((0,), (0,)), ((), ())), precision=precision,
        preferred_element_type=jnp.float32,
    )


def optics_matrices(molecular_ref, table_ref, optics_ref, weight_ref):
    level_count, gpoints = molecular_ref.shape[1:]
    groups = level_count // GROUP
    width = GROUP * TERMS
    level = lax.broadcasted_iota(jnp.int32, (level_count, groups * width), 0)
    lane = lax.broadcasted_iota(jnp.int32, (level_count, groups * width), 1)
    here = level == lane // TERMS
    term = lane % TERMS
    gases = []
    for k in range(3):
        high, low = high_low(molecular_ref[k])
        spread = [
            jnp.where(here & chosen, 1.0, 0.0).astype(jnp.bfloat16)
            for chosen in ((term == k) | (term == k + 10), term == k + 5)
        ]
        gases.append(across(high, spread[0]) + across(low, spread[1]))
    w = [table_ref[n : n + 1, :] for n in range(7)]
    ls, li = w[0] * w[1], w[3] * w[4]
    la, ia = w[0] * (1.0 - w[1]), w[3] * (1.0 - w[4])
    place = lax.broadcasted_iota(jnp.int32, (8, width), 0)
    term = lax.broadcasted_iota(jnp.int32, (8, width), 1) % TERMS
    pattern = jnp.zeros((8, width), jnp.float32)
    for n, chosen in enumerate((
        (term == 3) | (term == 13), term == 8, (term == 4) | (term == 14), term == 9
    )):
        pattern = jnp.where((place == n) & chosen, 1.0, pattern)
    empty = jnp.zeros((4, gpoints), jnp.float32)

    def water(*values):
        parts = []
        for value in values:
            high = value.astype(jnp.bfloat16).astype(jnp.float32)
            parts += [high, value - high]
        return across(jnp.concatenate(parts + [empty], axis=0), pattern, lax.Precision.HIGHEST)

    absorbed = gases[0] + gases[1]
    gas = absorbed + gases[2]
    pairs = (
        (absorbed, water(la, ia)),
        (gas, water(la + ls * (1.0 - w[2]), ia + li * (1.0 - w[5]))),
        (gas + gas, water(2.0 * w[0], 2.0 * w[3])),
    )
    for n, (values, constant) in enumerate(pairs):
        for group in range(groups):
            optics_ref[group, n * gpoints : (n + 1) * gpoints, :] = (
                values[:, group * width : (group + 1) * width] + constant
            ).astype(jnp.bfloat16)
    only = jnp.where(place == 0, 1.0, 0.0)
    weight = jnp.broadcast_to(w[6], (8, gpoints))
    weight_ref[...] = across(weight, only, lax.Precision.HIGHEST)


def radiation_kernel(
    state_ref, temp_ref, cosine_ref, ground_ref, day_ref, molecular_ref, table_ref,
    edge_ref, heat_ref, first_ref, last_ref,
    optics_ref, weight_ref, terms_ref, right_ref, depths_ref, gain_ref, offset_ref, direct_ref, partial_ref, ratio_ref,
    source_ref, slant_ref, strip_ref,
):
    level_count = temp_ref.shape[0]
    gpoints = molecular_ref.shape[2]
    lanes = temp_ref.shape[2]
    row = pl.program_id(0)
    rows = pl.num_programs(0)
    rows_static = temp_ref.shape[1]
    blocks = level_count // BLOCK

    @pl.when(row == 0)
    def prepare():
        optics_matrices(molecular_ref, table_ref, optics_ref, weight_ref)
        right_ref[...] = jnp.zeros_like(right_ref)

        def level(l, carry):
            thickness = state_ref[2, l]
            weighted = thickness * temp_ref[l] * temp_ref[l]
            values = (
                weighted * state_ref[0, l], weighted * state_ref[1, l], thickness,
                state_ref[3, l], state_ref[4, l],
            )
            for k, value in enumerate(values):
                high = value.astype(jnp.bfloat16).astype(jnp.float32)
                for place, part in ((k, high), (k + 5, high), (k + 10, value - high)):
                    start = pl.multiple_of((l * TERMS + place) * 8, 8)
                    terms_ref[pl.ds(start, 8), :] = part
            last = pl.multiple_of((l * TERMS + 15) * 8, 8)
            terms_ref[pl.ds(last, 8), :] = jnp.zeros((8, lanes), jnp.float32)
            return carry

        lax.fori_loop(0, level_count, level, 0)

    def place_group(group, carry):
        for j in range(GROUP):
            start = (group * GROUP + j) * TERMS * 8 + row
            tile = terms_ref[pl.ds(start, TERMS, stride=8), :].astype(jnp.bfloat16)
            half = lanes * (j % 2)
            pair = group * (GROUP // 2) + j // 2
            right_ref[pair, TERMS * j : TERMS * (j + 1), half : half + lanes] = tile
        return carry

    lax.fori_loop(0, level_count // GROUP, place_group, 0)

    cosine = cosine_ref[pl.ds(row, 1), :]
    ground = ground_ref[pl.ds(row, 1), :]
    slant_ref[...] = jnp.broadcast_to((-0.5 * LOG2E) / cosine, (8, lanes))

    def over_rows(values):
        return jnp.broadcast_to(values[None], (gpoints // 8, 8, lanes)).reshape(gpoints, lanes)

    clear = 1.0 / (1.0 - ground)
    ratio_ref[...] = over_rows(jnp.broadcast_to((1.0 + ground) * clear, (8, lanes)))
    source_ref[...] = over_rows(jnp.broadcast_to(2.0 * ground * clear, (8, lanes)))

    def fill(block):
        for p in range(BLOCK // 2):
            pair = block * (BLOCK // 2) + p
            depths_ref[p] = jnp.dot(
                optics_ref[pair // (GROUP // 2)], right_ref[pair],
                preferred_element_type=jnp.float32,
            )

    def below_block(step, carry):
        block = blocks - 1 - step
        ratio, source = ratio_ref[...], source_ref[...]
        slant = over_rows(slant_ref[...])
        for j in reversed(range(BLOCK)):
            level = block * BLOCK + j
            part = depths_ref.at[j // 2, :, (j % 2) * lanes : (j % 2 + 1) * lanes]
            a, b, depth = [part[n * gpoints : (n + 1) * gpoints] for n in range(QUANTITIES)]
            away = b - a
            along = (depth - a) - b
            square = a * b
            inverse_root = lax.rsqrt(square)
            h = jnp.tanh(square * inverse_root)
            g = h * inverse_root
            g = g + g
            s, p = a * g, b * g
            h2 = h * h
            one = 1.0 + h2
            through = 1.0 - h2
            inverse = 1.0 / (one + s * ratio)
            direct = jnp.exp2(depth * slant)
            factor = (1.0 - direct) * (1.0 / depth)
            up, down = factor * away, factor * along
            push = inverse * (direct * source + (ratio - 1.0) * down)
            ratio = (one * ratio + p) * inverse
            gain = through * inverse
            source = through * push + (ratio + 1.0) * up
            gain_ref[level] = gain
            offset_ref[level] = (gain * up + down) - s * push
            direct_ref[level] = direct
        ratio_ref[...] = ratio
        source_ref[...] = source
        fill(jnp.maximum(block - 1, 0))
        return carry

    fill(blocks - 1)
    lax.fori_loop(0, blocks, below_block, 0)

    def folded(net):
        return sum(net[8 * k : 8 * (k + 1)] for k in range(gpoints // 8))

    beam = weight_ref[...] * cosine
    net = -(source_ref[...] * beam) / (1.0 + ratio_ref[...])
    partial_ref[pl.ds(pl.multiple_of(row * 8, 8), 8), :] = folded(beam) + folded(net)

    def down_group(group, carry):
        net, beam = carry
        for j in range(GROUP):
            level = group * GROUP + j
            net = gain_ref[level] * net + offset_ref[level] * beam
            beam = beam * direct_ref[level]
            start = pl.multiple_of(((level + 1) * rows + row) * 8, 8)
            partial_ref[pl.ds(start, 8), :] = folded(net) + folded(beam)
        return (net, beam)

    lax.fori_loop(0, level_count // GROUP, down_group, (net, beam))

    @pl.when(row == rows - 1)
    def finish():
        scale = jnp.where(day_ref[...] == 1, level_count / gpoints, 0.0)

        def flux(level):
            start = level * rows * 8
            return sum(
                partial_ref[pl.ds(start + k, rows, stride=8), :] for k in range(8)
            )

        def level_heat(level, upper):
            lower = flux(level + 1)
            start = pl.multiple_of(level * 8, 8)
            heat_ref[pl.ds(start, 8), :] = jnp.where(scale > 0.0, scale * (upper - lower), 0.0)
            return lower

        lax.fori_loop(0, level_count, level_heat, flux(0))

        parts = level_count // 8
        for r in range(rows_static):
            for k in range(parts):
                strip_ref[8 * r : 8 * (r + 1), lanes * k : lanes * (k + 1)] = heat_ref[
                    pl.ds(8 * k * rows_static + r, 8, stride=rows_static), :
                ]
        packed = split_dot(strip_ref[...], edge_ref[...])
        first_ref[...] = packed[:, :lanes]
        last_ref[...] = packed[:, lanes:]


def radiation(state, temper, cosine, ground, day, molecular, condensate):
    level_count, rows, lanes = temper.shape
    gpoints = molecular.shape[1]
    full = pltpu.VMEM((level_count, gpoints, lanes), jnp.float32)
    plane = pltpu.VMEM((gpoints, lanes), jnp.float32)
    whole = pl.BlockSpec(memory_space=pltpu.VMEM)
    edge = jax.ShapeDtypeStruct((8 * rows, lanes), jnp.float32)
    return pl.pallas_call(
        radiation_kernel,
        out_shape=(jax.ShapeDtypeStruct((level_count * rows, lanes), jnp.float32), edge, edge),
        grid=(rows,),
        in_specs=[whole] * 8,
        out_specs=(whole,) * 3,
        scratch_shapes=[
            pltpu.VMEM((level_count // GROUP, QUANTITIES * gpoints, GROUP * TERMS), jnp.bfloat16),
            plane,
            pltpu.VMEM((level_count * TERMS * 8, lanes), jnp.float32),
            pltpu.VMEM((level_count // 2, GROUP * TERMS, 2 * lanes), jnp.bfloat16),
            pltpu.VMEM((BLOCK // 2, QUANTITIES * gpoints, 2 * lanes), jnp.float32),
            full, full, full,
            pltpu.VMEM(((level_count + 1) * rows * 8, lanes), jnp.float32),
            plane, plane,
            pltpu.VMEM((8, lanes), jnp.float32),
            pltpu.VMEM((8 * rows, level_count // 8 * lanes), jnp.float32),
        ],
        compiler_params=pltpu.CompilerParams(vmem_limit_bytes=60 * 1024 * 1024),
        cost_estimate=pl.CostEstimate(
            flops=45 * level_count * gpoints * rows * lanes, bytes_accessed=4 * 8 * temper.size,
            transcendentals=5 * level_count * gpoints * rows * lanes,
        ),
        name="radiation",
    )(
        state, temper, cosine, ground, day, molecular.transpose(0, 2, 1), condensate,
        edge_matrix(level_count, lanes),
    )


def edge_matrix(level_count, lanes):
    parts = level_count // 8
    width = lanes // parts
    matrix = np.zeros((parts * lanes, 2 * lanes), np.float32)
    for k in range(parts):
        for c in range(width):
            matrix[lanes * k + c, width * k + c] = 1.0
            matrix[lanes * (k + 1) - width + c, lanes + width * k + c] = 1.0
    return jnp.asarray(matrix, jnp.bfloat16)


def slope_matrices(lanes):
    whole = np.kron(np.eye(2 * lanes // NODES), gll_derivative().T).astype(np.float32)
    high = np.asarray(whole, jnp.bfloat16)
    low = np.asarray(whole - high.astype(np.float32), jnp.bfloat16)
    return jnp.asarray(high), jnp.asarray(low)


def average_matrix(lanes):
    size = 2 * lanes
    matrix = np.eye(size, dtype=np.float32)
    for c in range(NODES - 1, size, NODES):
        after = (c + 1) % size
        matrix[c, c] = matrix[after, after] = matrix[c, after] = matrix[after, c] = 0.5
    return jnp.asarray(matrix, jnp.bfloat16)


def split_dot(values, *matrices):
    high, low = high_low(values)
    total = jnp.dot(high, matrices[0], preferred_element_type=jnp.float32)
    total = total + jnp.dot(low, matrices[0], preferred_element_type=jnp.float32)
    if len(matrices) > 1:
        total = total + jnp.dot(high, matrices[1], preferred_element_type=jnp.float32)
    return total


def slope_y(rows_of):
    derivative = gll_derivative()
    result = []
    for r in range(len(rows_of)):
        first = r // NODES * NODES
        total = None
        for n in range(NODES):
            weight = derivative[r - first, n]
            if abs(weight) > 1e-12:
                term = np.float32(weight) * rows_of[first + n]
                total = term if total is None else total + term
        result.append(total)
    return result


def average_y(rows_of, below, above):
    result = list(rows_of)
    count = len(rows_of)
    for r in range(NODES - 1, count - 1, NODES):
        result[r] = result[r + 1] = 0.5 * (rows_of[r] + rows_of[r + 1])
    result[0] = 0.5 * (below + rows_of[0])
    result[count - 1] = 0.5 * (rows_of[count - 1] + above)
    return result


def own_change_kernel(
    temp_ref, temp_after_ref, temp_before_ref, flow_ref, flow_after_ref, flow_before_ref,
    high_ref, low_ref, change_ref, wind_ref, temp_wide_ref, slope_ref,
):
    level_count = change_ref.shape[0] // ROWS
    lanes = temp_ref.shape[-1]
    lane = lax.broadcasted_iota(jnp.int32, (level_count, lanes), 1)

    def tiles(own, after, before, r):
        span = pl.ds(r, level_count, stride=ROWS)
        side = jnp.where(lane < EDGE, after[span, :], 0.0)
        return own[span, :], jnp.where(lane >= lanes - EDGE, before[span, :], side)

    for r in range(ROWS):
        rows = slice(r * level_count, (r + 1) * level_count)
        pairs = [tiles(temp_ref, temp_after_ref, temp_before_ref, r)] + [
            tiles(flow_ref.at[n], flow_after_ref.at[n], flow_before_ref.at[n], r) for n in range(2)
        ]
        for half in range(2):
            span = slice(half * lanes, (half + 1) * lanes)
            temp_wide_ref[rows, span] = pairs[0][half]
            wind_ref[0, rows, span] = pairs[1][half]
            wind_ref[1, rows, span] = pairs[2][half]
    slope_ref[...] = split_dot(temp_wide_ref[...], high_ref[...], low_ref[...])
    advect(temp_wide_ref, slope_ref, wind_ref, change_ref, level_count)


def advect(field_ref, slope_ref, wind_ref, change_ref, level_count):
    spans = [slice(r * level_count, (r + 1) * level_count) for r in range(ROWS)]
    for half in range(2):
        lanes = field_ref.shape[1] // 2
        part = slice(half * lanes, (half + 1) * lanes)
        slopes = slope_y([field_ref[span, part] for span in spans])
        for span, slope in zip(spans, slopes):
            change = wind_ref[0, span, part] * slope_ref[span, part]
            change_ref[span, part] = -TIME_INCREMENT * (change + wind_ref[1, span, part] * slope)


def write_averaged(change, average_ref, out_ref, first_ref, last_ref):
    level_count = first_ref.shape[0]
    out_ref[...] = split_dot(change, average_ref[...])
    width = first_ref.shape[1]
    first_ref[...] = out_ref[:level_count, :width]
    last_ref[...] = out_ref[out_ref.shape[0] - level_count :, :width]


def first_stage_kernel(
    change_ref, heat_ref, after_ref, before_ref, edge_ref, average_ref,
    out_ref, first_ref, last_ref, sum_ref,
):
    level_count = first_ref.shape[0]
    lanes = heat_ref.shape[1]
    sides = split_dot(
        jnp.concatenate([after_ref[...], before_ref[...]], axis=1), edge_ref[...]
    )
    for r in range(ROWS):
        rows = slice(r * level_count, (r + 1) * level_count)
        own = heat_ref[pl.ds(r, level_count, stride=ROWS), :]
        sum_ref[rows, :lanes] = change_ref[rows, :lanes] + TIME_INCREMENT * own
        for k in range(level_count // 8):
            side = sides[8 * r : 8 * (r + 1), lanes * k : lanes * (k + 1)]
            here = slice(r * level_count + 8 * k, r * level_count + 8 * (k + 1))
            sum_ref[here, lanes:] = change_ref[here, lanes:] + TIME_INCREMENT * side
    write_averaged(sum_ref[...], average_ref, out_ref, first_ref, last_ref)


def next_stage_kernel(
    share, native, field_ref, below_ref, above_ref, wind_ref, sum_ref, high_ref, low_ref,
    average_ref, out_ref, first_ref, last_ref, total_ref, wave_ref, slope_ref, change_ref,
):
    level_count = below_ref.shape[0]
    lanes = sum_ref.shape[1]
    spans = [slice(r * level_count, (r + 1) * level_count) for r in range(ROWS)]
    for half in range(2):
        part = slice(half * lanes, (half + 1) * lanes)
        wave = average_y(
            [field_ref[span, part] for span in spans], below_ref[:, part], above_ref[:, part]
        )
        for r, (span, row) in enumerate(zip(spans, wave)):
            wave_ref[span, part] = row
            if half == 0:
                before = sum_ref[pl.ds(r, level_count, stride=ROWS), :] if native else sum_ref[span]
                total_ref[span] = before + share * row
    slope_ref[...] = split_dot(wave_ref[...], high_ref[...], low_ref[...])
    advect(wave_ref, slope_ref, wind_ref, change_ref, level_count)
    write_averaged(change_ref[...], average_ref, out_ref, first_ref, last_ref)


def last_kernel(share, field_ref, below_ref, above_ref, sum_ref, total_ref):
    level_count, lanes = below_ref.shape
    spans = [slice(r * level_count, (r + 1) * level_count) for r in range(ROWS)]
    wave = average_y([field_ref[span, :lanes] for span in spans], below_ref[...], above_ref[...])
    for r, (span, row) in enumerate(zip(spans, wave)):
        total_ref[pl.ds(r, level_count, stride=ROWS), :] = sum_ref[span] + share * row


def shifted(value, axis, steps):
    count = lax.axis_size(axis)
    return lax.ppermute(value, axis, [(i, (i + steps) % count) for i in range(count)])


def local(
    atmospheric_constituents,
    thermal_ratio,
    flow_velocity,
    solar_elevation_factor,
    ground_reflectivity,
    sunlit_indicator,
    molecular_optics_lookup,
    condensate_optics_lookup,
):
    level_count, rows, lanes = thermal_ratio.shape
    size = level_count * rows
    temper = thermal_ratio.reshape(size, lanes)
    flow = flow_velocity.reshape(2, size, lanes)
    field = jax.ShapeDtypeStruct((size, lanes), jnp.float32)
    wide = jax.ShapeDtypeStruct((size, 2 * lanes), jnp.float32)
    line = jax.ShapeDtypeStruct((level_count, 2 * lanes), jnp.float32)
    short = jax.ShapeDtypeStruct((level_count, lanes), jnp.float32)
    wide_scratch = pltpu.VMEM(wide.shape, jnp.float32)
    whole = pl.BlockSpec(memory_space=pltpu.VMEM)

    def call(kernel, name, outs, scratch, *values):
        return pl.pallas_call(
            kernel, out_shape=outs, in_specs=[whole] * len(values),
            out_specs=jax.tree.map(lambda _: whole, outs), scratch_shapes=[wide_scratch] * scratch,
            compiler_params=pltpu.CompilerParams(vmem_limit_bytes=40 * 1024 * 1024), name=name,
        )(*values)

    slopes = slope_matrices(lanes)
    average = average_matrix(lanes)
    temper_after, temper_before = shifted(temper, "gx", -1), shifted(temper, "gx", 1)
    flow_after, flow_before = shifted(flow, "gx", -1), shifted(flow, "gx", 1)
    heat, heat_first, heat_last = radiation(
        atmospheric_constituents, thermal_ratio, solar_elevation_factor, ground_reflectivity,
        sunlit_indicator, molecular_optics_lookup, condensate_optics_lookup,
    )
    heat_after, heat_before = shifted(heat_first, "gx", -1), shifted(heat_last, "gx", 1)
    change, wind = call(
        own_change_kernel, "own_change",
        (wide, jax.ShapeDtypeStruct((2, size, 2 * lanes), jnp.float32)), 2,
        temper, temper_after, temper_before, flow, flow_after, flow_before, *slopes,
    )
    wave, first, last = call(
        first_stage_kernel, "first_stage", (wide, line, line), 1,
        change, heat, heat_after, heat_before, edge_matrix(level_count, lanes).T, average,
    )
    below, above = shifted(last, "gy", 1), shifted(first, "gy", -1)
    wave, first, last, total = call(
        functools.partial(next_stage_kernel, 1.0, True), "second_stage",
        (wide, line, line, field), 3, wave, below, above, wind, temper, *slopes, average,
    )
    below, above = shifted(last, "gy", 1), shifted(first, "gy", -1)
    wave, first, last, total = call(
        functools.partial(next_stage_kernel, 0.5, False), "third_stage",
        (wide, short, short, field), 3, wave, below, above, wind, total, *slopes, average,
    )
    below, above = shifted(last, "gy", 1), shifted(first, "gy", -1)
    total = call(
        functools.partial(last_kernel, 1.0 / 6.0), "last_stage", field, 0,
        wave, below, above, total,
    )
    return (heat.reshape(thermal_ratio.shape), total.reshape(thermal_ratio.shape))


def solution(mesh):
    in_specs = (
        P(None, None, "gy", "gx"),
        P(None, "gy", "gx"),
        P(None, None, "gy", "gx"),
        P("gy", "gx"),
        P("gy", "gx"),
        P("gy", "gx"),
        P(),
        P(),
    )
    out_specs = (P(None, "gy", "gx"), P(None, "gy", "gx"))
    return jax.shard_map(local, mesh=mesh, in_specs=in_specs, out_specs=out_specs, check_vma=False)
```

```python
import functools

import jax
import jax.numpy as jnp
import numpy as np
from jax import lax
from jax.experimental import pallas as pl
from jax.experimental.pallas import tpu as pltpu
from jax.sharding import PartitionSpec as P

NODES = 4
TIME_INCREMENT = 0.05
EDGE = 16
ROWS = 8
LOG2E = 1.4426950408889634

GROUP = 8
TERMS = 16
BLOCK = 8
QUANTITIES = 3


def shifted(value, axis, steps):
    count = lax.axis_size(axis)
    return lax.ppermute(value, axis, [(i, (i + steps) % count) for i in range(count)])


def gll_derivative():
    points = np.array([-1.0, -1.0 / np.sqrt(5.0), 1.0 / np.sqrt(5.0), 1.0])
    legendre = 0.5 * (5.0 * points**3 - 3.0 * points)
    derivative = np.zeros((4, 4))
    for source in range(4):
        for target in range(4):
            if source != target:
                derivative[source, target] = legendre[source] / (
                    legendre[target] * (points[source] - points[target])
                )
    derivative[0, 0] = -3.0
    derivative[3, 3] = 3.0
    return derivative


def high_low(values):
    high = values.astype(jnp.bfloat16)
    return high, (values - high.astype(jnp.float32)).astype(jnp.bfloat16)


def across(left, right, precision=None):
    return lax.dot_general(
        left, right, (((0,), (0,)), ((), ())), precision=precision,
        preferred_element_type=jnp.float32,
    )


def optics_matrices(molecular_ref, table_ref, optics_ref, weight_ref):
    level_count, gpoints = molecular_ref.shape[1:]
    groups = level_count // GROUP
    width = GROUP * TERMS
    level = lax.broadcasted_iota(jnp.int32, (level_count, groups * width), 0)
    lane = lax.broadcasted_iota(jnp.int32, (level_count, groups * width), 1)
    here = level == lane // TERMS
    term = lane % TERMS
    gases = []
    for k in range(3):
        high, low = high_low(molecular_ref[k])
        spread = [
            jnp.where(here & chosen, 1.0, 0.0).astype(jnp.bfloat16)
            for chosen in ((term == k) | (term == k + 10), term == k + 5)
        ]
        gases.append(across(high, spread[0]) + across(low, spread[1]))
    w = [table_ref[n : n + 1, :] for n in range(7)]
    ls, li = w[0] * w[1], w[3] * w[4]
    la, ia = w[0] * (1.0 - w[1]), w[3] * (1.0 - w[4])
    place = lax.broadcasted_iota(jnp.int32, (8, width), 0)
    term = lax.broadcasted_iota(jnp.int32, (8, width), 1) % TERMS
    pattern = jnp.zeros((8, width), jnp.float32)
    for n, chosen in enumerate((
        (term == 3) | (term == 13), term == 8, (term == 4) | (term == 14), term == 9
    )):
        pattern = jnp.where((place == n) & chosen, 1.0, pattern)
    empty = jnp.zeros((4, gpoints), jnp.float32)

    def water(*values):
        parts = []
        for value in values:
            high = value.astype(jnp.bfloat16).astype(jnp.float32)
            parts += [high, value - high]
        return across(jnp.concatenate(parts + [empty], axis=0), pattern, lax.Precision.HIGHEST)

    absorbed = gases[0] + gases[1]
    gas = absorbed + gases[2]
    pairs = (
        (absorbed, water(la, ia)),
        (gas, water(la + ls * (1.0 - w[2]), ia + li * (1.0 - w[5]))),
        (gas + gas, water(2.0 * w[0], 2.0 * w[3])),
    )
    for n, (values, constant) in enumerate(pairs):
        for group in range(groups):
            optics_ref[group, n * gpoints : (n + 1) * gpoints, :] = (
                values[:, group * width : (group + 1) * width] + constant
            ).astype(jnp.bfloat16)
    only = jnp.where(place == 0, 1.0, 0.0)
    weight = jnp.broadcast_to(w[6], (8, gpoints))
    weight_ref[...] = across(weight, only, lax.Precision.HIGHEST)


def layer_terms(state_ref, temp_ref, level):
    thickness = state_ref[2, level]
    weighted = thickness * temp_ref[level] * temp_ref[level]
    return (
        weighted * state_ref[0, level], weighted * state_ref[1, level], thickness,
        state_ref[3, level], state_ref[4, level],
    )


def write_terms(terms_ref, level, values, lines):
    parts = [None] * TERMS
    for k, value in enumerate(values):
        high = value.astype(jnp.bfloat16).astype(jnp.float32)
        parts[k], parts[k + 5], parts[k + 10] = high, high, value - high
    parts[15] = jnp.zeros_like(values[0])
    for k, part in enumerate(parts):
        start = (level * TERMS + k) * lines
        start = pl.multiple_of(start, 8) if lines % 8 == 0 else start
        terms_ref[pl.ds(start, lines), :] = part


def sweep_row(
    row, lines, count, cosine, ground, optics_ref, weight_ref, terms_ref, right_ref, depths_ref,
    gain_ref, offset_ref, direct_ref, partial_ref, ratio_ref, source_ref, slant_ref,
):
    level_count, gpoints, lanes = gain_ref.shape
    blocks = level_count // BLOCK

    def place_group(group, carry):
        for j in range(GROUP):
            start = (group * GROUP + j) * TERMS * lines + row
            tile = terms_ref[pl.ds(start, TERMS, stride=lines), :].astype(jnp.bfloat16)
            half = lanes * (j % 2)
            pair = group * (GROUP // 2) + j // 2
            right_ref[pair, TERMS * j : TERMS * (j + 1), half : half + lanes] = tile
        return carry

    lax.fori_loop(0, level_count // GROUP, place_group, 0)
    slant_ref[...] = jnp.broadcast_to((-0.5 * LOG2E) / cosine, (8, lanes))

    def over_rows(values):
        return jnp.broadcast_to(values[None], (gpoints // 8, 8, lanes)).reshape(gpoints, lanes)

    clear = 1.0 / (1.0 - ground)
    ratio_ref[...] = over_rows(jnp.broadcast_to((1.0 + ground) * clear, (8, lanes)))
    source_ref[...] = over_rows(jnp.broadcast_to(2.0 * ground * clear, (8, lanes)))

    def below_block(step, carry):
        block = blocks - 1 - step
        for p in range(BLOCK // 2):
            pair = block * (BLOCK // 2) + p
            depths_ref[p] = jnp.dot(
                optics_ref[pair // (GROUP // 2)], right_ref[pair],
                preferred_element_type=jnp.float32,
            )
        ratio, source = ratio_ref[...], source_ref[...]
        slant = over_rows(slant_ref[...])
        for j in reversed(range(BLOCK)):
            level = block * BLOCK + j
            part = depths_ref.at[j // 2, :, (j % 2) * lanes : (j % 2 + 1) * lanes]
            a, b, depth = [part[n * gpoints : (n + 1) * gpoints] for n in range(QUANTITIES)]
            away = b - a
            along = (depth - a) - b
            square = a * b
            inverse_root = lax.rsqrt(square)
            h = jnp.tanh(square * inverse_root)
            g = h * inverse_root
            g = g + g
            s, p = a * g, b * g
            h2 = h * h
            one = 1.0 + h2
            through = 1.0 - h2
            inverse = 1.0 / (one + s * ratio)
            direct = jnp.exp2(depth * slant)
            factor = (1.0 - direct) * (1.0 / depth)
            up, down = factor * away, factor * along
            push = inverse * (direct * source + (ratio - 1.0) * down)
            ratio = (one * ratio + p) * inverse
            gain = through * inverse
            source = through * push + (ratio + 1.0) * up
            gain_ref[level] = gain
            offset_ref[level] = (gain * up + down) - s * push
            direct_ref[level] = direct
        ratio_ref[...] = ratio
        source_ref[...] = source
        return carry

    lax.fori_loop(0, blocks, below_block, 0)

    def folded(net):
        return sum(net[8 * k : 8 * (k + 1)] for k in range(gpoints // 8))

    def top(step, carry):
        beam = weight_ref[...] * cosine
        net = -(source_ref[...] * beam) / (1.0 + ratio_ref[...])
        partial_ref[pl.ds(pl.multiple_of(row * 8, 8), 8), :] = folded(beam) + folded(net)
        return net, beam

    nothing = jnp.zeros((gpoints, lanes), jnp.float32)
    carry = lax.fori_loop(0, 1 + jnp.minimum(row, 0), top, (nothing, nothing))

    def down_group(group, carry):
        net, beam = carry
        for j in range(GROUP):
            level = group * GROUP + j
            net = gain_ref[level] * net + offset_ref[level] * beam
            beam = beam * direct_ref[level]
            start = pl.multiple_of(((level + 1) * count + row) * 8, 8)
            partial_ref[pl.ds(start, 8), :] = folded(net) + folded(beam)
        return (net, beam)

    lax.fori_loop(0, level_count // GROUP, down_group, carry)


def level_heating(partial_ref, level_count, gpoints, count, write):
    def flux(level):
        start = level * count * 8
        return sum(partial_ref[pl.ds(start + k, count, stride=8), :] for k in range(8))

    def step(level, upper):
        lower = flux(level + 1)
        write(level, (level_count / gpoints) * (upper - lower))
        return lower

    lax.fori_loop(0, level_count, step, flux(0))


def home_kernel(
    state_ref, temp_ref, cosine_ref, ground_ref, day_ref, molecular_ref, table_ref,
    heat_ref, optics_ref, weight_ref, terms_ref, right_ref, *scratch,
):
    level_count, lines, lanes = temp_ref.shape
    gpoints = weight_ref.shape[0]
    row, count = pl.program_id(0), pl.num_programs(0)

    @pl.when(row == 0)
    def prepare():
        optics_matrices(molecular_ref, table_ref, optics_ref, weight_ref)
        right_ref[...] = jnp.zeros_like(right_ref)
        heat_ref[...] = jnp.zeros_like(heat_ref)

        def level(l, carry):
            write_terms(terms_ref, l, layer_terms(state_ref, temp_ref, l), lines)
            return carry

        lax.fori_loop(0, level_count, level, 0)

    sweep_row(
        row, lines, count, cosine_ref[pl.ds(row, 1), :], ground_ref[pl.ds(row, 1), :],
        optics_ref, weight_ref, terms_ref, right_ref, *scratch,
    )

    @pl.when(row == count - 1)
    def finish():
        home = lines // 2
        day = day_ref[:home, :] == 1

        def write(level, value):
            start = pl.multiple_of(level * lines, 8)
            heat_ref[pl.ds(start, home), :] = jnp.where(day, value, 0.0)

        level_heating(scratch[4], level_count, gpoints, home, write)


def pack_kernel(theirs_ref, state_ref, temp_ref, cosine_ref, ground_ref, out_ref, own_ref):
    level_count, lines, lanes = temp_ref.shape
    count = out_ref.shape[1]
    first = theirs_ref[0]

    def level(l, carry):
        for k, value in enumerate(layer_terms(state_ref, temp_ref, l)):
            own_ref[pl.ds(pl.multiple_of((5 * l + k) * lines, 8), lines), :] = value
        return carry

    lax.fori_loop(0, level_count, level, 0)

    def copy(n, carry):
        out_ref[n] = own_ref[pl.ds(n * lines + first, count), :]
        return carry

    lax.fori_loop(0, 5 * level_count, copy, 0, unroll=8)
    out_ref[5 * level_count] = cosine_ref[pl.ds(first, count), :]
    out_ref[5 * level_count + 1] = ground_ref[pl.ds(first, count), :]


def shared_kernel(
    mine_ref, state_ref, temp_ref, cosine_ref, ground_ref, day_ref, received_ref, optics_ref,
    weight_ref, edge_ref, home_ref,
    heat_ref, theirs_ref, first_ref, last_ref, their_first_ref, their_last_ref,
    own_ref, strip_ref, surface_ref, terms_ref, right_ref, *scratch,
):
    level_count, lines, lanes = temp_ref.shape
    gpoints = weight_ref.shape[0]
    row, count = pl.program_id(0), pl.num_programs(0)
    shared = received_ref.shape[1]
    first = mine_ref[0]
    day = day_ref[pl.ds(first, shared), :] == 1

    @pl.when(row == 0)
    def prepare():
        right_ref[...] = jnp.zeros_like(right_ref)

        def own(l, carry):
            for k, value in enumerate(layer_terms(state_ref, temp_ref, l)):
                own_ref[pl.ds(pl.multiple_of((5 * l + k) * lines, 8), lines), :] = value
            return carry

        lax.fori_loop(0, level_count, own, 0)

        def level(l, carry):
            values = [
                jnp.where(
                    day, own_ref[pl.ds((5 * l + k) * lines + first, shared), :],
                    received_ref[5 * l + k],
                )
                for k in range(5)
            ]
            write_terms(terms_ref, l, values, shared)
            return carry

        lax.fori_loop(0, level_count, level, 0)
        for n, ref in enumerate((cosine_ref, ground_ref)):
            surface_ref[n, :shared, :] = jnp.where(
                day, ref[pl.ds(first, shared), :], received_ref[5 * level_count + n]
            )

    sweep_row(
        row, shared, count, surface_ref[0, pl.ds(row, 1), :], surface_ref[1, pl.ds(row, 1), :],
        optics_ref, weight_ref, terms_ref, right_ref, *scratch,
    )

    @pl.when(row == count - 1)
    def finish():
        heat_ref[...] = home_ref[...]

        def write(level, value):
            heat_ref[pl.ds(level * lines + first, shared), :] = jnp.where(day, value, 0.0)
            theirs_ref[pl.ds(level * shared, shared), :] = jnp.where(day, 0.0, value)

        level_heating(scratch[4], level_count, gpoints, shared, write)
        strip_ref[...] = jnp.zeros_like(strip_ref)
        for k in range(level_count // 8):
            span = slice(lanes * k, lanes * (k + 1))
            for r in range(lines):
                strip_ref[8 * r : 8 * (r + 1), span] = heat_ref[
                    pl.ds(8 * k * lines + r, 8, stride=lines), :
                ]
            for r in range(shared):
                start = pl.multiple_of(8 * (lines + first + r), 8)
                strip_ref[pl.ds(start, 8), span] = theirs_ref[
                    pl.ds(8 * k * shared + r, 8, stride=shared), :
                ]
        packed = split_dot(strip_ref[...], edge_ref[...])
        half = 8 * lines
        first_ref[...] = packed[:half, :lanes]
        last_ref[...] = packed[:half, lanes:]
        their_first_ref[...] = packed[half:, :lanes]
        their_last_ref[...] = packed[half:, lanes:]


def radiation(state, temper, cosine, ground, day, molecular, condensate):
    level_count, rows, lanes = temper.shape
    gpoints = molecular.shape[1]
    home, shared = rows // 2, rows // 4
    partner = lax.axis_size("gx") // 2
    low = lax.axis_index("gx") < partner
    mine = jnp.where(low, home, home + shared).astype(jnp.int32).reshape(1)
    theirs = jnp.where(low, home + shared, home).astype(jnp.int32).reshape(1)
    full = pltpu.VMEM((level_count, gpoints, lanes), jnp.float32)
    plane = pltpu.VMEM((gpoints, lanes), jnp.float32)
    whole = pl.BlockSpec(memory_space=pltpu.VMEM)
    scalar = pl.BlockSpec(memory_space=pltpu.SMEM)
    field = jax.ShapeDtypeStruct((level_count * rows, lanes), jnp.float32)
    own = pltpu.VMEM((5 * level_count * rows, lanes), jnp.float32)
    params = pltpu.CompilerParams(vmem_limit_bytes=60 * 1024 * 1024)

    def scratch(lines, count):
        return [
            pltpu.VMEM((level_count * TERMS * lines, lanes), jnp.float32),
            pltpu.VMEM((level_count // 2, GROUP * TERMS, 2 * lanes), jnp.bfloat16),
            pltpu.VMEM((BLOCK // 2, QUANTITIES * gpoints, 2 * lanes), jnp.float32),
            full, full, full,
            pltpu.VMEM(((level_count + 1) * count * 8, lanes), jnp.float32),
            plane, plane,
            pltpu.VMEM((8, lanes), jnp.float32),
        ]

    def cost(count):
        cells = level_count * gpoints * count * lanes
        return pl.CostEstimate(
            flops=45 * cells, bytes_accessed=32 * temper.size, transcendentals=5 * cells
        )

    sent = pl.pallas_call(
        pack_kernel,
        out_shape=jax.ShapeDtypeStruct((5 * level_count + 2, shared, lanes), jnp.float32),
        in_specs=[scalar] + [whole] * 4, out_specs=whole, scratch_shapes=[own],
        compiler_params=params, name="pack",
    )(theirs, state, temper, cosine, ground)
    received = shifted(sent, "gx", partner)
    optics = (level_count // GROUP, QUANTITIES * gpoints, GROUP * TERMS)
    heat, optics, weight = pl.pallas_call(
        home_kernel,
        out_shape=(
            field, jax.ShapeDtypeStruct(optics, jnp.bfloat16),
            jax.ShapeDtypeStruct((gpoints, lanes), jnp.float32),
        ),
        grid=(home,), in_specs=[whole] * 7, out_specs=(whole,) * 3,
        scratch_shapes=scratch(rows, home), compiler_params=params, cost_estimate=cost(home),
        name="home_radiation",
    )(state, temper, cosine, ground, day, molecular.transpose(0, 2, 1), condensate)
    edge = jax.ShapeDtypeStruct((8 * rows, lanes), jnp.float32)
    return pl.pallas_call(
        shared_kernel,
        out_shape=(
            field, jax.ShapeDtypeStruct((level_count * shared, lanes), jnp.float32),
            edge, edge, edge, edge,
        ),
        grid=(shared,), in_specs=[scalar] + [whole] * 10, out_specs=(whole,) * 6,
        scratch_shapes=[
            own,
            pltpu.VMEM((16 * rows, level_count // 8 * lanes), jnp.float32),
            pltpu.VMEM((2, 8, lanes), jnp.float32),
        ] + scratch(shared, shared),
        compiler_params=params, cost_estimate=cost(shared), name="shared_radiation",
    )(
        mine, state, temper, cosine, ground, day, received, optics, weight,
        edge_matrix(level_count, lanes), heat,
    ) + (theirs,)


def edge_matrix(level_count, lanes):
    parts = level_count // 8
    width = lanes // parts
    matrix = np.zeros((parts * lanes, 2 * lanes), np.float32)
    for k in range(parts):
        for c in range(width):
            matrix[lanes * k + c, width * k + c] = 1.0
            matrix[lanes * (k + 1) - width + c, lanes + width * k + c] = 1.0
    return jnp.asarray(matrix, jnp.bfloat16)


def slope_matrices(lanes):
    whole = np.kron(np.eye(2 * lanes // NODES), gll_derivative().T).astype(np.float32)
    high = np.asarray(whole, jnp.bfloat16)
    low = np.asarray(whole - high.astype(np.float32), jnp.bfloat16)
    return jnp.asarray(high), jnp.asarray(low)


def average_matrix(lanes):
    size = 2 * lanes
    matrix = np.eye(size, dtype=np.float32)
    for c in range(NODES - 1, size, NODES):
        after = (c + 1) % size
        matrix[c, c] = matrix[after, after] = matrix[c, after] = matrix[after, c] = 0.5
    return jnp.asarray(matrix, jnp.bfloat16)


def split_dot(values, *matrices):
    high, low = high_low(values)
    total = jnp.dot(high, matrices[0], preferred_element_type=jnp.float32)
    total = total + jnp.dot(low, matrices[0], preferred_element_type=jnp.float32)
    if len(matrices) > 1:
        total = total + jnp.dot(high, matrices[1], preferred_element_type=jnp.float32)
    return total


def slope_y(rows_of):
    derivative = gll_derivative()
    result = []
    for r in range(len(rows_of)):
        first = r // NODES * NODES
        total = None
        for n in range(NODES):
            weight = derivative[r - first, n]
            if abs(weight) > 1e-12:
                term = np.float32(weight) * rows_of[first + n]
                total = term if total is None else total + term
        result.append(total)
    return result


def average_y(rows_of, below, above):
    result = list(rows_of)
    count = len(rows_of)
    for r in range(NODES - 1, count - 1, NODES):
        result[r] = result[r + 1] = 0.5 * (rows_of[r] + rows_of[r + 1])
    result[0] = 0.5 * (below + rows_of[0])
    result[count - 1] = 0.5 * (rows_of[count - 1] + above)
    return result


def own_change_kernel(
    temp_ref, temp_after_ref, temp_before_ref, flow_ref, flow_after_ref, flow_before_ref,
    high_ref, low_ref, change_ref, wind_ref, temp_wide_ref, slope_ref,
):
    level_count = change_ref.shape[0] // ROWS
    lanes = temp_ref.shape[-1]
    lane = lax.broadcasted_iota(jnp.int32, (level_count, lanes), 1)

    def tiles(own, after, before, r):
        span = pl.ds(r, level_count, stride=ROWS)
        side = jnp.where(lane < EDGE, after[span, :], 0.0)
        return own[span, :], jnp.where(lane >= lanes - EDGE, before[span, :], side)

    for r in range(ROWS):
        rows = slice(r * level_count, (r + 1) * level_count)
        pairs = [tiles(temp_ref, temp_after_ref, temp_before_ref, r)] + [
            tiles(flow_ref.at[n], flow_after_ref.at[n], flow_before_ref.at[n], r) for n in range(2)
        ]
        for half in range(2):
            span = slice(half * lanes, (half + 1) * lanes)
            temp_wide_ref[rows, span] = pairs[0][half]
            wind_ref[0, rows, span] = pairs[1][half]
            wind_ref[1, rows, span] = pairs[2][half]
    slope_ref[...] = split_dot(temp_wide_ref[...], high_ref[...], low_ref[...])
    advect(temp_wide_ref, slope_ref, wind_ref, change_ref, level_count)


def advect(field_ref, slope_ref, wind_ref, change_ref, level_count):
    spans = [slice(r * level_count, (r + 1) * level_count) for r in range(ROWS)]
    for half in range(2):
        lanes = field_ref.shape[1] // 2
        part = slice(half * lanes, (half + 1) * lanes)
        slopes = slope_y([field_ref[span, part] for span in spans])
        for span, slope in zip(spans, slopes):
            change = wind_ref[0, span, part] * slope_ref[span, part]
            change_ref[span, part] = -TIME_INCREMENT * (change + wind_ref[1, span, part] * slope)


def write_averaged(change, average_ref, out_ref, first_ref, last_ref):
    level_count = first_ref.shape[0]
    out_ref[...] = split_dot(change, average_ref[...])
    width = first_ref.shape[1]
    first_ref[...] = out_ref[:level_count, :width]
    last_ref[...] = out_ref[out_ref.shape[0] - level_count :, :width]


def first_stage_kernel(
    theirs_ref, change_ref, heat_ref, returned_ref, after_ref, before_ref, after_more_ref,
    before_more_ref, edge_ref, average_ref,
    out_ref, first_ref, last_ref, heat_out_ref, sum_ref,
):
    level_count = first_ref.shape[0]
    lanes = heat_ref.shape[1]
    shared = returned_ref.shape[0] // level_count
    after = after_ref[...] + after_more_ref[...]
    before = before_ref[...] + before_more_ref[...]
    sides = split_dot(jnp.concatenate([after, before], axis=1), edge_ref[...])
    for r in range(ROWS):
        rows = slice(r * level_count, (r + 1) * level_count)
        span = pl.ds(r, level_count, stride=ROWS)
        own = heat_ref[span, :]
        if r >= ROWS // 2:
            n = r % shared
            here = theirs_ref[0] == r - n
            own = own + jnp.where(
                here, returned_ref[pl.ds(n, level_count, stride=shared), :], 0.0
            )
        heat_out_ref[span, :] = own
        sum_ref[rows, :lanes] = change_ref[rows, :lanes] + TIME_INCREMENT * own
        for k in range(level_count // 8):
            side = sides[8 * r : 8 * (r + 1), lanes * k : lanes * (k + 1)]
            here = slice(r * level_count + 8 * k, r * level_count + 8 * (k + 1))
            sum_ref[here, lanes:] = change_ref[here, lanes:] + TIME_INCREMENT * side
    write_averaged(sum_ref[...], average_ref, out_ref, first_ref, last_ref)


def next_stage_kernel(
    share, native, field_ref, below_ref, above_ref, wind_ref, sum_ref, high_ref, low_ref,
    average_ref, out_ref, first_ref, last_ref, total_ref, wave_ref, slope_ref, change_ref,
):
    level_count = below_ref.shape[0]
    lanes = sum_ref.shape[1]
    spans = [slice(r * level_count, (r + 1) * level_count) for r in range(ROWS)]
    for half in range(2):
        part = slice(half * lanes, (half + 1) * lanes)
        wave = average_y(
            [field_ref[span, part] for span in spans], below_ref[:, part], above_ref[:, part]
        )
        for r, (span, row) in enumerate(zip(spans, wave)):
            wave_ref[span, part] = row
            if half == 0:
                before = sum_ref[pl.ds(r, level_count, stride=ROWS), :] if native else sum_ref[span]
                total_ref[span] = before + share * row
    slope_ref[...] = split_dot(wave_ref[...], high_ref[...], low_ref[...])
    advect(wave_ref, slope_ref, wind_ref, change_ref, level_count)
    write_averaged(change_ref[...], average_ref, out_ref, first_ref, last_ref)


def last_kernel(share, field_ref, below_ref, above_ref, sum_ref, total_ref):
    level_count, lanes = below_ref.shape
    spans = [slice(r * level_count, (r + 1) * level_count) for r in range(ROWS)]
    wave = average_y([field_ref[span, :lanes] for span in spans], below_ref[...], above_ref[...])
    for r, (span, row) in enumerate(zip(spans, wave)):
        total_ref[pl.ds(r, level_count, stride=ROWS), :] = sum_ref[span] + share * row


def local(
    atmospheric_constituents,
    thermal_ratio,
    flow_velocity,
    solar_elevation_factor,
    ground_reflectivity,
    sunlit_indicator,
    molecular_optics_lookup,
    condensate_optics_lookup,
):
    level_count, rows, lanes = thermal_ratio.shape
    size = level_count * rows
    temper = thermal_ratio.reshape(size, lanes)
    flow = flow_velocity.reshape(2, size, lanes)
    field = jax.ShapeDtypeStruct((size, lanes), jnp.float32)
    wide = jax.ShapeDtypeStruct((size, 2 * lanes), jnp.float32)
    line = jax.ShapeDtypeStruct((level_count, 2 * lanes), jnp.float32)
    short = jax.ShapeDtypeStruct((level_count, lanes), jnp.float32)
    wide_scratch = pltpu.VMEM(wide.shape, jnp.float32)
    whole = pl.BlockSpec(memory_space=pltpu.VMEM)
    scalar = pl.BlockSpec(memory_space=pltpu.SMEM)

    def call(kernel, name, outs, scratch, *values):
        return pl.pallas_call(
            kernel, out_shape=outs,
            in_specs=[scalar if value.size == 1 else whole for value in values],
            out_specs=jax.tree.map(lambda _: whole, outs), scratch_shapes=[wide_scratch] * scratch,
            compiler_params=pltpu.CompilerParams(vmem_limit_bytes=40 * 1024 * 1024), name=name,
        )(*values)

    slopes = slope_matrices(lanes)
    average = average_matrix(lanes)
    temper_after, temper_before = shifted(temper, "gx", -1), shifted(temper, "gx", 1)
    flow_after, flow_before = shifted(flow, "gx", -1), shifted(flow, "gx", 1)
    heat, heat_theirs, heat_first, heat_last, their_first, their_last, theirs = radiation(
        atmospheric_constituents, thermal_ratio, solar_elevation_factor, ground_reflectivity,
        sunlit_indicator, molecular_optics_lookup, condensate_optics_lookup,
    )
    partner = lax.axis_size("gx") // 2
    heat_after, heat_before = shifted(heat_first, "gx", -1), shifted(heat_last, "gx", 1)
    after_more = shifted(their_first, "gx", partner - 1)
    before_more = shifted(their_last, "gx", partner + 1)
    returned = shifted(heat_theirs, "gx", partner)
    change, wind = call(
        own_change_kernel, "own_change",
        (wide, jax.ShapeDtypeStruct((2, size, 2 * lanes), jnp.float32)), 2,
        temper, temper_after, temper_before, flow, flow_after, flow_before, *slopes,
    )
    wave, first, last, heat = call(
        first_stage_kernel, "first_stage", (wide, line, line, field), 1,
        theirs, change, heat, returned, heat_after, heat_before, after_more, before_more,
        edge_matrix(level_count, lanes).T, average,
    )
    below, above = shifted(last, "gy", 1), shifted(first, "gy", -1)
    wave, first, last, total = call(
        functools.partial(next_stage_kernel, 1.0, True), "second_stage",
        (wide, line, line, field), 3, wave, below, above, wind, temper, *slopes, average,
    )
    below, above = shifted(last, "gy", 1), shifted(first, "gy", -1)
    wave, first, last, total = call(
        functools.partial(next_stage_kernel, 0.5, False), "third_stage",
        (wide, short, short, field), 3, wave, below, above, wind, total, *slopes, average,
    )
    below, above = shifted(last, "gy", 1), shifted(first, "gy", -1)
    total = call(
        functools.partial(last_kernel, 1.0 / 6.0), "last_stage", field, 0,
        wave, below, above, total,
    )
    return (heat.reshape(thermal_ratio.shape), total.reshape(thermal_ratio.shape))


def solution(mesh):
    in_specs = (
        P(None, None, "gy", "gx"),
        P(None, "gy", "gx"),
        P(None, None, "gy", "gx"),
        P("gy", "gx"),
        P("gy", "gx"),
        P("gy", "gx"),
        P(),
        P(),
    )
    out_specs = (P(None, "gy", "gx"), P(None, "gy", "gx"))
    return jax.shard_map(local, mesh=mesh, in_specs=in_specs, out_specs=out_specs, check_vma=False)
```

```python
import functools

import jax
import jax.numpy as jnp
import numpy as np
from jax import lax
from jax.experimental import pallas as pl
from jax.experimental.pallas import tpu as pltpu
from jax.sharding import PartitionSpec as P

NODES = 4
TIME_INCREMENT = 0.05
EDGE = 16
ROWS = 8
LOG2E = 1.4426950408889634

GROUP = 8
TERMS = 16
BLOCK = 12
PARTIAL = 5
CHUNKS = 2
QUANTITIES = 4


def shifted(value, axis, steps):
    count = lax.axis_size(axis)
    return lax.ppermute(value, axis, [(i, (i + steps) % count) for i in range(count)])


def gll_derivative():
    points = np.array([-1.0, -1.0 / np.sqrt(5.0), 1.0 / np.sqrt(5.0), 1.0])
    legendre = 0.5 * (5.0 * points**3 - 3.0 * points)
    derivative = np.zeros((4, 4))
    for source in range(4):
        for target in range(4):
            if source != target:
                derivative[source, target] = legendre[source] / (
                    legendre[target] * (points[source] - points[target])
                )
    derivative[0, 0] = -3.0
    derivative[3, 3] = 3.0
    return derivative


def high_low(values):
    high = values.astype(jnp.bfloat16)
    return high, (values - high.astype(jnp.float32)).astype(jnp.bfloat16)


def across(left, right, precision=None):
    return lax.dot_general(
        left, right, (((0,), (0,)), ((), ())), precision=precision,
        preferred_element_type=jnp.float32,
    )


def optics_matrices(molecular_ref, table_ref, optics_ref, weight_ref):
    level_count, gpoints = molecular_ref.shape[1:]
    groups = level_count // GROUP
    width = GROUP * TERMS
    level = lax.broadcasted_iota(jnp.int32, (level_count, groups * width), 0)
    lane = lax.broadcasted_iota(jnp.int32, (level_count, groups * width), 1)
    here = level == lane // TERMS
    term = lane % TERMS
    gases = []
    for k in range(3):
        high, low = high_low(molecular_ref[k])
        spread = [
            jnp.where(here & chosen, 1.0, 0.0).astype(jnp.bfloat16)
            for chosen in ((term == k) | (term == k + 10), term == k + 5)
        ]
        gases.append(across(high, spread[0]) + across(low, spread[1]))
    w = [table_ref[n : n + 1, :] for n in range(7)]
    ls, li = w[0] * w[1], w[3] * w[4]
    la, ia = w[0] * (1.0 - w[1]), w[3] * (1.0 - w[4])
    place = lax.broadcasted_iota(jnp.int32, (8, width), 0)
    term = lax.broadcasted_iota(jnp.int32, (8, width), 1) % TERMS
    pattern = jnp.zeros((8, width), jnp.float32)
    for n, chosen in enumerate((
        (term == 3) | (term == 13), term == 8, (term == 4) | (term == 14), term == 9
    )):
        pattern = jnp.where((place == n) & chosen, 1.0, pattern)
    empty = jnp.zeros((4, gpoints), jnp.float32)

    def water(*values):
        parts = []
        for value in values:
            high = value.astype(jnp.bfloat16).astype(jnp.float32)
            parts += [high, value - high]
        return across(jnp.concatenate(parts + [empty], axis=0), pattern, lax.Precision.HIGHEST)

    absorbed = gases[0] + gases[1]
    gas = absorbed + gases[2]
    pairs = (
        (absorbed, water(la, ia)),
        (gas, water(la + ls * (1.0 - w[2]), ia + li * (1.0 - w[5]))),
        (gas + gas, water(2.0 * w[0], 2.0 * w[3])),
        (gases[2], water(ls * (1.0 + w[2]), li * (1.0 + w[5]))),
    )
    chunk = gpoints // CHUNKS
    for group in range(groups):
        span = slice(group * width, (group + 1) * width)
        tables = [values[:, span] + constant for values, constant in pairs]
        for c in range(CHUNKS):
            rows = [table[c * chunk : (c + 1) * chunk] for table in tables]
            optics_ref[group, c] = jnp.concatenate(rows, axis=0).astype(jnp.bfloat16)
    only = jnp.where(place == 0, 1.0, 0.0)
    weight = jnp.broadcast_to(w[6], (8, gpoints))
    weight_ref[...] = across(weight, only, lax.Precision.HIGHEST)


def layer_terms(state_ref, temp_ref, level):
    thickness = state_ref[2, level]
    weighted = thickness * temp_ref[level] * temp_ref[level]
    return (
        weighted * state_ref[0, level], weighted * state_ref[1, level], thickness,
        state_ref[3, level], state_ref[4, level],
    )


def write_terms(terms_ref, level, values, lines):
    parts = [None] * TERMS
    for k, value in enumerate(values):
        high = value.astype(jnp.bfloat16).astype(jnp.float32)
        parts[k], parts[k + 5], parts[k + 10] = high, high, value - high
    parts[15] = jnp.zeros_like(values[0])
    for k, part in enumerate(parts):
        start = (level * TERMS + k) * lines
        start = pl.multiple_of(start, 8) if lines % 8 == 0 else start
        terms_ref[pl.ds(start, lines), :] = part


def sweep_row(
    row, line, lines, count, cosine, ground, optics_ref, weight_ref, terms_ref, right_ref,
    depths_0, depths_1, gain_ref, offset_ref, direct_ref, partial_ref, ratio_ref, source_ref, slant_ref,
):
    level_count, gpoints, lanes = gain_ref.shape
    blocks = level_count // BLOCK
    chunk = gpoints // CHUNKS
    slots = (depths_0, depths_1)
    once = 1 + jnp.minimum(row, 0)

    def place_group(group, carry):
        for j in range(GROUP):
            start = (group * GROUP + j) * TERMS * lines + line
            tile = terms_ref[pl.ds(start, TERMS, stride=lines), :].astype(jnp.bfloat16)
            half = lanes * (j % 2)
            pair = group * (GROUP // 2) + j // 2
            right_ref[pair, TERMS * j : TERMS * (j + 1), half : half + lanes] = tile
        return carry

    lax.fori_loop(0, level_count // GROUP, place_group, 0)
    slant_ref[...] = jnp.broadcast_to((-0.5 * LOG2E) / cosine, (8, lanes))

    def over_rows(values):
        return jnp.broadcast_to(values[None], (gpoints // 8, 8, lanes)).reshape(gpoints, lanes)

    clear = 1.0 / (1.0 - ground)
    ratio_ref[...] = over_rows(jnp.broadcast_to((1.0 + ground) * clear, (8, lanes)))
    source_ref[...] = over_rows(jnp.broadcast_to(2.0 * ground * clear, (8, lanes)))

    def fill(block, c):
        for p in range(BLOCK // 2):
            pair = block * (BLOCK // 2) + p
            slots[c % 2][p] = jnp.dot(
                optics_ref[pair // (GROUP // 2), c], right_ref[pair],
                preferred_element_type=jnp.float32,
            )

    def below(block, c):
        span = slice(c * chunk, (c + 1) * chunk)
        ratio, source = ratio_ref[span], source_ref[span]
        slant = jnp.broadcast_to(slant_ref[...][None], (chunk // 8, 8, lanes))
        slant = slant.reshape(chunk, lanes)
        for j in reversed(range(BLOCK)):
            level = block * BLOCK + j
            part = slots[c % 2].at[j // 2, :, (j % 2) * lanes : (j % 2 + 1) * lanes]
            a, b, depth, along = [part[n * chunk : (n + 1) * chunk] for n in range(QUANTITIES)]
            away = b - a
            square = a * b
            inverse_root = lax.rsqrt(square)
            h = jnp.tanh(square * inverse_root)
            g = h * inverse_root
            g = g + g
            s, p = a * g, b * g
            h2 = h * h
            one = 1.0 + h2
            through = 1.0 - h2
            inverse = 1.0 / (one + s * ratio)
            direct = jnp.exp2(depth * slant)
            factor = (1.0 - direct) * (1.0 / depth)
            up, down = factor * away, factor * along
            push = inverse * (direct * source + (ratio - 1.0) * down)
            ratio = (one * ratio + p) * inverse
            gain = through * inverse
            source = through * push + (ratio + 1.0) * up
            gain_ref[level, span] = gain
            offset_ref[level, span] = (gain * up + down) - s * push
            direct_ref[level, span] = direct
        ratio_ref[span] = ratio
        source_ref[span] = source

    def below_block(step, carry):
        block = blocks - 1 - step
        for c in range(CHUNKS):
            def turn(n, carry, c=c):
                below(block, c)
                if c + 1 < CHUNKS:
                    fill(block, c + 1)
                else:
                    fill(jnp.maximum(block - 1, 0), 0)
                return carry

            lax.fori_loop(0, once, turn, 0)
        return carry

    fill(blocks - 1, 0)
    lax.fori_loop(0, blocks, below_block, 0)

    def folded(net):
        return sum(net[8 * k : 8 * (k + 1)] for k in range(gpoints // 8))

    def top(step, carry):
        beam = weight_ref[...] * cosine
        net = -(source_ref[...] * beam) / (1.0 + ratio_ref[...])
        partial_ref[pl.ds(pl.multiple_of(row * 8, 8), 8), :] = folded(beam) + folded(net)
        return net, beam

    nothing = jnp.zeros((gpoints, lanes), jnp.float32)
    carry = lax.fori_loop(0, once, top, (nothing, nothing))

    def down_group(group, carry):
        net, beam = carry
        for j in range(GROUP):
            level = group * GROUP + j
            net = gain_ref[level] * net + offset_ref[level] * beam
            beam = beam * direct_ref[level]
            start = pl.multiple_of(((level + 1) * count + row) * 8, 8)
            partial_ref[pl.ds(start, 8), :] = folded(net) + folded(beam)
        return (net, beam)

    lax.fori_loop(0, level_count // GROUP, down_group, carry)


def level_heating(partial_ref, level_count, gpoints, count, write):
    def flux(level):
        start = level * count * 8
        return sum(partial_ref[pl.ds(start + k, count, stride=8), :] for k in range(8))

    def step(level, upper):
        lower = flux(level + 1)
        write(level, (level_count / gpoints) * (upper - lower))
        return lower

    lax.fori_loop(0, level_count, step, flux(0))


def home_kernel(
    first, state_ref, temp_ref, cosine_ref, ground_ref, day_ref, molecular_ref, table_ref,
    heat_ref, optics_ref, weight_ref, terms_ref, right_ref, *scratch,
):
    level_count, lines, lanes = temp_ref.shape
    gpoints = weight_ref.shape[0]
    row, count = pl.program_id(0), pl.num_programs(0)

    @pl.when(row == 0)
    def prepare():
        optics_matrices(molecular_ref, table_ref, optics_ref, weight_ref)
        heat_ref[...] = jnp.zeros_like(heat_ref)
        prepare_terms(state_ref, temp_ref, terms_ref, right_ref)

    line = first + row
    sweep_row(
        row, line, lines, count, cosine_ref[pl.ds(line, 1), :], ground_ref[pl.ds(line, 1), :],
        optics_ref, weight_ref, terms_ref, right_ref, *scratch,
    )

    @pl.when(row == count - 1)
    def finish():
        size = heat_ref.shape[0] // level_count
        rows = slice(first, first + size)
        day = day_ref[rows, :] == 1

        def write(level, value):
            heat_ref[pl.ds(level * size, size), :] = jnp.where(day, value, 0.0)

        level_heating(scratch[PARTIAL], level_count, gpoints, size, write)


def prepare_terms(state_ref, temp_ref, terms_ref, right_ref):
    level_count, lines, lanes = temp_ref.shape
    right_ref[...] = jnp.zeros_like(right_ref)

    def level(l, carry):
        write_terms(terms_ref, l, layer_terms(state_ref, temp_ref, l), lines)
        return carry

    lax.fori_loop(0, level_count, level, 0, unroll=2)


def pack_kernel(
    places_ref, state_ref, temp_ref, flow_ref, cosine_ref, ground_ref,
    sent_ref, kept_ref, fields_ref, own_ref,
):
    level_count, lines, lanes = temp_ref.shape
    count = sent_ref.shape[1]

    def level(l, carry):
        for k, value in enumerate(layer_terms(state_ref, temp_ref, l)):
            own_ref[pl.ds(pl.multiple_of((5 * l + k) * lines, 8), lines), :] = value
        fields_ref[0, l] = temp_ref[l]
        fields_ref[1, l] = flow_ref[0, l]
        fields_ref[2, l] = flow_ref[1, l]
        return carry

    lax.fori_loop(0, level_count, level, 0, unroll=4)
    for n, ref in enumerate((kept_ref, sent_ref)):
        first = places_ref[n]

        def copy(n, carry, ref=ref, first=first):
            ref[n] = own_ref[pl.ds(n * lines + first, count), :]
            return carry

        lax.fori_loop(0, 5 * level_count, copy, 0, unroll=8)
        ref[5 * level_count] = cosine_ref[pl.ds(first, count), :]
        ref[5 * level_count + 1] = ground_ref[pl.ds(first, count), :]


def shared_kernel(
    places_ref, kept_ref, received_ref, day_ref, optics_ref, weight_ref, edge_ref,
    mine_ref, theirs_ref, their_first_ref, their_last_ref,
    surface_ref, strip_ref, terms_ref, right_ref, *scratch,
):
    level_count = kept_ref.shape[0] // 5
    shared, lanes = kept_ref.shape[1:]
    gpoints = weight_ref.shape[0]
    row, count = pl.program_id(0), pl.num_programs(0)
    first = places_ref[0]
    day = day_ref[pl.ds(first, shared), :] == 1

    @pl.when(row == 0)
    def prepare():
        right_ref[...] = jnp.zeros_like(right_ref)

        def level(l, carry):
            values = [
                jnp.where(day, kept_ref[5 * l + k], received_ref[5 * l + k]) for k in range(5)
            ]
            write_terms(terms_ref, l, values, shared)
            return carry

        lax.fori_loop(0, level_count, level, 0, unroll=4)
        for n in range(2):
            place = 5 * level_count + n
            surface_ref[n, :shared, :] = jnp.where(day, kept_ref[place], received_ref[place])

    sweep_row(
        row, row, shared, count, surface_ref[0, pl.ds(row, 1), :],
        surface_ref[1, pl.ds(row, 1), :], optics_ref, weight_ref, terms_ref, right_ref, *scratch,
    )

    @pl.when(row == count - 1)
    def finish():
        def write(level, value):
            span = pl.ds(level * shared, shared)
            mine_ref[span, :] = jnp.where(day, value, 0.0)
            theirs_ref[span, :] = jnp.where(day, 0.0, value)

        level_heating(scratch[PARTIAL], level_count, gpoints, shared, write)
        strip_ref[...] = jnp.zeros_like(strip_ref)
        for r in range(shared):
            start = pl.multiple_of(8 * (first + r), 8)
            write_strip(theirs_ref, r, shared, strip_ref, start)
        packed = split_dot(strip_ref[...], edge_ref[...])
        their_first_ref[...] = packed[:, :lanes]
        their_last_ref[...] = packed[:, lanes:]


def write_strip(source_ref, r, lines, strip_ref, start):
    lanes = source_ref.shape[1]
    for k in range(strip_ref.shape[1] // lanes):
        strip_ref[pl.ds(start, 8), lanes * k : lanes * (k + 1)] = source_ref[
            pl.ds(8 * k * lines + r, 8, stride=lines), :
        ]


def last_home_kernel(
    places_ref, state_ref, temp_ref, cosine_ref, ground_ref, day_ref, optics_ref, weight_ref,
    edge_ref, home_ref, mine_ref,
    heat_ref, first_ref, last_ref, strip_ref, terms_ref, right_ref, *scratch,
):
    level_count, lines, lanes = temp_ref.shape
    gpoints = weight_ref.shape[0]
    row = pl.program_id(0)
    line = lines // 2 - 1
    prepare_terms(state_ref, temp_ref, terms_ref, right_ref)
    sweep_row(
        row, line, lines, 1, cosine_ref[pl.ds(line, 1), :], ground_ref[pl.ds(line, 1), :],
        optics_ref, weight_ref, terms_ref, right_ref, *scratch,
    )
    first = places_ref[0]
    shared = mine_ref.shape[0] // level_count
    day = day_ref[line : line + 1, :] == 1
    heat_ref[...] = jnp.zeros_like(heat_ref)

    def write(level, value):
        start = pl.multiple_of(level * lines, 8)
        heat_ref[pl.ds(start, line), :] = home_ref[pl.ds(level * line, line), :]
        heat_ref[pl.ds(start + line, 1), :] = jnp.where(day, value, 0.0)
        heat_ref[pl.ds(start + first, shared), :] = mine_ref[pl.ds(level * shared, shared), :]

    level_heating(scratch[PARTIAL], level_count, gpoints, 1, write)
    for r in range(lines):
        write_strip(heat_ref, r, lines, strip_ref, 8 * r)
    packed = split_dot(strip_ref[...], edge_ref[...])
    first_ref[...] = packed[:, :lanes]
    last_ref[...] = packed[:, lanes:]


def radiation(state, temper, flow, cosine, ground, day, molecular, condensate):
    level_count, rows, lanes = temper.shape
    gpoints = molecular.shape[1]
    home, shared = rows // 2, rows // 4
    partner = lax.axis_size("gx") // 2
    low = lax.axis_index("gx") < partner
    places = jnp.where(
        low, jnp.array([home, home + shared], jnp.int32), jnp.array([home + shared, home], jnp.int32)
    )
    full = pltpu.VMEM((level_count, gpoints, lanes), jnp.float32)
    plane = pltpu.VMEM((gpoints, lanes), jnp.float32)
    whole = pl.BlockSpec(memory_space=pltpu.VMEM)
    scalar = pl.BlockSpec(memory_space=pltpu.SMEM)
    params = pltpu.CompilerParams(vmem_limit_bytes=60 * 1024 * 1024)
    part = (QUANTITIES * gpoints // CHUNKS, GROUP * TERMS)
    strip = pltpu.VMEM((8 * rows, level_count // 8 * lanes), jnp.float32)

    def field(lines):
        return jax.ShapeDtypeStruct((level_count * lines, lanes), jnp.float32)

    def scratch(lines, count):
        return [
            pltpu.VMEM((level_count * TERMS * lines, lanes), jnp.float32),
            pltpu.VMEM((level_count // 2, GROUP * TERMS, 2 * lanes), jnp.bfloat16),
            pltpu.VMEM((BLOCK // 2, part[0], 2 * lanes), jnp.float32),
            pltpu.VMEM((BLOCK // 2, part[0], 2 * lanes), jnp.float32),
            full, full, full,
            pltpu.VMEM(((level_count + 1) * count * 8, lanes), jnp.float32),
            plane, plane,
            pltpu.VMEM((8, lanes), jnp.float32),
        ]

    def cost(count):
        cells = level_count * gpoints * count * lanes
        return pl.CostEstimate(
            flops=45 * cells, bytes_accessed=32 * temper.size, transcendentals=5 * cells
        )

    state_rows = jax.ShapeDtypeStruct((5 * level_count + 2, shared, lanes), jnp.float32)
    sent, kept, fields = pl.pallas_call(
        pack_kernel,
        out_shape=(
            state_rows, state_rows,
            jax.ShapeDtypeStruct((3, level_count, rows, lanes), jnp.float32),
        ),
        in_specs=[scalar] + [whole] * 5, out_specs=(whole,) * 3,
        scratch_shapes=[pltpu.VMEM((5 * level_count * rows, lanes), jnp.float32)],
        compiler_params=params, name="pack",
    )(places, state, temper, flow, cosine, ground)
    received = shifted(sent, "gx", partner)
    fields_after, fields_before = shifted(fields, "gx", -1), shifted(fields, "gx", 1)
    early = home - 1
    home_heat, optics, weight = pl.pallas_call(
        functools.partial(home_kernel, 0),
        out_shape=(
            field(early),
            jax.ShapeDtypeStruct((level_count // GROUP, CHUNKS) + part, jnp.bfloat16),
            jax.ShapeDtypeStruct((gpoints, lanes), jnp.float32),
        ),
        grid=(early,), in_specs=[whole] * 7, out_specs=(whole,) * 3,
        scratch_shapes=scratch(rows, early), compiler_params=params, cost_estimate=cost(early),
        name="home_radiation",
    )(state, temper, cosine, ground, day, molecular.transpose(0, 2, 1), condensate)
    edge = jax.ShapeDtypeStruct((8 * rows, lanes), jnp.float32)
    edges = edge_matrix(level_count, lanes)
    mine, theirs, their_first, their_last = pl.pallas_call(
        shared_kernel,
        out_shape=(field(shared), field(shared), edge, edge),
        grid=(shared,), in_specs=[scalar] + [whole] * 6, out_specs=(whole,) * 4,
        scratch_shapes=[pltpu.VMEM((2, 8, lanes), jnp.float32), strip] + scratch(shared, shared),
        compiler_params=params, cost_estimate=cost(shared), name="shared_radiation",
    )(places, kept, received, day, optics, weight, edges)
    returned = shifted(theirs, "gx", partner)
    after_more = shifted(their_first, "gx", partner - 1)
    before_more = shifted(their_last, "gx", partner + 1)
    heat, first, last = pl.pallas_call(
        last_home_kernel,
        out_shape=(field(rows), edge, edge),
        grid=(1,), in_specs=[scalar] + [whole] * 10, out_specs=(whole,) * 3,
        scratch_shapes=[strip] + scratch(rows, 1),
        compiler_params=params, cost_estimate=cost(1), name="last_home_radiation",
    )(places, state, temper, cosine, ground, day, optics, weight, edges, home_heat, mine)
    after, before = shifted(first, "gx", -1), shifted(last, "gx", 1)
    return (
        heat, returned, places, after, before, after_more, before_more, fields_after, fields_before
    )


def edge_matrix(level_count, lanes):
    parts = level_count // 8
    width = lanes // parts
    matrix = np.zeros((parts * lanes, 2 * lanes), np.float32)
    for k in range(parts):
        for c in range(width):
            matrix[lanes * k + c, width * k + c] = 1.0
            matrix[lanes * (k + 1) - width + c, lanes + width * k + c] = 1.0
    return jnp.asarray(matrix, jnp.bfloat16)


def slope_matrices(lanes):
    whole = np.kron(np.eye(2 * lanes // NODES), gll_derivative().T).astype(np.float32)
    high = np.asarray(whole, jnp.bfloat16)
    low = np.asarray(whole - high.astype(np.float32), jnp.bfloat16)
    return jnp.asarray(high), jnp.asarray(low)


def average_matrix(lanes):
    size = 2 * lanes
    matrix = np.eye(size, dtype=np.float32)
    for c in range(NODES - 1, size, NODES):
        after = (c + 1) % size
        matrix[c, c] = matrix[after, after] = matrix[c, after] = matrix[after, c] = 0.5
    return jnp.asarray(matrix, jnp.bfloat16)


def split_dot(values, *matrices):
    high, low = high_low(values)
    total = jnp.dot(high, matrices[0], preferred_element_type=jnp.float32)
    total = total + jnp.dot(low, matrices[0], preferred_element_type=jnp.float32)
    if len(matrices) > 1:
        total = total + jnp.dot(high, matrices[1], preferred_element_type=jnp.float32)
    return total


def slope_y(rows_of):
    derivative = gll_derivative()
    result = []
    for r in range(len(rows_of)):
        first = r // NODES * NODES
        total = None
        for n in range(NODES):
            weight = derivative[r - first, n]
            if abs(weight) > 1e-12:
                term = np.float32(weight) * rows_of[first + n]
                total = term if total is None else total + term
        result.append(total)
    return result


def average_y(rows_of, below, above):
    result = list(rows_of)
    count = len(rows_of)
    for r in range(NODES - 1, count - 1, NODES):
        result[r] = result[r + 1] = 0.5 * (rows_of[r] + rows_of[r + 1])
    result[0] = 0.5 * (below + rows_of[0])
    result[count - 1] = 0.5 * (rows_of[count - 1] + above)
    return result


def own_change_kernel(
    temp_ref, flow_ref, after_ref, before_ref,
    high_ref, low_ref, change_ref, wind_ref, temp_wide_ref, slope_ref,
):
    level_count = change_ref.shape[0] // ROWS
    lanes = temp_ref.shape[-1]
    lane = lax.broadcasted_iota(jnp.int32, (level_count, lanes), 1)

    def tiles(own, after, before, r):
        span = pl.ds(r, level_count, stride=ROWS)
        side = jnp.where(lane < EDGE, after[span, :], 0.0)
        return own[span, :], jnp.where(lane >= lanes - EDGE, before[span, :], side)

    for r in range(ROWS):
        rows = slice(r * level_count, (r + 1) * level_count)
        pairs = [
            tiles(own, after_ref.at[n], before_ref.at[n], r)
            for n, own in enumerate((temp_ref, flow_ref.at[0], flow_ref.at[1]))
        ]
        for half in range(2):
            span = slice(half * lanes, (half + 1) * lanes)
            temp_wide_ref[rows, span] = pairs[0][half]
            wind_ref[0, rows, span] = pairs[1][half]
            wind_ref[1, rows, span] = pairs[2][half]
    slope_ref[...] = split_dot(temp_wide_ref[...], high_ref[...], low_ref[...])
    advect(temp_wide_ref, slope_ref, wind_ref, change_ref, level_count)


def advect(field_ref, slope_ref, wind_ref, change_ref, level_count):
    spans = [slice(r * level_count, (r + 1) * level_count) for r in range(ROWS)]
    for half in range(2):
        lanes = field_ref.shape[1] // 2
        part = slice(half * lanes, (half + 1) * lanes)
        slopes = slope_y([field_ref[span, part] for span in spans])
        for span, slope in zip(spans, slopes):
            change = wind_ref[0, span, part] * slope_ref[span, part]
            change_ref[span, part] = -TIME_INCREMENT * (change + wind_ref[1, span, part] * slope)


def write_averaged(change, average_ref, out_ref, first_ref, last_ref):
    level_count = first_ref.shape[0]
    out_ref[...] = split_dot(change, average_ref[...])
    width = first_ref.shape[1]
    first_ref[...] = out_ref[:level_count, :width]
    last_ref[...] = out_ref[out_ref.shape[0] - level_count :, :width]


def first_stage_kernel(
    places_ref, change_ref, heat_ref, returned_ref, after_ref, before_ref, after_more_ref,
    before_more_ref, edge_ref, average_ref,
    out_ref, first_ref, last_ref, heat_out_ref, sum_ref,
):
    level_count = first_ref.shape[0]
    lanes = heat_ref.shape[1]
    shared = returned_ref.shape[0] // level_count
    after = after_ref[...] + after_more_ref[...]
    before = before_ref[...] + before_more_ref[...]
    sides = split_dot(jnp.concatenate([after, before], axis=1), edge_ref[...])
    for r in range(ROWS):
        rows = slice(r * level_count, (r + 1) * level_count)
        span = pl.ds(r, level_count, stride=ROWS)
        own = heat_ref[span, :]
        if r >= ROWS // 2:
            n = r % shared
            here = places_ref[1] == r - n
            own = own + jnp.where(
                here, returned_ref[pl.ds(n, level_count, stride=shared), :], 0.0
            )
        heat_out_ref[span, :] = own
        sum_ref[rows, :lanes] = change_ref[rows, :lanes] + TIME_INCREMENT * own
        for k in range(level_count // 8):
            side = sides[8 * r : 8 * (r + 1), lanes * k : lanes * (k + 1)]
            here = slice(r * level_count + 8 * k, r * level_count + 8 * (k + 1))
            sum_ref[here, lanes:] = change_ref[here, lanes:] + TIME_INCREMENT * side
    write_averaged(sum_ref[...], average_ref, out_ref, first_ref, last_ref)


def next_stage_kernel(
    share, native, field_ref, below_ref, above_ref, wind_ref, sum_ref, high_ref, low_ref,
    average_ref, out_ref, first_ref, last_ref, total_ref, wave_ref, slope_ref, change_ref,
):
    level_count = below_ref.shape[0]
    lanes = sum_ref.shape[1]
    spans = [slice(r * level_count, (r + 1) * level_count) for r in range(ROWS)]
    for half in range(2):
        part = slice(half * lanes, (half + 1) * lanes)
        wave = average_y(
            [field_ref[span, part] for span in spans], below_ref[:, part], above_ref[:, part]
        )
        for r, (span, row) in enumerate(zip(spans, wave)):
            wave_ref[span, part] = row
            if half == 0:
                before = sum_ref[pl.ds(r, level_count, stride=ROWS), :] if native else sum_ref[span]
                total_ref[span] = before + share * row
    slope_ref[...] = split_dot(wave_ref[...], high_ref[...], low_ref[...])
    advect(wave_ref, slope_ref, wind_ref, change_ref, level_count)
    write_averaged(change_ref[...], average_ref, out_ref, first_ref, last_ref)


def last_kernel(share, field_ref, below_ref, above_ref, sum_ref, total_ref):
    level_count, lanes = below_ref.shape
    spans = [slice(r * level_count, (r + 1) * level_count) for r in range(ROWS)]
    wave = average_y([field_ref[span, :lanes] for span in spans], below_ref[...], above_ref[...])
    for r, (span, row) in enumerate(zip(spans, wave)):
        total_ref[pl.ds(r, level_count, stride=ROWS), :] = sum_ref[span] + share * row


def local(
    atmospheric_constituents,
    thermal_ratio,
    flow_velocity,
    solar_elevation_factor,
    ground_reflectivity,
    sunlit_indicator,
    molecular_optics_lookup,
    condensate_optics_lookup,
):
    level_count, rows, lanes = thermal_ratio.shape
    size = level_count * rows
    temper = thermal_ratio.reshape(size, lanes)
    flow = flow_velocity.reshape(2, size, lanes)
    field = jax.ShapeDtypeStruct((size, lanes), jnp.float32)
    wide = jax.ShapeDtypeStruct((size, 2 * lanes), jnp.float32)
    line = jax.ShapeDtypeStruct((level_count, 2 * lanes), jnp.float32)
    short = jax.ShapeDtypeStruct((level_count, lanes), jnp.float32)
    wide_scratch = pltpu.VMEM(wide.shape, jnp.float32)
    whole = pl.BlockSpec(memory_space=pltpu.VMEM)
    scalar = pl.BlockSpec(memory_space=pltpu.SMEM)

    def call(kernel, name, outs, scratch, *values):
        return pl.pallas_call(
            kernel, out_shape=outs,
            in_specs=[scalar if value.ndim == 1 else whole for value in values],
            out_specs=jax.tree.map(lambda _: whole, outs), scratch_shapes=[wide_scratch] * scratch,
            compiler_params=pltpu.CompilerParams(vmem_limit_bytes=40 * 1024 * 1024), name=name,
        )(*values)

    slopes = slope_matrices(lanes)
    average = average_matrix(lanes)
    (
        heat, returned, places, after, before, after_more, before_more, fields_after, fields_before
    ) = radiation(
        atmospheric_constituents, thermal_ratio, flow_velocity, solar_elevation_factor,
        ground_reflectivity, sunlit_indicator, molecular_optics_lookup, condensate_optics_lookup,
    )
    fields_after = fields_after.reshape(3, size, lanes)
    fields_before = fields_before.reshape(3, size, lanes)
    change, wind = call(
        own_change_kernel, "own_change",
        (wide, jax.ShapeDtypeStruct((2, size, 2 * lanes), jnp.float32)), 2,
        temper, flow, fields_after, fields_before, *slopes,
    )
    wave, first, last, heat = call(
        first_stage_kernel, "first_stage", (wide, line, line, field), 1,
        places, change, heat, returned, after, before, after_more, before_more,
        edge_matrix(level_count, lanes).T, average,
    )
    below, above = shifted(last, "gy", 1), shifted(first, "gy", -1)
    wave, first, last, total = call(
        functools.partial(next_stage_kernel, 1.0, True), "second_stage",
        (wide, line, line, field), 3, wave, below, above, wind, temper, *slopes, average,
    )
    below, above = shifted(last, "gy", 1), shifted(first, "gy", -1)
    wave, first, last, total = call(
        functools.partial(next_stage_kernel, 0.5, False), "third_stage",
        (wide, short, short, field), 3, wave, below, above, wind, total, *slopes, average,
    )
    below, above = shifted(last, "gy", 1), shifted(first, "gy", -1)
    total = call(
        functools.partial(last_kernel, 1.0 / 6.0), "last_stage", field, 0,
        wave, below, above, total,
    )
    return (heat.reshape(thermal_ratio.shape), total.reshape(thermal_ratio.shape))


def solution(mesh):
    in_specs = (
        P(None, None, "gy", "gx"),
        P(None, "gy", "gx"),
        P(None, None, "gy", "gx"),
        P("gy", "gx"),
        P("gy", "gx"),
        P("gy", "gx"),
        P(),
        P(),
    )
    out_specs = (P(None, "gy", "gx"), P(None, "gy", "gx"))
    return jax.shard_map(local, mesh=mesh, in_specs=in_specs, out_specs=out_specs, check_vma=False)
```

```python
import functools

import jax
import jax.numpy as jnp
import numpy as np
from jax import lax
from jax.experimental import pallas as pl
from jax.experimental.pallas import tpu as pltpu
from jax.sharding import PartitionSpec as P

NODES = 4
TIME_INCREMENT = 0.05
ROWS = 8
LOG2E = 1.4426950408889634

GROUP = 8
TERMS = 16
BLOCK = 12
PARTIAL = 5
CHUNKS = 2
QUANTITIES = 4


def shifted(value, axis, steps):
    count = lax.axis_size(axis)
    return lax.ppermute(value, axis, [(i, (i + steps) % count) for i in range(count)])


def gll_derivative():
    points = np.array([-1.0, -1.0 / np.sqrt(5.0), 1.0 / np.sqrt(5.0), 1.0])
    legendre = 0.5 * (5.0 * points**3 - 3.0 * points)
    derivative = np.zeros((4, 4))
    for source in range(4):
        for target in range(4):
            if source != target:
                derivative[source, target] = legendre[source] / (
                    legendre[target] * (points[source] - points[target])
                )
    derivative[0, 0] = -3.0
    derivative[3, 3] = 3.0
    return derivative


def high_low(values):
    high = values.astype(jnp.bfloat16)
    return high, (values - high.astype(jnp.float32)).astype(jnp.bfloat16)


def across(left, right, precision=None):
    return lax.dot_general(
        left, right, (((0,), (0,)), ((), ())), precision=precision,
        preferred_element_type=jnp.float32,
    )


def optics_matrices(molecular_ref, table_ref, optics_ref, weight_ref):
    level_count, gpoints = molecular_ref.shape[1:]
    groups = level_count // GROUP
    width = GROUP * TERMS
    level = lax.broadcasted_iota(jnp.int32, (level_count, groups * width), 0)
    lane = lax.broadcasted_iota(jnp.int32, (level_count, groups * width), 1)
    here = level == lane // TERMS
    term = lane % TERMS
    gases = []
    for k in range(3):
        high, low = high_low(molecular_ref[k])
        spread = [
            jnp.where(here & chosen, 1.0, 0.0).astype(jnp.bfloat16)
            for chosen in ((term == k) | (term == k + 10), term == k + 5)
        ]
        gases.append(across(high, spread[0]) + across(low, spread[1]))
    w = [table_ref[n : n + 1, :] for n in range(7)]
    ls, li = w[0] * w[1], w[3] * w[4]
    la, ia = w[0] * (1.0 - w[1]), w[3] * (1.0 - w[4])
    place = lax.broadcasted_iota(jnp.int32, (8, width), 0)
    term = lax.broadcasted_iota(jnp.int32, (8, width), 1) % TERMS
    pattern = jnp.zeros((8, width), jnp.float32)
    for n, chosen in enumerate((
        (term == 3) | (term == 13), term == 8, (term == 4) | (term == 14), term == 9
    )):
        pattern = jnp.where((place == n) & chosen, 1.0, pattern)
    empty = jnp.zeros((4, gpoints), jnp.float32)

    def water(*values):
        parts = []
        for value in values:
            high = value.astype(jnp.bfloat16).astype(jnp.float32)
            parts += [high, value - high]
        return across(jnp.concatenate(parts + [empty], axis=0), pattern, lax.Precision.HIGHEST)

    absorbed = gases[0] + gases[1]
    gas = absorbed + gases[2]
    pairs = (
        (absorbed, water(la, ia)),
        (gas, water(la + ls * (1.0 - w[2]), ia + li * (1.0 - w[5]))),
        (gas + gas, water(2.0 * w[0], 2.0 * w[3])),
        (gases[2], water(ls * (1.0 + w[2]), li * (1.0 + w[5]))),
    )
    chunk = gpoints // CHUNKS
    for group in range(groups):
        span = slice(group * width, (group + 1) * width)
        tables = [values[:, span] + constant for values, constant in pairs]
        for c in range(CHUNKS):
            rows = [table[c * chunk : (c + 1) * chunk] for table in tables]
            optics_ref[group, c] = jnp.concatenate(rows, axis=0).astype(jnp.bfloat16)
    only = jnp.where(place == 0, 1.0, 0.0)
    weight = jnp.broadcast_to(w[6], (8, gpoints))
    weight_ref[...] = across(weight, only, lax.Precision.HIGHEST)


def layer_terms(state_ref, temp_ref, level):
    lines = state_ref.shape[2]
    thickness = state_ref[2, level]
    temper = temp_ref[pl.ds(pl.multiple_of(level * lines, 8), lines), :]
    weighted = thickness * temper * temper
    return (
        weighted * state_ref[0, level], weighted * state_ref[1, level], thickness,
        state_ref[3, level], state_ref[4, level],
    )


def write_terms(terms_ref, level, values, lines):
    parts = [None] * TERMS
    for k, value in enumerate(values):
        high = value.astype(jnp.bfloat16).astype(jnp.float32)
        parts[k], parts[k + 5], parts[k + 10] = high, high, value - high
    parts[15] = jnp.zeros_like(values[0])
    for k, part in enumerate(parts):
        start = (level * TERMS + k) * lines
        start = pl.multiple_of(start, 8) if lines % 8 == 0 else start
        terms_ref[pl.ds(start, lines), :] = part


def sweep_row(
    row, line, lines, count, cosine, ground, optics_ref, weight_ref, terms_ref, right_ref,
    depths_0, depths_1, gain_ref, offset_ref, direct_ref, partial_ref, ratio_ref, source_ref, slant_ref,
):
    level_count, gpoints, lanes = gain_ref.shape
    blocks = level_count // BLOCK
    chunk = gpoints // CHUNKS
    slots = (depths_0, depths_1)
    once = 1 + jnp.minimum(row, 0)

    def place_group(group, carry):
        for j in range(GROUP):
            start = (group * GROUP + j) * TERMS * lines + line
            tile = terms_ref[pl.ds(start, TERMS, stride=lines), :].astype(jnp.bfloat16)
            half = lanes * (j % 2)
            pair = group * (GROUP // 2) + j // 2
            right_ref[pair, TERMS * j : TERMS * (j + 1), half : half + lanes] = tile
        return carry

    lax.fori_loop(0, level_count // GROUP, place_group, 0)
    slant_ref[...] = jnp.broadcast_to((-0.5 * LOG2E) / cosine, (8, lanes))

    def over_rows(values):
        return jnp.broadcast_to(values[None], (gpoints // 8, 8, lanes)).reshape(gpoints, lanes)

    clear = 1.0 / (1.0 - ground)
    ratio_ref[...] = over_rows(jnp.broadcast_to((1.0 + ground) * clear, (8, lanes)))
    source_ref[...] = over_rows(jnp.broadcast_to(2.0 * ground * clear, (8, lanes)))

    def fill(block, c):
        for p in range(BLOCK // 2):
            pair = block * (BLOCK // 2) + p
            slots[c % 2][p] = jnp.dot(
                optics_ref[pair // (GROUP // 2), c], right_ref[pair],
                preferred_element_type=jnp.float32,
            )

    def below(block, c):
        span = slice(c * chunk, (c + 1) * chunk)
        ratio, source = ratio_ref[span], source_ref[span]
        slant = jnp.broadcast_to(slant_ref[...][None], (chunk // 8, 8, lanes))
        slant = slant.reshape(chunk, lanes)
        for j in reversed(range(BLOCK)):
            level = block * BLOCK + j
            part = slots[c % 2].at[j // 2, :, (j % 2) * lanes : (j % 2 + 1) * lanes]
            a, b, depth, along = [part[n * chunk : (n + 1) * chunk] for n in range(QUANTITIES)]
            away = b - a
            square = a * b
            inverse_root = lax.rsqrt(square)
            h = jnp.tanh(square * inverse_root)
            g = h * inverse_root
            g = g + g
            s, p = a * g, b * g
            h2 = h * h
            one = 1.0 + h2
            through = 1.0 - h2
            inverse = 1.0 / (one + s * ratio)
            direct = jnp.exp2(depth * slant)
            factor = (1.0 - direct) * (1.0 / depth)
            up, down = factor * away, factor * along
            push = inverse * (direct * source + (ratio - 1.0) * down)
            ratio = (one * ratio + p) * inverse
            gain = through * inverse
            source = through * push + (ratio + 1.0) * up
            gain_ref[level, span] = gain
            offset_ref[level, span] = (gain * up + down) - s * push
            direct_ref[level, span] = direct
        ratio_ref[span] = ratio
        source_ref[span] = source

    def below_block(step, carry):
        block = blocks - 1 - step
        for c in range(CHUNKS):
            def turn(n, carry, c=c):
                below(block, c)
                if c + 1 < CHUNKS:
                    fill(block, c + 1)
                else:
                    fill(jnp.maximum(block - 1, 0), 0)
                return carry

            lax.fori_loop(0, once, turn, 0)
        return carry

    fill(blocks - 1, 0)
    lax.fori_loop(0, blocks, below_block, 0)

    def folded(net):
        return sum(net[8 * k : 8 * (k + 1)] for k in range(gpoints // 8))

    def top(step, carry):
        beam = weight_ref[...] * cosine
        net = -(source_ref[...] * beam) / (1.0 + ratio_ref[...])
        partial_ref[pl.ds(pl.multiple_of(row * 8, 8), 8), :] = folded(beam) + folded(net)
        return net, beam

    nothing = jnp.zeros((gpoints, lanes), jnp.float32)
    carry = lax.fori_loop(0, once, top, (nothing, nothing))

    def down_group(group, carry):
        net, beam = carry
        for j in range(GROUP):
            level = group * GROUP + j
            net = gain_ref[level] * net + offset_ref[level] * beam
            beam = beam * direct_ref[level]
            start = pl.multiple_of(((level + 1) * count + row) * 8, 8)
            partial_ref[pl.ds(start, 8), :] = folded(net) + folded(beam)
        return (net, beam)

    lax.fori_loop(0, level_count // GROUP, down_group, carry)


def level_heating(partial_ref, level_count, gpoints, count, write):
    def flux(level):
        start = level * count * 8
        return sum(partial_ref[pl.ds(start + k, count, stride=8), :] for k in range(8))

    def step(level, upper):
        lower = flux(level + 1)
        write(level, (level_count / gpoints) * (upper - lower))
        return lower

    lax.fori_loop(0, level_count, step, flux(0), unroll=4)


def home_kernel(
    first, state_ref, temp_ref, cosine_ref, ground_ref, day_ref, molecular_ref, table_ref,
    heat_ref, optics_ref, weight_ref, terms_ref, right_ref, *scratch,
):
    level_count, lines, lanes = state_ref.shape[1:]
    gpoints = weight_ref.shape[0]
    row, count = pl.program_id(0), pl.num_programs(0)

    @pl.when(row == 0)
    def prepare():
        optics_matrices(molecular_ref, table_ref, optics_ref, weight_ref)
        heat_ref[...] = jnp.zeros_like(heat_ref)
        prepare_terms(state_ref, temp_ref, terms_ref, right_ref)

    line = first + row
    sweep_row(
        row, line, lines, count, cosine_ref[pl.ds(line, 1), :], ground_ref[pl.ds(line, 1), :],
        optics_ref, weight_ref, terms_ref, right_ref, *scratch,
    )

    @pl.when(row == count - 1)
    def finish():
        size = heat_ref.shape[0] // level_count
        rows = slice(first, first + size)
        day = day_ref[rows, :] == 1

        def write(level, value):
            heat_ref[pl.ds(level * size, size), :] = jnp.where(day, value, 0.0)

        level_heating(scratch[PARTIAL], level_count, gpoints, size, write)


def prepare_terms(state_ref, temp_ref, terms_ref, right_ref):
    level_count, lines = state_ref.shape[1:3]
    right_ref[...] = jnp.zeros_like(right_ref)

    def level(l, carry):
        write_terms(terms_ref, l, layer_terms(state_ref, temp_ref, l), lines)
        return carry

    lax.fori_loop(0, level_count, level, 0, unroll=4)


def shared_places(lines):
    low = lax.axis_index("gx") < lax.axis_size("gx") // 2
    early, late = lines // 2, lines // 2 + lines // 4
    return jnp.where(low, early, late), jnp.where(low, late, early)


def pack_kernel(
    state_ref, temp_ref, flow_ref, cosine_ref, ground_ref, edge_ref,
    sent_ref, kept_ref, line_ref, first_ref, last_ref, own_ref, strip_ref,
):
    level_count, lines, lanes = state_ref.shape[1:]

    def level(l, carry):
        for k, value in enumerate(layer_terms(state_ref, temp_ref, l)):
            own_ref[pl.ds(pl.multiple_of((5 * l + k) * lines, 8), lines), :] = value
        return carry

    lax.fori_loop(0, level_count, level, 0, unroll=4)
    mine, theirs = shared_places(lines)
    copies = ((kept_ref, mine), (sent_ref, theirs), (line_ref, lines // 2 - 1))

    def copy(n, carry):
        for ref, place in copies:
            ref[n] = own_ref[pl.ds(n * lines + place, ref.shape[1]), :]
        return carry

    lax.fori_loop(0, 5 * level_count, copy, 0, unroll=8)
    for ref, place in copies:
        ref[5 * level_count] = cosine_ref[pl.ds(place, ref.shape[1]), :]
        ref[5 * level_count + 1] = ground_ref[pl.ds(place, ref.shape[1]), :]
    for n, ref in enumerate((temp_ref, flow_ref.at[0], flow_ref.at[1])):
        for r in range(lines):
            write_strip(ref, r, lines, strip_ref, 8 * (lines * n + r))
    packed = split_dot(strip_ref[...], edge_ref[...])
    first_ref[...] = packed[:, :lanes]
    last_ref[...] = packed[:, lanes:]


def shared_kernel(
    kept_ref, received_ref, day_ref, optics_ref, weight_ref, edge_ref,
    mine_ref, theirs_ref, their_first_ref, their_last_ref,
    surface_ref, strip_ref, terms_ref, right_ref, *scratch,
):
    level_count = kept_ref.shape[0] // 5
    shared, lanes = kept_ref.shape[1:]
    gpoints = weight_ref.shape[0]
    row, count = pl.program_id(0), pl.num_programs(0)
    first = shared_places(day_ref.shape[0])[0]
    day = day_ref[pl.ds(first, shared), :] == 1

    @pl.when(row == 0)
    def prepare():
        right_ref[...] = jnp.zeros_like(right_ref)

        def level(l, carry):
            values = [
                jnp.where(day, kept_ref[5 * l + k], received_ref[5 * l + k]) for k in range(5)
            ]
            write_terms(terms_ref, l, values, shared)
            return carry

        lax.fori_loop(0, level_count, level, 0, unroll=4)
        for n in range(2):
            place = 5 * level_count + n
            surface_ref[n, :shared, :] = jnp.where(day, kept_ref[place], received_ref[place])

    sweep_row(
        row, row, shared, count, surface_ref[0, pl.ds(row, 1), :],
        surface_ref[1, pl.ds(row, 1), :], optics_ref, weight_ref, terms_ref, right_ref, *scratch,
    )

    @pl.when(row == count - 1)
    def finish():
        def write(level, value):
            span = pl.ds(level * shared, shared)
            mine_ref[span, :] = jnp.where(day, value, 0.0)
            theirs_ref[span, :] = jnp.where(day, 0.0, value)

        level_heating(scratch[PARTIAL], level_count, gpoints, shared, write)
        strip_ref[...] = jnp.zeros_like(strip_ref)
        for r in range(shared):
            start = pl.multiple_of(8 * (first + r), 8)
            write_strip(theirs_ref, r, shared, strip_ref, start)
        packed = split_dot(strip_ref[...], edge_ref[...])
        their_first_ref[...] = packed[:, :lanes]
        their_last_ref[...] = packed[:, lanes:]


def write_strip(source_ref, r, lines, strip_ref, start):
    lanes = source_ref.shape[1]
    for k in range(strip_ref.shape[1] // lanes):
        strip_ref[pl.ds(start, 8), lanes * k : lanes * (k + 1)] = source_ref[
            pl.ds(8 * k * lines + r, 8, stride=lines), :
        ]


def last_home_kernel(
    line_ref, day_ref, optics_ref, weight_ref, edge_ref, home_ref, mine_ref,
    heat_ref, first_ref, last_ref, strip_ref, terms_ref, right_ref, *scratch,
):
    lines, lanes = day_ref.shape
    level_count = line_ref.shape[0] // 5
    gpoints = weight_ref.shape[0]
    row = pl.program_id(0)
    line = lines // 2 - 1
    right_ref[...] = jnp.zeros_like(right_ref)

    def level(l, carry):
        write_terms(terms_ref, l, [line_ref[5 * l + k] for k in range(5)], 1)
        return carry

    lax.fori_loop(0, level_count, level, 0, unroll=4)
    sweep_row(
        row, 0, 1, 1, line_ref[5 * level_count], line_ref[5 * level_count + 1],
        optics_ref, weight_ref, terms_ref, right_ref, *scratch,
    )
    first = shared_places(lines)[0]
    shared = mine_ref.shape[0] // level_count
    day = day_ref[line : line + 1, :] == 1
    heat_ref[...] = jnp.zeros_like(heat_ref)

    def write(level, value):
        start = pl.multiple_of(level * lines, 8)
        heat_ref[pl.ds(start, line), :] = home_ref[pl.ds(level * line, line), :]
        heat_ref[pl.ds(start + line, 1), :] = jnp.where(day, value, 0.0)
        heat_ref[pl.ds(start + first, shared), :] = mine_ref[pl.ds(level * shared, shared), :]

    level_heating(scratch[PARTIAL], level_count, gpoints, 1, write)
    for r in range(lines):
        write_strip(heat_ref, r, lines, strip_ref, 8 * r)
    packed = split_dot(strip_ref[...], edge_ref[...])
    first_ref[...] = packed[:, :lanes]
    last_ref[...] = packed[:, lanes:]


def radiation(state, temper, flow, cosine, ground, day, molecular, condensate):
    level_count, rows, lanes = temper.shape
    gpoints = molecular.shape[1]
    home, shared = rows // 2, rows // 4
    partner = lax.axis_size("gx") // 2
    temper = temper.reshape(level_count * rows, lanes)
    flow = flow.reshape(2, level_count * rows, lanes)
    full = pltpu.VMEM((level_count, gpoints, lanes), jnp.float32)
    plane = pltpu.VMEM((gpoints, lanes), jnp.float32)
    whole = pl.BlockSpec(memory_space=pltpu.VMEM)
    params = pltpu.CompilerParams(vmem_limit_bytes=60 * 1024 * 1024)
    part = (QUANTITIES * gpoints // CHUNKS, GROUP * TERMS)
    strip = pltpu.VMEM((8 * rows, level_count // 8 * lanes), jnp.float32)

    def field(lines):
        return jax.ShapeDtypeStruct((level_count * lines, lanes), jnp.float32)

    def scratch(lines, count):
        return [
            pltpu.VMEM((level_count * TERMS * lines, lanes), jnp.float32),
            pltpu.VMEM((level_count // 2, GROUP * TERMS, 2 * lanes), jnp.bfloat16),
            pltpu.VMEM((BLOCK // 2, part[0], 2 * lanes), jnp.float32),
            pltpu.VMEM((BLOCK // 2, part[0], 2 * lanes), jnp.float32),
            full, full, full,
            pltpu.VMEM(((level_count + 1) * count * 8, lanes), jnp.float32),
            plane, plane,
            pltpu.VMEM((8, lanes), jnp.float32),
        ]

    def cost(count):
        cells = level_count * gpoints * count * lanes
        return pl.CostEstimate(
            flops=10000 * cells, bytes_accessed=32 * temper.size, transcendentals=5 * cells
        )

    def state_rows(count):
        return jax.ShapeDtypeStruct((5 * level_count + 2, count, lanes), jnp.float32)

    edges = edge_matrix(level_count, lanes)
    three = jax.ShapeDtypeStruct((3 * 8 * rows, lanes), jnp.float32)
    sent, kept, line, fields_first, fields_last = pl.pallas_call(
        pack_kernel,
        out_shape=(state_rows(shared), state_rows(shared), state_rows(1), three, three),
        in_specs=[whole] * 6, out_specs=(whole,) * 5,
        scratch_shapes=[
            pltpu.VMEM((5 * level_count * rows, lanes), jnp.float32),
            pltpu.VMEM((3 * 8 * rows, level_count // 8 * lanes), jnp.float32),
        ],
        compiler_params=params, name="pack",
    )(state, temper, flow, cosine, ground, edges)
    received = shifted(sent, "gx", partner)
    fields_after, fields_before = shifted(fields_first, "gx", -1), shifted(fields_last, "gx", 1)
    early = home - 1
    home_heat, optics, weight = pl.pallas_call(
        functools.partial(home_kernel, 0),
        out_shape=(
            field(early),
            jax.ShapeDtypeStruct((level_count // GROUP, CHUNKS) + part, jnp.bfloat16),
            jax.ShapeDtypeStruct((gpoints, lanes), jnp.float32),
        ),
        grid=(early,), in_specs=[whole] * 7, out_specs=(whole,) * 3,
        scratch_shapes=scratch(rows, early), compiler_params=params, cost_estimate=cost(early),
        name="home_radiation",
    )(state, temper, cosine, ground, day, molecular.transpose(0, 2, 1), condensate)
    edge = jax.ShapeDtypeStruct((8 * rows, lanes), jnp.float32)
    mine, theirs, their_first, their_last = pl.pallas_call(
        shared_kernel,
        out_shape=(field(shared), field(shared), edge, edge),
        grid=(shared,), in_specs=[whole] * 6, out_specs=(whole,) * 4,
        scratch_shapes=[pltpu.VMEM((2, 8, lanes), jnp.float32), strip] + scratch(shared, shared),
        compiler_params=params, cost_estimate=cost(shared), name="shared_radiation",
    )(kept, received, day, optics, weight, edges)
    returned = shifted(theirs, "gx", partner)
    after_more = shifted(their_first, "gx", partner - 1)
    before_more = shifted(their_last, "gx", partner + 1)
    heat, first, last = pl.pallas_call(
        last_home_kernel,
        out_shape=(field(rows), edge, edge),
        grid=(1,), in_specs=[whole] * 7, out_specs=(whole,) * 3,
        scratch_shapes=[strip] + scratch(1, 1),
        compiler_params=params, cost_estimate=cost(1), name="last_home_radiation",
    )(line, day, optics, weight, edges, home_heat, mine)
    after, before = shifted(first, "gx", -1), shifted(last, "gx", 1)
    return (
        heat, returned, after, before, after_more, before_more, fields_after, fields_before
    )


def edge_matrix(level_count, lanes):
    parts = level_count // 8
    width = lanes // parts
    matrix = np.zeros((parts * lanes, 2 * lanes), np.float32)
    for k in range(parts):
        for c in range(width):
            matrix[lanes * k + c, width * k + c] = 1.0
            matrix[lanes * (k + 1) - width + c, lanes + width * k + c] = 1.0
    return jnp.asarray(matrix, jnp.bfloat16)


def slope_matrices(lanes):
    whole = np.kron(np.eye(2 * lanes // NODES), gll_derivative().T).astype(np.float32)
    high = np.asarray(whole, jnp.bfloat16)
    low = np.asarray(whole - high.astype(np.float32), jnp.bfloat16)
    return jnp.asarray(high), jnp.asarray(low)


def average_matrix(lanes):
    size = 2 * lanes
    matrix = np.eye(size, dtype=np.float32)
    for c in range(NODES - 1, size, NODES):
        after = (c + 1) % size
        matrix[c, c] = matrix[after, after] = matrix[c, after] = matrix[after, c] = 0.5
    return jnp.asarray(matrix, jnp.bfloat16)


def split_dot(values, *matrices):
    high, low = high_low(values)
    total = jnp.dot(high, matrices[0], preferred_element_type=jnp.float32)
    total = total + jnp.dot(low, matrices[0], preferred_element_type=jnp.float32)
    if len(matrices) > 1:
        total = total + jnp.dot(high, matrices[1], preferred_element_type=jnp.float32)
    return total


def slope_y(rows_of):
    derivative = gll_derivative()
    result = []
    for r in range(len(rows_of)):
        first = r // NODES * NODES
        total = None
        for n in range(NODES):
            weight = derivative[r - first, n]
            if abs(weight) > 1e-12:
                term = np.float32(weight) * rows_of[first + n]
                total = term if total is None else total + term
        result.append(total)
    return result


def average_y(rows_of, below, above):
    result = list(rows_of)
    count = len(rows_of)
    for r in range(NODES - 1, count - 1, NODES):
        result[r] = result[r + 1] = 0.5 * (rows_of[r] + rows_of[r + 1])
    result[0] = 0.5 * (below + rows_of[0])
    result[count - 1] = 0.5 * (rows_of[count - 1] + above)
    return result


def unpacked(after_ref, before_ref, edge_ref):
    both = jnp.concatenate([after_ref[...], before_ref[...]], axis=1)
    return split_dot(both, edge_ref[...])


def own_change_kernel(
    temp_ref, flow_ref, after_ref, before_ref, edge_ref, high_ref, low_ref,
    change_ref, wind_ref, temp_wide_ref, slope_ref,
):
    level_count = change_ref.shape[0] // ROWS
    lanes = temp_ref.shape[-1]
    sides = unpacked(after_ref, before_ref, edge_ref)
    fields = (
        (temp_ref, temp_wide_ref), (flow_ref.at[0], wind_ref.at[0]), (flow_ref.at[1], wind_ref.at[1])
    )
    for n, (own, wide) in enumerate(fields):
        for r in range(ROWS):
            start = r * level_count
            wide[start : start + level_count, :lanes] = own[pl.ds(r, level_count, stride=ROWS), :]
            here = 8 * (ROWS * n + r)
            for k in range(level_count // 8):
                wide[start + 8 * k : start + 8 * (k + 1), lanes:] = sides[
                    here : here + 8, lanes * k : lanes * (k + 1)
                ]
    slope_ref[...] = split_dot(temp_wide_ref[...], high_ref[...], low_ref[...])
    advect(temp_wide_ref, slope_ref, wind_ref, change_ref, level_count)


def advect(field_ref, slope_ref, wind_ref, change_ref, level_count):
    spans = [slice(r * level_count, (r + 1) * level_count) for r in range(ROWS)]
    for half in range(2):
        lanes = field_ref.shape[1] // 2
        part = slice(half * lanes, (half + 1) * lanes)
        slopes = slope_y([field_ref[span, part] for span in spans])
        for span, slope in zip(spans, slopes):
            change = wind_ref[0, span, part] * slope_ref[span, part]
            change_ref[span, part] = -TIME_INCREMENT * (change + wind_ref[1, span, part] * slope)


def write_averaged(change, average_ref, out_ref, first_ref, last_ref):
    level_count = first_ref.shape[0]
    out_ref[...] = split_dot(change, average_ref[...])
    width = first_ref.shape[1]
    first_ref[...] = out_ref[:level_count, :width]
    last_ref[...] = out_ref[out_ref.shape[0] - level_count :, :width]


def first_stage_kernel(
    change_ref, heat_ref, returned_ref, after_ref, before_ref, after_more_ref,
    before_more_ref, edge_ref, average_ref,
    out_ref, first_ref, last_ref, heat_out_ref, sum_ref,
):
    level_count = first_ref.shape[0]
    lanes = heat_ref.shape[1]
    shared = returned_ref.shape[0] // level_count
    after = after_ref[...] + after_more_ref[...]
    before = before_ref[...] + before_more_ref[...]
    sides = split_dot(jnp.concatenate([after, before], axis=1), edge_ref[...])
    for r in range(ROWS):
        rows = slice(r * level_count, (r + 1) * level_count)
        span = pl.ds(r, level_count, stride=ROWS)
        own = heat_ref[span, :]
        if r >= ROWS // 2:
            n = r % shared
            here = shared_places(ROWS)[1] == r - n
            own = own + jnp.where(
                here, returned_ref[pl.ds(n, level_count, stride=shared), :], 0.0
            )
        heat_out_ref[span, :] = own
        sum_ref[rows, :lanes] = change_ref[rows, :lanes] + TIME_INCREMENT * own
        for k in range(level_count // 8):
            side = sides[8 * r : 8 * (r + 1), lanes * k : lanes * (k + 1)]
            here = slice(r * level_count + 8 * k, r * level_count + 8 * (k + 1))
            sum_ref[here, lanes:] = change_ref[here, lanes:] + TIME_INCREMENT * side
    write_averaged(sum_ref[...], average_ref, out_ref, first_ref, last_ref)


def next_stage_kernel(
    share, native, field_ref, below_ref, above_ref, wind_ref, sum_ref, high_ref, low_ref,
    average_ref, out_ref, first_ref, last_ref, total_ref, wave_ref, slope_ref, change_ref,
):
    level_count = below_ref.shape[0]
    lanes = sum_ref.shape[1]
    spans = [slice(r * level_count, (r + 1) * level_count) for r in range(ROWS)]
    for half in range(2):
        part = slice(half * lanes, (half + 1) * lanes)
        wave = average_y(
            [field_ref[span, part] for span in spans], below_ref[:, part], above_ref[:, part]
        )
        for r, (span, row) in enumerate(zip(spans, wave)):
            wave_ref[span, part] = row
            if half == 0:
                before = sum_ref[pl.ds(r, level_count, stride=ROWS), :] if native else sum_ref[span]
                total_ref[span] = before + share * row
    slope_ref[...] = split_dot(wave_ref[...], high_ref[...], low_ref[...])
    advect(wave_ref, slope_ref, wind_ref, change_ref, level_count)
    write_averaged(change_ref[...], average_ref, out_ref, first_ref, last_ref)


def last_kernel(share, field_ref, below_ref, above_ref, sum_ref, total_ref):
    level_count, lanes = below_ref.shape
    spans = [slice(r * level_count, (r + 1) * level_count) for r in range(ROWS)]
    wave = average_y([field_ref[span, :lanes] for span in spans], below_ref[...], above_ref[...])
    for r, (span, row) in enumerate(zip(spans, wave)):
        total_ref[pl.ds(r, level_count, stride=ROWS), :] = sum_ref[span] + share * row


def local(
    atmospheric_constituents,
    thermal_ratio,
    flow_velocity,
    solar_elevation_factor,
    ground_reflectivity,
    sunlit_indicator,
    molecular_optics_lookup,
    condensate_optics_lookup,
):
    level_count, rows, lanes = thermal_ratio.shape
    size = level_count * rows
    temper = thermal_ratio.reshape(size, lanes)
    flow = flow_velocity.reshape(2, size, lanes)
    field = jax.ShapeDtypeStruct((size, lanes), jnp.float32)
    wide = jax.ShapeDtypeStruct((size, 2 * lanes), jnp.float32)
    line = jax.ShapeDtypeStruct((level_count, 2 * lanes), jnp.float32)
    short = jax.ShapeDtypeStruct((level_count, lanes), jnp.float32)
    wide_scratch = pltpu.VMEM(wide.shape, jnp.float32)
    whole = pl.BlockSpec(memory_space=pltpu.VMEM)

    def call(kernel, name, outs, scratch, *values):
        return pl.pallas_call(
            kernel, out_shape=outs,
            in_specs=[whole] * len(values),
            out_specs=jax.tree.map(lambda _: whole, outs), scratch_shapes=[wide_scratch] * scratch,
            compiler_params=pltpu.CompilerParams(vmem_limit_bytes=40 * 1024 * 1024), name=name,
        )(*values)

    slopes = slope_matrices(lanes)
    average = average_matrix(lanes)
    (
        heat, returned, after, before, after_more, before_more, fields_after, fields_before
    ) = radiation(
        atmospheric_constituents, thermal_ratio, flow_velocity, solar_elevation_factor,
        ground_reflectivity, sunlit_indicator, molecular_optics_lookup, condensate_optics_lookup,
    )
    back = edge_matrix(level_count, lanes).T
    change, wind = call(
        own_change_kernel, "own_change",
        (wide, jax.ShapeDtypeStruct((2, size, 2 * lanes), jnp.float32)), 2,
        temper, flow, fields_after, fields_before, back, *slopes,
    )
    wave, first, last, heat = call(
        first_stage_kernel, "first_stage", (wide, line, line, field), 1,
        change, heat, returned, after, before, after_more, before_more, back, average,
    )
    below, above = shifted(last, "gy", 1), shifted(first, "gy", -1)
    wave, first, last, total = call(
        functools.partial(next_stage_kernel, 1.0, True), "second_stage",
        (wide, line, line, field), 3, wave, below, above, wind, temper, *slopes, average,
    )
    below, above = shifted(last, "gy", 1), shifted(first, "gy", -1)
    wave, first, last, total = call(
        functools.partial(next_stage_kernel, 0.5, False), "third_stage",
        (wide, short, short, field), 3, wave, below, above, wind, total, *slopes, average,
    )
    below, above = shifted(last, "gy", 1), shifted(first, "gy", -1)
    total = call(
        functools.partial(last_kernel, 1.0 / 6.0), "last_stage", field, 0,
        wave, below, above, total,
    )
    return (heat.reshape(thermal_ratio.shape), total.reshape(thermal_ratio.shape))


def solution(mesh):
    in_specs = (
        P(None, None, "gy", "gx"),
        P(None, "gy", "gx"),
        P(None, None, "gy", "gx"),
        P("gy", "gx"),
        P("gy", "gx"),
        P("gy", "gx"),
        P(),
        P(),
    )
    out_specs = (P(None, "gy", "gx"), P(None, "gy", "gx"))
    return jax.shard_map(local, mesh=mesh, in_specs=in_specs, out_specs=out_specs, check_vma=False)
```

```python
import functools

import jax
import jax.numpy as jnp
import numpy as np
from jax import lax
from jax.experimental import pallas as pl
from jax.experimental.pallas import tpu as pltpu
from jax.sharding import PartitionSpec as P

NODES = 4
TIME_INCREMENT = 0.05
ROWS = 8
LOG2E = 1.4426950408889634

GROUP = 8
TERMS = 16
BLOCK = 12
PARTIAL = 5
CHUNKS = 2
QUANTITIES = 4


def shifted(value, axis, steps):
    count = lax.axis_size(axis)
    return lax.ppermute(value, axis, [(i, (i + steps) % count) for i in range(count)])


def gll_derivative():
    points = np.array([-1.0, -1.0 / np.sqrt(5.0), 1.0 / np.sqrt(5.0), 1.0])
    legendre = 0.5 * (5.0 * points**3 - 3.0 * points)
    derivative = np.zeros((4, 4))
    for source in range(4):
        for target in range(4):
            if source != target:
                derivative[source, target] = legendre[source] / (
                    legendre[target] * (points[source] - points[target])
                )
    derivative[0, 0] = -3.0
    derivative[3, 3] = 3.0
    return derivative


def high_low(values):
    high = values.astype(jnp.bfloat16)
    return high, (values - high.astype(jnp.float32)).astype(jnp.bfloat16)


def across(left, right, precision=None):
    return lax.dot_general(
        left, right, (((0,), (0,)), ((), ())), precision=precision,
        preferred_element_type=jnp.float32,
    )


def optics_matrices(molecular_ref, table_ref, optics_ref, weight_ref):
    level_count, gpoints = molecular_ref.shape[1:]
    groups = level_count // GROUP
    width = GROUP * TERMS
    level = lax.broadcasted_iota(jnp.int32, (level_count, groups * width), 0)
    lane = lax.broadcasted_iota(jnp.int32, (level_count, groups * width), 1)
    here = level == lane // TERMS
    term = lane % TERMS
    gases = []
    for k in range(3):
        high, low = high_low(molecular_ref[k])
        spread = [
            jnp.where(here & chosen, 1.0, 0.0).astype(jnp.bfloat16)
            for chosen in ((term == k) | (term == k + 10), term == k + 5)
        ]
        gases.append(across(high, spread[0]) + across(low, spread[1]))
    w = [table_ref[n : n + 1, :] for n in range(7)]
    ls, li = w[0] * w[1], w[3] * w[4]
    la, ia = w[0] * (1.0 - w[1]), w[3] * (1.0 - w[4])
    place = lax.broadcasted_iota(jnp.int32, (8, width), 0)
    term = lax.broadcasted_iota(jnp.int32, (8, width), 1) % TERMS
    pattern = jnp.zeros((8, width), jnp.float32)
    for n, chosen in enumerate((
        (term == 3) | (term == 13), term == 8, (term == 4) | (term == 14), term == 9
    )):
        pattern = jnp.where((place == n) & chosen, 1.0, pattern)
    empty = jnp.zeros((4, gpoints), jnp.float32)

    def water(*values):
        parts = []
        for value in values:
            high = value.astype(jnp.bfloat16).astype(jnp.float32)
            parts += [high, value - high]
        return across(jnp.concatenate(parts + [empty], axis=0), pattern, lax.Precision.HIGHEST)

    absorbed = gases[0] + gases[1]
    gas = absorbed + gases[2]
    pairs = (
        (absorbed, water(la, ia)),
        (gas, water(la + ls * (1.0 - w[2]), ia + li * (1.0 - w[5]))),
        (gas + gas, water(2.0 * w[0], 2.0 * w[3])),
        (gases[2], water(ls * (1.0 + w[2]), li * (1.0 + w[5]))),
    )
    chunk = gpoints // CHUNKS
    for group in range(groups):
        span = slice(group * width, (group + 1) * width)
        tables = [values[:, span] + constant for values, constant in pairs]
        for c in range(CHUNKS):
            rows = [table[c * chunk : (c + 1) * chunk] for table in tables]
            optics_ref[group, c] = jnp.concatenate(rows, axis=0).astype(jnp.bfloat16)
    only = jnp.where(place == 0, 1.0, 0.0)
    weight = jnp.broadcast_to(w[6], (8, gpoints))
    weight_ref[...] = across(weight, only, lax.Precision.HIGHEST)


def layer_terms(state_ref, temp_ref, level):
    lines = state_ref.shape[2]
    thickness = state_ref[2, level]
    temper = temp_ref[pl.ds(pl.multiple_of(level * lines, 8), lines), :]
    weighted = thickness * temper * temper
    return (
        weighted * state_ref[0, level], weighted * state_ref[1, level], thickness,
        state_ref[3, level], state_ref[4, level],
    )


def write_terms(terms_ref, level, values, lines):
    parts = [None] * TERMS
    for k, value in enumerate(values):
        high = value.astype(jnp.bfloat16).astype(jnp.float32)
        parts[k], parts[k + 5], parts[k + 10] = high, high, value - high
    parts[15] = jnp.zeros_like(values[0])
    for k, part in enumerate(parts):
        start = (level * TERMS + k) * lines
        start = pl.multiple_of(start, 8) if lines % 8 == 0 else start
        terms_ref[pl.ds(start, lines), :] = part


def sweep_row(
    row, line, lines, count, cosine, ground, optics_ref, weight_ref, terms_ref, right_ref,
    depths_0, depths_1, gain_ref, offset_ref, direct_ref, partial_ref, ratio_ref, source_ref, slant_ref,
):
    level_count, gpoints, lanes = gain_ref.shape
    blocks = level_count // BLOCK
    chunk = gpoints // CHUNKS
    slots = (depths_0, depths_1)
    once = 1 + jnp.minimum(row, 0)

    def place_group(group, carry):
        for j in range(GROUP):
            start = (group * GROUP + j) * TERMS * lines + line
            tile = terms_ref[pl.ds(start, TERMS, stride=lines), :].astype(jnp.bfloat16)
            half = lanes * (j % 2)
            pair = group * (GROUP // 2) + j // 2
            right_ref[pair, TERMS * j : TERMS * (j + 1), half : half + lanes] = tile
        return carry

    lax.fori_loop(0, level_count // GROUP, place_group, 0)
    slant_ref[...] = jnp.broadcast_to((-0.5 * LOG2E) / cosine, (8, lanes))

    def over_rows(values):
        return jnp.broadcast_to(values[None], (gpoints // 8, 8, lanes)).reshape(gpoints, lanes)

    clear = 1.0 / (1.0 - ground)
    ratio_ref[...] = over_rows(jnp.broadcast_to((1.0 + ground) * clear, (8, lanes)))
    source_ref[...] = over_rows(jnp.broadcast_to(2.0 * ground * clear, (8, lanes)))

    def fill(block, c):
        for p in range(BLOCK // 2):
            pair = block * (BLOCK // 2) + p
            slots[c % 2][p] = jnp.dot(
                optics_ref[pair // (GROUP // 2), c], right_ref[pair],
                preferred_element_type=jnp.float32,
            )

    def below(block, c):
        span = slice(c * chunk, (c + 1) * chunk)
        ratio, source = ratio_ref[span], source_ref[span]
        slant = jnp.broadcast_to(slant_ref[...][None], (chunk // 8, 8, lanes))
        slant = slant.reshape(chunk, lanes)
        for j in reversed(range(BLOCK)):
            level = block * BLOCK + j
            part = slots[c % 2].at[j // 2, :, (j % 2) * lanes : (j % 2 + 1) * lanes]
            a, b, depth, along = [part[n * chunk : (n + 1) * chunk] for n in range(QUANTITIES)]
            away = b - a
            square = a * b
            inverse_root = lax.rsqrt(square)
            h = jnp.tanh(square * inverse_root)
            g = h * inverse_root
            g = g + g
            s, p = a * g, b * g
            h2 = h * h
            one = 1.0 + h2
            through = 1.0 - h2
            inverse = 1.0 / (one + s * ratio)
            direct = jnp.exp2(depth * slant)
            factor = (1.0 - direct) * (1.0 / depth)
            up, down = factor * away, factor * along
            push = inverse * (direct * source + (ratio - 1.0) * down)
            ratio = (one * ratio + p) * inverse
            gain = through * inverse
            source = through * push + (ratio + 1.0) * up
            gain_ref[level, span] = gain
            offset_ref[level, span] = (gain * up + down) - s * push
            direct_ref[level, span] = direct
        ratio_ref[span] = ratio
        source_ref[span] = source

    def below_block(step, carry):
        block = blocks - 1 - step
        for c in range(CHUNKS):
            def turn(n, carry, c=c):
                below(block, c)
                if c + 1 < CHUNKS:
                    fill(block, c + 1)
                else:
                    fill(jnp.maximum(block - 1, 0), 0)
                return carry

            lax.fori_loop(0, once, turn, 0)
        return carry

    fill(blocks - 1, 0)
    lax.fori_loop(0, blocks, below_block, 0)

    def folded(net):
        return sum(net[8 * k : 8 * (k + 1)] for k in range(gpoints // 8))

    def top(step, carry):
        beam = weight_ref[...] * cosine
        net = -(source_ref[...] * beam) / (1.0 + ratio_ref[...])
        partial_ref[pl.ds(pl.multiple_of(row * 8, 8), 8), :] = folded(beam) + folded(net)
        return net, beam

    nothing = jnp.zeros((gpoints, lanes), jnp.float32)
    carry = lax.fori_loop(0, once, top, (nothing, nothing))

    def down_group(group, carry):
        net, beam = carry
        for j in range(GROUP):
            level = group * GROUP + j
            net = gain_ref[level] * net + offset_ref[level] * beam
            beam = beam * direct_ref[level]
            start = pl.multiple_of(((level + 1) * count + row) * 8, 8)
            partial_ref[pl.ds(start, 8), :] = folded(net) + folded(beam)
        return (net, beam)

    lax.fori_loop(0, level_count // GROUP, down_group, carry)


def level_heating(partial_ref, level_count, gpoints, count, write):
    def flux(level):
        start = level * count * 8
        return sum(partial_ref[pl.ds(start + k, count, stride=8), :] for k in range(8))

    def step(level, upper):
        lower = flux(level + 1)
        write(level, (level_count / gpoints) * (upper - lower))
        return lower

    lax.fori_loop(0, level_count, step, flux(0), unroll=4)


def home_kernel(
    first, state_ref, temp_ref, cosine_ref, ground_ref, day_ref, molecular_ref, table_ref,
    heat_ref, optics_ref, weight_ref, terms_ref, right_ref, *scratch,
):
    level_count, lines, lanes = state_ref.shape[1:]
    gpoints = weight_ref.shape[0]
    row, count = pl.program_id(0), pl.num_programs(0)

    @pl.when(row == 0)
    def prepare():
        optics_matrices(molecular_ref, table_ref, optics_ref, weight_ref)
        heat_ref[...] = jnp.zeros_like(heat_ref)
        prepare_terms(state_ref, temp_ref, terms_ref, right_ref)

    line = first + row
    sweep_row(
        row, line, lines, count, cosine_ref[pl.ds(line, 1), :], ground_ref[pl.ds(line, 1), :],
        optics_ref, weight_ref, terms_ref, right_ref, *scratch,
    )

    @pl.when(row == count - 1)
    def finish():
        size = heat_ref.shape[0] // level_count
        rows = slice(first, first + size)
        day = day_ref[rows, :] == 1

        def write(level, value):
            heat_ref[pl.ds(level * size, size), :] = jnp.where(day, value, 0.0)

        level_heating(scratch[PARTIAL], level_count, gpoints, size, write)


def prepare_terms(state_ref, temp_ref, terms_ref, right_ref):
    level_count, lines = state_ref.shape[1:3]
    right_ref[...] = jnp.zeros_like(right_ref)

    def level(l, carry):
        write_terms(terms_ref, l, layer_terms(state_ref, temp_ref, l), lines)
        return carry

    lax.fori_loop(0, level_count, level, 0, unroll=4)


def shared_places(lines):
    low = lax.axis_index("gx") < lax.axis_size("gx") // 2
    early, late = lines // 2, lines // 2 + lines // 4
    return jnp.where(low, early, late), jnp.where(low, late, early)


def pack_kernel(
    state_ref, temp_ref, flow_ref, cosine_ref, ground_ref, edge_ref,
    sent_ref, kept_ref, line_ref, first_ref, last_ref, own_ref, strip_ref,
):
    level_count, lines, lanes = state_ref.shape[1:]

    def level(l, carry):
        for k, value in enumerate(layer_terms(state_ref, temp_ref, l)):
            own_ref[pl.ds(pl.multiple_of((5 * l + k) * lines, 8), lines), :] = value
        return carry

    lax.fori_loop(0, level_count, level, 0, unroll=4)
    mine, theirs = shared_places(lines)
    copies = ((kept_ref, mine), (sent_ref, theirs), (line_ref, lines // 2 - 1))

    def copy(n, carry):
        for ref, place in copies:
            ref[n] = own_ref[pl.ds(n * lines + place, ref.shape[1]), :]
        return carry

    lax.fori_loop(0, 5 * level_count, copy, 0, unroll=8)
    for ref, place in copies:
        ref[5 * level_count] = cosine_ref[pl.ds(place, ref.shape[1]), :]
        ref[5 * level_count + 1] = ground_ref[pl.ds(place, ref.shape[1]), :]
    for n, ref in enumerate((temp_ref, flow_ref.at[0], flow_ref.at[1])):
        for r in range(lines):
            write_strip(ref, r, lines, strip_ref, 8 * (lines * n + r))
    packed = split_dot(strip_ref[...], edge_ref[...])
    first_ref[...] = packed[:, :lanes]
    last_ref[...] = packed[:, lanes:]


def shared_kernel(
    kept_ref, received_ref, day_ref, optics_ref, weight_ref, edge_ref,
    mine_ref, theirs_ref, surface_ref, strip_ref, terms_ref, right_ref, *scratch,
):
    level_count = kept_ref.shape[0] // 5
    shared, lanes = kept_ref.shape[1:]
    gpoints = weight_ref.shape[0]
    row, count = pl.program_id(0), pl.num_programs(0)
    first = shared_places(day_ref.shape[0])[0]
    day = day_ref[pl.ds(first, shared), :] == 1

    @pl.when(row == 0)
    def prepare():
        right_ref[...] = jnp.zeros_like(right_ref)

        def level(l, carry):
            values = [
                jnp.where(day, kept_ref[5 * l + k], received_ref[5 * l + k]) for k in range(5)
            ]
            write_terms(terms_ref, l, values, shared)
            return carry

        lax.fori_loop(0, level_count, level, 0, unroll=4)
        for n in range(2):
            place = 5 * level_count + n
            surface_ref[n, :shared, :] = jnp.where(day, kept_ref[place], received_ref[place])

    sweep_row(
        row, row, shared, count, surface_ref[0, pl.ds(row, 1), :],
        surface_ref[1, pl.ds(row, 1), :], optics_ref, weight_ref, terms_ref, right_ref, *scratch,
    )

    @pl.when(row == count - 1)
    def finish():
        def write(level, value):
            span = pl.ds(level * shared, shared)
            mine_ref[span, :] = jnp.where(day, value, 0.0)
            theirs_ref[span, :] = jnp.where(day, 0.0, value)

        level_heating(scratch[PARTIAL], level_count, gpoints, shared, write)
        strip_ref[...] = jnp.zeros_like(strip_ref)
        for r in range(shared):
            start = pl.multiple_of(8 * (first + r), 8)
            write_strip(theirs_ref, r, shared, strip_ref, start)
        packed = split_dot(strip_ref[...], edge_ref[...])
        size = level_count * shared
        half = packed.shape[0]
        theirs_ref[size : size + half, :] = packed[:, :lanes]
        theirs_ref[size + half :, :] = packed[:, lanes:]


def write_strip(source_ref, r, lines, strip_ref, start):
    lanes = source_ref.shape[1]
    for k in range(strip_ref.shape[1] // lanes):
        strip_ref[pl.ds(start, 8), lanes * k : lanes * (k + 1)] = source_ref[
            pl.ds(8 * k * lines + r, 8, stride=lines), :
        ]


def last_home_kernel(
    line_ref, day_ref, optics_ref, weight_ref, edge_ref, home_ref, mine_ref,
    heat_ref, first_ref, last_ref, strip_ref, terms_ref, right_ref, *scratch,
):
    lines, lanes = day_ref.shape
    level_count = line_ref.shape[0] // 5
    gpoints = weight_ref.shape[0]
    row = pl.program_id(0)
    line = lines // 2 - 1
    right_ref[...] = jnp.zeros_like(right_ref)

    def level(l, carry):
        write_terms(terms_ref, l, [line_ref[5 * l + k] for k in range(5)], 1)
        return carry

    lax.fori_loop(0, level_count, level, 0, unroll=4)
    sweep_row(
        row, 0, 1, 1, line_ref[5 * level_count], line_ref[5 * level_count + 1],
        optics_ref, weight_ref, terms_ref, right_ref, *scratch,
    )
    first = shared_places(lines)[0]
    shared = mine_ref.shape[0] // level_count
    day = day_ref[line : line + 1, :] == 1
    heat_ref[...] = jnp.zeros_like(heat_ref)

    def write(level, value):
        start = pl.multiple_of(level * lines, 8)
        heat_ref[pl.ds(start, line), :] = home_ref[pl.ds(level * line, line), :]
        heat_ref[pl.ds(start + line, 1), :] = jnp.where(day, value, 0.0)
        heat_ref[pl.ds(start + first, shared), :] = mine_ref[pl.ds(level * shared, shared), :]

    level_heating(scratch[PARTIAL], level_count, gpoints, 1, write)
    for r in range(lines):
        write_strip(heat_ref, r, lines, strip_ref, 8 * r)
    packed = split_dot(strip_ref[...], edge_ref[...])
    first_ref[...] = packed[:, :lanes]
    last_ref[...] = packed[:, lanes:]


def radiation(state, temper, flow, cosine, ground, day, molecular, condensate):
    level_count, rows, lanes = temper.shape
    gpoints = molecular.shape[1]
    home, shared = rows // 2, rows // 4
    partner = lax.axis_size("gx") // 2
    temper = temper.reshape(level_count * rows, lanes)
    flow = flow.reshape(2, level_count * rows, lanes)
    full = pltpu.VMEM((level_count, gpoints, lanes), jnp.float32)
    plane = pltpu.VMEM((gpoints, lanes), jnp.float32)
    whole = pl.BlockSpec(memory_space=pltpu.VMEM)
    params = pltpu.CompilerParams(vmem_limit_bytes=60 * 1024 * 1024)
    part = (QUANTITIES * gpoints // CHUNKS, GROUP * TERMS)
    strip = pltpu.VMEM((8 * rows, level_count // 8 * lanes), jnp.float32)

    def field(lines):
        return jax.ShapeDtypeStruct((level_count * lines, lanes), jnp.float32)

    def scratch(lines, count):
        return [
            pltpu.VMEM((level_count * TERMS * lines, lanes), jnp.float32),
            pltpu.VMEM((level_count // 2, GROUP * TERMS, 2 * lanes), jnp.bfloat16),
            pltpu.VMEM((BLOCK // 2, part[0], 2 * lanes), jnp.float32),
            pltpu.VMEM((BLOCK // 2, part[0], 2 * lanes), jnp.float32),
            full, full, full,
            pltpu.VMEM(((level_count + 1) * count * 8, lanes), jnp.float32),
            plane, plane,
            pltpu.VMEM((8, lanes), jnp.float32),
        ]

    def cost(count):
        cells = level_count * gpoints * count * lanes
        return pl.CostEstimate(
            flops=10000 * cells, bytes_accessed=32 * temper.size, transcendentals=5 * cells
        )

    def state_rows(count):
        return jax.ShapeDtypeStruct((5 * level_count + 2, count, lanes), jnp.float32)

    edges = edge_matrix(level_count, lanes)
    three = jax.ShapeDtypeStruct((3 * 8 * rows, lanes), jnp.float32)
    sent, kept, line, fields_first, fields_last = pl.pallas_call(
        pack_kernel,
        out_shape=(state_rows(shared), state_rows(shared), state_rows(1), three, three),
        in_specs=[whole] * 6, out_specs=(whole,) * 5,
        scratch_shapes=[
            pltpu.VMEM((5 * level_count * rows, lanes), jnp.float32),
            pltpu.VMEM((3 * 8 * rows, level_count // 8 * lanes), jnp.float32),
        ],
        compiler_params=params, name="pack",
    )(state, temper, flow, cosine, ground, edges)
    received = shifted(sent, "gx", partner)
    fields_after, fields_before = shifted(fields_first, "gx", -1), shifted(fields_last, "gx", 1)
    received, fields_after, fields_before = lax.optimization_barrier(
        (received, fields_after, fields_before)
    )
    early = home - 1
    home_heat, optics, weight = pl.pallas_call(
        functools.partial(home_kernel, 0),
        out_shape=(
            field(early),
            jax.ShapeDtypeStruct((level_count // GROUP, CHUNKS) + part, jnp.bfloat16),
            jax.ShapeDtypeStruct((gpoints, lanes), jnp.float32),
        ),
        grid=(early,), in_specs=[whole] * 7, out_specs=(whole,) * 3,
        scratch_shapes=scratch(rows, early), compiler_params=params, cost_estimate=cost(early),
        name="home_radiation",
    )(state, temper, cosine, ground, day, molecular.transpose(0, 2, 1), condensate)
    edge = jax.ShapeDtypeStruct((8 * rows, lanes), jnp.float32)
    theirs_size = level_count * shared + 16 * rows
    mine, theirs = pl.pallas_call(
        shared_kernel,
        out_shape=(field(shared), jax.ShapeDtypeStruct((theirs_size, lanes), jnp.float32)),
        grid=(shared,), in_specs=[whole] * 6, out_specs=(whole,) * 2,
        scratch_shapes=[pltpu.VMEM((2, 8, lanes), jnp.float32), strip] + scratch(shared, shared),
        compiler_params=params, cost_estimate=cost(shared), name="shared_radiation",
    )(kept, received, day, optics, weight, edges)
    returned = shifted(theirs, "gx", partner)
    after_more = shifted(theirs, "gx", partner - 1)
    before_more = shifted(theirs, "gx", partner + 1)
    heat, first, last = pl.pallas_call(
        last_home_kernel,
        out_shape=(field(rows), edge, edge),
        grid=(1,), in_specs=[whole] * 7, out_specs=(whole,) * 3,
        scratch_shapes=[strip] + scratch(1, 1),
        compiler_params=params, cost_estimate=cost(1), name="last_home_radiation",
    )(line, day, optics, weight, edges, home_heat, mine)
    after, before = shifted(first, "gx", -1), shifted(last, "gx", 1)
    return (
        heat, returned, after, before, after_more, before_more, fields_after, fields_before
    )


def edge_matrix(level_count, lanes):
    parts = level_count // 8
    width = lanes // parts
    matrix = np.zeros((parts * lanes, 2 * lanes), np.float32)
    for k in range(parts):
        for c in range(width):
            matrix[lanes * k + c, width * k + c] = 1.0
            matrix[lanes * (k + 1) - width + c, lanes + width * k + c] = 1.0
    return jnp.asarray(matrix, jnp.bfloat16)


def slope_matrices(lanes):
    whole = np.kron(np.eye(2 * lanes // NODES), gll_derivative().T).astype(np.float32)
    high = np.asarray(whole, jnp.bfloat16)
    low = np.asarray(whole - high.astype(np.float32), jnp.bfloat16)
    return jnp.asarray(high), jnp.asarray(low)


def average_matrix(lanes):
    size = 2 * lanes
    matrix = np.eye(size, dtype=np.float32)
    for c in range(NODES - 1, size, NODES):
        after = (c + 1) % size
        matrix[c, c] = matrix[after, after] = matrix[c, after] = matrix[after, c] = 0.5
    return jnp.asarray(matrix, jnp.bfloat16)


def split_dot(values, *matrices):
    high, low = high_low(values)
    total = jnp.dot(high, matrices[0], preferred_element_type=jnp.float32)
    total = total + jnp.dot(low, matrices[0], preferred_element_type=jnp.float32)
    if len(matrices) > 1:
        total = total + jnp.dot(high, matrices[1], preferred_element_type=jnp.float32)
    return total


def slope_y(rows_of):
    derivative = gll_derivative()
    result = []
    for r in range(len(rows_of)):
        first = r // NODES * NODES
        total = None
        for n in range(NODES):
            weight = derivative[r - first, n]
            if abs(weight) > 1e-12:
                term = np.float32(weight) * rows_of[first + n]
                total = term if total is None else total + term
        result.append(total)
    return result


def average_y(rows_of, below, above):
    result = list(rows_of)
    count = len(rows_of)
    for r in range(NODES - 1, count - 1, NODES):
        result[r] = result[r + 1] = 0.5 * (rows_of[r] + rows_of[r + 1])
    result[0] = 0.5 * (below + rows_of[0])
    result[count - 1] = 0.5 * (rows_of[count - 1] + above)
    return result


def unpacked(after_ref, before_ref, edge_ref):
    both = jnp.concatenate([after_ref[...], before_ref[...]], axis=1)
    return split_dot(both, edge_ref[...])


def own_change_kernel(
    temp_ref, flow_ref, after_ref, before_ref, edge_ref, high_ref, low_ref,
    change_ref, wind_ref, temp_wide_ref, slope_ref,
):
    level_count = change_ref.shape[0] // ROWS
    lanes = temp_ref.shape[-1]
    sides = unpacked(after_ref, before_ref, edge_ref)
    fields = (
        (temp_ref, temp_wide_ref), (flow_ref.at[0], wind_ref.at[0]), (flow_ref.at[1], wind_ref.at[1])
    )
    for n, (own, wide) in enumerate(fields):
        for r in range(ROWS):
            start = r * level_count
            wide[start : start + level_count, :lanes] = own[pl.ds(r, level_count, stride=ROWS), :]
            here = 8 * (ROWS * n + r)
            for k in range(level_count // 8):
                wide[start + 8 * k : start + 8 * (k + 1), lanes:] = sides[
                    here : here + 8, lanes * k : lanes * (k + 1)
                ]
    slope_ref[...] = split_dot(temp_wide_ref[...], high_ref[...], low_ref[...])
    advect(temp_wide_ref, slope_ref, wind_ref, change_ref, level_count)


def advect(field_ref, slope_ref, wind_ref, change_ref, level_count):
    spans = [slice(r * level_count, (r + 1) * level_count) for r in range(ROWS)]
    for half in range(2):
        lanes = field_ref.shape[1] // 2
        part = slice(half * lanes, (half + 1) * lanes)
        slopes = slope_y([field_ref[span, part] for span in spans])
        for span, slope in zip(spans, slopes):
            change = wind_ref[0, span, part] * slope_ref[span, part]
            change_ref[span, part] = -TIME_INCREMENT * (change + wind_ref[1, span, part] * slope)


def write_averaged(change, average_ref, out_ref, first_ref, last_ref):
    level_count = first_ref.shape[0]
    out_ref[...] = split_dot(change, average_ref[...])
    width = first_ref.shape[1]
    first_ref[...] = out_ref[:level_count, :width]
    last_ref[...] = out_ref[out_ref.shape[0] - level_count :, :width]


def first_stage_kernel(
    change_ref, heat_ref, returned_ref, after_ref, before_ref, after_more_ref,
    before_more_ref, edge_ref, average_ref,
    out_ref, first_ref, last_ref, heat_out_ref, sum_ref,
):
    level_count = first_ref.shape[0]
    lanes = heat_ref.shape[1]
    shared = ROWS // 4
    size, half = level_count * shared, after_ref.shape[0]
    after = after_ref[...] + after_more_ref[size : size + half, :]
    before = before_ref[...] + before_more_ref[size + half :, :]
    sides = split_dot(jnp.concatenate([after, before], axis=1), edge_ref[...])
    for r in range(ROWS):
        rows = slice(r * level_count, (r + 1) * level_count)
        span = pl.ds(r, level_count, stride=ROWS)
        own = heat_ref[span, :]
        if r >= ROWS // 2:
            n = r % shared
            here = shared_places(ROWS)[1] == r - n
            own = own + jnp.where(
                here, returned_ref[pl.ds(n, level_count, stride=shared), :], 0.0
            )
        heat_out_ref[span, :] = own
        sum_ref[rows, :lanes] = change_ref[rows, :lanes] + TIME_INCREMENT * own
        for k in range(level_count // 8):
            side = sides[8 * r : 8 * (r + 1), lanes * k : lanes * (k + 1)]
            here = slice(r * level_count + 8 * k, r * level_count + 8 * (k + 1))
            sum_ref[here, lanes:] = change_ref[here, lanes:] + TIME_INCREMENT * side
    write_averaged(sum_ref[...], average_ref, out_ref, first_ref, last_ref)


def next_stage_kernel(
    share, native, field_ref, below_ref, above_ref, wind_ref, sum_ref, high_ref, low_ref,
    average_ref, out_ref, first_ref, last_ref, total_ref, wave_ref, slope_ref, change_ref,
):
    level_count = below_ref.shape[0]
    lanes = sum_ref.shape[1]
    spans = [slice(r * level_count, (r + 1) * level_count) for r in range(ROWS)]
    for half in range(2):
        part = slice(half * lanes, (half + 1) * lanes)
        wave = average_y(
            [field_ref[span, part] for span in spans], below_ref[:, part], above_ref[:, part]
        )
        for r, (span, row) in enumerate(zip(spans, wave)):
            wave_ref[span, part] = row
            if half == 0:
                before = sum_ref[pl.ds(r, level_count, stride=ROWS), :] if native else sum_ref[span]
                total_ref[span] = before + share * row
    slope_ref[...] = split_dot(wave_ref[...], high_ref[...], low_ref[...])
    advect(wave_ref, slope_ref, wind_ref, change_ref, level_count)
    write_averaged(change_ref[...], average_ref, out_ref, first_ref, last_ref)


def last_kernel(share, field_ref, below_ref, above_ref, sum_ref, total_ref):
    level_count, lanes = below_ref.shape
    spans = [slice(r * level_count, (r + 1) * level_count) for r in range(ROWS)]
    wave = average_y([field_ref[span, :lanes] for span in spans], below_ref[...], above_ref[...])
    for r, (span, row) in enumerate(zip(spans, wave)):
        total_ref[pl.ds(r, level_count, stride=ROWS), :] = sum_ref[span] + share * row


def local(
    atmospheric_constituents,
    thermal_ratio,
    flow_velocity,
    solar_elevation_factor,
    ground_reflectivity,
    sunlit_indicator,
    molecular_optics_lookup,
    condensate_optics_lookup,
):
    level_count, rows, lanes = thermal_ratio.shape
    size = level_count * rows
    temper = thermal_ratio.reshape(size, lanes)
    flow = flow_velocity.reshape(2, size, lanes)
    field = jax.ShapeDtypeStruct((size, lanes), jnp.float32)
    wide = jax.ShapeDtypeStruct((size, 2 * lanes), jnp.float32)
    line = jax.ShapeDtypeStruct((level_count, 2 * lanes), jnp.float32)
    short = jax.ShapeDtypeStruct((level_count, lanes), jnp.float32)
    wide_scratch = pltpu.VMEM(wide.shape, jnp.float32)
    whole = pl.BlockSpec(memory_space=pltpu.VMEM)

    def call(kernel, name, outs, scratch, *values):
        return pl.pallas_call(
            kernel, out_shape=outs,
            in_specs=[whole] * len(values),
            out_specs=jax.tree.map(lambda _: whole, outs), scratch_shapes=[wide_scratch] * scratch,
            compiler_params=pltpu.CompilerParams(vmem_limit_bytes=40 * 1024 * 1024), name=name,
        )(*values)

    slopes = slope_matrices(lanes)
    average = average_matrix(lanes)
    (
        heat, returned, after, before, after_more, before_more, fields_after, fields_before
    ) = radiation(
        atmospheric_constituents, thermal_ratio, flow_velocity, solar_elevation_factor,
        ground_reflectivity, sunlit_indicator, molecular_optics_lookup, condensate_optics_lookup,
    )
    back = edge_matrix(level_count, lanes).T
    change, wind = call(
        own_change_kernel, "own_change",
        (wide, jax.ShapeDtypeStruct((2, size, 2 * lanes), jnp.float32)), 2,
        temper, flow, fields_after, fields_before, back, *slopes,
    )
    wave, first, last, heat = call(
        first_stage_kernel, "first_stage", (wide, line, line, field), 1,
        change, heat, returned, after, before, after_more, before_more, back, average,
    )
    below, above = shifted(last, "gy", 1), shifted(first, "gy", -1)
    wave, first, last, total = call(
        functools.partial(next_stage_kernel, 1.0, True), "second_stage",
        (wide, line, line, field), 3, wave, below, above, wind, temper, *slopes, average,
    )
    below, above = shifted(last, "gy", 1), shifted(first, "gy", -1)
    wave, first, last, total = call(
        functools.partial(next_stage_kernel, 0.5, False), "third_stage",
        (wide, short, short, field), 3, wave, below, above, wind, total, *slopes, average,
    )
    below, above = shifted(last, "gy", 1), shifted(first, "gy", -1)
    total = call(
        functools.partial(last_kernel, 1.0 / 6.0), "last_stage", field, 0,
        wave, below, above, total,
    )
    return (heat.reshape(thermal_ratio.shape), total.reshape(thermal_ratio.shape))


def solution(mesh):
    in_specs = (
        P(None, None, "gy", "gx"),
        P(None, "gy", "gx"),
        P(None, None, "gy", "gx"),
        P("gy", "gx"),
        P("gy", "gx"),
        P("gy", "gx"),
        P(),
        P(),
    )
    out_specs = (P(None, "gy", "gx"), P(None, "gy", "gx"))
    return jax.shard_map(local, mesh=mesh, in_specs=in_specs, out_specs=out_specs, check_vma=False)
```

```python
import functools

import jax
import jax.numpy as jnp
import numpy as np
from jax import lax
from jax.experimental import pallas as pl
from jax.experimental.pallas import tpu as pltpu
from jax.sharding import PartitionSpec as P

NODES = 4
TIME_INCREMENT = 0.05
ROWS = 8
LOG2E = 1.4426950408889634

GROUP = 8
TERMS = 16
BLOCK = 12
PARTIAL = 5
CHUNKS = 2
QUANTITIES = 4


def shifted(value, axis, steps):
    count = lax.axis_size(axis)
    return lax.ppermute(value, axis, [(i, (i + steps) % count) for i in range(count)])


def gll_derivative():
    points = np.array([-1.0, -1.0 / np.sqrt(5.0), 1.0 / np.sqrt(5.0), 1.0])
    legendre = 0.5 * (5.0 * points**3 - 3.0 * points)
    derivative = np.zeros((4, 4))
    for source in range(4):
        for target in range(4):
            if source != target:
                derivative[source, target] = legendre[source] / (
                    legendre[target] * (points[source] - points[target])
                )
    derivative[0, 0] = -3.0
    derivative[3, 3] = 3.0
    return derivative


def high_low(values):
    high = values.astype(jnp.bfloat16)
    return high, (values - high.astype(jnp.float32)).astype(jnp.bfloat16)


def across(left, right, precision=None):
    return lax.dot_general(
        left, right, (((0,), (0,)), ((), ())), precision=precision,
        preferred_element_type=jnp.float32,
    )


def optics_matrices(molecular_ref, table_ref, optics_ref, weight_ref):
    level_count, gpoints = molecular_ref.shape[1:]
    groups = level_count // GROUP
    width = GROUP * TERMS
    level = lax.broadcasted_iota(jnp.int32, (level_count, groups * width), 0)
    lane = lax.broadcasted_iota(jnp.int32, (level_count, groups * width), 1)
    here = level == lane // TERMS
    term = lane % TERMS
    gases = []
    for k in range(3):
        high, low = high_low(molecular_ref[k])
        spread = [
            jnp.where(here & chosen, 1.0, 0.0).astype(jnp.bfloat16)
            for chosen in ((term == k) | (term == k + 10), term == k + 5)
        ]
        gases.append(across(high, spread[0]) + across(low, spread[1]))
    w = [table_ref[n : n + 1, :] for n in range(7)]
    ls, li = w[0] * w[1], w[3] * w[4]
    la, ia = w[0] * (1.0 - w[1]), w[3] * (1.0 - w[4])
    place = lax.broadcasted_iota(jnp.int32, (8, width), 0)
    term = lax.broadcasted_iota(jnp.int32, (8, width), 1) % TERMS
    pattern = jnp.zeros((8, width), jnp.float32)
    for n, chosen in enumerate((
        (term == 3) | (term == 13), term == 8, (term == 4) | (term == 14), term == 9
    )):
        pattern = jnp.where((place == n) & chosen, 1.0, pattern)
    empty = jnp.zeros((4, gpoints), jnp.float32)

    def water(*values):
        parts = []
        for value in values:
            high = value.astype(jnp.bfloat16).astype(jnp.float32)
            parts += [high, value - high]
        return across(jnp.concatenate(parts + [empty], axis=0), pattern, lax.Precision.HIGHEST)

    absorbed = gases[0] + gases[1]
    gas = absorbed + gases[2]
    pairs = (
        (absorbed, water(la, ia)),
        (gas, water(la + ls * (1.0 - w[2]), ia + li * (1.0 - w[5]))),
        (gas + gas, water(2.0 * w[0], 2.0 * w[3])),
        (gases[2], water(ls * (1.0 + w[2]), li * (1.0 + w[5]))),
    )
    chunk = gpoints // CHUNKS
    for group in range(groups):
        span = slice(group * width, (group + 1) * width)
        tables = [values[:, span] + constant for values, constant in pairs]
        for c in range(CHUNKS):
            rows = [table[c * chunk : (c + 1) * chunk] for table in tables]
            optics_ref[group, c] = jnp.concatenate(rows, axis=0).astype(jnp.bfloat16)
    only = jnp.where(place == 0, 1.0, 0.0)
    weight = jnp.broadcast_to(w[6], (8, gpoints))
    weight_ref[...] = across(weight, only, lax.Precision.HIGHEST)


def layer_terms(state_ref, temp_ref, level):
    lines = state_ref.shape[2]
    thickness = state_ref[2, level]
    temper = temp_ref[pl.ds(pl.multiple_of(level * lines, 8), lines), :]
    weighted = thickness * temper * temper
    return (
        weighted * state_ref[0, level], weighted * state_ref[1, level], thickness,
        state_ref[3, level], state_ref[4, level],
    )


def write_terms(terms_ref, level, values, lines):
    parts = [None] * TERMS
    for k, value in enumerate(values):
        high = value.astype(jnp.bfloat16).astype(jnp.float32)
        parts[k], parts[k + 5], parts[k + 10] = high, high, value - high
    parts[15] = jnp.zeros_like(values[0])
    for k, part in enumerate(parts):
        start = (level * TERMS + k) * lines
        start = pl.multiple_of(start, 8) if lines % 8 == 0 else start
        terms_ref[pl.ds(start, lines), :] = part


def sweep_row(
    row, line, lines, count, cosine, ground, optics_ref, weight_ref, terms_ref, right_ref,
    depths_0, depths_1, gain_ref, offset_ref, direct_ref, partial_ref, ratio_ref, source_ref, slant_ref,
):
    level_count, gpoints, lanes = gain_ref.shape
    blocks = level_count // BLOCK
    chunk = gpoints // CHUNKS
    slots = (depths_0, depths_1)
    once = 1 + jnp.minimum(row, 0)

    def place_group(group, carry):
        for j in range(GROUP):
            start = (group * GROUP + j) * TERMS * lines + line
            tile = terms_ref[pl.ds(start, TERMS, stride=lines), :].astype(jnp.bfloat16)
            half = lanes * (j % 2)
            pair = group * (GROUP // 2) + j // 2
            right_ref[pair, TERMS * j : TERMS * (j + 1), half : half + lanes] = tile
        return carry

    lax.fori_loop(0, level_count // GROUP, place_group, 0)
    slant_ref[...] = jnp.broadcast_to((-0.5 * LOG2E) / cosine, (8, lanes))

    def over_rows(values):
        return jnp.broadcast_to(values[None], (gpoints // 8, 8, lanes)).reshape(gpoints, lanes)

    clear = 1.0 / (1.0 - ground)
    ratio_ref[...] = over_rows(jnp.broadcast_to((1.0 + ground) * clear, (8, lanes)))
    source_ref[...] = over_rows(jnp.broadcast_to(2.0 * ground * clear, (8, lanes)))

    def fill(block, c):
        for p in range(BLOCK // 2):
            pair = block * (BLOCK // 2) + p
            slots[c % 2][p] = jnp.dot(
                optics_ref[pair // (GROUP // 2), c], right_ref[pair],
                preferred_element_type=jnp.float32,
            )

    def below(block, c):
        span = slice(c * chunk, (c + 1) * chunk)
        ratio, source = ratio_ref[span], source_ref[span]
        slant = jnp.broadcast_to(slant_ref[...][None], (chunk // 8, 8, lanes))
        slant = slant.reshape(chunk, lanes)
        for j in reversed(range(BLOCK)):
            level = block * BLOCK + j
            part = slots[c % 2].at[j // 2, :, (j % 2) * lanes : (j % 2 + 1) * lanes]
            a, b, depth, along = [part[n * chunk : (n + 1) * chunk] for n in range(QUANTITIES)]
            away = b - a
            square = a * b
            inverse_root = lax.rsqrt(square)
            h = jnp.tanh(square * inverse_root)
            g = h * inverse_root
            g = g + g
            s, p = a * g, b * g
            h2 = h * h
            one = 1.0 + h2
            through = 1.0 - h2
            inverse = 1.0 / (one + s * ratio)
            direct = jnp.exp2(depth * slant)
            factor = (1.0 - direct) * (1.0 / depth)
            up, down = factor * away, factor * along
            push = inverse * (direct * source + (ratio - 1.0) * down)
            ratio = (one * ratio + p) * inverse
            gain = through * inverse
            source = through * push + (ratio + 1.0) * up
            gain_ref[level, span] = gain
            offset_ref[level, span] = (gain * up + down) - s * push
            direct_ref[level, span] = direct
        ratio_ref[span] = ratio
        source_ref[span] = source

    def below_block(step, carry):
        block = blocks - 1 - step
        for c in range(CHUNKS):
            def turn(n, carry, c=c):
                below(block, c)
                if c + 1 < CHUNKS:
                    fill(block, c + 1)
                else:
                    fill(jnp.maximum(block - 1, 0), 0)
                return carry

            lax.fori_loop(0, once, turn, 0)
        return carry

    fill(blocks - 1, 0)
    lax.fori_loop(0, blocks, below_block, 0)

    def folded(net):
        return sum(net[8 * k : 8 * (k + 1)] for k in range(gpoints // 8))

    def top(step, carry):
        beam = weight_ref[...] * cosine
        net = -(source_ref[...] * beam) / (1.0 + ratio_ref[...])
        partial_ref[pl.ds(pl.multiple_of(row * 8, 8), 8), :] = folded(beam) + folded(net)
        return net, beam

    nothing = jnp.zeros((gpoints, lanes), jnp.float32)
    carry = lax.fori_loop(0, once, top, (nothing, nothing))

    def down_group(group, carry):
        net, beam = carry
        for j in range(GROUP):
            level = group * GROUP + j
            net = gain_ref[level] * net + offset_ref[level] * beam
            beam = beam * direct_ref[level]
            start = pl.multiple_of(((level + 1) * count + row) * 8, 8)
            partial_ref[pl.ds(start, 8), :] = folded(net) + folded(beam)
        return (net, beam)

    lax.fori_loop(0, level_count // GROUP, down_group, carry)


def level_heating(partial_ref, level_count, gpoints, count, write):
    def flux(level):
        start = level * count * 8
        return sum(partial_ref[pl.ds(start + k, count, stride=8), :] for k in range(8))

    def step(level, upper):
        lower = flux(level + 1)
        write(level, (level_count / gpoints) * (upper - lower))
        return lower

    lax.fori_loop(0, level_count, step, flux(0), unroll=4)


def home_kernel(
    first, state_ref, temp_ref, cosine_ref, ground_ref, day_ref, molecular_ref, table_ref,
    heat_ref, optics_ref, weight_ref, terms_ref, right_ref, *scratch,
):
    level_count, lines, lanes = state_ref.shape[1:]
    gpoints = weight_ref.shape[0]
    row, count = pl.program_id(0), pl.num_programs(0)

    @pl.when(row == 0)
    def prepare():
        optics_matrices(molecular_ref, table_ref, optics_ref, weight_ref)
        heat_ref[...] = jnp.zeros_like(heat_ref)
        prepare_terms(state_ref, temp_ref, terms_ref, right_ref)

    line = first + row
    sweep_row(
        row, line, lines, count, cosine_ref[pl.ds(line, 1), :], ground_ref[pl.ds(line, 1), :],
        optics_ref, weight_ref, terms_ref, right_ref, *scratch,
    )

    @pl.when(row == count - 1)
    def finish():
        size = heat_ref.shape[0] // level_count
        rows = slice(first, first + size)
        day = day_ref[rows, :] == 1

        def write(level, value):
            heat_ref[pl.ds(level * size, size), :] = jnp.where(day, value, 0.0)

        level_heating(scratch[PARTIAL], level_count, gpoints, size, write)


def prepare_terms(state_ref, temp_ref, terms_ref, right_ref):
    level_count, lines = state_ref.shape[1:3]
    right_ref[...] = jnp.zeros_like(right_ref)

    def level(l, carry):
        write_terms(terms_ref, l, layer_terms(state_ref, temp_ref, l), lines)
        return carry

    lax.fori_loop(0, level_count, level, 0, unroll=4)


def shared_places(lines):
    low = lax.axis_index("gx") < lax.axis_size("gx") // 2
    early, late = lines // 2, lines // 2 + lines // 4
    return jnp.where(low, early, late), jnp.where(low, late, early)


def pack_kernel(
    state_ref, temp_ref, flow_ref, cosine_ref, ground_ref, edge_ref,
    sent_ref, kept_ref, line_ref, first_ref, last_ref, own_ref, strip_ref,
):
    level_count, lines, lanes = state_ref.shape[1:]

    def level(l, carry):
        for k, value in enumerate(layer_terms(state_ref, temp_ref, l)):
            own_ref[pl.ds(pl.multiple_of((5 * l + k) * lines, 8), lines), :] = value
        return carry

    lax.fori_loop(0, level_count, level, 0, unroll=4)
    mine, theirs = shared_places(lines)
    copies = ((kept_ref, mine), (sent_ref, theirs), (line_ref, lines // 2 - 1))

    def copy(n, carry):
        for ref, place in copies:
            ref[n] = own_ref[pl.ds(n * lines + place, ref.shape[1]), :]
        return carry

    lax.fori_loop(0, 5 * level_count, copy, 0, unroll=8)
    for ref, place in copies:
        ref[5 * level_count] = cosine_ref[pl.ds(place, ref.shape[1]), :]
        ref[5 * level_count + 1] = ground_ref[pl.ds(place, ref.shape[1]), :]
    for n, ref in enumerate((temp_ref, flow_ref.at[0], flow_ref.at[1])):
        for r in range(lines):
            write_strip(ref, r, lines, strip_ref, 8 * (lines * n + r))
    packed = split_dot(strip_ref[...], edge_ref[...])
    first_ref[...] = packed[:, :lanes]
    last_ref[...] = packed[:, lanes:]


def shared_kernel(
    kept_ref, received_ref, day_ref, optics_ref, weight_ref,
    mine_ref, theirs_ref, surface_ref, terms_ref, right_ref, *scratch,
):
    level_count = kept_ref.shape[0] // 5
    shared, lanes = kept_ref.shape[1:]
    gpoints = weight_ref.shape[0]
    row, count = pl.program_id(0), pl.num_programs(0)
    first = shared_places(day_ref.shape[0])[0]
    day = day_ref[pl.ds(first, shared), :] == 1

    @pl.when(row == 0)
    def prepare():
        right_ref[...] = jnp.zeros_like(right_ref)

        def level(l, carry):
            values = [
                jnp.where(day, kept_ref[5 * l + k], received_ref[5 * l + k]) for k in range(5)
            ]
            write_terms(terms_ref, l, values, shared)
            return carry

        lax.fori_loop(0, level_count, level, 0, unroll=4)
        for n in range(2):
            place = 5 * level_count + n
            surface_ref[n, :shared, :] = jnp.where(day, kept_ref[place], received_ref[place])

    sweep_row(
        row, row, shared, count, surface_ref[0, pl.ds(row, 1), :],
        surface_ref[1, pl.ds(row, 1), :], optics_ref, weight_ref, terms_ref, right_ref, *scratch,
    )

    @pl.when(row == count - 1)
    def finish():
        def write(level, value):
            span = pl.ds(level * shared, shared)
            mine_ref[span, :] = jnp.where(day, value, 0.0)
            theirs_ref[span, :] = jnp.where(day, 0.0, value)

        level_heating(scratch[PARTIAL], level_count, gpoints, shared, write)


def write_strip(source_ref, r, lines, strip_ref, start):
    lanes = source_ref.shape[1]
    for k in range(strip_ref.shape[1] // lanes):
        strip_ref[pl.ds(start, 8), lanes * k : lanes * (k + 1)] = source_ref[
            pl.ds(8 * k * lines + r, 8, stride=lines), :
        ]


def last_home_kernel(
    line_ref, day_ref, optics_ref, weight_ref, heat_ref, terms_ref, right_ref, *scratch,
):
    level_count = line_ref.shape[0] // 5
    row = pl.program_id(0)
    right_ref[...] = jnp.zeros_like(right_ref)

    def level(l, carry):
        write_terms(terms_ref, l, [line_ref[5 * l + k] for k in range(5)], 1)
        return carry

    lax.fori_loop(0, level_count, level, 0, unroll=4)
    sweep_row(
        row, 0, 1, 1, line_ref[5 * level_count], line_ref[5 * level_count + 1],
        optics_ref, weight_ref, terms_ref, right_ref, *scratch,
    )
    line = day_ref.shape[0] // 2 - 1
    day = day_ref[line : line + 1, :] == 1

    def write(level, value):
        heat_ref[pl.ds(level, 1), :] = jnp.where(day, value, 0.0)

    level_heating(scratch[PARTIAL], level_count, weight_ref.shape[0], 1, write)


def join_kernel(
    home_ref, line_ref, mine_ref, returned_ref, edge_ref, heat_ref, first_ref, last_ref, strip_ref
):
    level_count, lanes = line_ref.shape
    lines = heat_ref.shape[0] // level_count
    home, shared = lines // 2, lines // 4
    place = shared_places(lines)[0]
    for r in range(lines):
        if r < home - 1:
            row = home_ref[pl.ds(r, level_count, stride=home - 1), :]
        elif r == home - 1:
            row = line_ref[...]
        else:
            n = (r - home) % shared
            span = pl.ds(n, level_count, stride=shared)
            row = jnp.where(place == r - n, mine_ref[span, :], returned_ref[span, :])
        heat_ref[pl.ds(r, level_count, stride=lines), :] = row
        for k in range(level_count // 8):
            strip_ref[8 * r : 8 * (r + 1), lanes * k : lanes * (k + 1)] = row[8 * k : 8 * (k + 1)]
    packed = split_dot(strip_ref[...], edge_ref[...])
    first_ref[...] = packed[:, :lanes]
    last_ref[...] = packed[:, lanes:]


def radiation(state, temper, flow, cosine, ground, day, molecular, condensate):
    level_count, rows, lanes = temper.shape
    gpoints = molecular.shape[1]
    home, shared = rows // 2, rows // 4
    partner = lax.axis_size("gx") // 2
    temper = temper.reshape(level_count * rows, lanes)
    flow = flow.reshape(2, level_count * rows, lanes)
    full = pltpu.VMEM((level_count, gpoints, lanes), jnp.float32)
    plane = pltpu.VMEM((gpoints, lanes), jnp.float32)
    whole = pl.BlockSpec(memory_space=pltpu.VMEM)
    params = pltpu.CompilerParams(vmem_limit_bytes=60 * 1024 * 1024)
    part = (QUANTITIES * gpoints // CHUNKS, GROUP * TERMS)
    strip = pltpu.VMEM((8 * rows, level_count // 8 * lanes), jnp.float32)

    def field(lines):
        return jax.ShapeDtypeStruct((level_count * lines, lanes), jnp.float32)

    def scratch(lines, count):
        return [
            pltpu.VMEM((level_count * TERMS * lines, lanes), jnp.float32),
            pltpu.VMEM((level_count // 2, GROUP * TERMS, 2 * lanes), jnp.bfloat16),
            pltpu.VMEM((BLOCK // 2, part[0], 2 * lanes), jnp.float32),
            pltpu.VMEM((BLOCK // 2, part[0], 2 * lanes), jnp.float32),
            full, full, full,
            pltpu.VMEM(((level_count + 1) * count * 8, lanes), jnp.float32),
            plane, plane,
            pltpu.VMEM((8, lanes), jnp.float32),
        ]

    def cost(count):
        cells = level_count * gpoints * count * lanes
        return pl.CostEstimate(
            flops=10000 * cells, bytes_accessed=32 * temper.size, transcendentals=5 * cells
        )

    def state_rows(count):
        return jax.ShapeDtypeStruct((5 * level_count + 2, count, lanes), jnp.float32)

    edges = edge_matrix(level_count, lanes)
    three = jax.ShapeDtypeStruct((3 * 8 * rows, lanes), jnp.float32)
    sent, kept, line, fields_first, fields_last = pl.pallas_call(
        pack_kernel,
        out_shape=(state_rows(shared), state_rows(shared), state_rows(1), three, three),
        in_specs=[whole] * 6, out_specs=(whole,) * 5,
        scratch_shapes=[
            pltpu.VMEM((5 * level_count * rows, lanes), jnp.float32),
            pltpu.VMEM((3 * 8 * rows, level_count // 8 * lanes), jnp.float32),
        ],
        compiler_params=params, name="pack",
    )(state, temper, flow, cosine, ground, edges)
    received = shifted(sent, "gx", partner)
    fields_after, fields_before = shifted(fields_first, "gx", -1), shifted(fields_last, "gx", 1)
    received, fields_after, fields_before = lax.optimization_barrier(
        (received, fields_after, fields_before)
    )
    early = home - 1
    home_heat, optics, weight = pl.pallas_call(
        functools.partial(home_kernel, 0),
        out_shape=(
            field(early),
            jax.ShapeDtypeStruct((level_count // GROUP, CHUNKS) + part, jnp.bfloat16),
            jax.ShapeDtypeStruct((gpoints, lanes), jnp.float32),
        ),
        grid=(early,), in_specs=[whole] * 7, out_specs=(whole,) * 3,
        scratch_shapes=scratch(rows, early), compiler_params=params, cost_estimate=cost(early),
        name="home_radiation",
    )(state, temper, cosine, ground, day, molecular.transpose(0, 2, 1), condensate)
    edge = jax.ShapeDtypeStruct((8 * rows, lanes), jnp.float32)
    mine, theirs = pl.pallas_call(
        shared_kernel,
        out_shape=(field(shared), field(shared)),
        grid=(shared,), in_specs=[whole] * 5, out_specs=(whole,) * 2,
        scratch_shapes=[pltpu.VMEM((2, 8, lanes), jnp.float32)] + scratch(shared, shared),
        compiler_params=params, cost_estimate=cost(shared), name="shared_radiation",
    )(kept, received, day, optics, weight)
    returned = shifted(theirs, "gx", partner)
    line_heat = pl.pallas_call(
        last_home_kernel,
        out_shape=field(1),
        grid=(1,), in_specs=[whole] * 4, out_specs=whole, scratch_shapes=scratch(1, 1),
        compiler_params=params, cost_estimate=cost(1), name="last_home_radiation",
    )(line, day, optics, weight)
    heat, first, last = pl.pallas_call(
        join_kernel, out_shape=(field(rows), edge, edge),
        in_specs=[whole] * 5, out_specs=(whole,) * 3, scratch_shapes=[strip],
        compiler_params=params, name="join",
    )(home_heat, line_heat, mine, returned, edges)
    after, before = shifted(first, "gx", -1), shifted(last, "gx", 1)
    return heat, after, before, fields_after, fields_before


def edge_matrix(level_count, lanes):
    parts = level_count // 8
    width = lanes // parts
    matrix = np.zeros((parts * lanes, 2 * lanes), np.float32)
    for k in range(parts):
        for c in range(width):
            matrix[lanes * k + c, width * k + c] = 1.0
            matrix[lanes * (k + 1) - width + c, lanes + width * k + c] = 1.0
    return jnp.asarray(matrix, jnp.bfloat16)


def slope_matrices(lanes):
    whole = np.kron(np.eye(2 * lanes // NODES), gll_derivative().T).astype(np.float32)
    high = np.asarray(whole, jnp.bfloat16)
    low = np.asarray(whole - high.astype(np.float32), jnp.bfloat16)
    return jnp.asarray(high), jnp.asarray(low)


def average_matrix(lanes):
    size = 2 * lanes
    matrix = np.eye(size, dtype=np.float32)
    for c in range(NODES - 1, size, NODES):
        after = (c + 1) % size
        matrix[c, c] = matrix[after, after] = matrix[c, after] = matrix[after, c] = 0.5
    return jnp.asarray(matrix, jnp.bfloat16)


def split_dot(values, *matrices):
    high, low = high_low(values)
    total = jnp.dot(high, matrices[0], preferred_element_type=jnp.float32)
    total = total + jnp.dot(low, matrices[0], preferred_element_type=jnp.float32)
    if len(matrices) > 1:
        total = total + jnp.dot(high, matrices[1], preferred_element_type=jnp.float32)
    return total


def slope_y(rows_of):
    derivative = gll_derivative()
    result = []
    for r in range(len(rows_of)):
        first = r // NODES * NODES
        total = None
        for n in range(NODES):
            weight = derivative[r - first, n]
            if abs(weight) > 1e-12:
                term = np.float32(weight) * rows_of[first + n]
                total = term if total is None else total + term
        result.append(total)
    return result


def average_y(rows_of, below, above):
    result = list(rows_of)
    count = len(rows_of)
    for r in range(NODES - 1, count - 1, NODES):
        result[r] = result[r + 1] = 0.5 * (rows_of[r] + rows_of[r + 1])
    result[0] = 0.5 * (below + rows_of[0])
    result[count - 1] = 0.5 * (rows_of[count - 1] + above)
    return result


def unpacked(after_ref, before_ref, edge_ref):
    both = jnp.concatenate([after_ref[...], before_ref[...]], axis=1)
    return split_dot(both, edge_ref[...])


def own_change_kernel(
    temp_ref, flow_ref, after_ref, before_ref, edge_ref, high_ref, low_ref,
    change_ref, wind_ref, temp_wide_ref, slope_ref,
):
    level_count = change_ref.shape[0] // ROWS
    lanes = temp_ref.shape[-1]
    sides = unpacked(after_ref, before_ref, edge_ref)
    fields = (
        (temp_ref, temp_wide_ref), (flow_ref.at[0], wind_ref.at[0]), (flow_ref.at[1], wind_ref.at[1])
    )
    for n, (own, wide) in enumerate(fields):
        for r in range(ROWS):
            start = r * level_count
            wide[start : start + level_count, :lanes] = own[pl.ds(r, level_count, stride=ROWS), :]
            here = 8 * (ROWS * n + r)
            for k in range(level_count // 8):
                wide[start + 8 * k : start + 8 * (k + 1), lanes:] = sides[
                    here : here + 8, lanes * k : lanes * (k + 1)
                ]
    slope_ref[...] = split_dot(temp_wide_ref[...], high_ref[...], low_ref[...])
    advect(temp_wide_ref, slope_ref, wind_ref, change_ref, level_count)


def advect(field_ref, slope_ref, wind_ref, change_ref, level_count):
    spans = [slice(r * level_count, (r + 1) * level_count) for r in range(ROWS)]
    for half in range(2):
        lanes = field_ref.shape[1] // 2
        part = slice(half * lanes, (half + 1) * lanes)
        slopes = slope_y([field_ref[span, part] for span in spans])
        for span, slope in zip(spans, slopes):
            change = wind_ref[0, span, part] * slope_ref[span, part]
            change_ref[span, part] = -TIME_INCREMENT * (change + wind_ref[1, span, part] * slope)


def write_averaged(change, average_ref, out_ref, first_ref, last_ref):
    level_count = first_ref.shape[0]
    out_ref[...] = split_dot(change, average_ref[...])
    width = first_ref.shape[1]
    first_ref[...] = out_ref[:level_count, :width]
    last_ref[...] = out_ref[out_ref.shape[0] - level_count :, :width]


def first_stage_kernel(
    change_ref, heat_ref, after_ref, before_ref, edge_ref, average_ref,
    out_ref, first_ref, last_ref, sum_ref,
):
    level_count = first_ref.shape[0]
    lanes = heat_ref.shape[1]
    sides = unpacked(after_ref, before_ref, edge_ref)
    for r in range(ROWS):
        rows = slice(r * level_count, (r + 1) * level_count)
        own = heat_ref[pl.ds(r, level_count, stride=ROWS), :]
        sum_ref[rows, :lanes] = change_ref[rows, :lanes] + TIME_INCREMENT * own
        for k in range(level_count // 8):
            side = sides[8 * r : 8 * (r + 1), lanes * k : lanes * (k + 1)]
            here = slice(r * level_count + 8 * k, r * level_count + 8 * (k + 1))
            sum_ref[here, lanes:] = change_ref[here, lanes:] + TIME_INCREMENT * side
    write_averaged(sum_ref[...], average_ref, out_ref, first_ref, last_ref)


def next_stage_kernel(
    share, native, field_ref, below_ref, above_ref, wind_ref, sum_ref, high_ref, low_ref,
    average_ref, out_ref, first_ref, last_ref, total_ref, wave_ref, slope_ref, change_ref,
):
    level_count = below_ref.shape[0]
    lanes = sum_ref.shape[1]
    spans = [slice(r * level_count, (r + 1) * level_count) for r in range(ROWS)]
    for half in range(2):
        part = slice(half * lanes, (half + 1) * lanes)
        wave = average_y(
            [field_ref[span, part] for span in spans], below_ref[:, part], above_ref[:, part]
        )
        for r, (span, row) in enumerate(zip(spans, wave)):
            wave_ref[span, part] = row
            if half == 0:
                before = sum_ref[pl.ds(r, level_count, stride=ROWS), :] if native else sum_ref[span]
                total_ref[span] = before + share * row
    slope_ref[...] = split_dot(wave_ref[...], high_ref[...], low_ref[...])
    advect(wave_ref, slope_ref, wind_ref, change_ref, level_count)
    write_averaged(change_ref[...], average_ref, out_ref, first_ref, last_ref)


def last_kernel(share, field_ref, below_ref, above_ref, sum_ref, total_ref):
    level_count, lanes = below_ref.shape
    spans = [slice(r * level_count, (r + 1) * level_count) for r in range(ROWS)]
    wave = average_y([field_ref[span, :lanes] for span in spans], below_ref[...], above_ref[...])
    for r, (span, row) in enumerate(zip(spans, wave)):
        total_ref[pl.ds(r, level_count, stride=ROWS), :] = sum_ref[span] + share * row


def local(
    atmospheric_constituents,
    thermal_ratio,
    flow_velocity,
    solar_elevation_factor,
    ground_reflectivity,
    sunlit_indicator,
    molecular_optics_lookup,
    condensate_optics_lookup,
):
    level_count, rows, lanes = thermal_ratio.shape
    size = level_count * rows
    temper = thermal_ratio.reshape(size, lanes)
    flow = flow_velocity.reshape(2, size, lanes)
    field = jax.ShapeDtypeStruct((size, lanes), jnp.float32)
    wide = jax.ShapeDtypeStruct((size, 2 * lanes), jnp.float32)
    line = jax.ShapeDtypeStruct((level_count, 2 * lanes), jnp.float32)
    short = jax.ShapeDtypeStruct((level_count, lanes), jnp.float32)
    wide_scratch = pltpu.VMEM(wide.shape, jnp.float32)
    whole = pl.BlockSpec(memory_space=pltpu.VMEM)

    def call(kernel, name, outs, scratch, *values):
        return pl.pallas_call(
            kernel, out_shape=outs,
            in_specs=[whole] * len(values),
            out_specs=jax.tree.map(lambda _: whole, outs), scratch_shapes=[wide_scratch] * scratch,
            compiler_params=pltpu.CompilerParams(vmem_limit_bytes=40 * 1024 * 1024), name=name,
        )(*values)

    slopes = slope_matrices(lanes)
    average = average_matrix(lanes)
    heat, after, before, fields_after, fields_before = radiation(
        atmospheric_constituents, thermal_ratio, flow_velocity, solar_elevation_factor,
        ground_reflectivity, sunlit_indicator, molecular_optics_lookup, condensate_optics_lookup,
    )
    back = edge_matrix(level_count, lanes).T
    change, wind = call(
        own_change_kernel, "own_change",
        (wide, jax.ShapeDtypeStruct((2, size, 2 * lanes), jnp.float32)), 2,
        temper, flow, fields_after, fields_before, back, *slopes,
    )
    wave, first, last = call(
        first_stage_kernel, "first_stage", (wide, line, line), 1,
        change, heat, after, before, back, average,
    )
    below, above = shifted(last, "gy", 1), shifted(first, "gy", -1)
    wave, first, last, total = call(
        functools.partial(next_stage_kernel, 1.0, True), "second_stage",
        (wide, line, line, field), 3, wave, below, above, wind, temper, *slopes, average,
    )
    below, above = shifted(last, "gy", 1), shifted(first, "gy", -1)
    wave, first, last, total = call(
        functools.partial(next_stage_kernel, 0.5, False), "third_stage",
        (wide, short, short, field), 3, wave, below, above, wind, total, *slopes, average,
    )
    below, above = shifted(last, "gy", 1), shifted(first, "gy", -1)
    total = call(
        functools.partial(last_kernel, 1.0 / 6.0), "last_stage", field, 0,
        wave, below, above, total,
    )
    return (heat.reshape(thermal_ratio.shape), total.reshape(thermal_ratio.shape))


def solution(mesh):
    in_specs = (
        P(None, None, "gy", "gx"),
        P(None, "gy", "gx"),
        P(None, None, "gy", "gx"),
        P("gy", "gx"),
        P("gy", "gx"),
        P("gy", "gx"),
        P(),
        P(),
    )
    out_specs = (P(None, "gy", "gx"), P(None, "gy", "gx"))
    return jax.shard_map(local, mesh=mesh, in_specs=in_specs, out_specs=out_specs, check_vma=False)
```

```python
import functools

import jax
import jax.numpy as jnp
import numpy as np
from jax import lax
from jax.experimental import pallas as pl
from jax.experimental.pallas import tpu as pltpu
from jax.sharding import PartitionSpec as P

NODES = 4
TIME_INCREMENT = 0.05
ROWS = 8
LOG2E = 1.4426950408889634

GROUP = 8
TERMS = 16
BLOCK = 12
PARTIAL = 5
CHUNKS = 2
QUANTITIES = 4


def shifted(value, axis, steps):
    count = lax.axis_size(axis)
    return lax.ppermute(value, axis, [(i, (i + steps) % count) for i in range(count)])


def gll_derivative():
    points = np.array([-1.0, -1.0 / np.sqrt(5.0), 1.0 / np.sqrt(5.0), 1.0])
    legendre = 0.5 * (5.0 * points**3 - 3.0 * points)
    derivative = np.zeros((4, 4))
    for source in range(4):
        for target in range(4):
            if source != target:
                derivative[source, target] = legendre[source] / (
                    legendre[target] * (points[source] - points[target])
                )
    derivative[0, 0] = -3.0
    derivative[3, 3] = 3.0
    return derivative


def high_low(values):
    high = values.astype(jnp.bfloat16)
    return high, (values - high.astype(jnp.float32)).astype(jnp.bfloat16)


def across(left, right, precision=None):
    return lax.dot_general(
        left, right, (((0,), (0,)), ((), ())), precision=precision,
        preferred_element_type=jnp.float32,
    )


def optics_matrices(molecular_ref, table_ref, optics_ref, weight_ref):
    level_count, gpoints = molecular_ref.shape[1:]
    groups = level_count // GROUP
    width = GROUP * TERMS
    level = lax.broadcasted_iota(jnp.int32, (level_count, groups * width), 0)
    lane = lax.broadcasted_iota(jnp.int32, (level_count, groups * width), 1)
    here = level == lane // TERMS
    term = lane % TERMS
    gases = []
    for k in range(3):
        high, low = high_low(molecular_ref[k])
        spread = [
            jnp.where(here & chosen, 1.0, 0.0).astype(jnp.bfloat16)
            for chosen in ((term == k) | (term == k + 10), term == k + 5)
        ]
        gases.append(across(high, spread[0]) + across(low, spread[1]))
    w = [table_ref[n : n + 1, :] for n in range(7)]
    ls, li = w[0] * w[1], w[3] * w[4]
    la, ia = w[0] * (1.0 - w[1]), w[3] * (1.0 - w[4])
    place = lax.broadcasted_iota(jnp.int32, (8, width), 0)
    term = lax.broadcasted_iota(jnp.int32, (8, width), 1) % TERMS
    pattern = jnp.zeros((8, width), jnp.float32)
    for n, chosen in enumerate((
        (term == 3) | (term == 13), term == 8, (term == 4) | (term == 14), term == 9
    )):
        pattern = jnp.where((place == n) & chosen, 1.0, pattern)
    empty = jnp.zeros((4, gpoints), jnp.float32)

    def water(*values):
        parts = []
        for value in values:
            high = value.astype(jnp.bfloat16).astype(jnp.float32)
            parts += [high, value - high]
        return across(jnp.concatenate(parts + [empty], axis=0), pattern, lax.Precision.HIGHEST)

    absorbed = gases[0] + gases[1]
    gas = absorbed + gases[2]
    pairs = (
        (absorbed, water(la, ia)),
        (gas, water(la + ls * (1.0 - w[2]), ia + li * (1.0 - w[5]))),
        (gas + gas, water(2.0 * w[0], 2.0 * w[3])),
        (gases[2], water(ls * (1.0 + w[2]), li * (1.0 + w[5]))),
    )
    chunk = gpoints // CHUNKS
    for group in range(groups):
        span = slice(group * width, (group + 1) * width)
        tables = [values[:, span] + constant for values, constant in pairs]
        for c in range(CHUNKS):
            rows = [table[c * chunk : (c + 1) * chunk] for table in tables]
            optics_ref[group, c] = jnp.concatenate(rows, axis=0).astype(jnp.bfloat16)
    only = jnp.where(place == 0, 1.0, 0.0)
    weight = jnp.broadcast_to(w[6], (8, gpoints))
    weight_ref[...] = across(weight, only, lax.Precision.HIGHEST)


def layer_terms(state_ref, temp_ref, level):
    lines = state_ref.shape[2]
    thickness = state_ref[2, level]
    temper = temp_ref[pl.ds(pl.multiple_of(level * lines, 8), lines), :]
    weighted = thickness * temper * temper
    return (
        weighted * state_ref[0, level], weighted * state_ref[1, level], thickness,
        state_ref[3, level], state_ref[4, level],
    )


def write_terms(terms_ref, level, values, lines):
    parts = [None] * TERMS
    for k, value in enumerate(values):
        high = value.astype(jnp.bfloat16).astype(jnp.float32)
        parts[k], parts[k + 5], parts[k + 10] = high, high, value - high
    parts[15] = jnp.zeros_like(values[0])
    for k, part in enumerate(parts):
        start = (level * TERMS + k) * lines
        start = pl.multiple_of(start, 8) if lines % 8 == 0 else start
        terms_ref[pl.ds(start, lines), :] = part


def sweep_row(
    row, line, lines, count, cosine, ground, optics_ref, weight_ref, terms_ref, right_ref,
    depths_0, depths_1, gain_ref, offset_ref, direct_ref, partial_ref, ratio_ref, source_ref, slant_ref,
):
    level_count, gpoints, lanes = gain_ref.shape
    blocks = level_count // BLOCK
    chunk = gpoints // CHUNKS
    slots = (depths_0, depths_1)
    once = 1 + jnp.minimum(row, 0)

    def place_group(group, carry):
        for j in range(GROUP):
            start = (group * GROUP + j) * TERMS * lines + line
            tile = terms_ref[pl.ds(start, TERMS, stride=lines), :].astype(jnp.bfloat16)
            half = lanes * (j % 2)
            pair = group * (GROUP // 2) + j // 2
            right_ref[pair, TERMS * j : TERMS * (j + 1), half : half + lanes] = tile
        return carry

    lax.fori_loop(0, level_count // GROUP, place_group, 0)
    slant_ref[...] = jnp.broadcast_to((-0.5 * LOG2E) / cosine, (8, lanes))

    def over_rows(values):
        return jnp.broadcast_to(values[None], (gpoints // 8, 8, lanes)).reshape(gpoints, lanes)

    clear = 1.0 / (1.0 - ground)
    ratio_ref[...] = over_rows(jnp.broadcast_to((1.0 + ground) * clear, (8, lanes)))
    source_ref[...] = over_rows(jnp.broadcast_to(2.0 * ground * clear, (8, lanes)))

    def fill(block, c):
        for p in range(BLOCK // 2):
            pair = block * (BLOCK // 2) + p
            slots[c % 2][p] = jnp.dot(
                optics_ref[pair // (GROUP // 2), c], right_ref[pair],
                preferred_element_type=jnp.float32,
            )

    def below(block, c):
        span = slice(c * chunk, (c + 1) * chunk)
        ratio, source = ratio_ref[span], source_ref[span]
        slant = jnp.broadcast_to(slant_ref[...][None], (chunk // 8, 8, lanes))
        slant = slant.reshape(chunk, lanes)
        for j in reversed(range(BLOCK)):
            level = block * BLOCK + j
            part = slots[c % 2].at[j // 2, :, (j % 2) * lanes : (j % 2 + 1) * lanes]
            a, b, depth, along = [part[n * chunk : (n + 1) * chunk] for n in range(QUANTITIES)]
            away = b - a
            square = a * b
            inverse_root = lax.rsqrt(square)
            h = jnp.tanh(square * inverse_root)
            g = h * inverse_root
            g = g + g
            s, p = a * g, b * g
            h2 = h * h
            one = 1.0 + h2
            through = 1.0 - h2
            inverse = 1.0 / (one + s * ratio)
            direct = jnp.exp2(depth * slant)
            factor = (1.0 - direct) * (1.0 / depth)
            up, down = factor * away, factor * along
            push = inverse * (direct * source + (ratio - 1.0) * down)
            ratio = (one * ratio + p) * inverse
            gain = through * inverse
            source = through * push + (ratio + 1.0) * up
            gain_ref[level, span] = gain
            offset_ref[level, span] = (gain * up + down) - s * push
            direct_ref[level, span] = direct
        ratio_ref[span] = ratio
        source_ref[span] = source

    def below_block(step, carry):
        block = blocks - 1 - step
        for c in range(CHUNKS):
            def turn(n, carry, c=c):
                below(block, c)
                if c + 1 < CHUNKS:
                    fill(block, c + 1)
                else:
                    fill(jnp.maximum(block - 1, 0), 0)
                return carry

            lax.fori_loop(0, once, turn, 0)
        return carry

    fill(blocks - 1, 0)
    lax.fori_loop(0, blocks, below_block, 0)

    def folded(net):
        return sum(net[8 * k : 8 * (k + 1)] for k in range(gpoints // 8))

    def top(step, carry):
        beam = weight_ref[...] * cosine
        net = -(source_ref[...] * beam) / (1.0 + ratio_ref[...])
        partial_ref[pl.ds(pl.multiple_of(row * 8, 8), 8), :] = folded(beam) + folded(net)
        return net, beam

    nothing = jnp.zeros((gpoints, lanes), jnp.float32)
    carry = lax.fori_loop(0, once, top, (nothing, nothing))

    def down_group(group, carry):
        net, beam = carry
        for j in range(GROUP):
            level = group * GROUP + j
            net = gain_ref[level] * net + offset_ref[level] * beam
            beam = beam * direct_ref[level]
            start = pl.multiple_of(((level + 1) * count + row) * 8, 8)
            partial_ref[pl.ds(start, 8), :] = folded(net) + folded(beam)
        return (net, beam)

    lax.fori_loop(0, level_count // GROUP, down_group, carry)


def level_heating(partial_ref, level_count, gpoints, count, write):
    def flux(level):
        start = level * count * 8
        return sum(partial_ref[pl.ds(start + k, count, stride=8), :] for k in range(8))

    def step(level, upper):
        lower = flux(level + 1)
        write(level, (level_count / gpoints) * (upper - lower))
        return lower

    lax.fori_loop(0, level_count, step, flux(0), unroll=4)


def radiation_kernel(
    state_ref, temp_ref, flow_ref, cosine_ref, ground_ref, day_ref, molecular_ref, table_ref,
    edge_ref,
    heat_ref, first_ref, last_ref, optics_ref, weight_ref, strip_ref, terms_ref, right_ref, *scratch,
):
    level_count, lines, lanes = state_ref.shape[1:]
    gpoints = weight_ref.shape[0]
    row, count = pl.program_id(0), pl.num_programs(0)

    @pl.when(row == 0)
    def prepare():
        optics_matrices(molecular_ref, table_ref, optics_ref, weight_ref)
        prepare_terms(state_ref, temp_ref, terms_ref, right_ref)

    sweep_row(
        row, row, lines, count, cosine_ref[pl.ds(row, 1), :], ground_ref[pl.ds(row, 1), :],
        optics_ref, weight_ref, terms_ref, right_ref, *scratch,
    )

    @pl.when(row == count - 1)
    def finish():
        day = day_ref[...] == 1

        def write(level, value):
            start = pl.multiple_of(level * lines, 8)
            heat_ref[pl.ds(start, lines), :] = jnp.where(day, value, 0.0)

        level_heating(scratch[PARTIAL], level_count, gpoints, lines, write)
        for n, ref in enumerate((heat_ref, temp_ref, flow_ref.at[0], flow_ref.at[1])):
            for r in range(lines):
                write_strip(ref, r, lines, strip_ref, 8 * (lines * n + r))
        packed = split_dot(strip_ref[...], edge_ref[...])
        first_ref[...] = packed[:, :lanes]
        last_ref[...] = packed[:, lanes:]


def prepare_terms(state_ref, temp_ref, terms_ref, right_ref):
    level_count, lines = state_ref.shape[1:3]
    right_ref[...] = jnp.zeros_like(right_ref)

    def level(l, carry):
        write_terms(terms_ref, l, layer_terms(state_ref, temp_ref, l), lines)
        return carry

    lax.fori_loop(0, level_count, level, 0, unroll=4)


def write_strip(source_ref, r, lines, strip_ref, start):
    lanes = source_ref.shape[1]
    for k in range(strip_ref.shape[1] // lanes):
        strip_ref[pl.ds(start, 8), lanes * k : lanes * (k + 1)] = source_ref[
            pl.ds(8 * k * lines + r, 8, stride=lines), :
        ]


def radiation(state, temper, flow, cosine, ground, day, molecular, condensate):
    level_count, rows, lanes = state.shape[1:]
    gpoints = molecular.shape[1]
    full = pltpu.VMEM((level_count, gpoints, lanes), jnp.float32)
    plane = pltpu.VMEM((gpoints, lanes), jnp.float32)
    whole = pl.BlockSpec(memory_space=pltpu.VMEM)
    part = (QUANTITIES * gpoints // CHUNKS, GROUP * TERMS)
    depths = pltpu.VMEM((BLOCK // 2, part[0], 2 * lanes), jnp.float32)
    edge = jax.ShapeDtypeStruct((4 * 8 * rows, lanes), jnp.float32)
    cells = level_count * gpoints * rows * lanes
    return pl.pallas_call(
        radiation_kernel,
        out_shape=(jax.ShapeDtypeStruct((level_count * rows, lanes), jnp.float32), edge, edge),
        grid=(rows,), in_specs=[whole] * 9, out_specs=(whole,) * 3,
        scratch_shapes=[
            pltpu.VMEM((level_count // GROUP, CHUNKS) + part, jnp.bfloat16),
            plane,
            pltpu.VMEM((4 * 8 * rows, level_count // 8 * lanes), jnp.float32),
            pltpu.VMEM((level_count * TERMS * rows, lanes), jnp.float32),
            pltpu.VMEM((level_count // 2, GROUP * TERMS, 2 * lanes), jnp.bfloat16),
            depths, depths, full, full, full,
            pltpu.VMEM(((level_count + 1) * rows * 8, lanes), jnp.float32),
            plane, plane,
            pltpu.VMEM((8, lanes), jnp.float32),
        ],
        compiler_params=pltpu.CompilerParams(vmem_limit_bytes=60 * 1024 * 1024),
        cost_estimate=pl.CostEstimate(
            flops=10000 * cells, bytes_accessed=4 * 9 * temper.size, transcendentals=5 * cells
        ),
        name="radiation",
    )(
        state, temper, flow, cosine, ground, day, molecular.transpose(0, 2, 1), condensate,
        edge_matrix(level_count, lanes),
    )


def edge_matrix(level_count, lanes):
    parts = level_count // 8
    width = lanes // parts
    matrix = np.zeros((parts * lanes, 2 * lanes), np.float32)
    for k in range(parts):
        for c in range(width):
            matrix[lanes * k + c, width * k + c] = 1.0
            matrix[lanes * (k + 1) - width + c, lanes + width * k + c] = 1.0
    return jnp.asarray(matrix, jnp.bfloat16)


def slope_matrices(lanes):
    whole = np.kron(np.eye(2 * lanes // NODES), gll_derivative().T).astype(np.float32)
    high = np.asarray(whole, jnp.bfloat16)
    low = np.asarray(whole - high.astype(np.float32), jnp.bfloat16)
    return jnp.asarray(high), jnp.asarray(low)


def average_matrix(lanes):
    size = 2 * lanes
    matrix = np.eye(size, dtype=np.float32)
    for c in range(NODES - 1, size, NODES):
        after = (c + 1) % size
        matrix[c, c] = matrix[after, after] = matrix[c, after] = matrix[after, c] = 0.5
    return jnp.asarray(matrix, jnp.bfloat16)


def split_dot(values, *matrices):
    high, low = high_low(values)
    total = jnp.dot(high, matrices[0], preferred_element_type=jnp.float32)
    total = total + jnp.dot(low, matrices[0], preferred_element_type=jnp.float32)
    if len(matrices) > 1:
        total = total + jnp.dot(high, matrices[1], preferred_element_type=jnp.float32)
    return total


def slope_y(rows_of):
    derivative = gll_derivative()
    result = []
    for r in range(len(rows_of)):
        first = r // NODES * NODES
        total = None
        for n in range(NODES):
            weight = derivative[r - first, n]
            if abs(weight) > 1e-12:
                term = np.float32(weight) * rows_of[first + n]
                total = term if total is None else total + term
        result.append(total)
    return result


def average_y(rows_of, below, above):
    result = list(rows_of)
    count = len(rows_of)
    for r in range(NODES - 1, count - 1, NODES):
        result[r] = result[r + 1] = 0.5 * (rows_of[r] + rows_of[r + 1])
    result[0] = 0.5 * (below + rows_of[0])
    result[count - 1] = 0.5 * (rows_of[count - 1] + above)
    return result


def first_stage_kernel(
    temp_ref, flow_ref, heat_ref, after_ref, before_ref, edge_ref, high_ref, low_ref, average_ref,
    out_ref, first_ref, last_ref, wind_ref, temp_wide_ref, heat_wide_ref, slope_ref,
):
    level_count = first_ref.shape[0]
    lanes = temp_ref.shape[-1]
    both = jnp.concatenate([after_ref[...], before_ref[...]], axis=1)
    sides = split_dot(both, edge_ref[...])
    fields = (
        (heat_ref, heat_wide_ref), (temp_ref, temp_wide_ref),
        (flow_ref.at[0], wind_ref.at[0]), (flow_ref.at[1], wind_ref.at[1]),
    )
    for n, (own, wide) in enumerate(fields):
        for r in range(ROWS):
            start = r * level_count
            wide[start : start + level_count, :lanes] = own[pl.ds(r, level_count, stride=ROWS), :]
            here = 8 * (ROWS * n + r)
            for k in range(level_count // 8):
                wide[start + 8 * k : start + 8 * (k + 1), lanes:] = sides[
                    here : here + 8, lanes * k : lanes * (k + 1)
                ]
    slope_ref[...] = split_dot(temp_wide_ref[...], high_ref[...], low_ref[...])
    advect(temp_wide_ref, slope_ref, wind_ref, temp_wide_ref, level_count)
    change = temp_wide_ref[...] + TIME_INCREMENT * heat_wide_ref[...]
    write_averaged(change, average_ref, out_ref, first_ref, last_ref)


def advect(field_ref, slope_ref, wind_ref, change_ref, level_count):
    spans = [slice(r * level_count, (r + 1) * level_count) for r in range(ROWS)]
    for half in range(2):
        lanes = field_ref.shape[1] // 2
        part = slice(half * lanes, (half + 1) * lanes)
        slopes = slope_y([field_ref[span, part] for span in spans])
        for span, slope in zip(spans, slopes):
            change = wind_ref[0, span, part] * slope_ref[span, part]
            change_ref[span, part] = -TIME_INCREMENT * (change + wind_ref[1, span, part] * slope)


def write_averaged(change, average_ref, out_ref, first_ref, last_ref):
    level_count = first_ref.shape[0]
    out_ref[...] = split_dot(change, average_ref[...])
    width = first_ref.shape[1]
    first_ref[...] = out_ref[:level_count, :width]
    last_ref[...] = out_ref[out_ref.shape[0] - level_count :, :width]


def next_stage_kernel(
    share, native, field_ref, below_ref, above_ref, wind_ref, sum_ref, high_ref, low_ref,
    average_ref, out_ref, first_ref, last_ref, total_ref, wave_ref, slope_ref, change_ref,
):
    level_count = below_ref.shape[0]
    lanes = sum_ref.shape[1]
    spans = [slice(r * level_count, (r + 1) * level_count) for r in range(ROWS)]
    for half in range(2):
        part = slice(half * lanes, (half + 1) * lanes)
        wave = average_y(
            [field_ref[span, part] for span in spans], below_ref[:, part], above_ref[:, part]
        )
        for r, (span, row) in enumerate(zip(spans, wave)):
            wave_ref[span, part] = row
            if half == 0:
                before = sum_ref[pl.ds(r, level_count, stride=ROWS), :] if native else sum_ref[span]
                total_ref[span] = before + share * row
    slope_ref[...] = split_dot(wave_ref[...], high_ref[...], low_ref[...])
    advect(wave_ref, slope_ref, wind_ref, change_ref, level_count)
    write_averaged(change_ref[...], average_ref, out_ref, first_ref, last_ref)


def last_kernel(share, field_ref, below_ref, above_ref, sum_ref, total_ref):
    level_count, lanes = below_ref.shape
    spans = [slice(r * level_count, (r + 1) * level_count) for r in range(ROWS)]
    wave = average_y([field_ref[span, :lanes] for span in spans], below_ref[...], above_ref[...])
    for r, (span, row) in enumerate(zip(spans, wave)):
        total_ref[pl.ds(r, level_count, stride=ROWS), :] = sum_ref[span] + share * row


def local(
    atmospheric_constituents,
    thermal_ratio,
    flow_velocity,
    solar_elevation_factor,
    ground_reflectivity,
    sunlit_indicator,
    molecular_optics_lookup,
    condensate_optics_lookup,
):
    level_count, rows, lanes = thermal_ratio.shape
    size = level_count * rows
    temper = thermal_ratio.reshape(size, lanes)
    flow = flow_velocity.reshape(2, size, lanes)
    field = jax.ShapeDtypeStruct((size, lanes), jnp.float32)
    wide = jax.ShapeDtypeStruct((size, 2 * lanes), jnp.float32)
    line = jax.ShapeDtypeStruct((level_count, 2 * lanes), jnp.float32)
    short = jax.ShapeDtypeStruct((level_count, lanes), jnp.float32)
    wide_scratch = pltpu.VMEM(wide.shape, jnp.float32)
    whole = pl.BlockSpec(memory_space=pltpu.VMEM)

    def call(kernel, name, outs, scratch, *values):
        return pl.pallas_call(
            kernel, out_shape=outs,
            in_specs=[whole] * len(values),
            out_specs=jax.tree.map(lambda _: whole, outs), scratch_shapes=[wide_scratch] * scratch,
            compiler_params=pltpu.CompilerParams(vmem_limit_bytes=40 * 1024 * 1024), name=name,
        )(*values)

    slopes = slope_matrices(lanes)
    average = average_matrix(lanes)
    heat, first, last = radiation(
        atmospheric_constituents, temper, flow, solar_elevation_factor,
        ground_reflectivity, sunlit_indicator, molecular_optics_lookup, condensate_optics_lookup,
    )
    after, before = shifted(first, "gx", -1), shifted(last, "gx", 1)
    back = edge_matrix(level_count, lanes).T
    wave, first, last, wind = call(
        first_stage_kernel, "first_stage",
        (wide, line, line, jax.ShapeDtypeStruct((2, size, 2 * lanes), jnp.float32)), 3,
        temper, flow, heat, after, before, back, *slopes, average,
    )
    below, above = shifted(last, "gy", 1), shifted(first, "gy", -1)
    wave, first, last, total = call(
        functools.partial(next_stage_kernel, 1.0, True), "second_stage",
        (wide, line, line, field), 3, wave, below, above, wind, temper, *slopes, average,
    )
    below, above = shifted(last, "gy", 1), shifted(first, "gy", -1)
    wave, first, last, total = call(
        functools.partial(next_stage_kernel, 0.5, False), "third_stage",
        (wide, short, short, field), 3, wave, below, above, wind, total, *slopes, average,
    )
    below, above = shifted(last, "gy", 1), shifted(first, "gy", -1)
    total = call(
        functools.partial(last_kernel, 1.0 / 6.0), "last_stage", field, 0,
        wave, below, above, total,
    )
    return (heat.reshape(thermal_ratio.shape), total.reshape(thermal_ratio.shape))


def solution(mesh):
    in_specs = (
        P(None, None, "gy", "gx"),
        P(None, "gy", "gx"),
        P(None, None, "gy", "gx"),
        P("gy", "gx"),
        P("gy", "gx"),
        P("gy", "gx"),
        P(),
        P(),
    )
    out_specs = (P(None, "gy", "gx"), P(None, "gy", "gx"))
    return jax.shard_map(local, mesh=mesh, in_specs=in_specs, out_specs=out_specs, check_vma=False)
```

```python
import functools

import jax
import jax.numpy as jnp
import numpy as np
from jax import lax
from jax.experimental import pallas as pl
from jax.experimental.pallas import tpu as pltpu
from jax.sharding import PartitionSpec as P

NODES = 4
TIME_INCREMENT = 0.05
ROWS = 8
LOG2E = 1.4426950408889634

GROUP = 8
TERMS = 16
BLOCK = 12
PARTIAL = 5
DOWN = 24
CHUNKS = 2
QUANTITIES = 4


def shifted(value, axis, steps):
    count = lax.axis_size(axis)
    return lax.ppermute(value, axis, [(i, (i + steps) % count) for i in range(count)])


def gll_derivative():
    points = np.array([-1.0, -1.0 / np.sqrt(5.0), 1.0 / np.sqrt(5.0), 1.0])
    legendre = 0.5 * (5.0 * points**3 - 3.0 * points)
    derivative = np.zeros((4, 4))
    for source in range(4):
        for target in range(4):
            if source != target:
                derivative[source, target] = legendre[source] / (
                    legendre[target] * (points[source] - points[target])
                )
    derivative[0, 0] = -3.0
    derivative[3, 3] = 3.0
    return derivative


def high_low(values):
    high = values.astype(jnp.bfloat16)
    return high, (values - high.astype(jnp.float32)).astype(jnp.bfloat16)


def across(left, right, precision=None):
    return lax.dot_general(
        left, right, (((0,), (0,)), ((), ())), precision=precision,
        preferred_element_type=jnp.float32,
    )


def optics_matrices(molecular_ref, table_ref, optics_ref, weight_ref):
    level_count, gpoints = molecular_ref.shape[1:]
    groups = level_count // GROUP
    width = GROUP * TERMS
    level = lax.broadcasted_iota(jnp.int32, (level_count, groups * width), 0)
    lane = lax.broadcasted_iota(jnp.int32, (level_count, groups * width), 1)
    here = level == lane // TERMS
    term = lane % TERMS
    gases = []
    for k in range(3):
        high, low = high_low(molecular_ref[k])
        spread = [
            jnp.where(here & chosen, 1.0, 0.0).astype(jnp.bfloat16)
            for chosen in ((term == k) | (term == k + 10), term == k + 5)
        ]
        gases.append(across(high, spread[0]) + across(low, spread[1]))
    w = [table_ref[n : n + 1, :] for n in range(7)]
    ls, li = w[0] * w[1], w[3] * w[4]
    la, ia = w[0] * (1.0 - w[1]), w[3] * (1.0 - w[4])
    place = lax.broadcasted_iota(jnp.int32, (8, width), 0)
    term = lax.broadcasted_iota(jnp.int32, (8, width), 1) % TERMS
    pattern = jnp.zeros((8, width), jnp.float32)
    for n, chosen in enumerate((
        (term == 3) | (term == 13), term == 8, (term == 4) | (term == 14), term == 9
    )):
        pattern = jnp.where((place == n) & chosen, 1.0, pattern)
    empty = jnp.zeros((4, gpoints), jnp.float32)

    def water(*values):
        parts = []
        for value in values:
            high = value.astype(jnp.bfloat16).astype(jnp.float32)
            parts += [high, value - high]
        return across(jnp.concatenate(parts + [empty], axis=0), pattern, lax.Precision.HIGHEST)

    absorbed = gases[0] + gases[1]
    gas = absorbed + gases[2]
    pairs = (
        (absorbed, water(la, ia)),
        (gas, water(la + ls * (1.0 - w[2]), ia + li * (1.0 - w[5]))),
        (gas + gas, water(2.0 * w[0], 2.0 * w[3])),
        (gases[2], water(ls * (1.0 + w[2]), li * (1.0 + w[5]))),
    )
    chunk = gpoints // CHUNKS
    for group in range(groups):
        span = slice(group * width, (group + 1) * width)
        tables = [values[:, span] + constant for values, constant in pairs]
        for c in range(CHUNKS):
            rows = [table[c * chunk : (c + 1) * chunk] for table in tables]
            optics_ref[group, c] = jnp.concatenate(rows, axis=0).astype(jnp.bfloat16)
    only = jnp.where(place == 0, 1.0, 0.0)
    weight = jnp.broadcast_to(w[6], (8, gpoints))
    weight_ref[...] = across(weight, only, lax.Precision.HIGHEST)


def layer_terms(state_ref, temp_ref, level):
    lines = state_ref.shape[2]
    thickness = state_ref[2, level]
    temper = temp_ref[pl.ds(pl.multiple_of(level * lines, 8), lines), :]
    weighted = thickness * temper * temper
    return (
        weighted * state_ref[0, level], weighted * state_ref[1, level], thickness,
        state_ref[3, level], state_ref[4, level],
    )


def write_terms(terms_ref, level, values, lines):
    parts = [None] * TERMS
    for k, value in enumerate(values):
        high = value.astype(jnp.bfloat16).astype(jnp.float32)
        parts[k], parts[k + 5], parts[k + 10] = high, high, value - high
    parts[15] = jnp.zeros_like(values[0])
    for k, part in enumerate(parts):
        start = (level * TERMS + k) * lines
        start = pl.multiple_of(start, 8) if lines % 8 == 0 else start
        terms_ref[pl.ds(start, lines), :] = part


def sweep_row(
    row, line, lines, count, cosine, ground, optics_ref, weight_ref, terms_ref, right_ref,
    depths_0, depths_1, gain_ref, offset_ref, direct_ref, partial_ref, ratio_ref, source_ref, slant_ref,
):
    level_count, gpoints, lanes = gain_ref.shape
    blocks = level_count // BLOCK
    chunk = gpoints // CHUNKS
    slots = (depths_0, depths_1)
    once = 1 + jnp.minimum(row, 0)

    def place_group(group, carry=None):
        for j in range(GROUP):
            start = (group * GROUP + j) * TERMS * lines + line
            tile = terms_ref[pl.ds(start, TERMS, stride=lines), :].astype(jnp.bfloat16)
            half = lanes * (j % 2)
            pair = group * (GROUP // 2) + j // 2
            right_ref[pair, TERMS * j : TERMS * (j + 1), half : half + lanes] = tile
        return carry

    groups = level_count // GROUP
    ready = -(-BLOCK // GROUP)
    for group in range(groups - ready, groups):
        place_group(group)
    slant_ref[...] = jnp.broadcast_to((-0.5 * LOG2E) / cosine, (8, lanes))

    def over_rows(values):
        return jnp.broadcast_to(values[None], (gpoints // 8, 8, lanes)).reshape(gpoints, lanes)

    clear = 1.0 / (1.0 - ground)
    ratio_ref[...] = over_rows(jnp.broadcast_to((1.0 + ground) * clear, (8, lanes)))
    source_ref[...] = over_rows(jnp.broadcast_to(2.0 * ground * clear, (8, lanes)))

    def fill(block, c):
        for p in range(BLOCK // 2):
            pair = block * (BLOCK // 2) + p
            slots[c % 2][p] = jnp.dot(
                optics_ref[pair // (GROUP // 2), c], right_ref[pair],
                preferred_element_type=jnp.float32,
            )

    def below(block, c):
        span = slice(c * chunk, (c + 1) * chunk)
        ratio, source = ratio_ref[span], source_ref[span]
        slant = jnp.broadcast_to(slant_ref[...][None], (chunk // 8, 8, lanes))
        slant = slant.reshape(chunk, lanes)
        for j in reversed(range(BLOCK)):
            level = block * BLOCK + j
            part = slots[c % 2].at[j // 2, :, (j % 2) * lanes : (j % 2 + 1) * lanes]
            a, b, depth, along = [part[n * chunk : (n + 1) * chunk] for n in range(QUANTITIES)]
            away = b - a
            square = a * b
            inverse_root = lax.rsqrt(square)
            h = jnp.tanh(square * inverse_root)
            g = h * inverse_root
            g = g + g
            s, p = a * g, b * g
            h2 = h * h
            one = 1.0 + h2
            through = 1.0 - h2
            inverse = 1.0 / (one + s * ratio)
            direct = jnp.exp2(depth * slant)
            factor = (1.0 - direct) * (1.0 / depth)
            up, down = factor * away, factor * along
            push = inverse * (direct * source + (ratio - 1.0) * down)
            ratio = (one * ratio + p) * inverse
            gain = through * inverse
            source = through * push + (ratio + 1.0) * up
            gain_ref[level, span] = gain
            offset_ref[level, span] = (gain * up + down) - s * push
            direct_ref[level, span] = direct
        ratio_ref[span] = ratio
        source_ref[span] = source

    def below_block(step, carry):
        block = blocks - 1 - step
        for c in range(CHUNKS):
            def turn(n, carry, c=c):
                below(block, c)
                if c + 1 < CHUNKS:
                    fill(block, c + 1)
                else:
                    fill(jnp.maximum(block - 1, 0), 0)
                return carry

            lax.fori_loop(0, once, turn, 0)
        return carry

    fill(blocks - 1, 0)
    for group in range(groups - ready):
        place_group(group)
    lax.fori_loop(0, blocks, below_block, 0)

    def folded(net):
        return sum(net[8 * k : 8 * (k + 1)] for k in range(gpoints // 8))

    def top(step, carry):
        beam = weight_ref[...] * cosine
        net = -(source_ref[...] * beam) / (1.0 + ratio_ref[...])
        partial_ref[pl.ds(pl.multiple_of(row * 8, 8), 8), :] = folded(beam) + folded(net)
        return net, beam

    nothing = jnp.zeros((gpoints, lanes), jnp.float32)
    carry = lax.fori_loop(0, once, top, (nothing, nothing))

    def down_group(group, carry):
        net, beam = carry
        for j in range(DOWN):
            level = group * DOWN + j
            net = gain_ref[level] * net + offset_ref[level] * beam
            beam = beam * direct_ref[level]
            start = pl.multiple_of(((level + 1) * count + row) * 8, 8)
            partial_ref[pl.ds(start, 8), :] = folded(net) + folded(beam)
        return (net, beam)

    lax.fori_loop(0, level_count // DOWN, down_group, carry)


def level_heating(partial_ref, level_count, gpoints, count, write):
    def flux(level):
        start = level * count * 8
        return sum(partial_ref[pl.ds(start + k, count, stride=8), :] for k in range(8))

    def step(level, upper):
        lower = flux(level + 1)
        write(level, (level_count / gpoints) * (upper - lower))
        return lower

    lax.fori_loop(0, level_count, step, flux(0), unroll=4)


def radiation_kernel(
    state_ref, temp_ref, flow_ref, cosine_ref, ground_ref, day_ref, molecular_ref, table_ref,
    edge_ref, high_ref, low_ref,
    heat_ref, change_ref, wind_ref, first_ref, last_ref,
    optics_ref, weight_ref, strip_ref, slope_ref, terms_ref, right_ref, *scratch,
):
    level_count, lines, lanes = state_ref.shape[1:]
    gpoints = weight_ref.shape[0]
    row, count = pl.program_id(0), pl.num_programs(0)

    @pl.when(row == 0)
    def prepare():
        optics_matrices(molecular_ref, table_ref, optics_ref, weight_ref)
        prepare_terms(state_ref, temp_ref, terms_ref, right_ref)

    sweep_row(
        row, row, lines, count, cosine_ref[pl.ds(row, 1), :], ground_ref[pl.ds(row, 1), :],
        optics_ref, weight_ref, terms_ref, right_ref, *scratch,
    )

    @pl.when(row == count - 1)
    def finish():
        day = day_ref[...] == 1

        def write(level, value):
            start = pl.multiple_of(level * lines, 8)
            heat_ref[pl.ds(start, lines), :] = jnp.where(day, value, 0.0)

        level_heating(scratch[PARTIAL], level_count, gpoints, lines, write)
        spans = [slice(r * level_count, (r + 1) * level_count) for r in range(lines)]
        for r, span in enumerate(spans):
            native = pl.ds(r, level_count, stride=lines)
            change_ref[span, :] = temp_ref[native, :]
            for n in range(2):
                wind_ref[n, span, :] = flow_ref[n, native, :]
        slope_ref[...] = split_dot(
            change_ref[...], high_ref[:lanes, :lanes], low_ref[:lanes, :lanes]
        )
        changes = change_rows(change_ref, slope_ref, wind_ref, slice(0, lanes), spans)
        for r, (span, change) in enumerate(zip(spans, changes)):
            own = heat_ref[pl.ds(r, level_count, stride=lines), :]
            change_ref[span, :] = change + TIME_INCREMENT * own
        for n, ref in enumerate((change_ref, wind_ref.at[0], wind_ref.at[1])):
            for r in range(lines):
                here = slice(8 * (lines * n + r), 8 * (lines * n + r + 1))
                for k in range(level_count // 8):
                    start = r * level_count + 8 * k
                    strip_ref[here, lanes * k : lanes * (k + 1)] = ref[start : start + 8, :]
        packed = split_dot(strip_ref[...], edge_ref[...])
        first_ref[...] = packed[:, :lanes]
        last_ref[...] = packed[:, lanes:]


def prepare_terms(state_ref, temp_ref, terms_ref, right_ref):
    level_count, lines = state_ref.shape[1:3]
    right_ref[...] = jnp.zeros_like(right_ref)

    def level(l, carry):
        write_terms(terms_ref, l, layer_terms(state_ref, temp_ref, l), lines)
        return carry

    lax.fori_loop(0, level_count, level, 0, unroll=4)


def radiation(state, temper, flow, cosine, ground, day, molecular, condensate):
    level_count, rows, lanes = state.shape[1:]
    gpoints = molecular.shape[1]
    full = pltpu.VMEM((level_count, gpoints, lanes), jnp.float32)
    plane = pltpu.VMEM((gpoints, lanes), jnp.float32)
    whole = pl.BlockSpec(memory_space=pltpu.VMEM)
    part = (QUANTITIES * gpoints // CHUNKS, GROUP * TERMS)
    depths = pltpu.VMEM((BLOCK // 2, part[0], 2 * lanes), jnp.float32)
    field = jax.ShapeDtypeStruct((level_count * rows, lanes), jnp.float32)
    wind = jax.ShapeDtypeStruct((2, level_count * rows, lanes), jnp.float32)
    edge = jax.ShapeDtypeStruct((3 * 8 * rows, lanes), jnp.float32)
    cells = level_count * gpoints * rows * lanes
    return pl.pallas_call(
        radiation_kernel,
        out_shape=(field, field, wind, edge, edge),
        grid=(rows,), in_specs=[whole] * 11, out_specs=(whole,) * 5,
        scratch_shapes=[
            pltpu.VMEM((level_count // GROUP, CHUNKS) + part, jnp.bfloat16),
            plane,
            pltpu.VMEM((3 * 8 * rows, level_count // 8 * lanes), jnp.float32),
            pltpu.VMEM((level_count * rows, lanes), jnp.float32),
            pltpu.VMEM((level_count * TERMS * rows, lanes), jnp.float32),
            pltpu.VMEM((level_count // 2, GROUP * TERMS, 2 * lanes), jnp.bfloat16),
            depths, depths, full, full, full,
            pltpu.VMEM(((level_count + 1) * rows * 8, lanes), jnp.float32),
            plane, plane,
            pltpu.VMEM((8, lanes), jnp.float32),
        ],
        compiler_params=pltpu.CompilerParams(vmem_limit_bytes=60 * 1024 * 1024),
        cost_estimate=pl.CostEstimate(
            flops=10000 * cells, bytes_accessed=4 * 9 * temper.size, transcendentals=5 * cells
        ),
        name="radiation",
    )(
        state, temper, flow, cosine, ground, day, molecular.transpose(0, 2, 1), condensate,
        edge_matrix(level_count, lanes), *slope_matrices(lanes),
    )


def edge_matrix(level_count, lanes):
    parts = level_count // 8
    width = lanes // parts
    matrix = np.zeros((parts * lanes, 2 * lanes), np.float32)
    for k in range(parts):
        for c in range(width):
            matrix[lanes * k + c, width * k + c] = 1.0
            matrix[lanes * (k + 1) - width + c, lanes + width * k + c] = 1.0
    return jnp.asarray(matrix, jnp.bfloat16)


def slope_matrices(lanes):
    whole = np.kron(np.eye(2 * lanes // NODES), gll_derivative().T).astype(np.float32)
    high = np.asarray(whole, jnp.bfloat16)
    low = np.asarray(whole - high.astype(np.float32), jnp.bfloat16)
    return jnp.asarray(high), jnp.asarray(low)


def average_matrix(lanes):
    size = 2 * lanes
    matrix = np.eye(size, dtype=np.float32)
    for c in range(NODES - 1, size, NODES):
        after = (c + 1) % size
        matrix[c, c] = matrix[after, after] = matrix[c, after] = matrix[after, c] = 0.5
    return jnp.asarray(matrix, jnp.bfloat16)


def split_dot(values, *matrices):
    high, low = high_low(values)
    total = jnp.dot(high, matrices[0], preferred_element_type=jnp.float32)
    total = total + jnp.dot(low, matrices[0], preferred_element_type=jnp.float32)
    if len(matrices) > 1:
        total = total + jnp.dot(high, matrices[1], preferred_element_type=jnp.float32)
    return total


def slope_y(rows_of):
    derivative = gll_derivative()
    result = []
    for r in range(len(rows_of)):
        first = r // NODES * NODES
        total = None
        for n in range(NODES):
            weight = derivative[r - first, n]
            if abs(weight) > 1e-12:
                term = np.float32(weight) * rows_of[first + n]
                total = term if total is None else total + term
        result.append(total)
    return result


def average_y(rows_of, below, above):
    result = list(rows_of)
    count = len(rows_of)
    for r in range(NODES - 1, count - 1, NODES):
        result[r] = result[r + 1] = 0.5 * (rows_of[r] + rows_of[r + 1])
    result[0] = 0.5 * (below + rows_of[0])
    result[count - 1] = 0.5 * (rows_of[count - 1] + above)
    return result


def first_stage_kernel(
    change_ref, after_ref, before_ref, edge_ref, average_ref,
    out_ref, first_ref, last_ref, wind_side_ref, wide_ref,
):
    level_count = first_ref.shape[0]
    lanes = change_ref.shape[1]
    both = jnp.concatenate([after_ref[...], before_ref[...]], axis=1)
    sides = split_dot(both, edge_ref[...])
    wide_ref[:, :lanes] = change_ref[...]
    for r in range(ROWS):
        for k in range(level_count // 8):
            span = slice(r * level_count + 8 * k, r * level_count + 8 * (k + 1))
            part = slice(lanes * k, lanes * (k + 1))
            wide_ref[span, lanes:] = sides[8 * r : 8 * (r + 1), part]
            for n in range(2):
                here = 8 * (ROWS * (n + 1) + r)
                wind_side_ref[n, span, :] = sides[here : here + 8, part]
    write_averaged(wide_ref[...], average_ref, out_ref, first_ref, last_ref)


def change_rows(field_ref, slope_ref, wind_ref, part, spans):
    slopes = slope_y([field_ref[span, part] for span in spans])
    result = []
    for span, slope in zip(spans, slopes):
        change = wind_ref[0, span, :] * slope_ref[span, part] + wind_ref[1, span, :] * slope
        result.append(-TIME_INCREMENT * change)
    return result


def write_averaged(change, average_ref, out_ref, first_ref, last_ref):
    level_count = first_ref.shape[0]
    out_ref[...] = split_dot(change, average_ref[...])
    width = first_ref.shape[1]
    first_ref[...] = out_ref[:level_count, :width]
    last_ref[...] = out_ref[out_ref.shape[0] - level_count :, :width]


def next_stage_kernel(
    share, native, field_ref, below_ref, above_ref, wind_ref, wind_side_ref, sum_ref, high_ref,
    low_ref, average_ref, out_ref, first_ref, last_ref, total_ref, wave_ref, slope_ref, change_ref,
):
    level_count = below_ref.shape[0]
    lanes = sum_ref.shape[1]
    spans = [slice(r * level_count, (r + 1) * level_count) for r in range(ROWS)]
    for half in range(2):
        part = slice(half * lanes, (half + 1) * lanes)
        wave = average_y(
            [field_ref[span, part] for span in spans], below_ref[:, part], above_ref[:, part]
        )
        for r, (span, row) in enumerate(zip(spans, wave)):
            wave_ref[span, part] = row
            if half == 0:
                before = sum_ref[pl.ds(r, level_count, stride=ROWS), :] if native else sum_ref[span]
                total_ref[span] = before + share * row
    slope_ref[...] = split_dot(wave_ref[...], high_ref[...], low_ref[...])
    for half, wind in enumerate((wind_ref, wind_side_ref)):
        part = slice(half * lanes, (half + 1) * lanes)
        for span, change in zip(spans, change_rows(wave_ref, slope_ref, wind, part, spans)):
            change_ref[span, part] = change
    write_averaged(change_ref[...], average_ref, out_ref, first_ref, last_ref)


def last_kernel(share, field_ref, below_ref, above_ref, sum_ref, total_ref):
    level_count, lanes = below_ref.shape
    spans = [slice(r * level_count, (r + 1) * level_count) for r in range(ROWS)]
    wave = average_y([field_ref[span, :lanes] for span in spans], below_ref[...], above_ref[...])
    for r, (span, row) in enumerate(zip(spans, wave)):
        total_ref[pl.ds(r, level_count, stride=ROWS), :] = sum_ref[span] + share * row


def local(
    atmospheric_constituents,
    thermal_ratio,
    flow_velocity,
    solar_elevation_factor,
    ground_reflectivity,
    sunlit_indicator,
    molecular_optics_lookup,
    condensate_optics_lookup,
):
    level_count, rows, lanes = thermal_ratio.shape
    size = level_count * rows
    temper = thermal_ratio.reshape(size, lanes)
    flow = flow_velocity.reshape(2, size, lanes)
    field = jax.ShapeDtypeStruct((size, lanes), jnp.float32)
    wide = jax.ShapeDtypeStruct((size, 2 * lanes), jnp.float32)
    line = jax.ShapeDtypeStruct((level_count, 2 * lanes), jnp.float32)
    short = jax.ShapeDtypeStruct((level_count, lanes), jnp.float32)
    wide_scratch = pltpu.VMEM(wide.shape, jnp.float32)
    whole = pl.BlockSpec(memory_space=pltpu.VMEM)

    def call(kernel, name, outs, scratch, *values):
        return pl.pallas_call(
            kernel, out_shape=outs,
            in_specs=[whole] * len(values),
            out_specs=jax.tree.map(lambda _: whole, outs), scratch_shapes=[wide_scratch] * scratch,
            compiler_params=pltpu.CompilerParams(vmem_limit_bytes=40 * 1024 * 1024), name=name,
        )(*values)

    slopes = slope_matrices(lanes)
    average = average_matrix(lanes)
    heat, change, wind, first, last = radiation(
        atmospheric_constituents, temper, flow, solar_elevation_factor,
        ground_reflectivity, sunlit_indicator, molecular_optics_lookup, condensate_optics_lookup,
    )
    after, before = shifted(first, "gx", -1), shifted(last, "gx", 1)
    back = edge_matrix(level_count, lanes).T
    wave, first, last, wind_side = call(
        first_stage_kernel, "first_stage",
        (wide, line, line, jax.ShapeDtypeStruct((2, size, lanes), jnp.float32)), 1,
        change, after, before, back, average,
    )
    below, above = shifted(last, "gy", 1), shifted(first, "gy", -1)
    wave, first, last, total = call(
        functools.partial(next_stage_kernel, 1.0, True), "second_stage",
        (wide, line, line, field), 3, wave, below, above, wind, wind_side, temper, *slopes, average,
    )
    below, above = shifted(last, "gy", 1), shifted(first, "gy", -1)
    wave, first, last, total = call(
        functools.partial(next_stage_kernel, 0.5, False), "third_stage",
        (wide, short, short, field), 3, wave, below, above, wind, wind_side, total, *slopes, average,
    )
    below, above = shifted(last, "gy", 1), shifted(first, "gy", -1)
    total = call(
        functools.partial(last_kernel, 1.0 / 6.0), "last_stage", field, 0,
        wave, below, above, total,
    )
    return (heat.reshape(thermal_ratio.shape), total.reshape(thermal_ratio.shape))


def solution(mesh):
    in_specs = (
        P(None, None, "gy", "gx"),
        P(None, "gy", "gx"),
        P(None, None, "gy", "gx"),
        P("gy", "gx"),
        P("gy", "gx"),
        P("gy", "gx"),
        P(),
        P(),
    )
    out_specs = (P(None, "gy", "gx"), P(None, "gy", "gx"))
    return jax.shard_map(local, mesh=mesh, in_specs=in_specs, out_specs=out_specs, check_vma=False)
```

```python
import functools

import jax
import jax.numpy as jnp
import numpy as np
from jax import lax
from jax.experimental import pallas as pl
from jax.experimental.pallas import tpu as pltpu
from jax.sharding import PartitionSpec as P

NODES = 4
TIME_INCREMENT = 0.05
ROWS = 8
LOG2E = 1.4426950408889634

GROUP = 8
TERMS = 16
BLOCK = 12
PARTIAL = 5
DOWN = 24
CHUNKS = 2
QUANTITIES = 4


def shifted(value, axis, steps):
    count = lax.axis_size(axis)
    return lax.ppermute(value, axis, [(i, (i + steps) % count) for i in range(count)])


def gll_derivative():
    points = np.array([-1.0, -1.0 / np.sqrt(5.0), 1.0 / np.sqrt(5.0), 1.0])
    legendre = 0.5 * (5.0 * points**3 - 3.0 * points)
    derivative = np.zeros((4, 4))
    for source in range(4):
        for target in range(4):
            if source != target:
                derivative[source, target] = legendre[source] / (
                    legendre[target] * (points[source] - points[target])
                )
    derivative[0, 0] = -3.0
    derivative[3, 3] = 3.0
    return derivative


def high_low(values):
    high = values.astype(jnp.bfloat16)
    return high, (values - high.astype(jnp.float32)).astype(jnp.bfloat16)


def across(left, right, precision=None):
    return lax.dot_general(
        left, right, (((0,), (0,)), ((), ())), precision=precision,
        preferred_element_type=jnp.float32,
    )


def optics_matrices(molecular_ref, table_ref, optics_ref, weight_ref):
    level_count, gpoints = molecular_ref.shape[1:]
    groups = level_count // GROUP
    width = GROUP * TERMS
    level = lax.broadcasted_iota(jnp.int32, (level_count, groups * width), 0)
    lane = lax.broadcasted_iota(jnp.int32, (level_count, groups * width), 1)
    here = level == lane // TERMS
    term = lane % TERMS
    gases = []
    for k in range(3):
        high, low = high_low(molecular_ref[k])
        spread = [
            jnp.where(here & chosen, 1.0, 0.0).astype(jnp.bfloat16)
            for chosen in ((term == k) | (term == k + 10), term == k + 5)
        ]
        gases.append(across(high, spread[0]) + across(low, spread[1]))
    w = [table_ref[n : n + 1, :] for n in range(7)]
    ls, li = w[0] * w[1], w[3] * w[4]
    la, ia = w[0] * (1.0 - w[1]), w[3] * (1.0 - w[4])
    place = lax.broadcasted_iota(jnp.int32, (8, width), 0)
    term = lax.broadcasted_iota(jnp.int32, (8, width), 1) % TERMS
    pattern = jnp.zeros((8, width), jnp.float32)
    for n, chosen in enumerate((
        (term == 3) | (term == 13), term == 8, (term == 4) | (term == 14), term == 9
    )):
        pattern = jnp.where((place == n) & chosen, 1.0, pattern)
    empty = jnp.zeros((4, gpoints), jnp.float32)

    def water(*values):
        parts = []
        for value in values:
            high = value.astype(jnp.bfloat16).astype(jnp.float32)
            parts += [high, value - high]
        return across(jnp.concatenate(parts + [empty], axis=0), pattern, lax.Precision.HIGHEST)

    absorbed = gases[0] + gases[1]
    gas = absorbed + gases[2]
    pairs = (
        (absorbed, water(la, ia)),
        (gas, water(la + ls * (1.0 - w[2]), ia + li * (1.0 - w[5]))),
        (gas + gas, water(2.0 * w[0], 2.0 * w[3])),
        (gases[2], water(ls * (1.0 + w[2]), li * (1.0 + w[5]))),
    )
    chunk = gpoints // CHUNKS
    for group in range(groups):
        span = slice(group * width, (group + 1) * width)
        tables = [values[:, span] + constant for values, constant in pairs]
        for c in range(CHUNKS):
            rows = [table[c * chunk : (c + 1) * chunk] for table in tables]
            optics_ref[group, c] = jnp.concatenate(rows, axis=0).astype(jnp.bfloat16)
    only = jnp.where(place == 0, 1.0, 0.0)
    weight = jnp.broadcast_to(w[6], (8, gpoints))
    weight_ref[...] = across(weight, only, lax.Precision.HIGHEST)


def layer_terms(state_ref, temp_ref, level):
    lines = state_ref.shape[2]
    thickness = state_ref[2, level]
    temper = temp_ref[pl.ds(pl.multiple_of(level * lines, 8), lines), :]
    weighted = thickness * temper * temper
    return (
        weighted * state_ref[0, level], weighted * state_ref[1, level], thickness,
        state_ref[3, level], state_ref[4, level],
    )


def write_terms(terms_ref, level, values, lines):
    parts = [None] * TERMS
    for k, value in enumerate(values):
        high = value.astype(jnp.bfloat16).astype(jnp.float32)
        parts[k], parts[k + 5], parts[k + 10] = high, high, value - high
    parts[15] = jnp.zeros_like(values[0])
    for k, part in enumerate(parts):
        start = (level * TERMS + k) * lines
        start = pl.multiple_of(start, 8) if lines % 8 == 0 else start
        terms_ref[pl.ds(start, lines), :] = part


def sweep_row(
    row, line, lines, count, cosine, ground, optics_ref, weight_ref, terms_ref, right_ref,
    depths_0, depths_1, gain_ref, offset_ref, direct_ref, partial_ref, ratio_ref, source_ref, slant_ref,
):
    level_count, gpoints, lanes = gain_ref.shape
    blocks = level_count // BLOCK
    chunk = gpoints // CHUNKS
    slots = (depths_0, depths_1)
    once = 1 + jnp.minimum(row, 0)

    def place_group(group, carry=None):
        for j in range(GROUP):
            start = (group * GROUP + j) * TERMS * lines + line
            tile = terms_ref[pl.ds(start, TERMS, stride=lines), :].astype(jnp.bfloat16)
            half = lanes * (j % 2)
            pair = group * (GROUP // 2) + j // 2
            right_ref[pair, TERMS * j : TERMS * (j + 1), half : half + lanes] = tile
        return carry

    groups = level_count // GROUP
    ready = -(-BLOCK // GROUP)
    for group in range(groups - ready, groups):
        place_group(group)
    slant_ref[...] = jnp.broadcast_to((-0.5 * LOG2E) / cosine, (8, lanes))

    def over_rows(values):
        return jnp.broadcast_to(values[None], (gpoints // 8, 8, lanes)).reshape(gpoints, lanes)

    clear = 1.0 / (1.0 - ground)
    ratio_ref[...] = over_rows(jnp.broadcast_to((1.0 + ground) * clear, (8, lanes)))
    source_ref[...] = over_rows(jnp.broadcast_to(2.0 * ground * clear, (8, lanes)))

    def fill(block, c):
        for p in range(BLOCK // 2):
            pair = block * (BLOCK // 2) + p
            slots[c % 2][p] = jnp.dot(
                optics_ref[pair // (GROUP // 2), c], right_ref[pair],
                preferred_element_type=jnp.float32,
            )

    def below(block, c):
        span = slice(c * chunk, (c + 1) * chunk)
        ratio, source = ratio_ref[span], source_ref[span]
        slant = jnp.broadcast_to(slant_ref[...][None], (chunk // 8, 8, lanes))
        slant = slant.reshape(chunk, lanes)
        for j in reversed(range(BLOCK)):
            level = block * BLOCK + j
            part = slots[c % 2].at[j // 2, :, (j % 2) * lanes : (j % 2 + 1) * lanes]
            a, b, depth, along = [part[n * chunk : (n + 1) * chunk] for n in range(QUANTITIES)]
            away = b - a
            square = a * b
            inverse_root = lax.rsqrt(square)
            h = jnp.tanh(square * inverse_root)
            g = h * inverse_root
            g = g + g
            s, p = a * g, b * g
            h2 = h * h
            one = 1.0 + h2
            through = 1.0 - h2
            inverse = 1.0 / (one + s * ratio)
            direct = jnp.exp2(depth * slant)
            factor = (1.0 - direct) * (1.0 / depth)
            up, down = factor * away, factor * along
            push = inverse * (direct * source + (ratio - 1.0) * down)
            ratio = (one * ratio + p) * inverse
            gain = through * inverse
            source = through * push + (ratio + 1.0) * up
            gain_ref[level, span] = gain
            offset_ref[level, span] = (gain * up + down) - s * push
            direct_ref[level, span] = direct
        ratio_ref[span] = ratio
        source_ref[span] = source

    def below_block(step, carry):
        block = blocks - 1 - step
        for c in range(CHUNKS):
            def turn(n, carry, c=c):
                below(block, c)
                if c + 1 < CHUNKS:
                    fill(block, c + 1)
                else:
                    fill(jnp.maximum(block - 1, 0), 0)
                return carry

            lax.fori_loop(0, once, turn, 0)
        return carry

    fill(blocks - 1, 0)
    for group in range(groups - ready):
        place_group(group)
    lax.fori_loop(0, blocks, below_block, 0)

    def folded(net):
        return sum(net[8 * k : 8 * (k + 1)] for k in range(gpoints // 8))

    def top(step, carry):
        beam = weight_ref[...] * cosine
        net = -(source_ref[...] * beam) / (1.0 + ratio_ref[...])
        partial_ref[pl.ds(pl.multiple_of(row * 8, 8), 8), :] = folded(beam) + folded(net)
        return net, beam

    nothing = jnp.zeros((gpoints, lanes), jnp.float32)
    carry = lax.fori_loop(0, once, top, (nothing, nothing))

    def down_group(group, carry):
        net, beam = carry
        for j in range(DOWN):
            level = group * DOWN + j
            net = gain_ref[level] * net + offset_ref[level] * beam
            beam = beam * direct_ref[level]
            start = pl.multiple_of(((level + 1) * count + row) * 8, 8)
            partial_ref[pl.ds(start, 8), :] = folded(net) + folded(beam)
        return (net, beam)

    lax.fori_loop(0, level_count // DOWN, down_group, carry)


def level_heating(partial_ref, level_count, gpoints, count, write):
    def flux(level):
        start = level * count * 8
        return sum(partial_ref[pl.ds(start + k, count, stride=8), :] for k in range(8))

    def step(level, upper):
        lower = flux(level + 1)
        write(level, (level_count / gpoints) * (upper - lower))
        return lower

    lax.fori_loop(0, level_count, step, flux(0), unroll=4)


def radiation_kernel(
    state_ref, temp_ref, flow_ref, cosine_ref, ground_ref, day_ref, molecular_ref, table_ref,
    edge_ref, high_ref, low_ref,
    heat_ref, change_ref, wind_ref, first_ref, last_ref,
    optics_ref, weight_ref, strip_ref, slope_ref, terms_ref, right_ref, *scratch,
):
    level_count, lines, lanes = state_ref.shape[1:]
    gpoints = weight_ref.shape[0]
    row, count = pl.program_id(0), pl.num_programs(0)

    @pl.when(row == 0)
    def prepare():
        optics_matrices(molecular_ref, table_ref, optics_ref, weight_ref)
        prepare_terms(state_ref, temp_ref, terms_ref, right_ref)

    sweep_row(
        row, row, lines, count, cosine_ref[pl.ds(row, 1), :], ground_ref[pl.ds(row, 1), :],
        optics_ref, weight_ref, terms_ref, right_ref, *scratch,
    )

    @pl.when(row == count - 1)
    def finish():
        day = day_ref[...] == 1

        def write(level, value):
            start = pl.multiple_of(level * lines, 8)
            heat_ref[pl.ds(start, lines), :] = jnp.where(day, value, 0.0)

        level_heating(scratch[PARTIAL], level_count, gpoints, lines, write)
        spans = [slice(r * level_count, (r + 1) * level_count) for r in range(lines)]
        for r, span in enumerate(spans):
            native = pl.ds(r, level_count, stride=lines)
            change_ref[span, :] = temp_ref[native, :]
            for n in range(2):
                wind_ref[n, span, :] = flow_ref[n, native, :]
        slope_ref[...] = split_dot(
            change_ref[...], high_ref[:lanes, :lanes], low_ref[:lanes, :lanes]
        )
        changes = change_rows(change_ref, slope_ref, wind_ref, slice(0, lanes), spans)
        for r, (span, change) in enumerate(zip(spans, changes)):
            own = heat_ref[pl.ds(r, level_count, stride=lines), :]
            change_ref[span, :] = change + TIME_INCREMENT * own
        for n, ref in enumerate((change_ref, wind_ref.at[0], wind_ref.at[1])):
            for r in range(lines):
                here = slice(8 * (lines * n + r), 8 * (lines * n + r + 1))
                for k in range(level_count // 8):
                    start = r * level_count + 8 * k
                    strip_ref[here, lanes * k : lanes * (k + 1)] = ref[start : start + 8, :]
        packed = split_dot(strip_ref[...], edge_ref[...])
        first_ref[...] = packed[:, :lanes]
        last_ref[...] = packed[:, lanes:]


def prepare_terms(state_ref, temp_ref, terms_ref, right_ref):
    level_count, lines = state_ref.shape[1:3]
    right_ref[...] = jnp.zeros_like(right_ref)

    def level(l, carry):
        write_terms(terms_ref, l, layer_terms(state_ref, temp_ref, l), lines)
        return carry

    lax.fori_loop(0, level_count, level, 0, unroll=4)


def radiation(state, temper, flow, cosine, ground, day, molecular, condensate):
    level_count, rows, lanes = state.shape[1:]
    gpoints = molecular.shape[1]
    full = pltpu.VMEM((level_count, gpoints, lanes), jnp.float32)
    plane = pltpu.VMEM((gpoints, lanes), jnp.float32)
    whole = pl.BlockSpec(memory_space=pltpu.VMEM)
    part = (QUANTITIES * gpoints // CHUNKS, GROUP * TERMS)
    depths = pltpu.VMEM((BLOCK // 2, part[0], 2 * lanes), jnp.float32)
    field = jax.ShapeDtypeStruct((level_count * rows, lanes), jnp.float32)
    wind = jax.ShapeDtypeStruct((2, level_count * rows, lanes), jnp.float32)
    edge = jax.ShapeDtypeStruct((3 * 8 * rows, lanes), jnp.float32)
    cells = level_count * gpoints * rows * lanes
    return pl.pallas_call(
        radiation_kernel,
        out_shape=(field, field, wind, edge, edge),
        grid=(rows,), in_specs=[whole] * 11, out_specs=(whole,) * 5,
        scratch_shapes=[
            pltpu.VMEM((level_count // GROUP, CHUNKS) + part, jnp.bfloat16),
            plane,
            pltpu.VMEM((3 * 8 * rows, level_count // 8 * lanes), jnp.float32),
            pltpu.VMEM((level_count * rows, lanes), jnp.float32),
            pltpu.VMEM((level_count * TERMS * rows, lanes), jnp.float32),
            pltpu.VMEM((level_count // 2, GROUP * TERMS, 2 * lanes), jnp.bfloat16),
            depths, depths, full, full, full,
            pltpu.VMEM(((level_count + 1) * rows * 8, lanes), jnp.float32),
            plane, plane,
            pltpu.VMEM((8, lanes), jnp.float32),
        ],
        compiler_params=pltpu.CompilerParams(vmem_limit_bytes=60 * 1024 * 1024),
        cost_estimate=pl.CostEstimate(
            flops=10000 * cells, bytes_accessed=4 * 9 * temper.size, transcendentals=5 * cells
        ),
        name="radiation",
    )(
        state, temper, flow, cosine, ground, day, molecular.transpose(0, 2, 1), condensate,
        edge_matrix(level_count, lanes), *slope_matrices(lanes),
    )


def edge_matrix(level_count, lanes):
    parts = level_count // 8
    width = lanes // parts
    matrix = np.zeros((parts * lanes, 2 * lanes), np.float32)
    for k in range(parts):
        for c in range(width):
            matrix[lanes * k + c, width * k + c] = 1.0
            matrix[lanes * (k + 1) - width + c, lanes + width * k + c] = 1.0
    return jnp.asarray(matrix, jnp.bfloat16)


def slope_matrices(lanes):
    whole = np.kron(np.eye(2 * lanes // NODES), gll_derivative().T).astype(np.float32)
    high = np.asarray(whole, jnp.bfloat16)
    low = np.asarray(whole - high.astype(np.float32), jnp.bfloat16)
    return jnp.asarray(high), jnp.asarray(low)


def average_matrix(lanes):
    size = 2 * lanes
    matrix = np.eye(size, dtype=np.float32)
    for c in range(NODES - 1, size, NODES):
        after = (c + 1) % size
        matrix[c, c] = matrix[after, after] = matrix[c, after] = matrix[after, c] = 0.5
    return jnp.asarray(matrix, jnp.bfloat16)


def split_dot(values, *matrices):
    high, low = high_low(values)
    total = jnp.dot(high, matrices[0], preferred_element_type=jnp.float32)
    total = total + jnp.dot(low, matrices[0], preferred_element_type=jnp.float32)
    if len(matrices) > 1:
        total = total + jnp.dot(high, matrices[1], preferred_element_type=jnp.float32)
    return total


def slope_y(rows_of):
    derivative = gll_derivative()
    result = []
    for r in range(len(rows_of)):
        first = r // NODES * NODES
        total = None
        for n in range(NODES):
            weight = derivative[r - first, n]
            if abs(weight) > 1e-12:
                term = np.float32(weight) * rows_of[first + n]
                total = term if total is None else total + term
        result.append(total)
    return result


def average_y(rows_of, below, above):
    result = list(rows_of)
    count = len(rows_of)
    for r in range(NODES - 1, count - 1, NODES):
        result[r] = result[r + 1] = 0.5 * (rows_of[r] + rows_of[r + 1])
    result[0] = 0.5 * (below + rows_of[0])
    result[count - 1] = 0.5 * (rows_of[count - 1] + above)
    return result


def first_stage_kernel(
    change_ref, before_ref, after_ref, edge_ref, average_ref,
    out_ref, first_ref, last_ref, wind_side_ref, wide_ref,
):
    level_count = first_ref.shape[0]
    lanes = change_ref.shape[1]
    both = jnp.concatenate([after_ref[...], before_ref[...]], axis=1)
    sides = split_dot(both, edge_ref[...])
    wide_ref[:, :lanes] = change_ref[...]
    for r in range(ROWS):
        for k in range(level_count // 8):
            span = slice(r * level_count + 8 * k, r * level_count + 8 * (k + 1))
            part = slice(lanes * k, lanes * (k + 1))
            wide_ref[span, lanes:] = sides[8 * r : 8 * (r + 1), part]
            for n in range(2):
                here = 8 * (ROWS * (n + 1) + r)
                wind_side_ref[n, span, :] = sides[here : here + 8, part]
    write_averaged(wide_ref[...], average_ref, out_ref, first_ref, last_ref)


def change_rows(field_ref, slope_ref, wind_ref, part, spans):
    slopes = slope_y([field_ref[span, part] for span in spans])
    result = []
    for span, slope in zip(spans, slopes):
        change = wind_ref[0, span, :] * slope_ref[span, part] + wind_ref[1, span, :] * slope
        result.append(-TIME_INCREMENT * change)
    return result


def write_averaged(change, average_ref, out_ref, first_ref, last_ref):
    level_count = first_ref.shape[0]
    out_ref[...] = split_dot(change, average_ref[...])
    width = first_ref.shape[1]
    first_ref[...] = out_ref[:level_count, :width]
    last_ref[...] = out_ref[out_ref.shape[0] - level_count :, :width]


def next_stage_kernel(
    share, native, field_ref, below_ref, above_ref, wind_ref, wind_side_ref, sum_ref, high_ref,
    low_ref, average_ref, out_ref, first_ref, last_ref, total_ref, wave_ref, slope_ref, change_ref,
):
    level_count = below_ref.shape[0]
    lanes = sum_ref.shape[1]
    spans = [slice(r * level_count, (r + 1) * level_count) for r in range(ROWS)]
    for half in range(2):
        part = slice(half * lanes, (half + 1) * lanes)
        wave = average_y(
            [field_ref[span, part] for span in spans], below_ref[:, part], above_ref[:, part]
        )
        for r, (span, row) in enumerate(zip(spans, wave)):
            wave_ref[span, part] = row
            if half == 0:
                before = sum_ref[pl.ds(r, level_count, stride=ROWS), :] if native else sum_ref[span]
                total_ref[span] = before + share * row
    slope_ref[...] = split_dot(wave_ref[...], high_ref[...], low_ref[...])
    for half, wind in enumerate((wind_ref, wind_side_ref)):
        part = slice(half * lanes, (half + 1) * lanes)
        for span, change in zip(spans, change_rows(wave_ref, slope_ref, wind, part, spans)):
            change_ref[span, part] = change
    write_averaged(change_ref[...], average_ref, out_ref, first_ref, last_ref)


def last_kernel(share, field_ref, below_ref, above_ref, sum_ref, total_ref):
    level_count, lanes = below_ref.shape
    spans = [slice(r * level_count, (r + 1) * level_count) for r in range(ROWS)]
    wave = average_y([field_ref[span, :lanes] for span in spans], below_ref[...], above_ref[...])
    for r, (span, row) in enumerate(zip(spans, wave)):
        total_ref[pl.ds(r, level_count, stride=ROWS), :] = sum_ref[span] + share * row


def local(
    atmospheric_constituents,
    thermal_ratio,
    flow_velocity,
    solar_elevation_factor,
    ground_reflectivity,
    sunlit_indicator,
    molecular_optics_lookup,
    condensate_optics_lookup,
):
    level_count, rows, lanes = thermal_ratio.shape
    size = level_count * rows
    temper = thermal_ratio.reshape(size, lanes)
    flow = flow_velocity.reshape(2, size, lanes)
    field = jax.ShapeDtypeStruct((size, lanes), jnp.float32)
    wide = jax.ShapeDtypeStruct((size, 2 * lanes), jnp.float32)
    line = jax.ShapeDtypeStruct((level_count, 2 * lanes), jnp.float32)
    short = jax.ShapeDtypeStruct((level_count, lanes), jnp.float32)
    wide_scratch = pltpu.VMEM(wide.shape, jnp.float32)
    whole = pl.BlockSpec(memory_space=pltpu.VMEM)

    def call(kernel, name, outs, scratch, *values):
        return pl.pallas_call(
            kernel, out_shape=outs,
            in_specs=[whole] * len(values),
            out_specs=jax.tree.map(lambda _: whole, outs), scratch_shapes=[wide_scratch] * scratch,
            compiler_params=pltpu.CompilerParams(vmem_limit_bytes=40 * 1024 * 1024), name=name,
        )(*values)

    slopes = slope_matrices(lanes)
    average = average_matrix(lanes)
    heat, change, wind, first, last = radiation(
        atmospheric_constituents, temper, flow, solar_elevation_factor,
        ground_reflectivity, sunlit_indicator, molecular_optics_lookup, condensate_optics_lookup,
    )
    before, after = shifted(last, "gx", 1), shifted(first, "gx", -1)
    back = edge_matrix(level_count, lanes).T
    wave, first, last, wind_side = call(
        first_stage_kernel, "first_stage",
        (wide, line, line, jax.ShapeDtypeStruct((2, size, lanes), jnp.float32)), 1,
        change, before, after, back, average,
    )
    below, above = shifted(last, "gy", 1), shifted(first, "gy", -1)
    wave, first, last, total = call(
        functools.partial(next_stage_kernel, 1.0, True), "second_stage",
        (wide, line, line, field), 3, wave, below, above, wind, wind_side, temper, *slopes, average,
    )
    below, above = shifted(last, "gy", 1), shifted(first, "gy", -1)
    wave, first, last, total = call(
        functools.partial(next_stage_kernel, 0.5, False), "third_stage",
        (wide, short, short, field), 3, wave, below, above, wind, wind_side, total, *slopes, average,
    )
    below, above = shifted(last, "gy", 1), shifted(first, "gy", -1)
    total = call(
        functools.partial(last_kernel, 1.0 / 6.0), "last_stage", field, 0,
        wave, below, above, total,
    )
    return (heat.reshape(thermal_ratio.shape), total.reshape(thermal_ratio.shape))


def solution(mesh):
    in_specs = (
        P(None, None, "gy", "gx"),
        P(None, "gy", "gx"),
        P(None, None, "gy", "gx"),
        P("gy", "gx"),
        P("gy", "gx"),
        P("gy", "gx"),
        P(),
        P(),
    )
    out_specs = (P(None, "gy", "gx"), P(None, "gy", "gx"))
    return jax.shard_map(local, mesh=mesh, in_specs=in_specs, out_specs=out_specs, check_vma=False)
```

```python
import functools

import jax
import jax.numpy as jnp
import numpy as np
from jax import lax
from jax.experimental import pallas as pl
from jax.experimental.pallas import tpu as pltpu
from jax.sharding import PartitionSpec as P

NODES = 4
TIME_INCREMENT = 0.05
ROWS = 8
LOG2E = 1.4426950408889634

GROUP = 8
TERMS = 16
BLOCK = 12
PARTIAL = 5
DOWN = 24
CHUNKS = 2
QUANTITIES = 4


def shifted(value, axis, steps):
    count = lax.axis_size(axis)
    return lax.ppermute(value, axis, [(i, (i + steps) % count) for i in range(count)])


def gll_derivative():
    points = np.array([-1.0, -1.0 / np.sqrt(5.0), 1.0 / np.sqrt(5.0), 1.0])
    legendre = 0.5 * (5.0 * points**3 - 3.0 * points)
    derivative = np.zeros((4, 4))
    for source in range(4):
        for target in range(4):
            if source != target:
                derivative[source, target] = legendre[source] / (
                    legendre[target] * (points[source] - points[target])
                )
    derivative[0, 0] = -3.0
    derivative[3, 3] = 3.0
    return derivative


def high_low(values):
    high = values.astype(jnp.bfloat16)
    return high, (values - high.astype(jnp.float32)).astype(jnp.bfloat16)


def across(left, right, precision=None):
    return lax.dot_general(
        left, right, (((0,), (0,)), ((), ())), precision=precision,
        preferred_element_type=jnp.float32,
    )


def optics_matrices(molecular_ref, table_ref, optics_ref, weight_ref):
    level_count, gpoints = molecular_ref.shape[1:]
    groups = level_count // GROUP
    width = GROUP * TERMS
    level = lax.broadcasted_iota(jnp.int32, (level_count, groups * width), 0)
    lane = lax.broadcasted_iota(jnp.int32, (level_count, groups * width), 1)
    here = level == lane // TERMS
    term = lane % TERMS
    gases = []
    for k in range(3):
        high, low = high_low(molecular_ref[k])
        spread = [
            jnp.where(here & chosen, 1.0, 0.0).astype(jnp.bfloat16)
            for chosen in ((term == k) | (term == k + 10), term == k + 5)
        ]
        gases.append(across(high, spread[0]) + across(low, spread[1]))
    w = [table_ref[n : n + 1, :] for n in range(7)]
    ls, li = w[0] * w[1], w[3] * w[4]
    la, ia = w[0] * (1.0 - w[1]), w[3] * (1.0 - w[4])
    place = lax.broadcasted_iota(jnp.int32, (8, width), 0)
    term = lax.broadcasted_iota(jnp.int32, (8, width), 1) % TERMS
    pattern = jnp.zeros((8, width), jnp.float32)
    for n, chosen in enumerate((
        (term == 3) | (term == 13), term == 8, (term == 4) | (term == 14), term == 9
    )):
        pattern = jnp.where((place == n) & chosen, 1.0, pattern)
    empty = jnp.zeros((4, gpoints), jnp.float32)

    def water(*values):
        parts = []
        for value in values:
            high = value.astype(jnp.bfloat16).astype(jnp.float32)
            parts += [high, value - high]
        return across(jnp.concatenate(parts + [empty], axis=0), pattern, lax.Precision.HIGHEST)

    absorbed = gases[0] + gases[1]
    gas = absorbed + gases[2]
    pairs = (
        (absorbed, water(la, ia)),
        (gas, water(la + ls * (1.0 - w[2]), ia + li * (1.0 - w[5]))),
        (gas + gas, water(2.0 * w[0], 2.0 * w[3])),
        (gases[2], water(ls * (1.0 + w[2]), li * (1.0 + w[5]))),
    )
    chunk = gpoints // CHUNKS
    for group in range(groups):
        span = slice(group * width, (group + 1) * width)
        tables = [values[:, span] + constant for values, constant in pairs]
        for c in range(CHUNKS):
            rows = [table[c * chunk : (c + 1) * chunk] for table in tables]
            optics_ref[group, c] = jnp.concatenate(rows, axis=0).astype(jnp.bfloat16)
    only = jnp.where(place == 0, 1.0, 0.0)
    weight = jnp.broadcast_to(w[6], (8, gpoints))
    weight_ref[...] = across(weight, only, lax.Precision.HIGHEST)


def layer_terms(state_ref, temp_ref, level):
    lines = state_ref.shape[2]
    thickness = state_ref[2, level]
    temper = temp_ref[pl.ds(pl.multiple_of(level * lines, 8), lines), :]
    weighted = thickness * temper * temper
    return (
        weighted * state_ref[0, level], weighted * state_ref[1, level], thickness,
        state_ref[3, level], state_ref[4, level],
    )


def write_terms(terms_ref, level, values, lines):
    parts = [None] * TERMS
    for k, value in enumerate(values):
        high = value.astype(jnp.bfloat16).astype(jnp.float32)
        parts[k], parts[k + 5], parts[k + 10] = high, high, value - high
    parts[15] = jnp.zeros_like(values[0])
    for k, part in enumerate(parts):
        start = (level * TERMS + k) * lines
        start = pl.multiple_of(start, 8) if lines % 8 == 0 else start
        terms_ref[pl.ds(start, lines), :] = part


def sweep_row(
    row, line, lines, count, cosine, ground, optics_ref, weight_ref, terms_ref, right_ref,
    depths_0, depths_1, gain_ref, offset_ref, direct_ref, partial_ref, ratio_ref, source_ref, slant_ref,
):
    level_count, gpoints, lanes = gain_ref.shape
    blocks = level_count // BLOCK
    chunk = gpoints // CHUNKS
    slots = (depths_0, depths_1)
    once = 1 + jnp.minimum(row, 0)

    def place_group(group, carry=None):
        for j in range(GROUP):
            start = (group * GROUP + j) * TERMS * lines + line
            tile = terms_ref[pl.ds(start, TERMS, stride=lines), :].astype(jnp.bfloat16)
            half = lanes * (j % 2)
            pair = group * (GROUP // 2) + j // 2
            right_ref[pair, TERMS * j : TERMS * (j + 1), half : half + lanes] = tile
        return carry

    groups = level_count // GROUP
    ready = -(-BLOCK // GROUP)
    for group in range(groups - ready, groups):
        place_group(group)
    slant_ref[...] = jnp.broadcast_to((-0.5 * LOG2E) / cosine, (8, lanes))

    def over_rows(values):
        return jnp.broadcast_to(values[None], (gpoints // 8, 8, lanes)).reshape(gpoints, lanes)

    clear = 1.0 / (1.0 - ground)
    ratio_ref[...] = over_rows(jnp.broadcast_to((1.0 + ground) * clear, (8, lanes)))
    source_ref[...] = over_rows(jnp.broadcast_to(2.0 * ground * clear, (8, lanes)))

    def fill(block, c):
        for p in range(BLOCK // 2):
            pair = block * (BLOCK // 2) + p
            slots[c % 2][p] = jnp.dot(
                optics_ref[pair // (GROUP // 2), c], right_ref[pair],
                preferred_element_type=jnp.float32,
            )

    def below(block, c):
        span = slice(c * chunk, (c + 1) * chunk)
        ratio, source = ratio_ref[span], source_ref[span]
        slant = jnp.broadcast_to(slant_ref[...][None], (chunk // 8, 8, lanes))
        slant = slant.reshape(chunk, lanes)
        for j in reversed(range(BLOCK)):
            level = block * BLOCK + j
            part = slots[c % 2].at[j // 2, :, (j % 2) * lanes : (j % 2 + 1) * lanes]
            a, b, depth, along = [part[n * chunk : (n + 1) * chunk] for n in range(QUANTITIES)]
            away = b - a
            square = a * b
            inverse_root = lax.rsqrt(square)
            h = jnp.tanh(square * inverse_root)
            g = h * inverse_root
            g = g + g
            s, p = a * g, b * g
            h2 = h * h
            one = 1.0 + h2
            through = 1.0 - h2
            inverse = 1.0 / (one + s * ratio)
            direct = jnp.exp2(depth * slant)
            factor = (1.0 - direct) * (1.0 / depth)
            up, down = factor * away, factor * along
            push = inverse * (direct * source + (ratio - 1.0) * down)
            ratio = (one * ratio + p) * inverse
            gain = through * inverse
            source = through * push + (ratio + 1.0) * up
            gain_ref[level, span] = gain
            offset_ref[level, span] = (gain * up + down) - s * push
            direct_ref[level, span] = direct
        ratio_ref[span] = ratio
        source_ref[span] = source

    def below_block(step, carry):
        block = blocks - 1 - step
        for c in range(CHUNKS):
            def turn(n, carry, c=c):
                below(block, c)
                if c + 1 < CHUNKS:
                    fill(block, c + 1)
                else:
                    fill(jnp.maximum(block - 1, 0), 0)
                return carry

            lax.fori_loop(0, once, turn, 0)
        return carry

    fill(blocks - 1, 0)
    for group in range(groups - ready):
        place_group(group)
    lax.fori_loop(0, blocks, below_block, 0)

    def folded(net):
        return sum(net[8 * k : 8 * (k + 1)] for k in range(gpoints // 8))

    def top(step, carry):
        beam = weight_ref[...] * cosine
        net = -(source_ref[...] * beam) / (1.0 + ratio_ref[...])
        partial_ref[pl.ds(pl.multiple_of(row * 8, 8), 8), :] = folded(beam) + folded(net)
        return net, beam

    nothing = jnp.zeros((gpoints, lanes), jnp.float32)
    carry = lax.fori_loop(0, once, top, (nothing, nothing))

    def down_group(group, carry):
        net, beam = carry
        for j in range(DOWN):
            level = group * DOWN + j
            net = gain_ref[level] * net + offset_ref[level] * beam
            beam = beam * direct_ref[level]
            start = pl.multiple_of(((level + 1) * count + row) * 8, 8)
            partial_ref[pl.ds(start, 8), :] = folded(net) + folded(beam)
        return (net, beam)

    lax.fori_loop(0, level_count // DOWN, down_group, carry)


def level_heating(partial_ref, level_count, gpoints, count, write):
    def flux(level):
        start = level * count * 8
        return sum(partial_ref[pl.ds(start + k, count, stride=8), :] for k in range(8))

    def step(level, upper):
        lower = flux(level + 1)
        write(level, (level_count / gpoints) * (upper - lower))
        return lower

    lax.fori_loop(0, level_count, step, flux(0), unroll=4)


def radiation_kernel(
    state_ref, temp_ref, flow_ref, cosine_ref, ground_ref, day_ref, molecular_ref, table_ref,
    edge_ref, high_ref, low_ref,
    heat_ref, change_ref, wind_ref, first_ref, last_ref,
    optics_ref, weight_ref, strip_ref, slope_ref, terms_ref, right_ref, *scratch,
):
    level_count, lines, lanes = state_ref.shape[1:]
    gpoints = weight_ref.shape[0]
    row, count = pl.program_id(0), pl.num_programs(0)

    @pl.when(row == 0)
    def prepare():
        optics_matrices(molecular_ref, table_ref, optics_ref, weight_ref)
        prepare_terms(state_ref, temp_ref, terms_ref, right_ref)

    sweep_row(
        row, row, lines, count, cosine_ref[pl.ds(row, 1), :], ground_ref[pl.ds(row, 1), :],
        optics_ref, weight_ref, terms_ref, right_ref, *scratch,
    )

    @pl.when(row == count - 1)
    def finish():
        day = day_ref[...] == 1

        def write(level, value):
            start = pl.multiple_of(level * lines, 8)
            heat_ref[pl.ds(start, lines), :] = jnp.where(day, value, 0.0)

        level_heating(scratch[PARTIAL], level_count, gpoints, lines, write)
        spans = [slice(r * level_count, (r + 1) * level_count) for r in range(lines)]
        for r, span in enumerate(spans):
            native = pl.ds(r, level_count, stride=lines)
            change_ref[span, :] = temp_ref[native, :]
            for n in range(2):
                wind_ref[n, span, :] = flow_ref[n, native, :]
        slope_ref[...] = split_dot(
            change_ref[...], high_ref[:lanes, :lanes], low_ref[:lanes, :lanes]
        )
        changes = change_rows(change_ref, slope_ref, wind_ref, slice(0, lanes), spans)
        for r, (span, change) in enumerate(zip(spans, changes)):
            own = heat_ref[pl.ds(r, level_count, stride=lines), :]
            change_ref[span, :] = change + TIME_INCREMENT * own
        for n, ref in enumerate((change_ref, wind_ref.at[0], wind_ref.at[1])):
            for r in range(lines):
                here = slice(8 * (lines * n + r), 8 * (lines * n + r + 1))
                for k in range(level_count // 8):
                    start = r * level_count + 8 * k
                    strip_ref[here, lanes * k : lanes * (k + 1)] = ref[start : start + 8, :]
        packed = split_dot(strip_ref[...], edge_ref[...])
        first_ref[...] = packed[:, :lanes]
        last_ref[...] = packed[:, lanes:]


def prepare_terms(state_ref, temp_ref, terms_ref, right_ref):
    level_count, lines = state_ref.shape[1:3]
    right_ref[...] = jnp.zeros_like(right_ref)

    def level(l, carry):
        write_terms(terms_ref, l, layer_terms(state_ref, temp_ref, l), lines)
        return carry

    lax.fori_loop(0, level_count, level, 0, unroll=4)


def radiation(state, temper, flow, cosine, ground, day, molecular, condensate):
    level_count, rows, lanes = state.shape[1:]
    gpoints = molecular.shape[1]
    full = pltpu.VMEM((level_count, gpoints, lanes), jnp.float32)
    plane = pltpu.VMEM((gpoints, lanes), jnp.float32)
    whole = pl.BlockSpec(memory_space=pltpu.VMEM)
    part = (QUANTITIES * gpoints // CHUNKS, GROUP * TERMS)
    depths = pltpu.VMEM((BLOCK // 2, part[0], 2 * lanes), jnp.float32)
    field = jax.ShapeDtypeStruct((level_count * rows, lanes), jnp.float32)
    wind = jax.ShapeDtypeStruct((2, level_count * rows, lanes), jnp.float32)
    edge = jax.ShapeDtypeStruct((3 * 8 * rows, lanes), jnp.float32)
    cells = level_count * gpoints * rows * lanes
    return pl.pallas_call(
        radiation_kernel,
        out_shape=(field, field, wind, edge, edge),
        grid=(rows,), in_specs=[whole] * 11, out_specs=(whole,) * 5,
        scratch_shapes=[
            pltpu.VMEM((level_count // GROUP, CHUNKS) + part, jnp.bfloat16),
            plane,
            pltpu.VMEM((3 * 8 * rows, level_count // 8 * lanes), jnp.float32),
            pltpu.VMEM((level_count * rows, lanes), jnp.float32),
            pltpu.VMEM((level_count * TERMS * rows, lanes), jnp.float32),
            pltpu.VMEM((level_count // 2, GROUP * TERMS, 2 * lanes), jnp.bfloat16),
            depths, depths, full, full, full,
            pltpu.VMEM(((level_count + 1) * rows * 8, lanes), jnp.float32),
            plane, plane,
            pltpu.VMEM((8, lanes), jnp.float32),
        ],
        compiler_params=pltpu.CompilerParams(vmem_limit_bytes=60 * 1024 * 1024),
        cost_estimate=pl.CostEstimate(
            flops=10000 * cells, bytes_accessed=4 * 9 * temper.size, transcendentals=5 * cells
        ),
        name="radiation",
    )(
        state, temper, flow, cosine, ground, day, molecular.transpose(0, 2, 1), condensate,
        edge_matrix(level_count, lanes), *slope_matrices(lanes),
    )


def edge_matrix(level_count, lanes):
    parts = level_count // 8
    width = lanes // parts
    matrix = np.zeros((parts * lanes, 2 * lanes), np.float32)
    for k in range(parts):
        for c in range(width):
            matrix[lanes * k + c, width * k + c] = 1.0
            matrix[lanes * (k + 1) - width + c, lanes + width * k + c] = 1.0
    return jnp.asarray(matrix, jnp.bfloat16)


def slope_matrices(lanes):
    whole = np.kron(np.eye(2 * lanes // NODES), gll_derivative().T).astype(np.float32)
    high = np.asarray(whole, jnp.bfloat16)
    low = np.asarray(whole - high.astype(np.float32), jnp.bfloat16)
    return jnp.asarray(high), jnp.asarray(low)


def average_matrix(lanes):
    size = 2 * lanes
    matrix = np.eye(size, dtype=np.float32)
    for c in range(NODES - 1, size, NODES):
        after = (c + 1) % size
        matrix[c, c] = matrix[after, after] = matrix[c, after] = matrix[after, c] = 0.5
    return jnp.asarray(matrix, jnp.bfloat16)


def split_dot(values, *matrices):
    high, low = high_low(values)
    total = jnp.dot(high, matrices[0], preferred_element_type=jnp.float32)
    total = total + jnp.dot(low, matrices[0], preferred_element_type=jnp.float32)
    if len(matrices) > 1:
        total = total + jnp.dot(high, matrices[1], preferred_element_type=jnp.float32)
    return total


def slope_y(rows_of):
    derivative = gll_derivative()
    result = []
    for r in range(len(rows_of)):
        first = r // NODES * NODES
        total = None
        for n in range(NODES):
            weight = derivative[r - first, n]
            if abs(weight) > 1e-12:
                term = np.float32(weight) * rows_of[first + n]
                total = term if total is None else total + term
        result.append(total)
    return result


def average_y(rows_of, far, near):
    below = jnp.where(even_row(), far, near)
    above = jnp.where(even_row(), near, far)
    result = list(rows_of)
    count = len(rows_of)
    for r in range(NODES - 1, count - 1, NODES):
        result[r] = result[r + 1] = 0.5 * (rows_of[r] + rows_of[r + 1])
    result[0] = 0.5 * (below + rows_of[0])
    result[count - 1] = 0.5 * (rows_of[count - 1] + above)
    return result


def first_stage_kernel(
    change_ref, before_ref, after_ref, edge_ref, average_ref,
    out_ref, far_ref, near_ref, wind_side_ref, wide_ref,
):
    level_count = far_ref.shape[0]
    lanes = change_ref.shape[1]
    both = jnp.concatenate([after_ref[...], before_ref[...]], axis=1)
    sides = split_dot(both, edge_ref[...])
    wide_ref[:, :lanes] = change_ref[...]
    for r in range(ROWS):
        for k in range(level_count // 8):
            span = slice(r * level_count + 8 * k, r * level_count + 8 * (k + 1))
            part = slice(lanes * k, lanes * (k + 1))
            wide_ref[span, lanes:] = sides[8 * r : 8 * (r + 1), part]
            for n in range(2):
                here = 8 * (ROWS * (n + 1) + r)
                wind_side_ref[n, span, :] = sides[here : here + 8, part]
    write_averaged(wide_ref[...], average_ref, out_ref, far_ref, near_ref)


def change_rows(field_ref, slope_ref, wind_ref, part, spans):
    slopes = slope_y([field_ref[span, part] for span in spans])
    result = []
    for span, slope in zip(spans, slopes):
        change = wind_ref[0, span, :] * slope_ref[span, part] + wind_ref[1, span, :] * slope
        result.append(-TIME_INCREMENT * change)
    return result


def even_row():
    return lax.axis_index("gy") % 2 == 0


def write_averaged(change, average_ref, out_ref, far_ref, near_ref):
    level_count, width = far_ref.shape
    out_ref[...] = split_dot(change, average_ref[...])
    first = out_ref[:level_count, :width]
    last = out_ref[out_ref.shape[0] - level_count :, :width]
    far_ref[...] = jnp.where(even_row(), first, last)
    near_ref[...] = jnp.where(even_row(), last, first)


def next_stage_kernel(
    share, native, field_ref, far_ref, near_ref, wind_ref, wind_side_ref, sum_ref, high_ref,
    low_ref, average_ref, out_ref, far_out_ref, near_out_ref, total_ref, wave_ref, slope_ref, change_ref,
):
    level_count = far_ref.shape[0]
    lanes = sum_ref.shape[1]
    spans = [slice(r * level_count, (r + 1) * level_count) for r in range(ROWS)]
    for half in range(2):
        part = slice(half * lanes, (half + 1) * lanes)
        wave = average_y(
            [field_ref[span, part] for span in spans], far_ref[:, part], near_ref[:, part]
        )
        for r, (span, row) in enumerate(zip(spans, wave)):
            wave_ref[span, part] = row
            if half == 0:
                before = sum_ref[pl.ds(r, level_count, stride=ROWS), :] if native else sum_ref[span]
                total_ref[span] = before + share * row
    slope_ref[...] = split_dot(wave_ref[...], high_ref[...], low_ref[...])
    for half, wind in enumerate((wind_ref, wind_side_ref)):
        part = slice(half * lanes, (half + 1) * lanes)
        for span, change in zip(spans, change_rows(wave_ref, slope_ref, wind, part, spans)):
            change_ref[span, part] = change
    write_averaged(change_ref[...], average_ref, out_ref, far_out_ref, near_out_ref)


def last_kernel(share, field_ref, far_ref, near_ref, sum_ref, total_ref):
    level_count, lanes = far_ref.shape
    spans = [slice(r * level_count, (r + 1) * level_count) for r in range(ROWS)]
    wave = average_y([field_ref[span, :lanes] for span in spans], far_ref[...], near_ref[...])
    for r, (span, row) in enumerate(zip(spans, wave)):
        total_ref[pl.ds(r, level_count, stride=ROWS), :] = sum_ref[span] + share * row


def swapped(far, near):
    count = lax.axis_size("gy")
    far_pairs = [(i, (i - 1 if i % 2 == 0 else i + 1) % count) for i in range(count)]
    near_pairs = [(i, i + 1 if i % 2 == 0 else i - 1) for i in range(count)]
    return lax.ppermute(far, "gy", far_pairs), lax.ppermute(near, "gy", near_pairs)


def local(
    atmospheric_constituents,
    thermal_ratio,
    flow_velocity,
    solar_elevation_factor,
    ground_reflectivity,
    sunlit_indicator,
    molecular_optics_lookup,
    condensate_optics_lookup,
):
    level_count, rows, lanes = thermal_ratio.shape
    size = level_count * rows
    temper = thermal_ratio.reshape(size, lanes)
    flow = flow_velocity.reshape(2, size, lanes)
    field = jax.ShapeDtypeStruct((size, lanes), jnp.float32)
    wide = jax.ShapeDtypeStruct((size, 2 * lanes), jnp.float32)
    line = jax.ShapeDtypeStruct((level_count, 2 * lanes), jnp.float32)
    short = jax.ShapeDtypeStruct((level_count, lanes), jnp.float32)
    wide_scratch = pltpu.VMEM(wide.shape, jnp.float32)
    whole = pl.BlockSpec(memory_space=pltpu.VMEM)

    def call(kernel, name, outs, scratch, *values):
        return pl.pallas_call(
            kernel, out_shape=outs,
            in_specs=[whole] * len(values),
            out_specs=jax.tree.map(lambda _: whole, outs), scratch_shapes=[wide_scratch] * scratch,
            compiler_params=pltpu.CompilerParams(vmem_limit_bytes=40 * 1024 * 1024), name=name,
        )(*values)

    slopes = slope_matrices(lanes)
    average = average_matrix(lanes)
    heat, change, wind, first, last = radiation(
        atmospheric_constituents, temper, flow, solar_elevation_factor,
        ground_reflectivity, sunlit_indicator, molecular_optics_lookup, condensate_optics_lookup,
    )
    before, after = shifted(last, "gx", 1), shifted(first, "gx", -1)
    back = edge_matrix(level_count, lanes).T
    wave, far, near, wind_side = call(
        first_stage_kernel, "first_stage",
        (wide, line, line, jax.ShapeDtypeStruct((2, size, lanes), jnp.float32)), 1,
        change, before, after, back, average,
    )
    far, near = swapped(far, near)
    wave, far, near, total = call(
        functools.partial(next_stage_kernel, 1.0, True), "second_stage",
        (wide, line, line, field), 3, wave, far, near, wind, wind_side, temper, *slopes, average,
    )
    far, near = swapped(far, near)
    wave, far, near, total = call(
        functools.partial(next_stage_kernel, 0.5, False), "third_stage",
        (wide, short, short, field), 3, wave, far, near, wind, wind_side, total, *slopes, average,
    )
    far, near = swapped(far, near)
    total = call(
        functools.partial(last_kernel, 1.0 / 6.0), "last_stage", field, 0,
        wave, far, near, total,
    )
    return (heat.reshape(thermal_ratio.shape), total.reshape(thermal_ratio.shape))


def solution(mesh):
    in_specs = (
        P(None, None, "gy", "gx"),
        P(None, "gy", "gx"),
        P(None, None, "gy", "gx"),
        P("gy", "gx"),
        P("gy", "gx"),
        P("gy", "gx"),
        P(),
        P(),
    )
    out_specs = (P(None, "gy", "gx"), P(None, "gy", "gx"))
    return jax.shard_map(local, mesh=mesh, in_specs=in_specs, out_specs=out_specs, check_vma=False)
```

```python
import functools

import jax
import jax.numpy as jnp
import numpy as np
from jax import lax
from jax.experimental import pallas as pl
from jax.experimental.pallas import tpu as pltpu
from jax.sharding import PartitionSpec as P

NODES = 4
TIME_INCREMENT = 0.05
ROWS = 8
MARGIN = 8
LOG2E = 1.4426950408889634

GROUP = 8
TERMS = 16
BLOCK = 12
PARTIAL = 5
DOWN = 24
CHUNKS = 2
QUANTITIES = 4


def shifted(value, axis, steps):
    count = lax.axis_size(axis)
    return lax.ppermute(value, axis, [(i, (i + steps) % count) for i in range(count)])


def gll_derivative():
    points = np.array([-1.0, -1.0 / np.sqrt(5.0), 1.0 / np.sqrt(5.0), 1.0])
    legendre = 0.5 * (5.0 * points**3 - 3.0 * points)
    derivative = np.zeros((4, 4))
    for source in range(4):
        for target in range(4):
            if source != target:
                derivative[source, target] = legendre[source] / (
                    legendre[target] * (points[source] - points[target])
                )
    derivative[0, 0] = -3.0
    derivative[3, 3] = 3.0
    return derivative


def high_low(values):
    high = values.astype(jnp.bfloat16)
    return high, (values - high.astype(jnp.float32)).astype(jnp.bfloat16)


def across(left, right, precision=None):
    return lax.dot_general(
        left, right, (((0,), (0,)), ((), ())), precision=precision,
        preferred_element_type=jnp.float32,
    )


def optics_matrices(molecular_ref, table_ref, optics_ref, weight_ref):
    level_count, gpoints = molecular_ref.shape[1:]
    groups = level_count // GROUP
    width = GROUP * TERMS
    level = lax.broadcasted_iota(jnp.int32, (level_count, groups * width), 0)
    lane = lax.broadcasted_iota(jnp.int32, (level_count, groups * width), 1)
    here = level == lane // TERMS
    term = lane % TERMS
    gases = []
    for k in range(3):
        high, low = high_low(molecular_ref[k])
        spread = [
            jnp.where(here & chosen, 1.0, 0.0).astype(jnp.bfloat16)
            for chosen in ((term == k) | (term == k + 10), term == k + 5)
        ]
        gases.append(across(high, spread[0]) + across(low, spread[1]))
    w = [table_ref[n : n + 1, :] for n in range(7)]
    ls, li = w[0] * w[1], w[3] * w[4]
    la, ia = w[0] * (1.0 - w[1]), w[3] * (1.0 - w[4])
    place = lax.broadcasted_iota(jnp.int32, (8, width), 0)
    term = lax.broadcasted_iota(jnp.int32, (8, width), 1) % TERMS
    pattern = jnp.zeros((8, width), jnp.float32)
    for n, chosen in enumerate((
        (term == 3) | (term == 13), term == 8, (term == 4) | (term == 14), term == 9
    )):
        pattern = jnp.where((place == n) & chosen, 1.0, pattern)
    empty = jnp.zeros((4, gpoints), jnp.float32)

    def water(*values):
        parts = []
        for value in values:
            high = value.astype(jnp.bfloat16).astype(jnp.float32)
            parts += [high, value - high]
        return across(jnp.concatenate(parts + [empty], axis=0), pattern, lax.Precision.HIGHEST)

    absorbed = gases[0] + gases[1]
    gas = absorbed + gases[2]
    pairs = (
        (absorbed, water(la, ia)),
        (gas, water(la + ls * (1.0 - w[2]), ia + li * (1.0 - w[5]))),
        (gas + gas, water(2.0 * w[0], 2.0 * w[3])),
        (gases[2], water(ls * (1.0 + w[2]), li * (1.0 + w[5]))),
    )
    chunk = gpoints // CHUNKS
    for group in range(groups):
        span = slice(group * width, (group + 1) * width)
        tables = [values[:, span] + constant for values, constant in pairs]
        for c in range(CHUNKS):
            rows = [table[c * chunk : (c + 1) * chunk] for table in tables]
            optics_ref[group, c] = jnp.concatenate(rows, axis=0).astype(jnp.bfloat16)
    only = jnp.where(place == 0, 1.0, 0.0)
    weight = jnp.broadcast_to(w[6], (8, gpoints))
    weight_ref[...] = across(weight, only, lax.Precision.HIGHEST)


def layer_terms(state_ref, temp_ref, level):
    lines = state_ref.shape[2]
    thickness = state_ref[2, level]
    temper = temp_ref[pl.ds(pl.multiple_of(level * lines, 8), lines), :]
    weighted = thickness * temper * temper
    return (
        weighted * state_ref[0, level], weighted * state_ref[1, level], thickness,
        state_ref[3, level], state_ref[4, level],
    )


def write_terms(terms_ref, level, values, lines):
    parts = [None] * TERMS
    for k, value in enumerate(values):
        high = value.astype(jnp.bfloat16).astype(jnp.float32)
        parts[k], parts[k + 5], parts[k + 10] = high, high, value - high
    parts[15] = jnp.zeros_like(values[0])
    for k, part in enumerate(parts):
        start = (level * TERMS + k) * lines
        start = pl.multiple_of(start, 8) if lines % 8 == 0 else start
        terms_ref[pl.ds(start, lines), :] = part


def sweep_row(
    row, line, lines, count, cosine, ground, optics_ref, weight_ref, terms_ref, right_ref,
    depths_0, depths_1, gain_ref, offset_ref, direct_ref, partial_ref, ratio_ref, source_ref, slant_ref,
):
    level_count, gpoints, lanes = gain_ref.shape
    blocks = level_count // BLOCK
    chunk = gpoints // CHUNKS
    slots = (depths_0, depths_1)
    once = 1 + jnp.minimum(row, 0)

    def place_group(group, carry=None):
        for j in range(GROUP):
            start = (group * GROUP + j) * TERMS * lines + line
            tile = terms_ref[pl.ds(start, TERMS, stride=lines), :].astype(jnp.bfloat16)
            half = lanes * (j % 2)
            pair = group * (GROUP // 2) + j // 2
            right_ref[pair, TERMS * j : TERMS * (j + 1), half : half + lanes] = tile
        return carry

    groups = level_count // GROUP
    ready = -(-BLOCK // GROUP)
    for group in range(groups - ready, groups):
        place_group(group)
    slant_ref[...] = jnp.broadcast_to((-0.5 * LOG2E) / cosine, (8, lanes))

    def over_rows(values):
        return jnp.broadcast_to(values[None], (gpoints // 8, 8, lanes)).reshape(gpoints, lanes)

    clear = 1.0 / (1.0 - ground)
    ratio_ref[...] = over_rows(jnp.broadcast_to((1.0 + ground) * clear, (8, lanes)))
    source_ref[...] = over_rows(jnp.broadcast_to(2.0 * ground * clear, (8, lanes)))

    def fill(block, c):
        for p in range(BLOCK // 2):
            pair = block * (BLOCK // 2) + p
            slots[c % 2][p] = jnp.dot(
                optics_ref[pair // (GROUP // 2), c], right_ref[pair],
                preferred_element_type=jnp.float32,
            )

    def below(block, c):
        span = slice(c * chunk, (c + 1) * chunk)
        ratio, source = ratio_ref[span], source_ref[span]
        slant = jnp.broadcast_to(slant_ref[...][None], (chunk // 8, 8, lanes))
        slant = slant.reshape(chunk, lanes)
        for j in reversed(range(BLOCK)):
            level = block * BLOCK + j
            part = slots[c % 2].at[j // 2, :, (j % 2) * lanes : (j % 2 + 1) * lanes]
            a, b, depth, along = [part[n * chunk : (n + 1) * chunk] for n in range(QUANTITIES)]
            away = b - a
            square = a * b
            inverse_root = lax.rsqrt(square)
            h = jnp.tanh(square * inverse_root)
            g = h * inverse_root
            g = g + g
            s, p = a * g, b * g
            h2 = h * h
            one = 1.0 + h2
            through = 1.0 - h2
            inverse = 1.0 / (one + s * ratio)
            direct = jnp.exp2(depth * slant)
            factor = (1.0 - direct) * (1.0 / depth)
            up, down = factor * away, factor * along
            push = inverse * (direct * source + (ratio - 1.0) * down)
            ratio = (one * ratio + p) * inverse
            gain = through * inverse
            source = through * push + (ratio + 1.0) * up
            gain_ref[level, span] = gain
            offset_ref[level, span] = (gain * up + down) - s * push
            direct_ref[level, span] = direct
        ratio_ref[span] = ratio
        source_ref[span] = source

    def below_block(step, carry):
        block = blocks - 1 - step
        for c in range(CHUNKS):
            def turn(n, carry, c=c):
                below(block, c)
                if c + 1 < CHUNKS:
                    fill(block, c + 1)
                else:
                    fill(jnp.maximum(block - 1, 0), 0)
                return carry

            lax.fori_loop(0, once, turn, 0)
        return carry

    fill(blocks - 1, 0)
    for group in range(groups - ready):
        place_group(group)
    lax.fori_loop(0, blocks, below_block, 0)

    def folded(net):
        return sum(net[8 * k : 8 * (k + 1)] for k in range(gpoints // 8))

    def top(step, carry):
        beam = weight_ref[...] * cosine
        net = -(source_ref[...] * beam) / (1.0 + ratio_ref[...])
        partial_ref[pl.ds(pl.multiple_of(row * 8, 8), 8), :] = folded(beam) + folded(net)
        return net, beam

    nothing = jnp.zeros((gpoints, lanes), jnp.float32)
    carry = lax.fori_loop(0, once, top, (nothing, nothing))

    def down_group(group, carry):
        net, beam = carry
        for j in range(DOWN):
            level = group * DOWN + j
            net = gain_ref[level] * net + offset_ref[level] * beam
            beam = beam * direct_ref[level]
            start = pl.multiple_of(((level + 1) * count + row) * 8, 8)
            partial_ref[pl.ds(start, 8), :] = folded(net) + folded(beam)
        return (net, beam)

    lax.fori_loop(0, level_count // DOWN, down_group, carry)


def level_heating(partial_ref, level_count, gpoints, count, write):
    def flux(level):
        start = level * count * 8
        return sum(partial_ref[pl.ds(start + k, count, stride=8), :] for k in range(8))

    def step(level, upper):
        lower = flux(level + 1)
        write(level, (level_count / gpoints) * (upper - lower))
        return lower

    lax.fori_loop(0, level_count, step, flux(0), unroll=4)


def radiation_kernel(
    state_ref, temp_ref, flow_ref, cosine_ref, ground_ref, day_ref, molecular_ref, table_ref,
    edge_ref, high_ref, low_ref,
    heat_ref, change_ref, wind_ref, first_ref, last_ref,
    optics_ref, weight_ref, strip_ref, slope_ref, terms_ref, right_ref, *scratch,
):
    level_count, lines, lanes = state_ref.shape[1:]
    gpoints = weight_ref.shape[0]
    row, count = pl.program_id(0), pl.num_programs(0)

    @pl.when(row == 0)
    def prepare():
        optics_matrices(molecular_ref, table_ref, optics_ref, weight_ref)
        prepare_terms(state_ref, temp_ref, terms_ref, right_ref)

    sweep_row(
        row, row, lines, count, cosine_ref[pl.ds(row, 1), :], ground_ref[pl.ds(row, 1), :],
        optics_ref, weight_ref, terms_ref, right_ref, *scratch,
    )

    @pl.when(row == count - 1)
    def finish():
        day = day_ref[...] == 1

        def write(level, value):
            start = pl.multiple_of(level * lines, 8)
            heat_ref[pl.ds(start, lines), :] = jnp.where(day, value, 0.0)

        level_heating(scratch[PARTIAL], level_count, gpoints, lines, write)
        spans = [slice(r * level_count, (r + 1) * level_count) for r in range(lines)]
        for r, span in enumerate(spans):
            native = pl.ds(r, level_count, stride=lines)
            change_ref[span, :] = temp_ref[native, :]
            for n in range(2):
                wind_ref[n, span, :] = flow_ref[n, native, :]
        slope_ref[...] = split_dot(
            change_ref[...], high_ref[:lanes, :lanes], low_ref[:lanes, :lanes]
        )
        changes = change_rows(change_ref, slope_ref, wind_ref, slice(0, lanes), spans)
        for r, (span, change) in enumerate(zip(spans, changes)):
            own = heat_ref[pl.ds(r, level_count, stride=lines), :]
            change_ref[span, :] = change + TIME_INCREMENT * own
        for n, ref in enumerate((change_ref, wind_ref.at[0], wind_ref.at[1])):
            for r in range(lines):
                here = slice(8 * (lines * n + r), 8 * (lines * n + r + 1))
                for k in range(level_count // 8):
                    start = r * level_count + 8 * k
                    strip_ref[here, lanes * k : lanes * (k + 1)] = ref[start : start + 8, :]
        packed = split_dot(strip_ref[...], edge_ref[...])
        first_ref[...] = packed[:, :lanes]
        last_ref[...] = packed[:, lanes:]


def prepare_terms(state_ref, temp_ref, terms_ref, right_ref):
    level_count, lines = state_ref.shape[1:3]
    right_ref[...] = jnp.zeros_like(right_ref)

    def level(l, carry):
        write_terms(terms_ref, l, layer_terms(state_ref, temp_ref, l), lines)
        return carry

    lax.fori_loop(0, level_count, level, 0, unroll=4)


def radiation(state, temper, flow, cosine, ground, day, molecular, condensate):
    level_count, rows, lanes = state.shape[1:]
    gpoints = molecular.shape[1]
    full = pltpu.VMEM((level_count, gpoints, lanes), jnp.float32)
    plane = pltpu.VMEM((gpoints, lanes), jnp.float32)
    whole = pl.BlockSpec(memory_space=pltpu.VMEM)
    part = (QUANTITIES * gpoints // CHUNKS, GROUP * TERMS)
    depths = pltpu.VMEM((BLOCK // 2, part[0], 2 * lanes), jnp.float32)
    field = jax.ShapeDtypeStruct((level_count * rows, lanes), jnp.float32)
    wind = jax.ShapeDtypeStruct((2, level_count * rows, lanes), jnp.float32)
    edge = jax.ShapeDtypeStruct((3 * 8 * rows, lanes), jnp.float32)
    cells = level_count * gpoints * rows * lanes
    return pl.pallas_call(
        radiation_kernel,
        out_shape=(field, field, wind, edge, edge),
        grid=(rows,), in_specs=[whole] * 11, out_specs=(whole,) * 5,
        scratch_shapes=[
            pltpu.VMEM((level_count // GROUP, CHUNKS) + part, jnp.bfloat16),
            plane,
            pltpu.VMEM((3 * 8 * rows, level_count // 8 * lanes), jnp.float32),
            pltpu.VMEM((level_count * rows, lanes), jnp.float32),
            pltpu.VMEM((level_count * TERMS * rows, lanes), jnp.float32),
            pltpu.VMEM((level_count // 2, GROUP * TERMS, 2 * lanes), jnp.bfloat16),
            depths, depths, full, full, full,
            pltpu.VMEM(((level_count + 1) * rows * 8, lanes), jnp.float32),
            plane, plane,
            pltpu.VMEM((8, lanes), jnp.float32),
        ],
        compiler_params=pltpu.CompilerParams(vmem_limit_bytes=60 * 1024 * 1024),
        cost_estimate=pl.CostEstimate(
            flops=10000 * cells, bytes_accessed=4 * 9 * temper.size, transcendentals=5 * cells
        ),
        name="radiation",
    )(
        state, temper, flow, cosine, ground, day, molecular.transpose(0, 2, 1), condensate,
        edge_matrix(level_count, lanes), *slope_matrices(lanes),
    )


def edge_matrix(level_count, lanes):
    parts = level_count // 8
    width = lanes // parts
    matrix = np.zeros((parts * lanes, 2 * lanes), np.float32)
    for k in range(parts):
        for c in range(width):
            matrix[lanes * k + c, width * k + c] = 1.0
            matrix[lanes * (k + 1) - width + c, lanes + width * k + c] = 1.0
    return jnp.asarray(matrix, jnp.bfloat16)


def slope_matrices(lanes):
    whole = np.kron(np.eye(2 * lanes // NODES), gll_derivative().T).astype(np.float32)
    high = np.asarray(whole, jnp.bfloat16)
    low = np.asarray(whole - high.astype(np.float32), jnp.bfloat16)
    return jnp.asarray(high), jnp.asarray(low)


def average_matrix(lanes):
    size = 2 * lanes
    matrix = np.eye(size, dtype=np.float32)
    for c in range(NODES - 1, size, NODES):
        after = (c + 1) % size
        matrix[c, c] = matrix[after, after] = matrix[c, after] = matrix[after, c] = 0.5
    return jnp.asarray(matrix, jnp.bfloat16)


def split_dot(values, *matrices):
    high, low = high_low(values)
    total = jnp.dot(high, matrices[0], preferred_element_type=jnp.float32)
    total = total + jnp.dot(low, matrices[0], preferred_element_type=jnp.float32)
    if len(matrices) > 1:
        total = total + jnp.dot(high, matrices[1], preferred_element_type=jnp.float32)
    return total


def slope_y(rows_of):
    derivative = gll_derivative()
    result = []
    for r in range(len(rows_of)):
        first = r // NODES * NODES
        total = None
        for n in range(NODES):
            weight = derivative[r - first, n]
            if abs(weight) > 1e-12:
                term = np.float32(weight) * rows_of[first + n]
                total = term if total is None else total + term
        result.append(total)
    return result


def average_y(rows_of, far, near):
    below = jnp.where(even_row(), far, near)
    above = jnp.where(even_row(), near, far)
    result = list(rows_of)
    count = len(rows_of)
    for r in range(NODES - 1, count - 1, NODES):
        result[r] = result[r + 1] = 0.5 * (rows_of[r] + rows_of[r + 1])
    result[0] = 0.5 * (below + rows_of[0])
    result[count - 1] = 0.5 * (rows_of[count - 1] + above)
    return result


def first_stage_kernel(
    change_ref, before_ref, after_ref, edge_ref, average_ref,
    out_ref, far_ref, near_ref, wind_side_ref, wide_ref,
):
    lanes = change_ref.shape[1]
    level_count = change_ref.shape[0] // ROWS
    wide_ref[:, :lanes] = change_ref[...]
    both = jnp.concatenate([after_ref[...], before_ref[...]], axis=1)
    sides = split_dot(both, edge_ref[...])
    for r in range(ROWS):
        for k in range(level_count // 8):
            span = slice(r * level_count + 8 * k, r * level_count + 8 * (k + 1))
            part = slice(lanes * k, lanes * (k + 1))
            wide_ref[span, lanes:] = sides[8 * r : 8 * (r + 1), part]
            for n in range(2):
                here = 8 * (ROWS * (n + 1) + r)
                wind_side_ref[n, span, :] = sides[here : here + 8, part]
    write_averaged(wide_ref[...], average_ref, out_ref, far_ref, near_ref, level_count, True)


def change_rows(field_ref, slope_ref, wind_ref, part, spans):
    slopes = slope_y([field_ref[span, part] for span in spans])
    result = []
    for span, slope in zip(spans, slopes):
        change = wind_ref[0, span, :] * slope_ref[span, part] + wind_ref[1, span, :] * slope
        result.append(-TIME_INCREMENT * change)
    return result


def even_row():
    return lax.axis_index("gy") % 2 == 0


def packed_side(side):
    lanes = side.shape[1]
    lane = lax.broadcasted_iota(jnp.int32, (8, lanes), 1)
    fit = lanes // (2 * MARGIN)
    tiles = []
    for k in range(side.shape[0] // 8):
        turned = pltpu.roll(side[8 * k : 8 * (k + 1)], (MARGIN + 2 * MARGIN * (k % fit)) % lanes, 1)
        if k % fit == 0:
            tiles.append(turned)
        else:
            tiles[-1] = jnp.where(lane // (2 * MARGIN) == k % fit, turned, tiles[-1])
    return tiles


def unpacked_side(tiles, level_count):
    lanes = tiles.shape[1]
    fit = lanes // (2 * MARGIN)
    result = []
    for k in range(level_count // 8):
        tile = tiles[8 * (k // fit) : 8 * (k // fit + 1)]
        result.append(pltpu.roll(tile, (lanes - MARGIN - 2 * MARGIN * (k % fit)) % lanes, 1))
    return jnp.concatenate(result, axis=0)


def write_averaged(change, average_ref, out_ref, far_ref, near_ref, level_count, with_side):
    lanes = far_ref.shape[1]
    out_ref[...] = split_dot(change, average_ref[...])
    parts = [slice(0, lanes), slice(lanes, 2 * lanes)] if with_side else [slice(0, lanes)]
    for n, part in enumerate(parts):
        first = out_ref[:level_count, part]
        last = out_ref[out_ref.shape[0] - level_count :, part]
        far = jnp.where(even_row(), first, last)
        near = jnp.where(even_row(), last, first)
        for ref, line in ((far_ref, far), (near_ref, near)):
            if n == 0:
                ref[:level_count, :] = line
                continue
            for k, tile in enumerate(packed_side(line)):
                ref[level_count + 8 * k : level_count + 8 * (k + 1), :] = tile


def next_stage_kernel(
    share, native, field_ref, far_ref, near_ref, wind_ref, wind_side_ref, sum_ref, high_ref,
    low_ref, average_ref, out_ref, far_out_ref, near_out_ref, total_ref, wave_ref, slope_ref, change_ref,
):
    level_count = field_ref.shape[0] // ROWS
    lanes = sum_ref.shape[1]
    spans = [slice(r * level_count, (r + 1) * level_count) for r in range(ROWS)]
    for half in range(2):
        part = slice(half * lanes, (half + 1) * lanes)
        far, near = far_ref[:level_count, :], near_ref[:level_count, :]
        if half:
            far = unpacked_side(far_ref[level_count:, :], level_count)
            near = unpacked_side(near_ref[level_count:, :], level_count)
        wave = average_y([field_ref[span, part] for span in spans], far, near)
        for r, (span, row) in enumerate(zip(spans, wave)):
            wave_ref[span, part] = row
            if half == 0:
                before = sum_ref[pl.ds(r, level_count, stride=ROWS), :] if native else sum_ref[span]
                total_ref[span] = before + share * row
    slope_ref[...] = split_dot(wave_ref[...], high_ref[...], low_ref[...])
    for half, wind in enumerate((wind_ref, wind_side_ref)):
        part = slice(half * lanes, (half + 1) * lanes)
        for span, change in zip(spans, change_rows(wave_ref, slope_ref, wind, part, spans)):
            change_ref[span, part] = change
    write_averaged(
        change_ref[...], average_ref, out_ref, far_out_ref, near_out_ref, level_count, native
    )


def last_kernel(share, field_ref, far_ref, near_ref, sum_ref, total_ref):
    level_count, lanes = far_ref.shape
    spans = [slice(r * level_count, (r + 1) * level_count) for r in range(ROWS)]
    wave = average_y([field_ref[span, :lanes] for span in spans], far_ref[...], near_ref[...])
    for r, (span, row) in enumerate(zip(spans, wave)):
        total_ref[pl.ds(r, level_count, stride=ROWS), :] = sum_ref[span] + share * row


def swapped(far, near):
    count = lax.axis_size("gy")
    far_pairs = [(i, (i - 1 if i % 2 == 0 else i + 1) % count) for i in range(count)]
    near_pairs = [(i, i + 1 if i % 2 == 0 else i - 1) for i in range(count)]
    return lax.ppermute(far, "gy", far_pairs), lax.ppermute(near, "gy", near_pairs)


def local(
    atmospheric_constituents,
    thermal_ratio,
    flow_velocity,
    solar_elevation_factor,
    ground_reflectivity,
    sunlit_indicator,
    molecular_optics_lookup,
    condensate_optics_lookup,
):
    level_count, rows, lanes = thermal_ratio.shape
    size = level_count * rows
    temper = thermal_ratio.reshape(size, lanes)
    flow = flow_velocity.reshape(2, size, lanes)
    field = jax.ShapeDtypeStruct((size, lanes), jnp.float32)
    wide = jax.ShapeDtypeStruct((size, 2 * lanes), jnp.float32)
    extra = -(-(level_count // 8) * 2 * MARGIN // lanes) * 8
    line = jax.ShapeDtypeStruct((level_count + extra, lanes), jnp.float32)
    short = jax.ShapeDtypeStruct((level_count, lanes), jnp.float32)
    wide_scratch = pltpu.VMEM(wide.shape, jnp.float32)
    whole = pl.BlockSpec(memory_space=pltpu.VMEM)

    def call(kernel, name, outs, scratch, *values):
        return pl.pallas_call(
            kernel, out_shape=outs,
            in_specs=[whole] * len(values),
            out_specs=jax.tree.map(lambda _: whole, outs), scratch_shapes=[wide_scratch] * scratch,
            compiler_params=pltpu.CompilerParams(vmem_limit_bytes=40 * 1024 * 1024), name=name,
        )(*values)

    slopes = slope_matrices(lanes)
    average = average_matrix(lanes)
    heat, change, wind, first, last = radiation(
        atmospheric_constituents, temper, flow, solar_elevation_factor,
        ground_reflectivity, sunlit_indicator, molecular_optics_lookup, condensate_optics_lookup,
    )
    before, after = shifted(last, "gx", 1), shifted(first, "gx", -1)
    back = edge_matrix(level_count, lanes).T
    wave, far, near, wind_side = call(
        first_stage_kernel, "first_stage",
        (wide, line, line, jax.ShapeDtypeStruct((2, size, lanes), jnp.float32)), 1,
        change, before, after, back, average,
    )
    far, near = swapped(far, near)
    wave, far, near, total = call(
        functools.partial(next_stage_kernel, 1.0, True), "second_stage",
        (wide, line, line, field), 3, wave, far, near, wind, wind_side, temper, *slopes, average,
    )
    far, near = swapped(far, near)
    wave, far, near, total = call(
        functools.partial(next_stage_kernel, 0.5, False), "third_stage",
        (wide, short, short, field), 3, wave, far, near, wind, wind_side, total, *slopes, average,
    )
    far, near = swapped(far, near)
    total = call(
        functools.partial(last_kernel, 1.0 / 6.0), "last_stage", field, 0,
        wave, far, near, total,
    )
    return (heat.reshape(thermal_ratio.shape), total.reshape(thermal_ratio.shape))


def solution(mesh):
    in_specs = (
        P(None, None, "gy", "gx"),
        P(None, "gy", "gx"),
        P(None, None, "gy", "gx"),
        P("gy", "gx"),
        P("gy", "gx"),
        P("gy", "gx"),
        P(),
        P(),
    )
    out_specs = (P(None, "gy", "gx"), P(None, "gy", "gx"))
    return jax.shard_map(local, mesh=mesh, in_specs=in_specs, out_specs=out_specs, check_vma=False)
```

```python
import functools

import jax
import jax.numpy as jnp
import numpy as np
from jax import lax
from jax.experimental import pallas as pl
from jax.experimental.pallas import tpu as pltpu
from jax.sharding import PartitionSpec as P

NODES = 4
TIME_INCREMENT = 0.05
ROWS = 8
MARGIN = 8
LOG2E = 1.4426950408889634

GROUP = 8
TERMS = 16
BLOCK = 12
PARTIAL = 5
DOWN = 24
CHUNKS = 2
QUANTITIES = 4


def shifted(value, axis, steps):
    count = lax.axis_size(axis)
    return lax.ppermute(value, axis, [(i, (i + steps) % count) for i in range(count)])


def gll_derivative():
    points = np.array([-1.0, -1.0 / np.sqrt(5.0), 1.0 / np.sqrt(5.0), 1.0])
    legendre = 0.5 * (5.0 * points**3 - 3.0 * points)
    derivative = np.zeros((4, 4))
    for source in range(4):
        for target in range(4):
            if source != target:
                derivative[source, target] = legendre[source] / (
                    legendre[target] * (points[source] - points[target])
                )
    derivative[0, 0] = -3.0
    derivative[3, 3] = 3.0
    return derivative


def high_low(values):
    high = values.astype(jnp.bfloat16)
    return high, (values - high.astype(jnp.float32)).astype(jnp.bfloat16)


def across(left, right, precision=None):
    return lax.dot_general(
        left, right, (((0,), (0,)), ((), ())), precision=precision,
        preferred_element_type=jnp.float32,
    )


def optics_matrices(molecular_ref, table_ref, optics_ref, weight_ref):
    level_count, gpoints = molecular_ref.shape[1:]
    groups = level_count // GROUP
    width = GROUP * TERMS
    level = lax.broadcasted_iota(jnp.int32, (level_count, groups * width), 0)
    lane = lax.broadcasted_iota(jnp.int32, (level_count, groups * width), 1)
    here = level == lane // TERMS
    term = lane % TERMS
    gases = []
    for k in range(3):
        high, low = high_low(molecular_ref[k])
        spread = [
            jnp.where(here & chosen, 1.0, 0.0).astype(jnp.bfloat16)
            for chosen in ((term == k) | (term == k + 10), term == k + 5)
        ]
        gases.append(across(high, spread[0]) + across(low, spread[1]))
    w = [table_ref[n : n + 1, :] for n in range(7)]
    ls, li = w[0] * w[1], w[3] * w[4]
    la, ia = w[0] * (1.0 - w[1]), w[3] * (1.0 - w[4])
    place = lax.broadcasted_iota(jnp.int32, (8, width), 0)
    term = lax.broadcasted_iota(jnp.int32, (8, width), 1) % TERMS
    pattern = jnp.zeros((8, width), jnp.float32)
    for n, chosen in enumerate((
        (term == 3) | (term == 13), term == 8, (term == 4) | (term == 14), term == 9
    )):
        pattern = jnp.where((place == n) & chosen, 1.0, pattern)
    empty = jnp.zeros((4, gpoints), jnp.float32)

    def water(*values):
        parts = []
        for value in values:
            high = value.astype(jnp.bfloat16).astype(jnp.float32)
            parts += [high, value - high]
        return across(jnp.concatenate(parts + [empty], axis=0), pattern, lax.Precision.HIGHEST)

    absorbed = gases[0] + gases[1]
    gas = absorbed + gases[2]
    pairs = (
        (absorbed, water(la, ia)),
        (gas, water(la + ls * (1.0 - w[2]), ia + li * (1.0 - w[5]))),
        (gas + gas, water(2.0 * w[0], 2.0 * w[3])),
        (gases[2], water(ls * (1.0 + w[2]), li * (1.0 + w[5]))),
    )
    chunk = gpoints // CHUNKS
    for group in range(groups):
        span = slice(group * width, (group + 1) * width)
        tables = [values[:, span] + constant for values, constant in pairs]
        for c in range(CHUNKS):
            rows = [table[c * chunk : (c + 1) * chunk] for table in tables]
            optics_ref[group, c] = jnp.concatenate(rows, axis=0).astype(jnp.bfloat16)
    only = jnp.where(place == 0, 1.0, 0.0)
    weight = jnp.broadcast_to(w[6], (8, gpoints))
    weight_ref[...] = across(weight, only, lax.Precision.HIGHEST)


def layer_terms(state_ref, temp_ref, level):
    lines = state_ref.shape[2]
    thickness = state_ref[2, level]
    temper = temp_ref[pl.ds(pl.multiple_of(level * lines, 8), lines), :]
    weighted = thickness * temper * temper
    return (
        weighted * state_ref[0, level], weighted * state_ref[1, level], thickness,
        state_ref[3, level], state_ref[4, level],
    )


def write_terms(terms_ref, level, values, lines):
    parts = [None] * TERMS
    for k, value in enumerate(values):
        high = value.astype(jnp.bfloat16).astype(jnp.float32)
        parts[k], parts[k + 5], parts[k + 10] = high, high, value - high
    parts[15] = jnp.zeros_like(values[0])
    for k, part in enumerate(parts):
        start = (level * TERMS + k) * lines
        start = pl.multiple_of(start, 8) if lines % 8 == 0 else start
        terms_ref[pl.ds(start, lines), :] = part


def sweep_row(
    row, line, lines, count, cosine, ground, optics_ref, weight_ref, terms_ref, right_ref,
    depths_0, depths_1, gain_ref, offset_ref, direct_ref, partial_ref, ratio_ref, source_ref, slant_ref,
):
    level_count, gpoints, lanes = gain_ref.shape
    blocks = level_count // BLOCK
    chunk = gpoints // CHUNKS
    slots = (depths_0, depths_1)
    once = 1 + jnp.minimum(row, 0)

    def place_group(group, carry=None):
        for j in range(GROUP):
            start = (group * GROUP + j) * TERMS * lines + line
            tile = terms_ref[pl.ds(start, TERMS, stride=lines), :].astype(jnp.bfloat16)
            half = lanes * (j % 2)
            pair = group * (GROUP // 2) + j // 2
            right_ref[pair, TERMS * j : TERMS * (j + 1), half : half + lanes] = tile
        return carry

    groups = level_count // GROUP
    ready = -(-BLOCK // GROUP)
    for group in range(groups - ready, groups):
        place_group(group)
    slant_ref[...] = jnp.broadcast_to((-0.5 * LOG2E) / cosine, (8, lanes))

    def over_rows(values):
        return jnp.broadcast_to(values[None], (gpoints // 8, 8, lanes)).reshape(gpoints, lanes)

    clear = 1.0 / (1.0 - ground)
    ratio_ref[...] = over_rows(jnp.broadcast_to((1.0 + ground) * clear, (8, lanes)))
    source_ref[...] = over_rows(jnp.broadcast_to(2.0 * ground * clear, (8, lanes)))

    def fill(block, c):
        for p in range(BLOCK // 2):
            pair = block * (BLOCK // 2) + p
            slots[c % 2][p] = jnp.dot(
                optics_ref[pair // (GROUP // 2), c], right_ref[pair],
                preferred_element_type=jnp.float32,
            )

    def below(block, c):
        span = slice(c * chunk, (c + 1) * chunk)
        ratio, source = ratio_ref[span], source_ref[span]
        slant = jnp.broadcast_to(slant_ref[...][None], (chunk // 8, 8, lanes))
        slant = slant.reshape(chunk, lanes)
        for j in reversed(range(BLOCK)):
            level = block * BLOCK + j
            part = slots[c % 2].at[j // 2, :, (j % 2) * lanes : (j % 2 + 1) * lanes]
            a, b, depth, along = [part[n * chunk : (n + 1) * chunk] for n in range(QUANTITIES)]
            away = b - a
            square = a * b
            inverse_root = lax.rsqrt(square)
            h = jnp.tanh(square * inverse_root)
            g = h * inverse_root
            g = g + g
            s, p = a * g, b * g
            h2 = h * h
            one = 1.0 + h2
            through = 1.0 - h2
            inverse = 1.0 / (one + s * ratio)
            direct = jnp.exp2(depth * slant)
            factor = (1.0 - direct) * (1.0 / depth)
            up, down = factor * away, factor * along
            push = inverse * (direct * source + (ratio - 1.0) * down)
            ratio = (one * ratio + p) * inverse
            gain = through * inverse
            source = through * push + (ratio + 1.0) * up
            gain_ref[level, span] = gain
            offset_ref[level, span] = (gain * up + down) - s * push
            direct_ref[level, span] = direct
        ratio_ref[span] = ratio
        source_ref[span] = source

    def below_block(step, carry):
        block = blocks - 1 - step
        for c in range(CHUNKS):
            def turn(n, carry, c=c):
                below(block, c)
                if c + 1 < CHUNKS:
                    fill(block, c + 1)
                else:
                    fill(jnp.maximum(block - 1, 0), 0)
                return carry

            lax.fori_loop(0, once, turn, 0)
        return carry

    fill(blocks - 1, 0)
    for group in range(groups - ready):
        place_group(group)
    lax.fori_loop(0, blocks, below_block, 0)

    def folded(net):
        return sum(net[8 * k : 8 * (k + 1)] for k in range(gpoints // 8))

    def top(step, carry):
        beam = weight_ref[...] * cosine
        net = -(source_ref[...] * beam) / (1.0 + ratio_ref[...])
        partial_ref[pl.ds(pl.multiple_of(row * 8, 8), 8), :] = folded(beam) + folded(net)
        return net, beam

    nothing = jnp.zeros((gpoints, lanes), jnp.float32)
    carry = lax.fori_loop(0, once, top, (nothing, nothing))

    def down_group(group, carry):
        net, beam = carry
        for j in range(DOWN):
            level = group * DOWN + j
            net = gain_ref[level] * net + offset_ref[level] * beam
            beam = beam * direct_ref[level]
            start = pl.multiple_of(((level + 1) * count + row) * 8, 8)
            partial_ref[pl.ds(start, 8), :] = folded(net) + folded(beam)
        return (net, beam)

    lax.fori_loop(0, level_count // DOWN, down_group, carry)


def level_heating(partial_ref, level_count, gpoints, count, write):
    def flux(level):
        start = level * count * 8
        return sum(partial_ref[pl.ds(start + k, count, stride=8), :] for k in range(8))

    def step(level, upper):
        lower = flux(level + 1)
        write(level, (level_count / gpoints) * (upper - lower))
        return lower

    lax.fori_loop(0, level_count, step, flux(0), unroll=4)


def radiation_kernel(
    state_ref, temp_ref, flow_ref, cosine_ref, ground_ref, day_ref, molecular_ref, table_ref,
    edge_ref, high_ref, low_ref,
    heat_ref, change_ref, wind_ref, first_ref, last_ref,
    optics_ref, weight_ref, strip_ref, slope_ref, terms_ref, right_ref, *scratch,
):
    level_count, lines, lanes = state_ref.shape[1:]
    gpoints = weight_ref.shape[0]
    row, count = pl.program_id(0), pl.num_programs(0)

    @pl.when(row == 0)
    def prepare():
        optics_matrices(molecular_ref, table_ref, optics_ref, weight_ref)
        prepare_terms(state_ref, temp_ref, terms_ref, right_ref)

    sweep_row(
        row, row, lines, count, cosine_ref[pl.ds(row, 1), :], ground_ref[pl.ds(row, 1), :],
        optics_ref, weight_ref, terms_ref, right_ref, *scratch,
    )

    @pl.when(row == count - 1)
    def finish():
        day = day_ref[...] == 1

        def write(level, value):
            start = pl.multiple_of(level * lines, 8)
            heat_ref[pl.ds(start, lines), :] = jnp.where(day, value, 0.0)

        level_heating(scratch[PARTIAL], level_count, gpoints, lines, write)
        spans = [slice(r * level_count, (r + 1) * level_count) for r in range(lines)]
        for r, span in enumerate(spans):
            native = pl.ds(r, level_count, stride=lines)
            change_ref[span, :] = temp_ref[native, :]
            for n in range(2):
                wind_ref[n, span, :] = flow_ref[n, native, :]
        slope_ref[...] = split_dot(
            change_ref[...], high_ref[:lanes, :lanes], low_ref[:lanes, :lanes]
        )
        changes = change_rows(change_ref, slope_ref, wind_ref, slice(0, lanes), spans)
        for r, (span, change) in enumerate(zip(spans, changes)):
            own = heat_ref[pl.ds(r, level_count, stride=lines), :]
            change_ref[span, :] = change + TIME_INCREMENT * own
        for n, ref in enumerate((change_ref, wind_ref.at[0], wind_ref.at[1])):
            for r in range(lines):
                here = slice(8 * (lines * n + r), 8 * (lines * n + r + 1))
                for k in range(level_count // 8):
                    start = r * level_count + 8 * k
                    strip_ref[here, lanes * k : lanes * (k + 1)] = ref[start : start + 8, :]
        packed = split_dot(strip_ref[...], edge_ref[...])
        size = 8 * lines
        used = (MARGIN + 1) * (level_count // 8)
        lane = lax.broadcasted_iota(jnp.int32, (size, lanes), 1)
        for ref, part in ((first_ref, slice(0, lanes)), (last_ref, slice(lanes, 2 * lanes))):
            one, two, three = [packed[size * n : size * (n + 1), part] for n in range(3)]
            turned = pltpu.roll(two, used, 1)
            ref[:size, :] = jnp.where(lane >= used, turned, one)
            rest = 2 * used - lanes
            ref[size:, :] = jnp.where(lane < rest, turned, pltpu.roll(three, rest, 1))


def prepare_terms(state_ref, temp_ref, terms_ref, right_ref):
    level_count, lines = state_ref.shape[1:3]
    right_ref[...] = jnp.zeros_like(right_ref)

    def level(l, carry):
        write_terms(terms_ref, l, layer_terms(state_ref, temp_ref, l), lines)
        return carry

    lax.fori_loop(0, level_count, level, 0, unroll=4)


def radiation(state, temper, flow, cosine, ground, day, molecular, condensate):
    level_count, rows, lanes = state.shape[1:]
    gpoints = molecular.shape[1]
    full = pltpu.VMEM((level_count, gpoints, lanes), jnp.float32)
    plane = pltpu.VMEM((gpoints, lanes), jnp.float32)
    whole = pl.BlockSpec(memory_space=pltpu.VMEM)
    part = (QUANTITIES * gpoints // CHUNKS, GROUP * TERMS)
    depths = pltpu.VMEM((BLOCK // 2, part[0], 2 * lanes), jnp.float32)
    field = jax.ShapeDtypeStruct((level_count * rows, lanes), jnp.float32)
    wind = jax.ShapeDtypeStruct((2, level_count * rows, lanes), jnp.float32)
    edge = jax.ShapeDtypeStruct((2 * 8 * rows, lanes), jnp.float32)
    cells = level_count * gpoints * rows * lanes
    return pl.pallas_call(
        radiation_kernel,
        out_shape=(field, field, wind, edge, edge),
        grid=(rows,), in_specs=[whole] * 11, out_specs=(whole,) * 5,
        scratch_shapes=[
            pltpu.VMEM((level_count // GROUP, CHUNKS) + part, jnp.bfloat16),
            plane,
            pltpu.VMEM((3 * 8 * rows, level_count // 8 * lanes), jnp.float32),
            pltpu.VMEM((level_count * rows, lanes), jnp.float32),
            pltpu.VMEM((level_count * TERMS * rows, lanes), jnp.float32),
            pltpu.VMEM((level_count // 2, GROUP * TERMS, 2 * lanes), jnp.bfloat16),
            depths, depths, full, full, full,
            pltpu.VMEM(((level_count + 1) * rows * 8, lanes), jnp.float32),
            plane, plane,
            pltpu.VMEM((8, lanes), jnp.float32),
        ],
        compiler_params=pltpu.CompilerParams(vmem_limit_bytes=60 * 1024 * 1024),
        cost_estimate=pl.CostEstimate(
            flops=10000 * cells, bytes_accessed=4 * 9 * temper.size, transcendentals=5 * cells
        ),
        name="radiation",
    )(
        state, temper, flow, cosine, ground, day, molecular.transpose(0, 2, 1), condensate,
        edge_matrix(level_count, lanes), *slope_matrices(lanes),
    )


def edge_matrix(level_count, lanes):
    parts = level_count // 8
    width = MARGIN + 1
    matrix = np.zeros((parts * lanes, 2 * lanes), np.float32)
    for k in range(parts):
        for c in range(width):
            matrix[lanes * k + c, width * k + c] = 1.0
            matrix[lanes * (k + 1) - width + c, lanes + width * k + c] = 1.0
    return jnp.asarray(matrix, jnp.bfloat16)


def slope_matrices(lanes):
    whole = np.kron(np.eye(2 * lanes // NODES), gll_derivative().T).astype(np.float32)
    high = np.asarray(whole, jnp.bfloat16)
    low = np.asarray(whole - high.astype(np.float32), jnp.bfloat16)
    return jnp.asarray(high), jnp.asarray(low)


def average_matrix(lanes):
    size = 2 * lanes
    matrix = np.eye(size, dtype=np.float32)
    for c in range(NODES - 1, size, NODES):
        after = (c + 1) % size
        matrix[c, c] = matrix[after, after] = matrix[c, after] = matrix[after, c] = 0.5
    return jnp.asarray(matrix, jnp.bfloat16)


def split_dot(values, *matrices):
    high, low = high_low(values)
    total = jnp.dot(high, matrices[0], preferred_element_type=jnp.float32)
    total = total + jnp.dot(low, matrices[0], preferred_element_type=jnp.float32)
    if len(matrices) > 1:
        total = total + jnp.dot(high, matrices[1], preferred_element_type=jnp.float32)
    return total


def slope_y(rows_of):
    derivative = gll_derivative()
    result = []
    for r in range(len(rows_of)):
        first = r // NODES * NODES
        total = None
        for n in range(NODES):
            weight = derivative[r - first, n]
            if abs(weight) > 1e-12:
                term = np.float32(weight) * rows_of[first + n]
                total = term if total is None else total + term
        result.append(total)
    return result


def average_y(rows_of, far, near):
    below = jnp.where(even_row(), far, near)
    above = jnp.where(even_row(), near, far)
    result = list(rows_of)
    count = len(rows_of)
    for r in range(NODES - 1, count - 1, NODES):
        result[r] = result[r + 1] = 0.5 * (rows_of[r] + rows_of[r + 1])
    result[0] = 0.5 * (below + rows_of[0])
    result[count - 1] = 0.5 * (rows_of[count - 1] + above)
    return result


def first_stage_kernel(
    change_ref, before_ref, after_ref, edge_ref, average_ref,
    out_ref, far_ref, near_ref, wind_side_ref, wide_ref,
):
    lanes = change_ref.shape[1]
    level_count = change_ref.shape[0] // ROWS
    wide_ref[:, :lanes] = change_ref[...]
    size = 8 * ROWS
    used = (MARGIN + 1) * (level_count // 8)
    lane = lax.broadcasted_iota(jnp.int32, (size, lanes), 1)
    fields = []
    for ref in (after_ref, before_ref):
        one, two = ref[:size, :], ref[size:, :]
        middle = pltpu.roll(jnp.where(lane >= used, one, two), lanes - used, 1)
        last = pltpu.roll(two, 2 * (lanes - used), 1)
        fields.append(jnp.concatenate([one, middle, last], axis=0))
    sides = split_dot(jnp.concatenate(fields, axis=1), edge_ref[...])
    for r in range(ROWS):
        for k in range(level_count // 8):
            span = slice(r * level_count + 8 * k, r * level_count + 8 * (k + 1))
            part = slice(lanes * k, lanes * (k + 1))
            wide_ref[span, lanes:] = sides[8 * r : 8 * (r + 1), part]
            for n in range(2):
                here = 8 * (ROWS * (n + 1) + r)
                wind_side_ref[n, span, :] = sides[here : here + 8, part]
    write_averaged(wide_ref[...], average_ref, out_ref, far_ref, near_ref, level_count, True)


def change_rows(field_ref, slope_ref, wind_ref, part, spans):
    slopes = slope_y([field_ref[span, part] for span in spans])
    result = []
    for span, slope in zip(spans, slopes):
        change = wind_ref[0, span, :] * slope_ref[span, part] + wind_ref[1, span, :] * slope
        result.append(-TIME_INCREMENT * change)
    return result


def even_row():
    return lax.axis_index("gy") % 2 == 0


def packed_side(side):
    lanes = side.shape[1]
    lane = lax.broadcasted_iota(jnp.int32, (8, lanes), 1)
    fit = lanes // (2 * MARGIN)
    tiles = []
    for k in range(side.shape[0] // 8):
        turned = pltpu.roll(side[8 * k : 8 * (k + 1)], (MARGIN + 2 * MARGIN * (k % fit)) % lanes, 1)
        if k % fit == 0:
            tiles.append(turned)
        else:
            tiles[-1] = jnp.where(lane // (2 * MARGIN) == k % fit, turned, tiles[-1])
    return tiles


def unpacked_side(tiles, level_count):
    lanes = tiles.shape[1]
    fit = lanes // (2 * MARGIN)
    result = []
    for k in range(level_count // 8):
        tile = tiles[8 * (k // fit) : 8 * (k // fit + 1)]
        result.append(pltpu.roll(tile, (lanes - MARGIN - 2 * MARGIN * (k % fit)) % lanes, 1))
    return jnp.concatenate(result, axis=0)


def write_averaged(change, average_ref, out_ref, far_ref, near_ref, level_count, with_side):
    lanes = far_ref.shape[1]
    out_ref[...] = split_dot(change, average_ref[...])
    parts = [slice(0, lanes), slice(lanes, 2 * lanes)] if with_side else [slice(0, lanes)]
    for n, part in enumerate(parts):
        first = out_ref[:level_count, part]
        last = out_ref[out_ref.shape[0] - level_count :, part]
        far = jnp.where(even_row(), first, last)
        near = jnp.where(even_row(), last, first)
        for ref, line in ((far_ref, far), (near_ref, near)):
            if n == 0:
                ref[:level_count, :] = line
                continue
            for k, tile in enumerate(packed_side(line)):
                ref[level_count + 8 * k : level_count + 8 * (k + 1), :] = tile


def next_stage_kernel(
    share, native, field_ref, far_ref, near_ref, wind_ref, wind_side_ref, sum_ref, high_ref,
    low_ref, average_ref, out_ref, far_out_ref, near_out_ref, total_ref, wave_ref, slope_ref, change_ref,
):
    level_count = field_ref.shape[0] // ROWS
    lanes = sum_ref.shape[1]
    spans = [slice(r * level_count, (r + 1) * level_count) for r in range(ROWS)]
    for half in range(2):
        part = slice(half * lanes, (half + 1) * lanes)
        far, near = far_ref[:level_count, :], near_ref[:level_count, :]
        if half:
            far = unpacked_side(far_ref[level_count:, :], level_count)
            near = unpacked_side(near_ref[level_count:, :], level_count)
        wave = average_y([field_ref[span, part] for span in spans], far, near)
        for r, (span, row) in enumerate(zip(spans, wave)):
            wave_ref[span, part] = row
            if half == 0:
                before = sum_ref[pl.ds(r, level_count, stride=ROWS), :] if native else sum_ref[span]
                total_ref[span] = before + share * row
    slope_ref[...] = split_dot(wave_ref[...], high_ref[...], low_ref[...])
    for half, wind in enumerate((wind_ref, wind_side_ref)):
        part = slice(half * lanes, (half + 1) * lanes)
        for span, change in zip(spans, change_rows(wave_ref, slope_ref, wind, part, spans)):
            change_ref[span, part] = change
    write_averaged(
        change_ref[...], average_ref, out_ref, far_out_ref, near_out_ref, level_count, native
    )


def last_kernel(share, field_ref, far_ref, near_ref, sum_ref, total_ref):
    level_count, lanes = far_ref.shape
    spans = [slice(r * level_count, (r + 1) * level_count) for r in range(ROWS)]
    wave = average_y([field_ref[span, :lanes] for span in spans], far_ref[...], near_ref[...])
    for r, (span, row) in enumerate(zip(spans, wave)):
        total_ref[pl.ds(r, level_count, stride=ROWS), :] = sum_ref[span] + share * row


def swapped(far, near):
    count = lax.axis_size("gy")
    far_pairs = [(i, (i - 1 if i % 2 == 0 else i + 1) % count) for i in range(count)]
    near_pairs = [(i, i + 1 if i % 2 == 0 else i - 1) for i in range(count)]
    return lax.ppermute(far, "gy", far_pairs), lax.ppermute(near, "gy", near_pairs)


def local(
    atmospheric_constituents,
    thermal_ratio,
    flow_velocity,
    solar_elevation_factor,
    ground_reflectivity,
    sunlit_indicator,
    molecular_optics_lookup,
    condensate_optics_lookup,
):
    level_count, rows, lanes = thermal_ratio.shape
    size = level_count * rows
    temper = thermal_ratio.reshape(size, lanes)
    flow = flow_velocity.reshape(2, size, lanes)
    field = jax.ShapeDtypeStruct((size, lanes), jnp.float32)
    wide = jax.ShapeDtypeStruct((size, 2 * lanes), jnp.float32)
    extra = -(-(level_count // 8) * 2 * MARGIN // lanes) * 8
    line = jax.ShapeDtypeStruct((level_count + extra, lanes), jnp.float32)
    short = jax.ShapeDtypeStruct((level_count, lanes), jnp.float32)
    wide_scratch = pltpu.VMEM(wide.shape, jnp.float32)
    whole = pl.BlockSpec(memory_space=pltpu.VMEM)

    def call(kernel, name, outs, scratch, *values):
        return pl.pallas_call(
            kernel, out_shape=outs,
            in_specs=[whole] * len(values),
            out_specs=jax.tree.map(lambda _: whole, outs), scratch_shapes=[wide_scratch] * scratch,
            compiler_params=pltpu.CompilerParams(vmem_limit_bytes=40 * 1024 * 1024), name=name,
        )(*values)

    slopes = slope_matrices(lanes)
    average = average_matrix(lanes)
    heat, change, wind, first, last = radiation(
        atmospheric_constituents, temper, flow, solar_elevation_factor,
        ground_reflectivity, sunlit_indicator, molecular_optics_lookup, condensate_optics_lookup,
    )
    before, after = shifted(last, "gx", 1), shifted(first, "gx", -1)
    back = edge_matrix(level_count, lanes).T
    wave, far, near, wind_side = call(
        first_stage_kernel, "first_stage",
        (wide, line, line, jax.ShapeDtypeStruct((2, size, lanes), jnp.float32)), 1,
        change, before, after, back, average,
    )
    far, near = swapped(far, near)
    wave, far, near, total = call(
        functools.partial(next_stage_kernel, 1.0, True), "second_stage",
        (wide, line, line, field), 3, wave, far, near, wind, wind_side, temper, *slopes, average,
    )
    far, near = swapped(far, near)
    wave, far, near, total = call(
        functools.partial(next_stage_kernel, 0.5, False), "third_stage",
        (wide, short, short, field), 3, wave, far, near, wind, wind_side, total, *slopes, average,
    )
    far, near = swapped(far, near)
    total = call(
        functools.partial(last_kernel, 1.0 / 6.0), "last_stage", field, 0,
        wave, far, near, total,
    )
    return (heat.reshape(thermal_ratio.shape), total.reshape(thermal_ratio.shape))


def solution(mesh):
    in_specs = (
        P(None, None, "gy", "gx"),
        P(None, "gy", "gx"),
        P(None, None, "gy", "gx"),
        P("gy", "gx"),
        P("gy", "gx"),
        P("gy", "gx"),
        P(),
        P(),
    )
    out_specs = (P(None, "gy", "gx"), P(None, "gy", "gx"))
    return jax.shard_map(local, mesh=mesh, in_specs=in_specs, out_specs=out_specs, check_vma=False)
```

```python
import functools

import jax
import jax.numpy as jnp
import numpy as np
from jax import lax
from jax.experimental import pallas as pl
from jax.experimental.pallas import tpu as pltpu
from jax.sharding import PartitionSpec as P

NODES = 4
TIME_INCREMENT = 0.05
ROWS = 8
MARGIN = 8
LOG2E = 1.4426950408889634

GROUP = 8
TERMS = 16
BLOCK = 12
PARTIAL = 5
DOWN = 24
CHUNKS = 2
QUANTITIES = 4


def shifted(value, axis, steps):
    count = lax.axis_size(axis)
    return lax.ppermute(value, axis, [(i, (i + steps) % count) for i in range(count)])


def gll_derivative():
    points = np.array([-1.0, -1.0 / np.sqrt(5.0), 1.0 / np.sqrt(5.0), 1.0])
    legendre = 0.5 * (5.0 * points**3 - 3.0 * points)
    derivative = np.zeros((4, 4))
    for source in range(4):
        for target in range(4):
            if source != target:
                derivative[source, target] = legendre[source] / (
                    legendre[target] * (points[source] - points[target])
                )
    derivative[0, 0] = -3.0
    derivative[3, 3] = 3.0
    return derivative


def high_low(values):
    high = values.astype(jnp.bfloat16)
    return high, (values - high.astype(jnp.float32)).astype(jnp.bfloat16)


def across(left, right, precision=None):
    return lax.dot_general(
        left, right, (((0,), (0,)), ((), ())), precision=precision,
        preferred_element_type=jnp.float32,
    )


def optics_matrices(molecular_ref, table_ref, optics_ref, weight_ref):
    level_count, gpoints = molecular_ref.shape[1:]
    groups = level_count // GROUP
    width = GROUP * TERMS
    level = lax.broadcasted_iota(jnp.int32, (level_count, groups * width), 0)
    lane = lax.broadcasted_iota(jnp.int32, (level_count, groups * width), 1)
    here = level == lane // TERMS
    term = lane % TERMS
    gases = []
    for k in range(3):
        high, low = high_low(molecular_ref[k])
        spread = [
            jnp.where(here & chosen, 1.0, 0.0).astype(jnp.bfloat16)
            for chosen in ((term == k) | (term == k + 10), term == k + 5)
        ]
        gases.append(across(high, spread[0]) + across(low, spread[1]))
    w = [table_ref[n : n + 1, :] for n in range(7)]
    ls, li = w[0] * w[1], w[3] * w[4]
    la, ia = w[0] * (1.0 - w[1]), w[3] * (1.0 - w[4])
    place = lax.broadcasted_iota(jnp.int32, (8, width), 0)
    term = lax.broadcasted_iota(jnp.int32, (8, width), 1) % TERMS
    pattern = jnp.zeros((8, width), jnp.float32)
    for n, chosen in enumerate((
        (term == 3) | (term == 13), term == 8, (term == 4) | (term == 14), term == 9
    )):
        pattern = jnp.where((place == n) & chosen, 1.0, pattern)
    empty = jnp.zeros((4, gpoints), jnp.float32)

    def water(*values):
        parts = []
        for value in values:
            high = value.astype(jnp.bfloat16).astype(jnp.float32)
            parts += [high, value - high]
        return across(jnp.concatenate(parts + [empty], axis=0), pattern, lax.Precision.HIGHEST)

    absorbed = gases[0] + gases[1]
    gas = absorbed + gases[2]
    pairs = (
        (absorbed, water(la, ia)),
        (gas, water(la + ls * (1.0 - w[2]), ia + li * (1.0 - w[5]))),
        (gas + gas, water(2.0 * w[0], 2.0 * w[3])),
        (gases[2], water(ls * (1.0 + w[2]), li * (1.0 + w[5]))),
    )
    chunk = gpoints // CHUNKS
    for group in range(groups):
        span = slice(group * width, (group + 1) * width)
        tables = [values[:, span] + constant for values, constant in pairs]
        for c in range(CHUNKS):
            rows = [table[c * chunk : (c + 1) * chunk] for table in tables]
            optics_ref[group, c] = jnp.concatenate(rows, axis=0).astype(jnp.bfloat16)
    only = jnp.where(place == 0, 1.0, 0.0)
    weight = jnp.broadcast_to(w[6], (8, gpoints))
    weight_ref[...] = across(weight, only, lax.Precision.HIGHEST)


def layer_terms(state_ref, temp_ref, level):
    lines = state_ref.shape[2]
    thickness = state_ref[2, level]
    temper = temp_ref[pl.ds(pl.multiple_of(level * lines, 8), lines), :]
    weighted = thickness * temper * temper
    return (
        weighted * state_ref[0, level], weighted * state_ref[1, level], thickness,
        state_ref[3, level], state_ref[4, level],
    )


def write_terms(terms_ref, level, values, lines):
    parts = [None] * TERMS
    for k, value in enumerate(values):
        high = value.astype(jnp.bfloat16).astype(jnp.float32)
        parts[k], parts[k + 5], parts[k + 10] = high, high, value - high
    parts[15] = jnp.zeros_like(values[0])
    for k, part in enumerate(parts):
        start = (level * TERMS + k) * lines
        start = pl.multiple_of(start, 8) if lines % 8 == 0 else start
        terms_ref[pl.ds(start, lines), :] = part


def sweep_row(
    row, line, lines, count, cosine, ground, optics_ref, weight_ref, terms_ref, right_ref,
    depths_0, depths_1, gain_ref, offset_ref, direct_ref, partial_ref, ratio_ref, source_ref, slant_ref,
):
    level_count, gpoints, lanes = gain_ref.shape
    blocks = level_count // BLOCK
    chunk = gpoints // CHUNKS
    slots = (depths_0, depths_1)
    once = 1 + jnp.minimum(row, 0)

    def place_group(group, carry=None):
        for j in range(GROUP):
            start = (group * GROUP + j) * TERMS * lines + line
            tile = terms_ref[pl.ds(start, TERMS, stride=lines), :].astype(jnp.bfloat16)
            half = lanes * (j % 2)
            pair = group * (GROUP // 2) + j // 2
            right_ref[pair, TERMS * j : TERMS * (j + 1), half : half + lanes] = tile
        return carry

    groups = level_count // GROUP
    ready = -(-BLOCK // GROUP)
    for group in range(groups - ready, groups):
        place_group(group)
    slant_ref[...] = jnp.broadcast_to((-0.5 * LOG2E) / cosine, (8, lanes))

    def over_rows(values):
        return jnp.broadcast_to(values[None], (gpoints // 8, 8, lanes)).reshape(gpoints, lanes)

    clear = 1.0 / (1.0 - ground)
    ratio_ref[...] = over_rows(jnp.broadcast_to((1.0 + ground) * clear, (8, lanes)))
    source_ref[...] = over_rows(jnp.broadcast_to(2.0 * ground * clear, (8, lanes)))

    def fill(block, c):
        for p in range(BLOCK // 2):
            pair = block * (BLOCK // 2) + p
            slots[c % 2][p] = jnp.dot(
                optics_ref[pair // (GROUP // 2), c], right_ref[pair],
                preferred_element_type=jnp.float32,
            )

    def below(block, c):
        span = slice(c * chunk, (c + 1) * chunk)
        ratio, source = ratio_ref[span], source_ref[span]
        slant = jnp.broadcast_to(slant_ref[...][None], (chunk // 8, 8, lanes))
        slant = slant.reshape(chunk, lanes)
        for j in reversed(range(BLOCK)):
            level = block * BLOCK + j
            part = slots[c % 2].at[j // 2, :, (j % 2) * lanes : (j % 2 + 1) * lanes]
            a, b, depth, along = [part[n * chunk : (n + 1) * chunk] for n in range(QUANTITIES)]
            away = b - a
            square = a * b
            inverse_root = lax.rsqrt(square)
            h = jnp.tanh(square * inverse_root)
            g = h * inverse_root
            g = g + g
            s, p = a * g, b * g
            h2 = h * h
            one = 1.0 + h2
            through = 1.0 - h2
            inverse = 1.0 / (one + s * ratio)
            direct = jnp.exp2(depth * slant)
            factor = (1.0 - direct) * (1.0 / depth)
            up, down = factor * away, factor * along
            push = inverse * (direct * source + (ratio - 1.0) * down)
            ratio = (one * ratio + p) * inverse
            gain = through * inverse
            source = through * push + (ratio + 1.0) * up
            gain_ref[level, span] = gain
            offset_ref[level, span] = (gain * up + down) - s * push
            direct_ref[level, span] = direct
        ratio_ref[span] = ratio
        source_ref[span] = source

    def below_block(step, carry):
        block = blocks - 1 - step
        for c in range(CHUNKS):
            def turn(n, carry, c=c):
                below(block, c)
                if c + 1 < CHUNKS:
                    fill(block, c + 1)
                else:
                    fill(jnp.maximum(block - 1, 0), 0)
                return carry

            lax.fori_loop(0, once, turn, 0)
        return carry

    fill(blocks - 1, 0)
    for group in range(groups - ready):
        place_group(group)
    lax.fori_loop(0, blocks, below_block, 0)

    def folded(net):
        return sum(net[8 * k : 8 * (k + 1)] for k in range(gpoints // 8))

    def top(step, carry):
        beam = weight_ref[...] * cosine
        net = -(source_ref[...] * beam) / (1.0 + ratio_ref[...])
        partial_ref[pl.ds(pl.multiple_of(row * 8, 8), 8), :] = folded(beam) + folded(net)
        return net, beam

    nothing = jnp.zeros((gpoints, lanes), jnp.float32)
    carry = lax.fori_loop(0, once, top, (nothing, nothing))

    def down_group(group, carry):
        net, beam = carry
        for j in range(DOWN):
            level = group * DOWN + j
            net = gain_ref[level] * net + offset_ref[level] * beam
            beam = beam * direct_ref[level]
            start = pl.multiple_of(((level + 1) * count + row) * 8, 8)
            partial_ref[pl.ds(start, 8), :] = folded(net) + folded(beam)
        return (net, beam)

    lax.fori_loop(0, level_count // DOWN, down_group, carry)


def level_heating(partial_ref, level_count, gpoints, count, write):
    def flux(level):
        start = level * count * 8
        return sum(partial_ref[pl.ds(start + k, count, stride=8), :] for k in range(8))

    def step(level, upper):
        lower = flux(level + 1)
        write(level, (level_count / gpoints) * (upper - lower))
        return lower

    lax.fori_loop(0, level_count, step, flux(0), unroll=4)


def radiation_kernel(
    state_ref, temp_ref, flow_ref, cosine_ref, ground_ref, day_ref, molecular_ref, table_ref,
    edge_ref, high_ref, low_ref,
    heat_ref, change_ref, wind_ref, first_ref, last_ref,
    optics_ref, weight_ref, strip_ref, slope_ref, terms_ref, right_ref, *scratch,
):
    level_count, lines, lanes = state_ref.shape[1:]
    gpoints = weight_ref.shape[0]
    row, count = pl.program_id(0), pl.num_programs(0)

    @pl.when(row == 0)
    def prepare():
        optics_matrices(molecular_ref, table_ref, optics_ref, weight_ref)
        prepare_terms(state_ref, temp_ref, terms_ref, right_ref)

    sweep_row(
        row, row, lines, count, cosine_ref[pl.ds(row, 1), :], ground_ref[pl.ds(row, 1), :],
        optics_ref, weight_ref, terms_ref, right_ref, *scratch,
    )

    @pl.when(row == count - 1)
    def finish():
        day = day_ref[...] == 1

        def write(level, value):
            start = pl.multiple_of(level * lines, 8)
            heat_ref[pl.ds(start, lines), :] = jnp.where(day, value, 0.0)

        level_heating(scratch[PARTIAL], level_count, gpoints, lines, write)
        spans = [slice(r * level_count, (r + 1) * level_count) for r in range(lines)]
        for r, span in enumerate(spans):
            native = pl.ds(r, level_count, stride=lines)
            change_ref[span, :] = temp_ref[native, :]
            for n in range(2):
                wind_ref[n, span, :] = flow_ref[n, native, :]
        slope_ref[...] = split_dot(
            change_ref[...], high_ref[:lanes, :lanes], low_ref[:lanes, :lanes]
        )
        changes = change_rows(change_ref, slope_ref, wind_ref, slice(0, lanes), spans)
        for r, (span, change) in enumerate(zip(spans, changes)):
            own = heat_ref[pl.ds(r, level_count, stride=lines), :]
            change_ref[span, :] = change + TIME_INCREMENT * own
        for n, ref in enumerate((change_ref, wind_ref.at[0], wind_ref.at[1])):
            for r in range(lines):
                here = slice(8 * (lines * n + r), 8 * (lines * n + r + 1))
                for k in range(level_count // 8):
                    start = r * level_count + 8 * k
                    strip_ref[here, lanes * k : lanes * (k + 1)] = ref[start : start + 8, :]
        packed = split_dot(strip_ref[...], edge_ref[...])
        size = 8 * lines
        used = (MARGIN + 1) * (level_count // 8)
        lane = lax.broadcasted_iota(jnp.int32, (size, lanes), 1)
        for ref, part in ((first_ref, slice(0, lanes)), (last_ref, slice(lanes, 2 * lanes))):
            one, two, three = [packed[size * n : size * (n + 1), part] for n in range(3)]
            turned = pltpu.roll(two, used, 1)
            ref[:size, :] = jnp.where(lane >= used, turned, one)
            rest = 2 * used - lanes
            ref[size:, :] = jnp.where(lane < rest, turned, pltpu.roll(three, rest, 1))


def prepare_terms(state_ref, temp_ref, terms_ref, right_ref):
    level_count, lines = state_ref.shape[1:3]
    right_ref[...] = jnp.zeros_like(right_ref)

    def level(l, carry):
        write_terms(terms_ref, l, layer_terms(state_ref, temp_ref, l), lines)
        return carry

    lax.fori_loop(0, level_count, level, 0, unroll=4)


def radiation(state, temper, flow, cosine, ground, day, molecular, condensate):
    level_count, rows, lanes = state.shape[1:]
    gpoints = molecular.shape[1]
    full = pltpu.VMEM((level_count, gpoints, lanes), jnp.float32)
    plane = pltpu.VMEM((gpoints, lanes), jnp.float32)
    whole = pl.BlockSpec(memory_space=pltpu.VMEM)
    part = (QUANTITIES * gpoints // CHUNKS, GROUP * TERMS)
    depths = pltpu.VMEM((BLOCK // 2, part[0], 2 * lanes), jnp.float32)
    field = jax.ShapeDtypeStruct((level_count * rows, lanes), jnp.float32)
    wind = jax.ShapeDtypeStruct((2, level_count * rows, lanes), jnp.float32)
    edge = jax.ShapeDtypeStruct((2 * 8 * rows, lanes), jnp.float32)
    cells = level_count * gpoints * rows * lanes
    return pl.pallas_call(
        radiation_kernel,
        out_shape=(field, field, wind, edge, edge),
        grid=(rows,), in_specs=[whole] * 11, out_specs=(whole,) * 5,
        scratch_shapes=[
            pltpu.VMEM((level_count // GROUP, CHUNKS) + part, jnp.bfloat16),
            plane,
            pltpu.VMEM((3 * 8 * rows, level_count // 8 * lanes), jnp.float32),
            pltpu.VMEM((level_count * rows, lanes), jnp.float32),
            pltpu.VMEM((level_count * TERMS * rows, lanes), jnp.float32),
            pltpu.VMEM((level_count // 2, GROUP * TERMS, 2 * lanes), jnp.bfloat16),
            depths, depths, full, full, full,
            pltpu.VMEM(((level_count + 1) * rows * 8, lanes), jnp.float32),
            plane, plane,
            pltpu.VMEM((8, lanes), jnp.float32),
        ],
        compiler_params=pltpu.CompilerParams(vmem_limit_bytes=40 * 1024 * 1024),
        cost_estimate=pl.CostEstimate(
            flops=10000 * cells, bytes_accessed=4 * 9 * temper.size, transcendentals=5 * cells
        ),
        name="radiation",
    )(
        state, temper, flow, cosine, ground, day, molecular.transpose(0, 2, 1), condensate,
        edge_matrix(level_count, lanes), *slope_matrices(lanes),
    )


def edge_matrix(level_count, lanes):
    parts = level_count // 8
    width = MARGIN + 1
    matrix = np.zeros((parts * lanes, 2 * lanes), np.float32)
    for k in range(parts):
        for c in range(width):
            matrix[lanes * k + c, width * k + c] = 1.0
            matrix[lanes * (k + 1) - width + c, lanes + width * k + c] = 1.0
    return jnp.asarray(matrix, jnp.bfloat16)


def slope_matrices(lanes):
    whole = np.kron(np.eye(2 * lanes // NODES), gll_derivative().T).astype(np.float32)
    high = np.asarray(whole, jnp.bfloat16)
    low = np.asarray(whole - high.astype(np.float32), jnp.bfloat16)
    return jnp.asarray(high), jnp.asarray(low)


def average_matrix(lanes):
    size = 2 * lanes
    matrix = np.eye(size, dtype=np.float32)
    for c in range(NODES - 1, size, NODES):
        after = (c + 1) % size
        matrix[c, c] = matrix[after, after] = matrix[c, after] = matrix[after, c] = 0.5
    return jnp.asarray(matrix, jnp.bfloat16)


def split_dot(values, *matrices):
    high, low = high_low(values)
    total = jnp.dot(high, matrices[0], preferred_element_type=jnp.float32)
    total = total + jnp.dot(low, matrices[0], preferred_element_type=jnp.float32)
    if len(matrices) > 1:
        total = total + jnp.dot(high, matrices[1], preferred_element_type=jnp.float32)
    return total


def slope_y(rows_of):
    derivative = gll_derivative()
    result = []
    for r in range(len(rows_of)):
        first = r // NODES * NODES
        total = None
        for n in range(NODES):
            weight = derivative[r - first, n]
            if abs(weight) > 1e-12:
                term = np.float32(weight) * rows_of[first + n]
                total = term if total is None else total + term
        result.append(total)
    return result


def average_y(rows_of, far, near):
    below = jnp.where(even_row(), far, near)
    above = jnp.where(even_row(), near, far)
    result = list(rows_of)
    count = len(rows_of)
    for r in range(NODES - 1, count - 1, NODES):
        result[r] = result[r + 1] = 0.5 * (rows_of[r] + rows_of[r + 1])
    result[0] = 0.5 * (below + rows_of[0])
    result[count - 1] = 0.5 * (rows_of[count - 1] + above)
    return result


def first_stage_kernel(
    change_ref, before_ref, after_ref, edge_ref, average_ref,
    out_ref, far_ref, near_ref, wind_side_ref, wide_ref,
):
    lanes = change_ref.shape[1]
    level_count = change_ref.shape[0] // ROWS
    wide_ref[:, :lanes] = change_ref[...]
    size = 8 * ROWS
    used = (MARGIN + 1) * (level_count // 8)
    lane = lax.broadcasted_iota(jnp.int32, (size, lanes), 1)
    fields = []
    for ref in (after_ref, before_ref):
        one, two = ref[:size, :], ref[size:, :]
        middle = pltpu.roll(jnp.where(lane >= used, one, two), lanes - used, 1)
        last = pltpu.roll(two, 2 * (lanes - used), 1)
        fields.append(jnp.concatenate([one, middle, last], axis=0))
    sides = split_dot(jnp.concatenate(fields, axis=1), edge_ref[...])
    for r in range(ROWS):
        for k in range(level_count // 8):
            span = slice(r * level_count + 8 * k, r * level_count + 8 * (k + 1))
            part = slice(lanes * k, lanes * (k + 1))
            wide_ref[span, lanes:] = sides[8 * r : 8 * (r + 1), part]
            for n in range(2):
                here = 8 * (ROWS * (n + 1) + r)
                wind_side_ref[n, span, :] = sides[here : here + 8, part]
    write_averaged(wide_ref[...], average_ref, out_ref, far_ref, near_ref, level_count, True)


def change_rows(field_ref, slope_ref, wind_ref, part, spans):
    slopes = slope_y([field_ref[span, part] for span in spans])
    result = []
    for span, slope in zip(spans, slopes):
        change = wind_ref[0, span, :] * slope_ref[span, part] + wind_ref[1, span, :] * slope
        result.append(-TIME_INCREMENT * change)
    return result


def even_row():
    return lax.axis_index("gy") % 2 == 0


def packed_side(side):
    lanes = side.shape[1]
    lane = lax.broadcasted_iota(jnp.int32, (8, lanes), 1)
    fit = lanes // (2 * MARGIN)
    tiles = []
    for k in range(side.shape[0] // 8):
        turned = pltpu.roll(side[8 * k : 8 * (k + 1)], (MARGIN + 2 * MARGIN * (k % fit)) % lanes, 1)
        if k % fit == 0:
            tiles.append(turned)
        else:
            tiles[-1] = jnp.where(lane // (2 * MARGIN) == k % fit, turned, tiles[-1])
    return tiles


def unpacked_side(tiles, level_count):
    lanes = tiles.shape[1]
    fit = lanes // (2 * MARGIN)
    result = []
    for k in range(level_count // 8):
        tile = tiles[8 * (k // fit) : 8 * (k // fit + 1)]
        result.append(pltpu.roll(tile, (lanes - MARGIN - 2 * MARGIN * (k % fit)) % lanes, 1))
    return jnp.concatenate(result, axis=0)


def write_averaged(change, average_ref, out_ref, far_ref, near_ref, level_count, with_side):
    lanes = far_ref.shape[1]
    out_ref[...] = split_dot(change, average_ref[...])
    parts = [slice(0, lanes), slice(lanes, 2 * lanes)] if with_side else [slice(0, lanes)]
    for n, part in enumerate(parts):
        first = out_ref[:level_count, part]
        last = out_ref[out_ref.shape[0] - level_count :, part]
        far = jnp.where(even_row(), first, last)
        near = jnp.where(even_row(), last, first)
        for ref, line in ((far_ref, far), (near_ref, near)):
            if n == 0:
                ref[:level_count, :] = line
                continue
            for k, tile in enumerate(packed_side(line)):
                ref[level_count + 8 * k : level_count + 8 * (k + 1), :] = tile


def next_stage_kernel(
    share, native, field_ref, far_ref, near_ref, wind_ref, wind_side_ref, sum_ref, high_ref,
    low_ref, average_ref, out_ref, far_out_ref, near_out_ref, total_ref, wave_ref, slope_ref, change_ref,
):
    level_count = field_ref.shape[0] // ROWS
    lanes = sum_ref.shape[1]
    spans = [slice(r * level_count, (r + 1) * level_count) for r in range(ROWS)]
    for half in range(2):
        part = slice(half * lanes, (half + 1) * lanes)
        far, near = far_ref[:level_count, :], near_ref[:level_count, :]
        if half:
            far = unpacked_side(far_ref[level_count:, :], level_count)
            near = unpacked_side(near_ref[level_count:, :], level_count)
        wave = average_y([field_ref[span, part] for span in spans], far, near)
        for r, (span, row) in enumerate(zip(spans, wave)):
            wave_ref[span, part] = row
            if half == 0:
                before = sum_ref[pl.ds(r, level_count, stride=ROWS), :] if native else sum_ref[span]
                total_ref[span] = before + share * row
    slope_ref[...] = split_dot(wave_ref[...], high_ref[...], low_ref[...])
    for half, wind in enumerate((wind_ref, wind_side_ref)):
        part = slice(half * lanes, (half + 1) * lanes)
        for span, change in zip(spans, change_rows(wave_ref, slope_ref, wind, part, spans)):
            change_ref[span, part] = change
    write_averaged(
        change_ref[...], average_ref, out_ref, far_out_ref, near_out_ref, level_count, native
    )


def last_kernel(share, field_ref, far_ref, near_ref, sum_ref, total_ref):
    level_count, lanes = far_ref.shape
    spans = [slice(r * level_count, (r + 1) * level_count) for r in range(ROWS)]
    wave = average_y([field_ref[span, :lanes] for span in spans], far_ref[...], near_ref[...])
    for r, (span, row) in enumerate(zip(spans, wave)):
        total_ref[pl.ds(r, level_count, stride=ROWS), :] = sum_ref[span] + share * row


def swapped(far, near):
    count = lax.axis_size("gy")
    far_pairs = [(i, (i - 1 if i % 2 == 0 else i + 1) % count) for i in range(count)]
    near_pairs = [(i, i + 1 if i % 2 == 0 else i - 1) for i in range(count)]
    return lax.ppermute(far, "gy", far_pairs), lax.ppermute(near, "gy", near_pairs)


def local(
    atmospheric_constituents,
    thermal_ratio,
    flow_velocity,
    solar_elevation_factor,
    ground_reflectivity,
    sunlit_indicator,
    molecular_optics_lookup,
    condensate_optics_lookup,
):
    level_count, rows, lanes = thermal_ratio.shape
    size = level_count * rows
    temper = thermal_ratio.reshape(size, lanes)
    flow = flow_velocity.reshape(2, size, lanes)
    field = jax.ShapeDtypeStruct((size, lanes), jnp.float32)
    wide = jax.ShapeDtypeStruct((size, 2 * lanes), jnp.float32)
    extra = -(-(level_count // 8) * 2 * MARGIN // lanes) * 8
    line = jax.ShapeDtypeStruct((level_count + extra, lanes), jnp.float32)
    short = jax.ShapeDtypeStruct((level_count, lanes), jnp.float32)
    wide_scratch = pltpu.VMEM(wide.shape, jnp.float32)
    whole = pl.BlockSpec(memory_space=pltpu.VMEM)

    def call(kernel, name, outs, scratch, *values):
        return pl.pallas_call(
            kernel, out_shape=outs,
            in_specs=[whole] * len(values),
            out_specs=jax.tree.map(lambda _: whole, outs), scratch_shapes=[wide_scratch] * scratch,
            compiler_params=pltpu.CompilerParams(vmem_limit_bytes=40 * 1024 * 1024), name=name,
        )(*values)

    slopes = slope_matrices(lanes)
    average = average_matrix(lanes)
    heat, change, wind, first, last = radiation(
        atmospheric_constituents, temper, flow, solar_elevation_factor,
        ground_reflectivity, sunlit_indicator, molecular_optics_lookup, condensate_optics_lookup,
    )
    before, after = shifted(last, "gx", 1), shifted(first, "gx", -1)
    back = edge_matrix(level_count, lanes).T
    wave, far, near, wind_side = call(
        first_stage_kernel, "first_stage",
        (wide, line, line, jax.ShapeDtypeStruct((2, size, lanes), jnp.float32)), 1,
        change, before, after, back, average,
    )
    far, near = swapped(far, near)
    wave, far, near, total = call(
        functools.partial(next_stage_kernel, 1.0, True), "second_stage",
        (wide, line, line, field), 3, wave, far, near, wind, wind_side, temper, *slopes, average,
    )
    far, near = swapped(far, near)
    wave, far, near, total = call(
        functools.partial(next_stage_kernel, 0.5, False), "third_stage",
        (wide, short, short, field), 3, wave, far, near, wind, wind_side, total, *slopes, average,
    )
    far, near = swapped(far, near)
    total = call(
        functools.partial(last_kernel, 1.0 / 6.0), "last_stage", field, 0,
        wave, far, near, total,
    )
    return (heat.reshape(thermal_ratio.shape), total.reshape(thermal_ratio.shape))


def solution(mesh):
    in_specs = (
        P(None, None, "gy", "gx"),
        P(None, "gy", "gx"),
        P(None, None, "gy", "gx"),
        P("gy", "gx"),
        P("gy", "gx"),
        P("gy", "gx"),
        P(),
        P(),
    )
    out_specs = (P(None, "gy", "gx"), P(None, "gy", "gx"))
    return jax.shard_map(local, mesh=mesh, in_specs=in_specs, out_specs=out_specs, check_vma=False)
```
